32 devices in a mesh: tm: 8 (over z, x), seq: 4 (over y, core).
Axes of the slice: x: 2, y: 2, z: 4, core: 2. Of those that a mesh axis runs over, the one named last changes fastest.
Arguments:
- large_view: bfloat16 [8, 2048, 768], P('seq', 'tm'), may hold values from -6 to 6
- small_view: bfloat16 [8, 1024, 768], P('seq', 'tm'), may hold values from -6 to 6
- clip_ids: int32 [8, 2048], P('seq', 'tm'), may hold values from 0 to 3, as said below
- first_gain: bfloat16 [768], replicated, may hold values from 0.099609375 to 1.8984375
- query_weight: bfloat16 [768, 768], replicated, may hold values from -0.21875 to 0.21875
- key_weight: bfloat16 [768, 768], replicated, may hold values from -0.21875 to 0.21875
- value_weight: bfloat16 [768, 768], replicated, may hold values from -0.21875 to 0.21875
- output_weight: bfloat16 [768, 768], replicated, may hold values from -0.875 to 0.875
- second_gain: bfloat16 [768], replicated, may hold values from 0.099609375 to 1.8984375
- up_weight: bfloat16 [768, 3072], replicated, may hold values from -0.21875 to 0.21875
- down_weight: bfloat16 [3072, 768], replicated, may hold values from -0.109375 to 0.109375
- query_gain: bfloat16 [768], replicated, may hold values from 0.099609375 to 1.8984375
- context_gain: bfloat16 [768], replicated, may hold values from 0.099609375 to 1.8984375
- cross_query: bfloat16 [768, 768], replicated, may hold values from -0.21875 to 0.21875
- cross_key: bfloat16 [768, 768], replicated, may hold values from -0.21875 to 0.21875
- cross_value: bfloat16 [768, 768], replicated, may hold values from -0.21875 to 0.21875
- cross_output: bfloat16 [768, 768], replicated, may hold values from -0.875 to 0.875
- cotangent: bfloat16 [8, 2048, 768], P('seq', 'tm'), may hold values from -6 to 6
Outputs:
- united_view: bfloat16 [8, 2048, 768], P('seq', 'tm')
- large_grad: float32 [8, 2048, 768], P('seq', 'tm')
- small_grad: float32 [8, 1024, 768], P('seq', 'tm')
- first_gain_grad: float32 [768], P('tm')
- query_weight_grad: float32 [768, 768], P('tm')
- key_weight_grad: float32 [768, 768], P('tm')
- value_weight_grad: float32 [768, 768], P('tm')
- output_weight_grad: float32 [768, 768], P('tm')
- second_gain_grad: float32 [768], P('tm')
- up_weight_grad: float32 [768, 3072], P('tm')
- down_weight_grad: float32 [3072, 768], P('tm')
- query_gain_grad: float32 [768], P('tm')
- context_gain_grad: float32 [768], P('tm')
- cross_query_grad: float32 [768, 768], P('tm')
- cross_key_grad: float32 [768, 768], P('tm')
- cross_value_grad: float32 [768, 768], P('tm')
- cross_output_grad: float32 [768, 768], P('tm')
The draws below stay inside these ranges and needn't reach their ends.
Inputs may be any that keep to these rules, and one draw needn't show every extreme that they name: `clip_ids`: clip numbers start at 0 and never fall along a sequence; every clip starts at an even position and has an even number of tokens; of the 2 sequences on one index of seq, one is a single clip, and each of the others holds exactly four clips.
All inputs are finite; a program needn't handle non-finite values.
Results may differ from the reference program's by a relative error of at most 0.034.
Values may be sent and summed in bfloat16 or wider, within the bound.
A program may use at most 512 MiB of HBM per device.

```python
import jax
import jax.numpy as jnp
from jax import lax

D = 768
HEADS = 12
FF = 3072
SEQ_DEV = 2
LEN = 2048
SHORT = 1024
SEQS = 8


def draw_clip_ids(key, part):
    key = jax.random.fold_in(key, 17)
    cut_key, pick_key = jax.random.split(key)
    pairs = LEN // 2
    row_keys = jax.random.split(cut_key, SEQS)
    orders = jax.vmap(lambda one_key: jax.random.permutation(one_key, pairs - 1))(row_keys)
    cuts = (orders[:, :3] + 1).astype(jnp.int32)
    position = jnp.arange(pairs, dtype=jnp.int32)[None, :]
    starts = jnp.sum((position[:, :, None] == cuts[:, None, :]).astype(jnp.int32), axis=2).astype(jnp.int32)
    numbers = jnp.cumsum(starts, axis=1).astype(jnp.int32)
    chosen = jax.random.randint(pick_key, (SEQS // SEQ_DEV,), 0, SEQ_DEV)
    row_index = jnp.arange(SEQS, dtype=jnp.int32)
    single = row_index % SEQ_DEV == jnp.repeat(chosen, SEQ_DEV)
    numbers = jnp.where(single[:, None], 0, numbers).astype(jnp.int32)
    return jnp.repeat(numbers, 2, axis=1)


def block_levels(own_key, extent, cuts, least, largest):
    def one(axis_at, shards_of):
        heights = jax.random.uniform(jax.random.fold_in(jax.random.fold_in(own_key, 6), axis_at), (shards_of,), jnp.float32, least / len(cuts), largest / len(cuts))
        return jnp.repeat(jnp.exp(heights), extent[axis_at] // shards_of).reshape((-1,) + (1,) * (len(extent) - axis_at - 1))

    level = one(*cuts[0])
    for cut in cuts[1:]:
        level = level * one(*cut)
    return level


def normal_values(rng, shape, scale, bound, pieces=(), kind=jnp.bfloat16):
    drawn = jax.random.normal(rng, shape, jnp.float32) * scale
    if len(pieces) > 0:
        drawn = block_levels(rng, shape, pieces, -0.22, 0.18) * drawn
    return jnp.clip(drawn, min=-bound, max=bound).astype(kind)


def setup_inputs(seed: int = 0) -> dict:
    streams_of = jax.random.split(jax.random.key(seed), 19)
    large_view = normal_values(streams_of[0], (SEQS, LEN, D), 1.0, 6.0, ((0, 4), (1, 8)))
    small_view = normal_values(streams_of[1], (SEQS, SHORT, D), 1.0, 6.0, ((0, 4), (1, 8)))
    clip_ids = draw_clip_ids(jax.random.fold_in(streams_of[18], 71), 0)
    first_gain = jnp.clip(1.0 + 0.18 * jax.random.normal(streams_of[3], (D,), jnp.float32), 0.099609375, 1.8984375).astype(jnp.bfloat16)
    query_weight = normal_values(streams_of[4], (D, D), D ** -0.5, 0.21875)
    key_weight = normal_values(streams_of[5], (D, D), D ** -0.5, 0.21875)
    value_weight = normal_values(streams_of[6], (D, D), D ** -0.5, 0.21875)
    output_weight = normal_values(streams_of[7], (D, D), (D // 16) ** -0.5, 0.875)
    second_gain = jnp.clip(1.0 + 0.18 * jax.random.normal(streams_of[8], (D,), jnp.float32), 0.099609375, 1.8984375).astype(jnp.bfloat16)
    up_weight = normal_values(streams_of[9], (D, FF), D ** -0.5, 0.21875)
    down_weight = normal_values(streams_of[10], (FF, D), FF ** -0.5, 0.109375)
    query_gain = jnp.clip(1.0 + 0.18 * jax.random.normal(streams_of[11], (D,), jnp.float32), 0.099609375, 1.8984375).astype(jnp.bfloat16)
    context_gain = jnp.clip(1.0 + 0.18 * jax.random.normal(streams_of[12], (D,), jnp.float32), 0.099609375, 1.8984375).astype(jnp.bfloat16)
    cross_query = normal_values(streams_of[13], (D, D), D ** -0.5, 0.21875)
    cross_key = normal_values(streams_of[14], (D, D), D ** -0.5, 0.21875)
    cross_value = normal_values(streams_of[15], (D, D), D ** -0.5, 0.21875)
    cross_output = normal_values(streams_of[16], (D, D), (D // 16) ** -0.5, 0.875)
    cotangent = normal_values(streams_of[17], (SEQS, LEN, D), 1.0, 6.0, ((0, 4), (1, 8)))
    return {"large_view": large_view, "small_view": small_view, "clip_ids": clip_ids, "first_gain": first_gain, "query_weight": query_weight, "key_weight": key_weight, "value_weight": value_weight, "output_weight": output_weight, "second_gain": second_gain, "up_weight": up_weight, "down_weight": down_weight, "query_gain": query_gain, "context_gain": context_gain, "cross_query": cross_query, "cross_key": cross_key, "cross_value": cross_value, "cross_output": cross_output, "cotangent": cotangent}


HIGHEST = lax.Precision.HIGHEST
EPS = 1e-05
NEGATIVE = -1e+30

@jax.custom_vjp
def low(v):
    return lax.optimization_barrier(v.astype(jnp.bfloat16)).astype(jnp.float32)

@jax.custom_vjp
def low_back(v):
    return v

def low_keep(v):
    return (low(v), None)

def low_pass(kept, grad):
    return (grad,)

def back_keep(v):
    return (v, None)

def back_low(kept, grad):
    return (low(grad),)
low.defvjp(low_keep, low_pass)
low_back.defvjp(back_keep, back_low)

def layer_norm(value, gain):
    mean = lax.optimization_barrier(jnp.mean(value, axis=-1, keepdims=True))
    centred = value - mean
    spread = lax.optimization_barrier(jnp.mean(centred * centred, axis=-1, keepdims=True))
    return centred * lax.rsqrt(spread + EPS) * gain

def project(value, weight):
    return jnp.dot(value, weight, precision=HIGHEST)

def attention(query, keys, values, query_clip, key_clip):
    count, width = query.shape
    size = width // HEADS
    scale = size ** (-0.5)
    block = 512 if count % 512 == 0 else count
    keys_split = keys.reshape(keys.shape[0], HEADS, size)
    values_split = values.reshape(values.shape[0], HEADS, size)

    def one_block(pair):
        rows, clips = pair
        rows_split = rows.reshape(block, HEADS, size)
        score = low_back(jnp.einsum('qhe,khe->hqk', rows_split, keys_split, precision=HIGHEST) * scale)
        allowed = clips[None, :, None] == key_clip[None, None, :]
        score = jnp.where(allowed, score, NEGATIVE)
        highest = lax.optimization_barrier(jnp.max(score, axis=-1, keepdims=True))
        weight = jnp.where(allowed, jnp.exp(score - highest), 0.0)
        prob = weight / lax.optimization_barrier(jnp.sum(weight, axis=-1, keepdims=True))
        mixed = jnp.einsum('hqk,khe->qhe', low(prob), values_split, precision=HIGHEST)
        return mixed.reshape(block, width)
    result = lax.map(jax.checkpoint(one_block), (query.reshape(count // block, block, width), query_clip.reshape(count // block, block)))
    return result.reshape(count, width)

def encode(view, clips, weights):
    first_gain, query_weight, key_weight, value_weight, output_weight, second_gain, up_weight, down_weight = weights
    normed = low(layer_norm(view, first_gain))
    query = low(low_back(project(normed, query_weight)))
    keys = low(low_back(project(normed, key_weight)))
    values = low(low_back(project(normed, value_weight)))
    mixed = low(low_back(attention(query, keys, values, clips, clips)))
    hidden = view + low_back(project(mixed, output_weight))
    second = low(layer_norm(hidden, second_gain))
    inner = low_back(project(second, up_weight))
    active = low(jax.nn.gelu(inner, approximate=True))
    return hidden + low_back(project(active, down_weight))

def one_sequence(large, small, clips, params):
    shared = params[:8]
    query_gain, context_gain, cross_query, cross_key, cross_value, cross_output = params[8:]
    short_clips = clips[::2]
    large_merged = encode(large, clips, shared)
    small_merged = encode(small, short_clips, shared)
    asked = low(layer_norm(large_merged, query_gain))
    context = low(layer_norm(small_merged, context_gain))
    cross_q = low(low_back(project(asked, cross_query)))
    cross_k = low(low_back(project(context, cross_key)))
    cross_v = low(low_back(project(context, cross_value)))
    united = low(low_back(attention(cross_q, cross_k, cross_v, clips, short_clips)))
    return large_merged + low_back(project(united, cross_output))

def reference(large_view, small_view, clip_ids, first_gain, query_weight, key_weight, value_weight, output_weight, second_gain, up_weight, down_weight, query_gain, context_gain, cross_query, cross_key, cross_value, cross_output, cotangent):
    params = tuple((w.astype(jnp.float32) for w in (first_gain, query_weight, key_weight, value_weight, output_weight, second_gain, up_weight, down_weight, query_gain, context_gain, cross_query, cross_key, cross_value, cross_output)))
    large = large_view.astype(jnp.float32)
    small = small_view.astype(jnp.float32)

    def forward(large_all, small_all, weights):

        def per_sequence(items):
            return one_sequence(items[0], items[1], items[2], weights)
        return lax.map(jax.checkpoint(per_sequence), (large_all, small_all, clip_ids))
    united_view, pull = jax.vjp(forward, large, small, params)
    large_grad, small_grad, grads = pull(cotangent.astype(jnp.float32))
    return (united_view.astype(jnp.bfloat16), large_grad, small_grad, grads[0], grads[1], grads[2], grads[3], grads[4], grads[5], grads[6], grads[7], grads[8], grads[9], grads[10], grads[11], grads[12], grads[13])
```

```python
import functools

import jax
import jax.numpy as jnp
from jax import lax
from jax.experimental import pallas as pl
from jax.experimental.pallas import tpu as pltpu
from jax.sharding import PartitionSpec as P

HEADS = 12
EPS = 1e-05
NEGATIVE = -1e30
LOG2E = 1.4426950408889634
LN2 = 0.6931471805599453
LANES = 128
HALF = 64

bf16 = jnp.bfloat16
f32 = jnp.float32
NT = (((1,), (1,)), ((), ()))
NN = (((1,), (0,)), ((), ()))
TN = (((0,), (0,)), ((), ()))


def dot(a, b, dims=NN):
    return lax.dot_general(a, b, dims, preferred_element_type=f32)


def part_block(rows):
    block = min(rows, 512)
    while rows % block or block % 16:
        block -= 1
    return block


def attend_kernel(parts, block, *refs):
    q_ref, mq_ref, mk_ref = refs[0], refs[1], refs[2]
    k_refs = refs[3 : 3 + parts]
    v_refs = refs[3 + parts : 3 + 2 * parts]
    o_ref, l_ref, ka0, ka1, va0, va1 = refs[3 + 2 * parts :]
    count = q_ref.shape[0]
    first = 0
    for part in range(parts):
        rows = k_refs[part].shape[0]
        lane = lax.broadcasted_iota(jnp.int32, (rows, LANES), 1)
        here = pl.ds(first, rows)
        keys, values, mask = k_refs[part][...], v_refs[part][...], mk_ref[here, :]
        one = jnp.ones_like(values)
        ka0[here, :] = jnp.where(lane < HALF, keys, mask)
        ka1[here, :] = jnp.where(lane < HALF, mask, keys)
        va0[here, :] = jnp.where(lane < HALF, values, one)
        va1[here, :] = jnp.where(lane < HALF, one, values)
        first += rows
    lane = lax.broadcasted_iota(jnp.int32, (block, LANES), 1)
    low = lane < HALF
    for number in range(count // block):
        here = pl.ds(number * block, block)
        query, mask = q_ref[here, :], mq_ref[here, :]
        tops, sums = [], []
        for head, keys, values in ((0, ka0, va0), (1, ka1, va1)):
            mine = jnp.where(low, query, mask) if head == 0 else jnp.where(low, mask, query)
            score = dot(mine, keys[...], NT)
            top = jnp.max(score, axis=1, keepdims=True)
            weight = jnp.exp2(score - top).astype(bf16)
            sums.append(dot(weight, values[...]))
            tops.append(jnp.broadcast_to(top, (block, LANES)))
        total = jnp.where(low, sums[1], sums[0])
        top = jnp.where(low, tops[1], tops[0])
        out = jnp.where(low, sums[0], sums[1])
        o_ref[here, :] = (out / pltpu.roll(total, HALF, 1)).astype(bf16)
        l_ref[here, :] = top + jnp.log2(total)


def attend(query, keys, values, mask_q, mask_k):
    count, width = query.shape
    parts = len(keys)
    total = sum(k.shape[0] for k in keys)
    block = min(count, 256)
    if count % block:
        block = count
    pair = lambda rows: pl.BlockSpec((rows, LANES), lambda i: (0, i))
    whole = lambda rows: pl.BlockSpec((rows, LANES), lambda i: (0, 0))
    return pl.pallas_call(
        functools.partial(attend_kernel, parts, block),
        grid=(width // LANES,),
        in_specs=[pair(count), whole(count), whole(total)]
        + [pair(k.shape[0]) for k in keys]
        + [pair(v.shape[0]) for v in values],
        out_specs=[pair(count), pair(count)],
        out_shape=[
            jax.ShapeDtypeStruct((count, width), bf16),
            jax.ShapeDtypeStruct((count, width), f32),
        ],
        scratch_shapes=[pltpu.VMEM((total, LANES), bf16)] * 4,
        compiler_params=pltpu.CompilerParams(vmem_limit_bytes=40 << 20),
        cost_estimate=pl.CostEstimate(
            flops=16 * count * total * width,
            bytes_accessed=width * (count * 8 + total * 4),
            transcendentals=count * total * width // HALF,
        ),
        name="attend",
    )(query, mask_q, mask_k, *keys, *values)


def three(value):
    first = value.astype(bf16)
    rest = value - first.astype(f32)
    second = rest.astype(bf16)
    return first, second, (rest - second.astype(f32)).astype(bf16)


def attend_back_kernel(parts, *refs):
    q_ref, do_ref, o_ref, l_ref, mq_ref, mk_ref = refs[:6]
    k_refs = refs[6 : 6 + parts]
    v_refs = refs[6 + parts : 6 + 2 * parts]
    dq_ref = refs[6 + 2 * parts]
    dk_refs = refs[7 + 2 * parts : 7 + 3 * parts]
    dv_refs = refs[7 + 3 * parts : 7 + 4 * parts]
    count = q_ref.shape[0]
    lane = lax.broadcasted_iota(jnp.int32, (count, LANES), 1)
    low = lane < HALF
    spot = lane % HALF
    query, grad, mask = q_ref[...], do_ref[...], mq_ref[...]
    zero = jnp.zeros_like(query)
    product = grad.astype(f32) * o_ref[...].astype(f32)
    delta0 = jnp.sum(jnp.where(low, product, 0.0), axis=1, keepdims=True)
    delta1 = jnp.sum(jnp.where(low, 0.0, product), axis=1, keepdims=True)
    delta = jnp.where(low, delta1, delta0)

    def beside(base, value):
        a, b, c = three(-value)
        return jnp.where(spot == 4, a, jnp.where(spot == 5, b, jnp.where(spot == 6, c, base)))

    query_side = beside(mask, l_ref[...])
    grad_side = beside(zero, delta)
    query_a = (jnp.where(low, query, query_side), jnp.where(low, query_side, query))
    grad_a = (jnp.where(low, grad, grad_side), jnp.where(low, grad_side, grad))
    query_m = (jnp.where(low, query, zero), jnp.where(low, zero, query))
    grad_m = (jnp.where(low, grad, zero), jnp.where(low, zero, grad))
    dq = jnp.zeros((count, LANES), f32)
    first = 0
    for part in range(parts):
        rows = k_refs[part].shape[0]
        block = part_block(rows)
        lane_k = lax.broadcasted_iota(jnp.int32, (block, LANES), 1)
        low_k = lane_k < HALF
        spot_k = lane_k % HALF
        one = jnp.where((spot_k >= 4) & (spot_k < 7), 1.0, 0.0).astype(bf16)
        for number in range(rows // block):
            here = pl.ds(number * block, block)
            keys, values = k_refs[part][here, :], v_refs[part][here, :]
            side = mk_ref[pl.ds(first + number * block, block), :] + one
            nought = jnp.zeros_like(keys)
            dk = jnp.zeros((block, LANES), f32)
            dv = jnp.zeros((block, LANES), f32)
            for head in (0, 1):
                pick = lambda a, b: jnp.where(low_k, a, b) if head == 0 else jnp.where(low_k, b, a)
                prob = jnp.exp2(dot(query_a[head], pick(keys, side), NT))
                change = dot(grad_a[head], pick(values, one), NT)
                score_grad = (prob * change).astype(bf16)
                dv += dot(prob.astype(bf16), grad_m[head], TN)
                dk += dot(score_grad, query_m[head], TN)
                dq += dot(score_grad, pick(keys, nought))
            dk_refs[part][here, :] = (dk * LN2).astype(bf16)
            dv_refs[part][here, :] = dv.astype(bf16)
        first += rows
    dq_ref[...] = (dq * HALF**-0.5).astype(bf16)


def attend_back(query, keys, values, grad, out, logsum, mask_q, mask_k):
    count, width = query.shape
    parts = len(keys)
    total = sum(k.shape[0] for k in keys)
    pair = lambda rows: pl.BlockSpec((rows, LANES), lambda i: (0, i))
    whole = lambda rows: pl.BlockSpec((rows, LANES), lambda i: (0, 0))
    result = pl.pallas_call(
        functools.partial(attend_back_kernel, parts),
        grid=(width // LANES,),
        in_specs=[pair(count)] * 4
        + [whole(count), whole(total)]
        + [pair(k.shape[0]) for k in keys]
        + [pair(v.shape[0]) for v in values],
        out_specs=[pair(count)]
        + [pair(k.shape[0]) for k in keys]
        + [pair(v.shape[0]) for v in values],
        out_shape=[jax.ShapeDtypeStruct((count, width), bf16)]
        + [jax.ShapeDtypeStruct(k.shape, bf16) for k in keys]
        + [jax.ShapeDtypeStruct(v.shape, bf16) for v in values],
        compiler_params=pltpu.CompilerParams(vmem_limit_bytes=40 << 20),
        cost_estimate=pl.CostEstimate(
            flops=40 * count * total * width // 2,
            bytes_accessed=width * (count * 12 + total * 8),
            transcendentals=count * total * width // HALF,
        ),
        name="attend_back",
    )(query, grad, out, logsum, mask_q, mask_k, *keys, *values)
    return result[0], result[1 : 1 + parts], result[1 + parts :]


def norm_stats(value):
    mean = jnp.mean(value, axis=-1, keepdims=True)
    centred = value - mean
    spread = jnp.mean(centred * centred, axis=-1, keepdims=True)
    return mean, lax.rsqrt(spread + EPS)


def norm(value, gain):
    mean, scale = norm_stats(value)
    return ((value - mean) * scale * gain).astype(bf16)


def norm_back(grad, value, gain):
    mean, scale = norm_stats(value)
    unit = (value - mean) * scale
    gain_grad = jnp.sum(grad * unit, axis=0)
    grad = grad * gain
    extra = scale * (
        grad
        - jnp.mean(grad, axis=-1, keepdims=True)
        - unit * jnp.mean(grad * unit, axis=-1, keepdims=True)
    )
    return extra, gain_grad


def gelu_tanh(value):
    return jax.nn.gelu(value, approximate=True)


def per_device(tm, seq_size, *args):
    (
        large_view,
        small_view,
        clip_ids,
        first_gain,
        query_weight,
        key_weight,
        value_weight,
        output_weight,
        second_gain,
        up_weight,
        down_weight,
        query_gain,
        context_gain,
        cross_query,
        cross_key,
        cross_value,
        cross_output,
        cotangent,
    ) = args
    seqs, count, width = large_view.shape
    half = count // 2
    side = tm // 4
    gains = [g.astype(f32) for g in (first_gain, second_gain, query_gain, context_gain)]
    first_gain, second_gain, query_gain, context_gain = gains

    tm_at = lax.axis_index("tm")
    seq_at = lax.axis_index("seq")
    z, x = tm_at // side, tm_at % side
    y, core = seq_at // 2, seq_at % 2

    def permute(value, place):
        pairs = []
        for pz in range(4):
            for px in range(side):
                for py in range(2):
                    for pc in range(2):
                        to = place(pz, px, py, pc)
                        source = (pz * side + px) * seq_size + py * 2 + pc
                        target = (to[0] * side + to[1]) * seq_size + to[2] * 2 + to[3]
                        pairs.append((source, target))
        return lax.ppermute(value, ("tm", "seq"), pairs)

    def inverse(place):
        table = {}
        for pz in range(4):
            for px in range(side):
                for py in range(2):
                    for pc in range(2):
                        table[place(pz, px, py, pc)] = (pz, px, py, pc)
        return lambda *at: table[at]

    go = (
        lambda z, x, y, c: (2 * c + z % 2, x, y, z // 2),
        lambda z, x, y, c: (2 * c + 1 - z % 2, x, y, z // 2),
    )
    back = tuple(inverse(place) for place in go)
    other_core = lambda value: permute(value, lambda z, x, y, c: (z, x, y, 1 - c))
    other_y = lambda value: permute(value, lambda z, x, y, c: (z, x, 1 - y, c))
    by_x = lambda value, d: permute(value, lambda z, x, y, c: (z, (x + d) % side, y, c))
    by_z = lambda value, d: permute(value, lambda z, x, y, c: (z ^ d, x, y, c))

    odd = z % 2 == 1

    def relocate(value):
        near = jnp.where(odd, value[1], value[0])
        far = jnp.where(odd, value[0], value[1])
        return jnp.concatenate([permute(near, go[0]), permute(far, go[1])], axis=0)

    def restore(value):
        rows = value.shape[0] // 2
        near, far = permute(value[:rows], back[0]), permute(value[rows:], back[1])
        return jnp.where(odd, jnp.stack([far, near]), jnp.stack([near, far]))

    all_clips = lax.all_gather(clip_ids, ("tm", "seq"), axis=0, tiled=False)
    owner = 2 * y + z // 2
    mine = lax.dynamic_index_in_dim(
        all_clips.reshape(tm, seq_size, seqs, count), owner, 1, keepdims=False
    )
    mine = lax.dynamic_index_in_dim(mine, z % 2, 1, keepdims=False)
    order = []
    for dx in range(side):
        for dc in ((0, 1) if dx == 0 else (0,)):
            order.append((dx, dc))
    order += [(dx, 1) for dx in range(1, side)]
    slots = []
    for dx, dc in order:
        held = (core + dc) % 2
        for slot in (0, 1):
            from_z = 2 * held + (z + slot) % 2
            slots.append(from_z * side + (x - dx) % side)
    clips = jnp.concatenate(
        [lax.dynamic_index_in_dim(mine, at, 0, keepdims=False) for at in slots]
    )
    short_clips = clips[::2]
    spot = lax.broadcasted_iota(jnp.int32, (1, LANES), 1) % HALF

    def mask_of_keys(numbers):
        return jnp.where((spot < 4) & (numbers[:, None] != spot), NEGATIVE, 0.0).astype(bf16)

    def mask_of_queries(numbers):
        return jnp.where((spot < 4) & (numbers[:, None] == spot), 1.0, 0.0).astype(bf16)

    large_mask_k, small_mask_k = mask_of_keys(clips), mask_of_keys(short_clips)
    large_mask_q = mask_of_queries(clips[: 2 * count])
    small_mask_q = mask_of_queries(short_clips[: 2 * half])

    def gather(value):
        beside = other_core(value)
        across = [by_x(value, d) for d in range(1, side)]
        across = across[0] if len(across) == 1 else jnp.concatenate(across, axis=0)
        return (value, beside, across, other_core(across))

    def scatter(pieces):
        own, beside, across, diagonal = pieces
        across = across.astype(f32) + other_core(diagonal).astype(f32)
        across = across.astype(bf16)
        total = own.astype(f32) + other_core(beside).astype(f32)
        rows = own.shape[0]
        for d in range(1, side):
            part = across[(d - 1) * rows : d * rows]
            total = total + by_x(part, -d).astype(f32)
        return total.astype(bf16)

    small = relocate(small_view)
    large = relocate(large_view)
    grad_out = relocate(cotangent)
    small, large = small.astype(f32), large.astype(f32)
    q_scale = LOG2E * HALF**-0.5

    def front(view):
        normed = norm(view, first_gain)
        keys = dot(normed, key_weight).astype(bf16)
        values = dot(normed, value_weight).astype(bf16)
        query = (dot(normed, query_weight) * q_scale).astype(bf16)
        return normed, query, gather(keys), gather(values)

    def rest(view, mixed):
        hidden = view + dot(mixed, output_weight)
        second = norm(hidden, second_gain)
        inner = dot(second, up_weight)
        active = gelu_tanh(inner).astype(bf16)
        merged = hidden + dot(active, down_weight)
        return merged, (hidden, second, inner, active)

    small_normed, small_q, small_k, small_v = front(small)
    large_normed, large_q, large_k, large_v = front(large)
    small_mixed, small_logsum = attend(small_q, small_k, small_v, small_mask_q, small_mask_k)
    small_merged, small_saved = rest(small, small_mixed)
    context = norm(small_merged, context_gain)
    cross_k = gather(dot(context, cross_key).astype(bf16))
    cross_v = gather(dot(context, cross_value).astype(bf16))
    large_mixed, large_logsum = attend(large_q, large_k, large_v, large_mask_q, large_mask_k)
    large_merged, large_saved = rest(large, large_mixed)
    asked = norm(large_merged, query_gain)
    cross_q = (dot(asked, cross_query) * q_scale).astype(bf16)
    united, cross_logsum = attend(cross_q, cross_k, cross_v, large_mask_q, small_mask_k)
    united_view = restore((large_merged + dot(united, cross_output)).astype(bf16))

    def bucket(pieces):
        parts = []
        for piece in pieces:
            rows, columns = piece.shape
            piece = piece.reshape(tm, rows // tm, columns)
            for at in range(0, columns, width):
                parts.append(piece[:, :, at : at + width])
        return jnp.concatenate(parts, axis=1) if len(parts) > 1 else parts[0]

    def unbucket(total, shapes):
        out, at = [], 0
        for rows, columns in shapes:
            rows //= tm
            parts = []
            for _ in range(columns // width):
                parts.append(total[at : at + rows])
                at += rows
            out.append(jnp.concatenate(parts, axis=1) if len(parts) > 1 else parts[0])
        return out

    def pick(value, axis, size, at):
        return lax.dynamic_slice_in_dim(value, at * size, size, axis)

    def add(a, b):
        return (a.astype(f32) + b.astype(f32)).astype(bf16)

    def reduce(local):
        rows = local.shape[1] // 2
        columns = local.shape[2] // 2
        value = add(
            pick(local, 1, rows, core), other_core(pick(local, 1, rows, 1 - core))
        )
        value = add(pick(value, 2, columns, y), other_y(pick(value, 2, columns, 1 - y)))
        value = value.reshape(4, side, rows, columns)
        total = lax.dynamic_index_in_dim(value, x, 1, keepdims=False).astype(f32)
        for d in range(1, side):
            sent = lax.dynamic_index_in_dim(value, (x + d) % side, 1, keepdims=False)
            total = total + by_x(sent, d).astype(f32)
        value = total.astype(bf16)
        total = lax.dynamic_index_in_dim(value, z, 0, keepdims=False).astype(f32)
        for d in range(1, 4):
            sent = lax.dynamic_index_in_dim(value, z ^ d, 0, keepdims=False)
            total = total + by_z(sent, d).astype(f32)
        value = total.astype(bf16)
        other = other_y(value)
        value = jnp.where(
            y == 0,
            jnp.concatenate([value, other], axis=1),
            jnp.concatenate([other, value], axis=1),
        )
        other = other_core(value)
        return jnp.where(
            core == 0,
            jnp.concatenate([value, other], axis=0),
            jnp.concatenate([other, value], axis=0),
        ).astype(f32)

    def encode_back(merged_grad, saved, mixed):
        hidden, second, inner, active = saved
        branch = merged_grad.astype(bf16)
        down_part = dot(active, branch, TN)
        _, pull = jax.vjp(gelu_tanh, inner)
        inner_grad = pull(dot(branch, down_weight, NT))[0].astype(bf16)
        up_part = dot(second, inner_grad, TN)
        extra, gain_part = norm_back(dot(inner_grad, up_weight, NT), hidden, second_gain)
        hidden_grad = merged_grad + extra
        attend_grad = hidden_grad.astype(bf16)
        output_part = dot(mixed, attend_grad, TN)
        mixed_grad = dot(attend_grad, output_weight, NT).astype(bf16)
        return hidden_grad, mixed_grad, (gain_part, up_part, down_part, output_part)

    def front_back(view, hidden_grad, normed, dq, dk, dv):
        parts = (dot(normed, dq, TN), dot(normed, dk, TN), dot(normed, dv, TN))
        grad = (
            dot(dq, query_weight, NT) + dot(dk, key_weight, NT) + dot(dv, value_weight, NT)
        )
        extra, gain_part = norm_back(grad, view, first_gain)
        return (hidden_grad + extra).astype(bf16), (gain_part,) + parts

    cross_output_grad = dot(united, grad_out, TN)
    united_grad = dot(grad_out, cross_output, NT).astype(bf16)
    dcq, dck, dcv = attend_back(
        cross_q, cross_k, cross_v, united_grad, united, cross_logsum, large_mask_q, small_mask_k
    )
    dck, dcv = scatter(dck), scatter(dcv)
    cross_query_grad = dot(asked, dcq, TN)
    extra, query_gain_grad = norm_back(dot(dcq, cross_query, NT), large_merged, query_gain)
    large_hidden, large_mixed_grad, large_parts = encode_back(
        grad_out.astype(f32) + extra, large_saved, large_mixed
    )
    large_dq, large_dk, large_dv = attend_back(
        large_q, large_k, large_v, large_mixed_grad, large_mixed, large_logsum,
        large_mask_q, large_mask_k,
    )
    large_dk, large_dv = scatter(large_dk), scatter(large_dv)
    cross_key_grad = dot(context, dck, TN)
    cross_value_grad = dot(context, dcv, TN)
    small_merged_grad, context_gain_grad = norm_back(
        dot(dck, cross_key, NT) + dot(dcv, cross_value, NT), small_merged, context_gain
    )
    small_hidden, small_mixed_grad, small_parts = encode_back(
        small_merged_grad, small_saved, small_mixed
    )
    small_dq, small_dk, small_dv = attend_back(
        small_q, small_k, small_v, small_mixed_grad, small_mixed, small_logsum,
        small_mask_q, small_mask_k,
    )
    small_dk, small_dv = scatter(small_dk), scatter(small_dv)
    large_grad, large_front = front_back(
        large, large_hidden, large_normed, large_dq, large_dk, large_dv
    )
    small_grad, small_front = front_back(
        small, small_hidden, small_normed, small_dq, small_dk, small_dv
    )
    large_grad = restore(large_grad).astype(f32)
    small_grad = restore(small_grad).astype(f32)

    square = (width, width)
    cross_shapes = [square] * 4
    cross_total = reduce(
        bucket(
            [
                g.astype(bf16)
                for g in (cross_output_grad, cross_query_grad, cross_key_grad, cross_value_grad)
            ]
        )
    )
    cross_grads = unbucket(cross_total, cross_shapes)
    dense_shapes = [up_weight.shape, down_weight.shape, square]
    dense_total = reduce(
        bucket([(large_parts[i] + small_parts[i]).astype(bf16) for i in (1, 2, 3)])
    )
    dense_grads = unbucket(dense_total, dense_shapes)
    gain_rows = jnp.stack(
        [
            large_front[0] + small_front[0],
            large_parts[0] + small_parts[0],
            query_gain_grad,
            context_gain_grad,
        ]
    )
    gain_rows = jnp.transpose(gain_rows.reshape(4, tm, width // tm), (1, 0, 2)).astype(bf16)
    gain_rows = jnp.pad(gain_rows, ((0, 0), (0, 28), (0, width - width // tm)))
    last = bucket([(large_front[i] + small_front[i]).astype(bf16) for i in (1, 2, 3)])
    last_total = reduce(jnp.concatenate([last, gain_rows], axis=1))
    last_grads = unbucket(last_total, [square] * 3)
    gain_at = 3 * width // tm
    gain_grads = [last_total[gain_at + i, : width // tm] for i in range(4)]
    return (
        united_view,
        large_grad,
        small_grad,
        gain_grads[0],
        last_grads[0],
        last_grads[1],
        last_grads[2],
        dense_grads[2],
        gain_grads[1],
        dense_grads[0],
        dense_grads[1],
        gain_grads[2],
        gain_grads[3],
        cross_grads[1],
        cross_grads[2],
        cross_grads[3],
        cross_grads[0],
    )


def solution(mesh):
    token = P("seq", "tm", None)
    in_specs = (token, token, P("seq", "tm")) + (P(),) * 14 + (token,)
    vector, matrix = P("tm"), P("tm", None)
    out_specs = (
        (token, token, token, vector)
        + (matrix,) * 4
        + (vector, matrix, matrix, vector, vector)
        + (matrix,) * 4
    )
    return jax.shard_map(
        functools.partial(per_device, mesh.shape["tm"], mesh.shape["seq"]),
        mesh=mesh,
        in_specs=in_specs,
        out_specs=out_specs,
        check_vma=False,
    )
```

```python
import functools

import jax
import jax.numpy as jnp
from jax import lax
from jax.experimental import pallas as pl
from jax.experimental.pallas import tpu as pltpu
from jax.sharding import PartitionSpec as P

HEADS = 12
EPS = 1e-05
NEGATIVE = -1e30
LOG2E = 1.4426950408889634
LN2 = 0.6931471805599453
LANES = 128
HALF = 64

bf16 = jnp.bfloat16
f32 = jnp.float32
NT = (((1,), (1,)), ((), ()))
NN = (((1,), (0,)), ((), ()))
TN = (((0,), (0,)), ((), ()))


def dot(a, b, dims=NN):
    return lax.dot_general(a, b, dims, preferred_element_type=f32)


def largest_block(rows, most):
    block = min(rows, most)
    while rows % block or block % 16:
        block -= 1
    return block


def columns(rows, at):
    return pl.BlockSpec((rows, LANES), lambda i: (0, i + at))


def pair_columns(rows, at):
    return pl.BlockSpec((2, rows, LANES), lambda i: (0, 0, i + at))


def whole(shape):
    return pl.BlockSpec(shape, lambda i: (0,) * len(shape))


def attend_kernel(parts, block, *refs):
    q_ref, mq_ref, mk_ref = refs[:3]
    kv_refs = refs[3 : 3 + parts]
    o_ref, l_ref, ka0, ka1, va0, va1 = refs[-6:]
    count = q_ref.shape[0]
    first = 0
    for kv_ref in kv_refs:
        rows = kv_ref.shape[1]
        low = lax.broadcasted_iota(jnp.int32, (rows, LANES), 1) < HALF
        here = pl.ds(first, rows)
        keys, values, mask = kv_ref[0], kv_ref[1], mk_ref[here, :]
        one = jnp.ones_like(values)
        ka0[here, :] = jnp.where(low, keys, mask)
        ka1[here, :] = jnp.where(low, mask, keys)
        va0[here, :] = jnp.where(low, values, one)
        va1[here, :] = jnp.where(low, one, values)
        first += rows
    low = lax.broadcasted_iota(jnp.int32, (block, LANES), 1) < HALF
    for number in range(count // block):
        here = pl.ds(number * block, block)
        query, mask = q_ref[here, :], mq_ref[here, :]
        tops, sums = [], []
        for head, keys, values in ((0, ka0, va0), (1, ka1, va1)):
            mine = jnp.where(low, query, mask) if head == 0 else jnp.where(low, mask, query)
            score = dot(mine, keys[...], NT)
            top = jnp.max(score, axis=1, keepdims=True)
            weight = jnp.exp2(score - top).astype(bf16)
            sums.append(dot(weight, values[...]))
            tops.append(jnp.broadcast_to(top, (block, LANES)))
        total = jnp.where(low, sums[1], sums[0])
        top = jnp.where(low, tops[1], tops[0])
        out = jnp.where(low, sums[0], sums[1])
        o_ref[here, :] = (out / pltpu.roll(total, HALF, 1)).astype(bf16)
        l_ref[here, :] = top + jnp.log2(total)


def attend(query, kv, mask_q, mask_k, at, width, earlier=()):
    count = query.shape[0]
    total = sum(part.shape[1] for part in kv)
    out = lambda kind: jax.ShapeDtypeStruct((count, query.shape[1]), kind)
    given = 3 + len(kv)
    return pl.pallas_call(
        functools.partial(attend_kernel, len(kv), largest_block(count, 256)),
        grid=(width // LANES,),
        in_specs=[columns(count, at // LANES), whole((count, LANES)), whole((total, LANES))]
        + [pair_columns(part.shape[1], 0) for part in kv]
        + [pl.BlockSpec(memory_space=pl.ANY)] * len(earlier),
        out_specs=[columns(count, at // LANES)] * 2,
        out_shape=[out(bf16), out(f32)],
        scratch_shapes=[pltpu.VMEM((total, LANES), bf16)] * 4,
        input_output_aliases={given + i: i for i in range(len(earlier))},
        compiler_params=pltpu.CompilerParams(vmem_limit_bytes=40 << 20),
        cost_estimate=pl.CostEstimate(
            flops=16 * count * total * width,
            bytes_accessed=width * (count * 8 + total * 4),
            transcendentals=count * total * width // HALF,
        ),
        name="attend",
    )(query, mask_q, mask_k, *kv, *earlier)


def three(value):
    first = value.astype(bf16)
    rest = value - first.astype(f32)
    second = rest.astype(bf16)
    return first, second, (rest - second.astype(f32)).astype(bf16)


def attend_back_kernel(parts, block, *refs):
    q_ref, do_ref, o_ref, l_ref, mq_ref, mk_ref = refs[:6]
    kv_refs = refs[6 : 6 + parts]
    dq_ref, keep_ref, send_ref, keys_at, values_at = refs[6 + parts :]
    count = q_ref.shape[0]
    first = 0
    for kv_ref in kv_refs:
        here = pl.ds(first, kv_ref.shape[1])
        keys_at[here, :] = kv_ref[0]
        values_at[here, :] = kv_ref[1]
        first += kv_ref.shape[1]
    lane = lax.broadcasted_iota(jnp.int32, (count, LANES), 1)
    low = lane < HALF
    spot = lane % HALF
    query, grad, mask = q_ref[...], do_ref[...], mq_ref[...]
    zero = jnp.zeros_like(query)
    product = grad.astype(f32) * o_ref[...].astype(f32)
    delta0 = jnp.sum(jnp.where(low, product, 0.0), axis=1, keepdims=True)
    delta1 = jnp.sum(jnp.where(low, 0.0, product), axis=1, keepdims=True)
    delta = jnp.where(low, delta1, delta0)

    def beside(base, value):
        a, b, c = three(-value)
        return jnp.where(spot == 4, a, jnp.where(spot == 5, b, jnp.where(spot == 6, c, base)))

    query_side = beside(mask, l_ref[...])
    grad_side = beside(zero, delta)
    query_a = (jnp.where(low, query, query_side), jnp.where(low, query_side, query))
    grad_a = (jnp.where(low, grad, grad_side), jnp.where(low, grad_side, grad))
    query_m = (jnp.where(low, query, zero), jnp.where(low, zero, query))
    grad_m = (jnp.where(low, grad, zero), jnp.where(low, zero, grad))
    lane_k = lax.broadcasted_iota(jnp.int32, (block, LANES), 1)
    low_k = lane_k < HALF
    spot_k = lane_k % HALF
    one = jnp.where((spot_k >= 4) & (spot_k < 7), 1.0, 0.0).astype(bf16)
    dq = jnp.zeros((count, LANES), f32)
    for number in range(first // block):
        here = pl.ds(number * block, block)
        keys, values = keys_at[here, :], values_at[here, :]
        side = mk_ref[here, :] + one
        nought = jnp.zeros_like(keys)
        dk = jnp.zeros((block, LANES), f32)
        dv = jnp.zeros((block, LANES), f32)
        for head in (0, 1):
            pick = lambda a, b: jnp.where(low_k, a, b) if head == 0 else jnp.where(low_k, b, a)
            prob = jnp.exp2(dot(query_a[head], pick(keys, side), NT))
            change = dot(grad_a[head], pick(values, one), NT)
            score_grad = (prob * change).astype(bf16)
            dv += dot(prob.astype(bf16), grad_m[head], TN)
            dk += dot(score_grad, query_m[head], TN)
            dq += dot(score_grad, pick(keys, nought))
        out_ref = keep_ref if number * block < first // 2 else send_ref
        there = pl.ds(number * block % (first // 2), block)
        out_ref[0, there, :] = (dk * LN2).astype(bf16)
        out_ref[1, there, :] = dv.astype(bf16)
    dq_ref[...] = (dq * HALF**-0.5).astype(bf16)


def attend_back(query, kv, grad, out, logsum, mask_q, mask_k, at, at_out, at_kv, width):
    count = query.shape[0]
    total = sum(part.shape[1] for part in kv)
    return pl.pallas_call(
        functools.partial(attend_back_kernel, len(kv), largest_block(total // 2, 512)),
        grid=(width // LANES,),
        in_specs=[columns(count, at // LANES)] * 2
        + [columns(count, at_out // LANES)] * 2
        + [whole((count, LANES)), whole((total, LANES))]
        + [pair_columns(part.shape[1], at_kv // LANES) for part in kv],
        out_specs=[columns(count, 0)] + [pair_columns(total // 2, 0)] * 2,
        out_shape=[jax.ShapeDtypeStruct((count, width), bf16)]
        + [jax.ShapeDtypeStruct((2, total // 2, width), bf16)] * 2,
        scratch_shapes=[pltpu.VMEM((total, LANES), bf16)] * 2,
        compiler_params=pltpu.CompilerParams(vmem_limit_bytes=40 << 20),
        cost_estimate=pl.CostEstimate(
            flops=20 * count * total * width,
            bytes_accessed=width * (count * 12 + total * 8),
            transcendentals=count * total * width // HALF,
        ),
        name="attend_back",
    )(query, grad, out, logsum, mask_q, mask_k, *kv)


def norm_stats(value):
    mean = jnp.mean(value, axis=-1, keepdims=True)
    centred = value - mean
    spread = jnp.mean(centred * centred, axis=-1, keepdims=True)
    return centred, lax.rsqrt(spread + EPS)


def norm(value, gain):
    centred, scale = norm_stats(value)
    return (centred * scale * gain).astype(bf16)


def norm_back(grad, value, gain):
    centred, scale = norm_stats(value)
    unit = centred * scale
    gain_grad = jnp.sum(grad * unit, axis=0, keepdims=True)
    grad = grad * gain
    extra = scale * (
        grad
        - jnp.mean(grad, axis=-1, keepdims=True)
        - unit * jnp.mean(grad * unit, axis=-1, keepdims=True)
    )
    return extra, gain_grad


Q_SCALE = LOG2E * HALF**-0.5


def front_kernel(x_ref, gain_ref, wq_ref, wk_ref, wv_ref, n_ref, q_ref, *kv_refs):
    normed = norm(x_ref[...].astype(f32), gain_ref[...])
    n_ref[...] = normed
    width = kv_refs[0].shape[2]
    keys = dot(normed, wk_ref[...]).astype(bf16)
    values = dot(normed, wv_ref[...]).astype(bf16)
    for group, kv_ref in enumerate(kv_refs):
        kv_ref[0] = keys[:, group * width : (group + 1) * width]
        kv_ref[1] = values[:, group * width : (group + 1) * width]
    q_ref[...] = (dot(normed, wq_ref[...]) * Q_SCALE).astype(bf16)


def front(view, gain, wq, wk, wv, groups):
    rows, width = view.shape
    part = width // groups
    result = pl.pallas_call(
        front_kernel,
        out_shape=[jax.ShapeDtypeStruct((rows, width), bf16)] * 2
        + [jax.ShapeDtypeStruct((2, rows, part), bf16)] * groups,
        compiler_params=pltpu.CompilerParams(vmem_limit_bytes=40 << 20),
        cost_estimate=pl.CostEstimate(
            flops=6 * rows * width * width,
            bytes_accessed=6 * width * width + 10 * rows * width,
            transcendentals=0,
        ),
        name="front",
    )(view, gain, wq, wk, wv)
    return result[0], result[1], result[2:]


GELU_A = 0.7978845608028654
GELU_B = 0.044715


def gelu_both(value):
    square = value * value
    bent = jnp.tanh(GELU_A * value * (1.0 + GELU_B * square))
    half = 0.5 * (1.0 + bent)
    slope = half + 0.5 * value * (1.0 - bent * bent) * (
        GELU_A * (1.0 + 3.0 * GELU_B * square)
    )
    return value * half, slope


def rest_kernel(steps, mixes, is_query, *refs):
    x_ref = refs[0]
    mixed_refs = refs[1 : 1 + mixes]
    wo_ref, gain_ref, up_ref, down_ref, next_gain_ref = refs[1 + mixes : 6 + mixes]
    next_refs = refs[6 + mixes : -9]
    merged_ref, hidden_ref, second_ref, active_ref, slope_ref = refs[-9:-4]
    asked_ref, out_ref, total, scratch = refs[-4:]
    step = pl.program_id(0)

    @pl.when(step == 0)
    def _():
        at = 0
        hidden = x_ref[...].astype(f32)
        for mixed_ref in mixed_refs:
            wide = mixed_ref.shape[1]
            scratch[:, pl.ds(at, wide)] = mixed_ref[...]
            at += wide
        hidden = hidden + dot(scratch[...], wo_ref[...])
        hidden_ref[...] = hidden
        second_ref[...] = norm(hidden, gain_ref[...])
        total[...] = hidden

    inner = dot(second_ref[...], up_ref[...])
    active, slope = gelu_both(inner)
    active = active.astype(bf16)
    active_ref[...] = active
    slope_ref[...] = slope.astype(bf16)
    total[...] += dot(active, down_ref[...])

    @pl.when(step == steps - 1)
    def _():
        merged = total[...]
        merged_ref[...] = merged
        asked = norm(merged, next_gain_ref[...])
        asked_ref[...] = asked
        if is_query:
            out_ref[...] = (dot(asked, next_refs[0][...]) * Q_SCALE).astype(bf16)
        else:
            out_ref[0] = dot(asked, next_refs[0][...]).astype(bf16)
            out_ref[1] = dot(asked, next_refs[1][...]).astype(bf16)


def rest(view, mixed, wo, gain, up, down, next_gain, next_weights):
    rows, width = view.shape
    steps = up.shape[1] // width
    is_query = len(next_weights) == 1
    flat = whole((rows, width))
    slab = pl.BlockSpec((rows, width), lambda i: (0, i))
    square = whole((width, width))
    shape = lambda kind: jax.ShapeDtypeStruct((rows, width), kind)
    wide = jax.ShapeDtypeStruct((rows, up.shape[1]), bf16)
    last = (rows, width) if is_query else (2, rows, width)
    return pl.pallas_call(
        functools.partial(rest_kernel, steps, len(mixed), is_query),
        grid=(steps,),
        in_specs=[flat]
        + [whole(m.shape) for m in mixed]
        + [square, whole((1, width))]
        + [slab_of(width, width), pl.BlockSpec((width, width), lambda i: (i, 0))]
        + [whole((1, width))]
        + [square] * len(next_weights),
        out_specs=[flat, flat, flat, slab, slab, flat, whole(last)],
        out_shape=[shape(f32), shape(f32), shape(bf16), wide, wide, shape(bf16)]
        + [jax.ShapeDtypeStruct(last, bf16)],
        scratch_shapes=[pltpu.VMEM((rows, width), f32), pltpu.VMEM((rows, width), bf16)],
        compiler_params=pltpu.CompilerParams(vmem_limit_bytes=48 << 20),
        cost_estimate=pl.CostEstimate(
            flops=2 * rows * width * (4 * up.shape[1] // 2 + 2 * width),
            bytes_accessed=width * width * 22 + rows * width * 32,
            transcendentals=rows * up.shape[1],
        ),
        name="rest",
    )(view, *mixed, wo, gain, up, down, next_gain, *next_weights)


def slab_of(rows, width):
    return pl.BlockSpec((rows, width), lambda i: (0, i))


def back_kernel(steps, mixes, sizes, laid, *refs):
    gl_ref, gs_ref, al_ref, as_ref, sl_ref, ss_ref = refs[:6]
    cl_ref, cs_ref, hl_ref, hs_ref = refs[6:10]
    mixed_refs = refs[10 : 10 + mixes]
    mixed_s_ref, wo_ref, gain_ref, up_ref, down_ref = refs[10 + mixes : 15 + mixes]
    outs = refs[15 + mixes :]
    (hgl_ref, hgs_ref, ml_ref, ms_ref, dup_ref, ddown_ref, dwo_ref, dgain_ref) = outs[:8]
    branch, second, total, active, inner_grad, mixed = outs[8:]
    large, small = sizes
    top, bottom = pl.ds(0, large), pl.ds(large, small)
    step = pl.program_id(0)

    @pl.when(step == 0)
    def _():
        branch[top, :] = gl_ref[...].astype(bf16)
        branch[bottom, :] = gs_ref[...].astype(bf16)
        second[top, :] = cl_ref[...]
        second[bottom, :] = cs_ref[...]
        total[...] = jnp.zeros_like(total)

    grad = dot(branch[...], down_ref[...], NT)
    inner_grad[top, :] = (grad[:large] * sl_ref[...].astype(f32)).astype(bf16)
    inner_grad[bottom, :] = (grad[large:] * ss_ref[...].astype(f32)).astype(bf16)
    active[top, :] = al_ref[...]
    active[bottom, :] = as_ref[...]
    down = dot(active[...], branch[...], TN).astype(bf16)
    upper = dot(second[...], inner_grad[...], TN).astype(bf16)
    if laid:
        rows = dup_ref.shape[1]
        for at in range(8):
            zl, x, zh = at // 4, at // 2 % 2, at % 2
            first = ((zh * 2 + zl) * 2 + x) * rows
            dup_ref[at] = upper[first : first + rows]
        for x, core, y in ((a, b, c) for a in (0, 1) for b in (0, 1) for c in (0, 1)):
            first = (x * 4 + core * 2 + y) * rows
            there = core * 16 + (step % 2) * 8 + y * 4 + x * 2 + step // 2
            ddown_ref[there] = down[first : first + rows]
    else:
        dup_ref[...] = upper
        ddown_ref[...] = down
    total[...] += dot(inner_grad[...], up_ref[...], NT)

    @pl.when(step == steps - 1)
    def _():
        extra, gain_l = norm_back(total[top, :], hl_ref[...], gain_ref[...])
        hidden_grad = gl_ref[...] + extra
        hgl_ref[...] = hidden_grad
        branch[top, :] = hidden_grad.astype(bf16)
        extra, gain_s = norm_back(total[bottom, :], hs_ref[...], gain_ref[...])
        hidden_grad = gs_ref[...] + extra
        hgs_ref[...] = hidden_grad
        branch[bottom, :] = hidden_grad.astype(bf16)
        dgain_ref[...] = gain_l + gain_s
        mixed_grad = dot(branch[...], wo_ref[...], NT).astype(bf16)
        ml_ref[...] = mixed_grad[:large]
        ms_ref[...] = mixed_grad[large:]
        at = 0
        for mixed_ref in mixed_refs:
            wide = mixed_ref.shape[1]
            mixed[top, pl.ds(at, wide)] = mixed_ref[...]
            at += wide
        mixed[bottom, :] = mixed_s_ref[...]
        value = dot(mixed[...], branch[...], TN).astype(bf16)
        if laid:
            rows, wide = dwo_ref.shape[1:]
            for at, (core, y, tm) in enumerate(spots(BY_Y)):
                first = (tm * 2 + core) * rows
                dwo_ref[at] = value[first : first + rows, y * wide : (y + 1) * wide]
        else:
            dwo_ref[...] = value


def back(grad_l, grad_s, saved_l, saved_s, mixed_l, mixed_s, wo, gain, up, down, laid=False):
    (hidden_l, second_l, active_l, slope_l) = saved_l
    (hidden_s, second_s, active_s, slope_s) = saved_s
    large, width = grad_l.shape
    small = grad_s.shape[0]
    rows = large + small
    hidden = up.shape[1]
    part = width
    steps = hidden // part
    fl, fs = whole((large, width)), whole((small, width))
    square = whole((width, width))
    up_slab = slab_of(width, part)
    down_slab = pl.BlockSpec((part, width), lambda i: (i, 0))
    shape = jax.ShapeDtypeStruct
    out_up, out_down, out_square = up_slab, down_slab, square
    up_shape, down_shape, square_shape = up.shape, down.shape, (width, width)
    if laid:
        block = (width // 8, width)
        up_shape = down_shape = (32,) + block
        square_shape = (32, width // 16, width // 2)
        out_up = pl.BlockSpec((8,) + block, lambda i: (i, 0, 0))
        out_down, out_square = whole(down_shape), whole(square_shape)
    return pl.pallas_call(
        functools.partial(back_kernel, steps, len(mixed_l), (large, small), laid),
        grid=(steps,),
        in_specs=[fl, fs]
        + [slab_of(large, part), slab_of(small, part)] * 2
        + [fl, fs, fl, fs]
        + [whole(m.shape) for m in mixed_l]
        + [fs, square, whole((1, width)), up_slab, down_slab],
        out_specs=[fl, fs, fl, fs, out_up, out_down, out_square, whole((1, width))],
        out_shape=[
            shape((large, width), f32),
            shape((small, width), f32),
            shape((large, width), bf16),
            shape((small, width), bf16),
            shape(up_shape, bf16),
            shape(down_shape, bf16),
            shape(square_shape, bf16),
            shape((1, width), f32),
        ],
        scratch_shapes=[
            pltpu.VMEM((rows, width), bf16),
            pltpu.VMEM((rows, width), bf16),
            pltpu.VMEM((rows, width), f32),
            pltpu.VMEM((rows, part), bf16),
            pltpu.VMEM((rows, part), bf16),
            pltpu.VMEM((rows, width), bf16),
        ],
        compiler_params=pltpu.CompilerParams(vmem_limit_bytes=56 << 20),
        cost_estimate=pl.CostEstimate(
            flops=2 * rows * width * (4 * hidden + 2 * width),
            bytes_accessed=width * width * 36 + rows * width * 40,
            transcendentals=0,
        ),
        name="back",
    )(
        grad_l, grad_s, active_l, active_s, slope_l, slope_s, second_l, second_s, hidden_l, hidden_s,
        *mixed_l, mixed_s, wo, gain, up, down,
    )


MESH = pl.DeviceIdType.MESH
BY_Y = ("core", "y", "zl", "x", "zh")
BY_ZL = ("core", "zl", "y", "x", "zh")
BY_X = ("core", "x", "zl", "y", "zh")
BY_YX = ("core", "y", "x", "zl", "zh")


def spots(order):
    out = []
    for at in range(32):
        bit = {name: (at >> (4 - i)) & 1 for i, name in enumerate(order)}
        out.append((bit["core"], bit["y"], (bit["zh"] * 2 + bit["zl"]) * 2 + bit["x"]))
    return out


class Here:
    def __init__(self):
        tm, seq = lax.axis_index("tm"), lax.axis_index("seq")
        self.tm, self.seq = tm, seq
        self.bit = {
            "zh": tm // 4,
            "zl": (tm // 2) % 2,
            "x": tm % 2,
            "y": seq // 2,
            "core": seq % 2,
        }

    def partner(self, *names):
        tm, seq = self.tm, self.seq
        for name in names:
            one = 1 - 2 * self.bit[name]
            if name in ("y", "core"):
                seq = seq + one * (2 if name == "y" else 1)
            else:
                tm = tm + one * {"zh": 4, "zl": 2, "x": 1}[name]
        return (tm, seq)

    def greet(self, partners):
        barrier = pltpu.get_barrier_semaphore()
        for names in partners:
            pl.semaphore_signal(
                barrier, inc=1, device_id=self.partner(*names), device_id_type=MESH
            )
        pl.semaphore_wait(barrier, len(partners))


ALL_PARTNERS = (("core",), ("y",), ("zl",), ("x",), ("zh",), ("y", "core"))


class Flow:
    def __init__(self, here, order, refs):
        self.here, self.order = here, order
        self.local, self.keep = refs[0], refs[1]
        self.got = refs[2:7]
        self.out = refs[7]
        self.send_sem, self.recv_sem = refs[8], refs[9]

    def copy(self, step):
        name = self.order[step]
        half = 16 >> step
        source = self.local if step == 0 else self.got[step - 1]
        at = (1 - self.here.bit[name]) * half
        return pltpu.make_async_remote_copy(
            src_ref=source.at[pl.ds(at, half)],
            dst_ref=self.got[step],
            send_sem=self.send_sem.at[step],
            recv_sem=self.recv_sem.at[step],
            device_id=self.here.partner(name),
            device_id_type=MESH,
        )

    def keep_copy(self):
        at = self.here.bit[self.order[0]] * 16
        return pltpu.make_async_copy(
            self.local.at[pl.ds(at, 16)], self.keep, self.send_sem.at[8]
        )

    def start(self, step):
        self.copy(step).start()
        if step == 0 and self.keep is not None:
            self.keep_copy().start()

    def finish(self, step):
        half = 16 >> step
        self.copy(step).wait()
        got = self.got[step]
        at = self.here.bit[self.order[step]] * half
        if step == 0 and self.keep is not None:
            self.keep_copy().wait()
            source, at = self.keep, 0
        else:
            source = self.local if step == 0 else self.got[step - 1]

        def body(i, carry):
            got[i] = got[i] + source[at + i]
            return carry

        if half == 1:
            got[0] = got[0] + source[at]
        else:
            lax.fori_loop(0, half, body, 0)

    def spread_copies(self):
        here = self.here
        slot = here.bit["core"] * 2 + here.bit["y"]
        return [
            pltpu.make_async_remote_copy(
                src_ref=self.got[4].at[0],
                dst_ref=self.out.at[slot],
                send_sem=self.send_sem.at[5 + i],
                recv_sem=self.recv_sem.at[5 + i],
                device_id=here.partner(*names),
                device_id_type=MESH,
            )
            for i, names in enumerate((("core",), ("y",), ("y", "core")))
        ]

    def spread(self):
        for copy in self.spread_copies():
            copy.start()
        slot = self.here.bit["core"] * 2 + self.here.bit["y"]
        self.out[slot] = self.got[4][0]

    def gathered(self):
        for copy in self.spread_copies():
            copy.wait()

    def act(self, stage):
        if stage == 0:
            self.start(0)
        elif stage < 5:
            self.finish(stage - 1)
            self.start(stage)
        elif stage == 5:
            self.finish(4)
            self.spread()
        else:
            self.gathered()


def flow_scratch(rows, wide, keep):
    blocks = [pltpu.VMEM((16, rows, wide), bf16)] if keep else []
    for half in (16, 8, 4, 2, 1):
        blocks.append(pltpu.VMEM((half, rows, wide), bf16))
    blocks.append(pltpu.VMEM((4, rows, wide), bf16))
    return blocks + [pltpu.SemaphoreType.DMA((9,)), pltpu.SemaphoreType.DMA((8,))]


def pair_back(query, grad, out, logsum, mask, keys_at, values_at, mk_ref, block, store):
    count = query.shape[0]
    total = keys_at.shape[0]
    lane = lax.broadcasted_iota(jnp.int32, (count, LANES), 1)
    low = lane < HALF
    spot = lane % HALF
    zero = jnp.zeros_like(query)
    product = grad.astype(f32) * out.astype(f32)
    delta0 = jnp.sum(jnp.where(low, product, 0.0), axis=1, keepdims=True)
    delta1 = jnp.sum(jnp.where(low, 0.0, product), axis=1, keepdims=True)
    delta = jnp.where(low, delta1, delta0)

    def beside(base, value):
        a, b, c = three(-value)
        return jnp.where(spot == 4, a, jnp.where(spot == 5, b, jnp.where(spot == 6, c, base)))

    query_side = beside(mask, logsum)
    grad_side = beside(zero, delta)
    query_a = (jnp.where(low, query, query_side), jnp.where(low, query_side, query))
    grad_a = (jnp.where(low, grad, grad_side), jnp.where(low, grad_side, grad))
    query_m = (jnp.where(low, query, zero), jnp.where(low, zero, query))
    grad_m = (jnp.where(low, grad, zero), jnp.where(low, zero, grad))
    lane_k = lax.broadcasted_iota(jnp.int32, (block, LANES), 1)
    low_k = lane_k < HALF
    spot_k = lane_k % HALF
    one = jnp.where((spot_k >= 4) & (spot_k < 7), 1.0, 0.0).astype(bf16)
    dq = jnp.zeros((count, LANES), f32)
    for number in range(total // block):
        here = pl.ds(number * block, block)
        keys, values = keys_at[here, :], values_at[here, :]
        side = mk_ref[here, :] + one
        nought = jnp.zeros_like(keys)
        dk = jnp.zeros((block, LANES), f32)
        dv = jnp.zeros((block, LANES), f32)
        for head in (0, 1):
            pick = lambda a, b: jnp.where(low_k, a, b) if head == 0 else jnp.where(low_k, b, a)
            prob = jnp.exp2(dot(query_a[head], pick(keys, side), NT))
            change = dot(grad_a[head], pick(values, one), NT)
            score_grad = (prob * change).astype(bf16)
            dv += dot(prob.astype(bf16), grad_m[head], TN)
            dk += dot(score_grad, query_m[head], TN)
            dq += dot(score_grad, pick(keys, nought))
        store(number, (dk * LN2).astype(bf16), dv.astype(bf16))
    return (dq * HALF**-0.5).astype(bf16)


class Exchange:
    def __init__(self, here, rows, refs):
        self.here, self.rows = here, rows
        self.sums, self.send, self.got_core, self.across, self.got_x = refs[:5]
        self.sems = refs[5]

    def copy_core(self, pair):
        return pltpu.make_async_remote_copy(
            src_ref=self.send.at[pair % 2],
            dst_ref=self.got_core.at[pair],
            send_sem=self.sems.at[0, pair],
            recv_sem=self.sems.at[1, pair],
            device_id=self.here.partner("core"),
            device_id_type=MESH,
        )

    def copy_x(self, pair):
        return pltpu.make_async_remote_copy(
            src_ref=self.across.at[pair % 2],
            dst_ref=self.got_x.at[pair],
            send_sem=self.sems.at[2, pair],
            recv_sem=self.sems.at[3, pair],
            device_id=self.here.partner("x"),
            device_id_type=MESH,
        )

    def free(self, pair):
        self.copy_core(pair).wait_send()

    def put(self, pair, total, block):
        half = total // 2

        def store(number, dk, dv):
            there = pl.ds(number * block % half, block)
            if number * block < half:
                self.sums[pair % 3, 0, there, :] = dk
                self.sums[pair % 3, 1, there, :] = dv
            else:
                self.send[pair % 2, 0, there, :] = dk
                self.send[pair % 2, 1, there, :] = dv

        return store

    def pass_on(self, pair, wait_before):
        rows = self.rows
        self.copy_core(pair).wait_recv()
        if wait_before:
            self.copy_x(pair - 2).wait_send()
        far = pl.ds(rows, rows)
        for i in (0, 1):
            self.across[pair % 2, i] = (
                self.sums[pair % 3, i, far, :] + self.got_core[pair, i, far, :]
            )
        self.copy_x(pair).start()

    def take(self, pair, out_ref):
        near = pl.ds(0, self.rows)
        self.copy_x(pair).wait_recv()
        for i in (0, 1):
            out_ref[pair, i] = (
                self.sums[pair % 3, i, near, :].astype(f32)
                + self.got_core[pair, i, near, :].astype(f32)
                + self.got_x[pair, i].astype(f32)
            ).astype(bf16)


def exchange_scratch(pairs, rows):
    return [
        pltpu.VMEM((3, 2, 2 * rows, LANES), bf16),
        pltpu.VMEM((2, 2, 2 * rows, LANES), bf16),
        pltpu.VMEM((pairs, 2, 2 * rows, LANES), bf16),
        pltpu.VMEM((2, 2, rows, LANES), bf16),
        pltpu.VMEM((pairs, 2, rows, LANES), bf16),
        pltpu.SemaphoreType.DMA((4, pairs)),
    ]


def selves_kernel(pairs, plan, blocks, *refs):
    orders, shapes, stages = plan
    large_refs, refs = refs[:6], refs[6:]
    groups = 3
    kv_large = [refs[4 * g : 4 * g + 4] for g in range(groups)]
    refs = refs[4 * groups :]
    small_refs, kv_small, refs = refs[:6], refs[6:10], refs[10:]
    flows = len(orders)
    locals_, refs = refs[:flows], refs[flows:]
    dq_l, dkv_l, dq_s, dkv_s = refs[:4]
    sums, refs = refs[4 : 4 + flows], refs[4 + flows :]
    keys_l, values_l, keys_s, values_s = refs[:4]
    ex_l, ex_s, refs = refs[4:10], refs[10:16], refs[16:]
    here = Here()
    rows_l, rows_s = keys_l.shape[0] // 4, keys_s.shape[0] // 4
    large, small = Exchange(here, rows_l, ex_l), Exchange(here, rows_s, ex_s)
    running = []
    for flow in range(flows):
        running.append(Flow(here, orders[flow], [locals_[flow]] + list(refs[:9])))
        refs = refs[9:]
    step = pl.program_id(0)

    @pl.when(step == 0)
    def _():
        here.greet(ALL_PARTNERS)
        for flow in running:
            flow.act(0)

    def move(exchange, pair, out_ref):
        exchange.copy_core(pair).start()

        @pl.when((pair >= 1) & (pair < 3))
        def _():
            exchange.pass_on(pair - 1, False)

        @pl.when(pair >= 3)
        def _():
            exchange.pass_on(pair - 1, True)

        @pl.when(pair >= 2)
        def _():
            exchange.take(pair - 2, out_ref)

    def attention(exchange, pair, refs, kv_of, keys_at, values_at, block, dq_ref):
        q_ref, do_ref, o_ref, l_ref, mq_ref, mk_ref = refs
        for when, kv_refs in kv_of:

            def fill(kv_refs=kv_refs):
                at = 0
                for kv_ref in kv_refs:
                    there = pl.ds(at, kv_ref.shape[1])
                    keys_at[there, :] = kv_ref[0]
                    values_at[there, :] = kv_ref[1]
                    at += kv_ref.shape[1]

            if when is None:
                fill()
            else:
                pl.when(when)(fill)

        @pl.when(pair >= 2)
        def _():
            exchange.free(pair - 2)

        dq_ref[...] = pair_back(
            q_ref[...], do_ref[...], o_ref[...], l_ref[...], mq_ref[...],
            keys_at, values_at, mk_ref, block, exchange.put(pair, keys_at.shape[0], block),
        )

    @pl.when(step < pairs)
    def _():
        kv_of = [(step // 2 == g, kv_large[g]) for g in range(groups)]
        attention(large, step, large_refs, kv_of, keys_l, values_l, blocks[0], dq_l)
        move(large, step, dkv_l)

    @pl.when(step >= pairs)
    def _():
        pair = step - pairs
        attention(small, pair, small_refs, [(None, kv_small)], keys_s, values_s, blocks[1], dq_s)
        move(small, pair, dkv_s)

    @pl.when(step == pairs)
    def _():
        large.pass_on(pairs - 1, True)
        large.take(pairs - 2, dkv_l)

    @pl.when(step == pairs + 1)
    def _():
        large.take(pairs - 1, dkv_l)
        for pair in (pairs - 2, pairs - 1):
            large.free(pair)
            large.copy_x(pair).wait_send()

    @pl.when(step == 2 * pairs - 1)
    def _():
        small.pass_on(pairs - 1, True)

    for at in range(2 * pairs):
        todo = []
        for stage in range(1, 7):
            for flow in range(flows):
                if stages[flow][stage - 1] == at:
                    todo.append((running[flow], stage))
        if todo:

            @pl.when(step == at)
            def _(todo=todo):
                for flow, stage in todo:
                    flow.act(stage)

    @pl.when(step == 2 * pairs - 1)
    def _():
        small.take(pairs - 2, dkv_s)
        small.take(pairs - 1, dkv_s)
        for pair in (pairs - 2, pairs - 1):
            small.free(pair)
            small.copy_x(pair).wait_send()
        for flow, sum_ref in zip(running, sums):
            sum_ref[...] = flow.out[...]


def selves_back(large, large_kv, small, small_kv, flows, orders, stages):
    count, width = large[0].shape
    few = small[0].shape[0]
    pairs = width // LANES
    total, less = large[5].shape[0], small[5].shape[0]
    shapes = [flow.shape[1:] for flow in flows]
    blocks = (largest_block(total // 2, 512), largest_block(less // 2, 512))
    first = lambda i: jnp.minimum(i, pairs - 1)
    last = lambda i: jnp.maximum(i - pairs, 0)
    in_specs = [pl.BlockSpec((count, LANES), lambda i: (0, first(i)))] * 4
    in_specs += [whole((count, LANES)), whole((total, LANES))]
    for group in range(3):
        spec = pl.BlockSpec(
            (2, count, LANES), lambda i, g=group: (0, 0, jnp.clip(i - 2 * g, 0, 1))
        )
        in_specs += [spec] * 4
    in_specs += [pl.BlockSpec((few, LANES), lambda i: (0, last(i)))] * 4
    in_specs += [whole((few, LANES)), whole((less, LANES))]
    in_specs += [pl.BlockSpec((2, few, LANES), lambda i: (0, 0, last(i)))] * 4
    in_specs += [pl.BlockSpec(memory_space=pl.ANY)] * len(flows)
    shape = jax.ShapeDtypeStruct
    out_shape = [
        shape((count, width), bf16),
        shape((pairs, 2, count, LANES), bf16),
        shape((few, width), bf16),
        shape((pairs, 2, few, LANES), bf16),
    ] + [shape((4,) + block, bf16) for block in shapes]
    out_specs = [
        pl.BlockSpec((count, LANES), lambda i: (0, first(i))),
        whole((pairs, 2, count, LANES)),
        pl.BlockSpec((few, LANES), lambda i: (0, last(i))),
        whole((pairs, 2, few, LANES)),
    ] + [whole((4,) + block) for block in shapes]
    scratch = [pltpu.VMEM((total, LANES), bf16)] * 2 + [pltpu.VMEM((less, LANES), bf16)] * 2
    scratch += exchange_scratch(pairs, count) + exchange_scratch(pairs, few)
    for block in shapes:
        scratch += flow_scratch(*block, True)
    result = pl.pallas_call(
        functools.partial(selves_kernel, pairs, (orders, shapes, stages), blocks),
        grid=(2 * pairs,),
        in_specs=in_specs,
        out_specs=out_specs,
        out_shape=out_shape,
        scratch_shapes=scratch,
        compiler_params=pltpu.CompilerParams(
            vmem_limit_bytes=60 << 20, collective_id=1, has_side_effects=True
        ),
        cost_estimate=pl.CostEstimate(
            flops=20 * width * (count * total + few * less),
            bytes_accessed=64 * count * width,
            transcendentals=count * total * width // HALF,
        ),
        name="selves_back",
    )(*large, *[p for kv in large_kv for p in kv], *small, *small_kv, *flows)
    return result[:4], result[4:]


def view_kernel(pairs, sizes, *refs):
    (dql, dkvl, dqs, dkvs, xl, xs, hl, hs, gain, wq, wk, wv) = refs[:12]
    gl_ref, gs_ref, gain_ref, grads = refs[12:]
    large, small = sizes
    top, bottom = pl.ds(0, large), pl.ds(large, small)
    total = None
    for which, weight in enumerate((wq, wk, wv)):
        if which == 0:
            grads[top, :] = dql[...]
            grads[bottom, :] = dqs[...]
        else:
            for pair in range(pairs):
                lanes = pl.ds(pair * LANES, LANES)
                grads[top, lanes] = dkvl[pair, which - 1]
                grads[bottom, lanes] = dkvs[pair, which - 1]
        part = dot(grads[...], weight[...], NT)
        total = part if total is None else total + part
    extra, gain_l = norm_back(total[:large], xl[...].astype(f32), gain[...])
    gl_ref[...] = (hl[...] + extra).astype(bf16)
    extra, gain_s = norm_back(total[large:], xs[...].astype(f32), gain[...])
    gs_ref[...] = (hs[...] + extra).astype(bf16)
    gain_ref[...] = gain_l + gain_s


def view_grads(selves, large, small, hidden_l, hidden_s, gain, weights):
    count, width = large.shape
    few = small.shape[0]
    shape = jax.ShapeDtypeStruct
    return pl.pallas_call(
        functools.partial(view_kernel, width // LANES, (count, few)),
        out_shape=[
            shape((count, width), bf16),
            shape((few, width), bf16),
            shape((1, width), f32),
        ],
        scratch_shapes=[pltpu.VMEM((count + few, width), bf16)],
        compiler_params=pltpu.CompilerParams(vmem_limit_bytes=48 << 20),
        cost_estimate=pl.CostEstimate(
            flops=6 * (count + few) * width * width,
            bytes_accessed=6 * width * width + 20 * (count + few) * width,
            transcendentals=0,
        ),
        name="view_grads",
    )(*selves, large, small, hidden_l, hidden_s, gain, *weights)


LAST_ORDERS = (BY_YX, BY_X, BY_ZL)
GAIN_ORDER = ("core", "y", "x", "zl", "zh")


def last_kernel(pairs, sizes, *refs):
    dql, dkvl, dqs, dkvs, nl, ns, gains = refs[:7]
    sum_refs, gain_ref = refs[7:10], refs[10]
    normed, grads, refs = refs[11], refs[12], refs[13:]
    here = Here()
    flows = []
    for order in LAST_ORDERS:
        local, refs = refs[0], refs[1:]
        flows.append(Flow(here, order, [local, None] + list(refs[:8])))
        refs = refs[8:]
    state, got, gain_sems = refs
    large, small = sizes
    top, bottom = pl.ds(0, large), pl.ds(large, small)
    here.greet(ALL_PARTNERS)

    def gain_copy(step):
        return pltpu.make_async_remote_copy(
            src_ref=state.at[step],
            dst_ref=got.at[step],
            send_sem=gain_sems.at[0, step],
            recv_sem=gain_sems.at[1, step],
            device_id=here.partner(GAIN_ORDER[step]),
            device_id_type=MESH,
        )

    state[0] = gains[...]
    gain_copy(0).start()
    normed[top, :] = nl[...]
    normed[bottom, :] = ns[...]
    for which, flow in enumerate(flows):
        if which == 0:
            grads[top, :] = dql[...]
            grads[bottom, :] = dqs[...]
        else:
            for pair in range(pairs):
                lanes = pl.ds(pair * LANES, LANES)
                grads[top, lanes] = dkvl[pair, which - 1]
                grads[bottom, lanes] = dkvs[pair, which - 1]
        value = dot(normed[...], grads[...], TN).astype(bf16)
        rows, wide = flow.local.shape[1:]
        for at, (core, y, tm) in enumerate(spots(flow.order)):
            first = tm * 2 * rows + core * rows
            flow.local[at] = value[first : first + rows, y * wide : (y + 1) * wide]
        flow.act(0)
    for stage in range(1, 7):
        for flow in flows:
            flow.act(stage)
        if stage <= 5:
            gain_copy(stage - 1).wait()
            total = state[stage - 1] + got[stage - 1]
            if stage < 5:
                state[stage] = total
                gain_copy(stage).start()
            else:
                gain_ref[...] = total
    for flow, sum_ref in zip(flows, sum_refs):
        sum_ref[...] = flow.out[...]


def last_sums(selves, normed_l, normed_s, gains):
    count, width = normed_l.shape
    few = normed_s.shape[0]
    rows, wide = width // 16, width // 2
    shape = jax.ShapeDtypeStruct
    scratch = [pltpu.VMEM((count + few, width), bf16), pltpu.VMEM((count + few, width), bf16)]
    for _ in LAST_ORDERS:
        scratch += [pltpu.VMEM((32, rows, wide), bf16)] + flow_scratch(rows, wide, False)
    scratch += [
        pltpu.VMEM((5,) + gains.shape, f32),
        pltpu.VMEM((5,) + gains.shape, f32),
        pltpu.SemaphoreType.DMA((2, 5)),
    ]
    result = pl.pallas_call(
        functools.partial(last_kernel, width // LANES, (count, few)),
        out_shape=[shape((4, rows, wide), bf16)] * 3 + [shape(gains.shape, f32)],
        scratch_shapes=scratch,
        compiler_params=pltpu.CompilerParams(
            vmem_limit_bytes=48 << 20, collective_id=2, has_side_effects=True
        ),
        cost_estimate=pl.CostEstimate(
            flops=40 * (count + few) * width * width,
            bytes_accessed=40 * (count + few) * width,
            transcendentals=0,
        ),
        name="last_sums",
    )(*selves, normed_l, normed_s, gains)
    return result[:3], result[3]


def after(value, *needed):
    return lax.optimization_barrier((value, needed))[0]


SELVES_ORDERS = (BY_Y, BY_ZL, BY_Y, BY_ZL)
SELVES_STAGES = (
    (0, 4, 6, 8, 9, 11),
    (0, 4, 6, 8, 9, 11),
    (0, 4, 6, 8, 10, 11),
    (0, 6, 8, 9, 10, 11),
)


def paired_end(views, weights, large, large_kv, small, small_kv, grads, normed, gains, united_view, restore):
    large_view, small_view, large_hidden, small_hidden, first_gain = views
    up_grad, down_grad, output_grad, cross_parts = grads
    width = large_view.shape[1]
    rows = width // 8
    names = ("core", "y", "zh", "zl", "x")
    turn = [names.index(name) for name in SELVES_ORDERS[3]] + [5, 6]
    cross = jnp.stack(cross_parts).reshape(2, 2, 2, 2, 2, rows, width)
    cross = jnp.transpose(cross, turn).reshape(32, rows, width)
    selves, sums = selves_back(
        large, large_kv, small, small_kv, (up_grad, down_grad, output_grad, cross),
        SELVES_ORDERS, SELVES_STAGES,
    )
    large_grad, small_grad, gain = view_grads(
        selves, large_view, small_view, large_hidden, small_hidden, first_gain, weights
    )
    large_grad, small_grad = restore(large_grad), restore(small_grad)
    gains = jnp.concatenate((gain,) + gains + (jnp.zeros((4, width), f32),), axis=0)
    last, gains = last_sums(selves, *normed, gains)

    def square(total):
        total = total.astype(f32).reshape(2, 2, width // 16, width // 2)
        return jnp.transpose(total, (0, 2, 1, 3)).reshape(rows, width)

    up, down, output, cross = (total.astype(f32) for total in sums)
    at = lax.axis_index("tm") * rows
    gains = [lax.dynamic_slice(gains, (i, at), (1, rows))[0] for i in range(4)]
    return (
        united_view,
        large_grad.astype(f32),
        small_grad.astype(f32),
        gains[0],
        square(last[0]),
        square(last[1]),
        square(last[2]),
        square(output),
        gains[1],
        jnp.transpose(up, (1, 0, 2)).reshape(rows, 4 * width),
        down.reshape(4 * rows, width),
        gains[2],
        gains[3],
        cross[1],
        cross[2],
        cross[3],
        cross[0],
    )


def per_device(tm, seq_size, *args):
    (
        large_view,
        small_view,
        clip_ids,
        first_gain,
        query_weight,
        key_weight,
        value_weight,
        output_weight,
        second_gain,
        up_weight,
        down_weight,
        query_gain,
        context_gain,
        cross_query,
        cross_key,
        cross_value,
        cross_output,
        cotangent,
    ) = args
    seqs, count, width = large_view.shape
    side = tm // 4
    gains = [
        g.astype(f32).reshape(1, width)
        for g in (first_gain, second_gain, query_gain, context_gain)
    ]
    first_gain, second_gain, query_gain, context_gain = gains

    tm_at = lax.axis_index("tm")
    seq_at = lax.axis_index("seq")
    z, x = tm_at // side, tm_at % side
    y, core = seq_at // 2, seq_at % 2
    places = [
        (pz, px, py, pc)
        for pz in range(4)
        for px in range(side)
        for py in range(2)
        for pc in range(2)
    ]

    def number(place):
        return (place[0] * side + place[1]) * seq_size + place[2] * 2 + place[3]

    def permute(value, place):
        pairs = [(number(at), number(place(*at))) for at in places]
        return lax.ppermute(value, ("tm", "seq"), pairs)

    def inverse(place):
        table = {place(*at): at for at in places}
        return lambda *at: table[at]

    go = (
        lambda z, x, y, c: (2 * c + z % 2, x, y, z // 2),
        lambda z, x, y, c: (2 * c + 1 - z % 2, x, y, z // 2),
    )
    back_home = tuple(inverse(place) for place in go)
    other_core = lambda value: permute(value, lambda z, x, y, c: (z, x, y, 1 - c))
    other_y = lambda value: permute(value, lambda z, x, y, c: (z, x, 1 - y, c))
    by_x = lambda value, d: permute(value, lambda z, x, y, c: (z, (x + d) % side, y, c))
    odd = z % 2 == 1

    def relocate(value):
        near = jnp.where(odd, value[1], value[0])
        far = jnp.where(odd, value[0], value[1])
        return jnp.concatenate([permute(near, go[0]), permute(far, go[1])], axis=0)

    def restore(value):
        rows = value.shape[0] // 2
        near, far = permute(value[:rows], back_home[0]), permute(value[rows:], back_home[1])
        return jnp.where(odd, jnp.stack([far, near]), jnp.stack([near, far]))

    def join(parts, axis):
        return parts[0] if len(parts) == 1 else jnp.concatenate(parts, axis=axis)

    def gather(value, axis=1):
        across = join([by_x(value, d) for d in range(1, side)], axis)
        return (value, across, other_core(value), other_core(across))

    def add(a, b):
        return (a.astype(f32) + b.astype(f32)).astype(bf16)

    def scatter_core(keep, send):
        return add(keep, other_core(send))

    def scatter_x(sums):
        rows = sums.shape[1] // side
        total = sums[:, :rows].astype(f32)
        for d in range(1, side):
            total = total + by_x(sums[:, d * rows : (d + 1) * rows], -d).astype(f32)
        return total.astype(bf16)

    groups = 3
    part = width // groups
    short_clips = gather(relocate(clip_ids[:, ::2].astype(f32)), 0)
    small = relocate(small_view)
    large = relocate(large_view)
    grad_out = relocate(after(cotangent, large))
    spot = lax.broadcasted_iota(jnp.int32, (1, LANES), 1) % HALF

    def mask_of_keys(numbers):
        away = numbers.astype(jnp.int32)[:, None] != spot
        return jnp.where((spot < 4) & away, NEGATIVE, 0.0).astype(bf16)

    def mask_of_queries(numbers):
        same = numbers.astype(jnp.int32)[:, None] == spot
        return jnp.where((spot < 4) & same, 1.0, 0.0).astype(bf16)

    short = jnp.concatenate(short_clips)
    small_mask_k = mask_of_keys(short)
    large_mask_k = mask_of_keys(jnp.repeat(short, 2))
    small_mask_q = mask_of_queries(short_clips[0])
    large_mask_q = mask_of_queries(jnp.repeat(short_clips[0], 2))

    small_normed, small_q, small_kv = front(
        small, first_gain, query_weight, key_weight, value_weight, 1
    )
    small_kv = gather(small_kv[0])
    large_normed, large_q, large_kv = front(
        large, first_gain, query_weight, key_weight, value_weight, groups
    )
    large_kv = [gather(kv) for kv in large_kv]
    small_mixed, small_logsum = attend(small_q, small_kv, small_mask_q, small_mask_k, 0, width)
    small_merged, *small_saved, context, cross_kv = rest(
        small, [small_mixed], output_weight, second_gain, up_weight, down_weight,
        context_gain, (cross_key, cross_value),
    )
    cross_kv = gather(cross_kv)
    united_grad = dot(grad_out, cross_output, NT).astype(bf16)
    large_out = ()
    for group, kv in enumerate(large_kv):
        large_out = attend(large_q, kv, large_mask_q, large_mask_k, group * part, part, large_out)
    large_mixed, large_logsum = large_out
    large_merged, *large_saved, asked, cross_q = rest(
        large, [large_mixed], output_weight, second_gain, up_weight, down_weight,
        query_gain, (cross_query,),
    )
    united, cross_logsum = attend(cross_q, cross_kv, large_mask_q, small_mask_k, 0, width)
    united_view = restore((large_merged + dot(united, cross_output)).astype(bf16))

    bits = side.bit_length() - 1
    moves = {"zh": lambda z, x, y, c: (z ^ 2, x, y, c), "zl": lambda z, x, y, c: (z ^ 1, x, y, c)}
    mine = {"zh": z // 2, "zl": z % 2}
    axes = {"zh": 0, "zl": 1}
    for bit in range(bits):
        flip = 1 << (bits - 1 - bit)
        moves[f"x{bit}"] = lambda z, x, y, c, flip=flip: (z, x ^ flip, y, c)
        mine[f"x{bit}"] = (x // flip) % 2
        axes[f"x{bit}"] = 2 + bit
    moves["core"] = lambda z, x, y, c: (z, x, y, 1 - c)
    moves["y"] = lambda z, x, y, c: (z, x, 1 - y, c)
    mine["core"], mine["y"] = core, y
    axes["core"], axes["y"] = 2 + bits, 3 + bits
    by_y = ["core", "y", "zl"] + [f"x{bit}" for bit in range(bits)] + ["zh"]
    by_zl = ["core", "zl", "y"] + [f"x{bit}" for bit in range(bits)] + ["zh"]
    by_yx = ["core", "y"] + [f"x{bit}" for bit in range(bits)] + ["zl", "zh"]

    class Sum:
        def __init__(self, local, order):
            rows, wide = local.shape
            self.value = local.reshape((2,) * (2 + bits) + (rows // tm, wide))
            self.todo = list(order)
            self.rows, self.wide = rows // tm, wide

        def step(self, *needed):
            name = self.todo.pop(0)
            axis = axes[name]
            size = self.value.shape[axis] // 2
            at = mine[name]
            keep = lax.dynamic_slice_in_dim(self.value, at * size, size, axis)
            send = lax.dynamic_slice_in_dim(self.value, (1 - at) * size, size, axis)
            self.value = add(keep, permute(send, moves[name]))
            return self.value

        def finish(self):
            while self.todo:
                self.step()
            value = self.value.reshape(self.rows // 2, self.wide // 2)
            other = other_y(value)
            value = jnp.where(
                y == 0,
                jnp.concatenate([value, other], axis=1),
                jnp.concatenate([other, value], axis=1),
            )
            other = other_core(value)
            return jnp.where(
                core == 0,
                jnp.concatenate([value, other], axis=0),
                jnp.concatenate([other, value], axis=0),
            ).astype(f32)

    cross_groups = 2
    cross_part = width // cross_groups
    dcq, dckv = [], []
    for group in range(cross_groups):
        query = after(cross_q, *dcq[-1:])
        at = group * cross_part
        dq, keep, send = attend_back(
            query, cross_kv, united_grad, united, cross_logsum,
            large_mask_q, small_mask_k, at, at, at, cross_part,
        )
        dcq.append(dq)
        dckv.append(scatter_x(scatter_core(keep, send)))
    dcq = jnp.concatenate(dcq, axis=1)
    dck = jnp.concatenate([kv[0] for kv in dckv], axis=1)
    dcv = jnp.concatenate([kv[1] for kv in dckv], axis=1)
    extra, query_gain_grad = norm_back(dot(dcq, cross_query, NT), large_merged, query_gain)
    large_merged_grad = grad_out.astype(f32) + extra
    small_merged_grad, context_gain_grad = norm_back(
        dot(dck, cross_key, NT) + dot(dcv, cross_value, NT), small_merged, context_gain
    )
    cross_parts = [
        dot(united, grad_out, TN).astype(bf16),
        dot(asked, dcq, TN).astype(bf16),
        dot(context, dck, TN).astype(bf16),
        dot(context, dcv, TN).astype(bf16),
    ]
    (
        large_hidden_grad,
        small_hidden_grad,
        large_mixed_grad,
        small_mixed_grad,
        up_grad,
        down_grad,
        output_grad,
        second_gain_grad,
    ) = back(
        large_merged_grad, small_merged_grad, large_saved, small_saved, [large_mixed], small_mixed,
        output_weight, second_gain, up_weight, down_weight, side == 2,
    )
    if side == 2:
        return paired_end(
            (large, small, large_hidden_grad, small_hidden_grad, first_gain),
            (query_weight, key_weight, value_weight),
            (large_q, large_mixed_grad, large_mixed, large_logsum, large_mask_q, large_mask_k),
            large_kv,
            (small_q, small_mixed_grad, small_mixed, small_logsum, small_mask_q, small_mask_k),
            small_kv,
            (up_grad, down_grad, output_grad, cross_parts),
            (large_normed, small_normed),
            (second_gain_grad, query_gain_grad, context_gain_grad),
            united_view,
            restore,
        )
    cross_sum = Sum(jnp.concatenate(cross_parts, axis=1), by_y)
    up_sum = Sum(up_grad, by_y)
    down_sum = Sum(down_grad, by_zl)
    cross_sum.step()
    small_dq, keep, send = attend_back(
        after(small_q, cross_sum.value), small_kv, small_mixed_grad, small_mixed, small_logsum,
        small_mask_q, small_mask_k, 0, 0, 0, width,
    )
    small_sums = scatter_core(keep, send)
    up_sum.step()
    down_sum.step()
    cross_sum.step()
    needed = [small_dq, up_sum.value, down_sum.value]
    normed = jnp.concatenate([large_normed, small_normed], axis=0)
    last_sums, dqs, dkvs = [], [], []
    pending = None
    for group in range(groups):
        at = group * part
        dq, keep, send = attend_back(
            after(large_q, *needed), large_kv[group], large_mixed_grad, large_mixed, large_logsum,
            large_mask_q, large_mask_k, at, at, 0, part,
        )
        sums = scatter_core(keep, send)
        dqs.append(dq)
        needed = [dq]
        if group == 0:
            small_dkv = scatter_x(small_sums)
            needed += [cross_sum.value, small_sums]
        if group == 1:
            needed += [small_dkv, up_sum.step(), down_sum.step(), cross_sum.step()]
        if pending is not None:
            needed.append(pending.step())
        dkv = scatter_x(sums)
        dkvs.append(dkv)
        local = jnp.concatenate(
            [
                jnp.concatenate([dq, dkv[0], dkv[1]], axis=1),
                jnp.concatenate(
                    [
                        small_dq[:, at : at + part],
                        small_dkv[0, :, at : at + part],
                        small_dkv[1, :, at : at + part],
                    ],
                    axis=1,
                ),
            ],
            axis=0,
        )
        local = dot(normed, local, TN).astype(bf16)
        pending = Sum(local, by_yx)
        last_sums.append(pending)

    def front_back(view, hidden_grad, dq, dk, dv):
        grad = (
            dot(dq, query_weight, NT) + dot(dk, key_weight, NT) + dot(dv, value_weight, NT)
        )
        extra, gain_part = norm_back(grad, view.astype(f32), first_gain)
        return (hidden_grad + extra).astype(bf16), gain_part

    small_grad, small_gain = front_back(
        small, small_hidden_grad, small_dq, small_dkv[0], small_dkv[1]
    )
    large_grad, large_gain = front_back(
        large,
        large_hidden_grad,
        jnp.concatenate(dqs, axis=1),
        jnp.concatenate([kv[0] for kv in dkvs], axis=1),
        jnp.concatenate([kv[1] for kv in dkvs], axis=1),
    )
    small_grad = restore(small_grad).astype(f32)
    large_grad = restore(large_grad).astype(f32)
    output_sum = Sum(output_grad, by_yx)
    gain_rows = jnp.concatenate(
        [large_gain + small_gain, second_gain_grad, query_gain_grad, context_gain_grad], axis=0
    )
    wide = width // tm
    gain_rows = jnp.transpose(gain_rows.reshape(4, tm, wide), (1, 0, 2)).astype(bf16)
    gain_rows = jnp.pad(gain_rows, ((0, 0), (0, 28), (0, 2 * LANES - wide)))
    gain_sum = Sum(gain_rows.reshape(tm * 32, 2 * LANES), by_yx)

    cross_total = cross_sum.finish()
    up_total = up_sum.finish()
    down_total = down_sum.finish()
    output_total = output_sum.finish()
    last_totals = [total.finish() for total in last_sums]
    gain_total = gain_sum.finish()
    cross_grads = [cross_total[:, i * width : (i + 1) * width] for i in range(4)]
    last_grads = [
        jnp.concatenate([total[:, i * part : (i + 1) * part] for total in last_totals], axis=1)
        for i in range(3)
    ]
    gain_grads = [gain_total[i, :wide] for i in range(4)]
    return (
        united_view,
        large_grad,
        small_grad,
        gain_grads[0],
        last_grads[0],
        last_grads[1],
        last_grads[2],
        output_total,
        gain_grads[1],
        up_total,
        down_total,
        gain_grads[2],
        gain_grads[3],
        cross_grads[1],
        cross_grads[2],
        cross_grads[3],
        cross_grads[0],
    )


def solution(mesh):
    token = P("seq", "tm", None)
    in_specs = (token, token, P("seq", "tm")) + (P(),) * 14 + (token,)
    vector, matrix = P("tm"), P("tm", None)
    out_specs = (
        (token, token, token, vector)
        + (matrix,) * 4
        + (vector, matrix, matrix, vector, vector)
        + (matrix,) * 4
    )
    return jax.shard_map(
        functools.partial(per_device, mesh.shape["tm"], mesh.shape["seq"]),
        mesh=mesh,
        in_specs=in_specs,
        out_specs=out_specs,
        check_vma=False,
    )
```

```python
import functools

import jax
import jax.numpy as jnp
from jax import lax
from jax.experimental import pallas as pl
from jax.experimental.pallas import tpu as pltpu
from jax.sharding import PartitionSpec as P

HEADS = 12
EPS = 1e-05
NEGATIVE = -1e30
LOG2E = 1.4426950408889634
LN2 = 0.6931471805599453
LANES = 128
HALF = 64

bf16 = jnp.bfloat16
f32 = jnp.float32
NT = (((1,), (1,)), ((), ()))
NN = (((1,), (0,)), ((), ()))
TN = (((0,), (0,)), ((), ()))


def dot(a, b, dims=NN):
    return lax.dot_general(a, b, dims, preferred_element_type=f32)


def largest_block(rows, most):
    block = min(rows, most)
    while rows % block or block % 16:
        block -= 1
    return block


def columns(rows, at):
    return pl.BlockSpec((rows, LANES), lambda i: (0, i + at))


def pair_columns(rows, at):
    return pl.BlockSpec((2, rows, LANES), lambda i: (0, 0, i + at))


def whole(shape):
    return pl.BlockSpec(shape, lambda i: (0,) * len(shape))


def attend_kernel(parts, block, *refs):
    q_ref, mq_ref, mk_ref = refs[:3]
    kv_refs = refs[3 : 3 + parts]
    o_ref, l_ref, ka0, ka1, va0, va1 = refs[-6:]
    count = q_ref.shape[0]
    first = 0
    for kv_ref in kv_refs:
        rows = kv_ref.shape[1]
        low = lax.broadcasted_iota(jnp.int32, (rows, LANES), 1) < HALF
        here = pl.ds(first, rows)
        keys, values, mask = kv_ref[0], kv_ref[1], mk_ref[here, :]
        one = jnp.ones_like(values)
        ka0[here, :] = jnp.where(low, keys, mask)
        ka1[here, :] = jnp.where(low, mask, keys)
        va0[here, :] = jnp.where(low, values, one)
        va1[here, :] = jnp.where(low, one, values)
        first += rows
    low = lax.broadcasted_iota(jnp.int32, (block, LANES), 1) < HALF
    for number in range(count // block):
        here = pl.ds(number * block, block)
        query, mask = q_ref[here, :], mq_ref[here, :]
        tops, sums = [], []
        for head, keys, values in ((0, ka0, va0), (1, ka1, va1)):
            mine = jnp.where(low, query, mask) if head == 0 else jnp.where(low, mask, query)
            score = dot(mine, keys[...], NT)
            top = jnp.max(score, axis=1, keepdims=True)
            weight = jnp.exp2(score - top).astype(bf16)
            sums.append(dot(weight, values[...]))
            tops.append(jnp.broadcast_to(top, (block, LANES)))
        total = jnp.where(low, sums[1], sums[0])
        top = jnp.where(low, tops[1], tops[0])
        out = jnp.where(low, sums[0], sums[1])
        o_ref[here, :] = (out / pltpu.roll(total, HALF, 1)).astype(bf16)
        l_ref[here, :] = top + jnp.log2(total)


def attend(query, kv, mask_q, mask_k, at, width, earlier=()):
    count = query.shape[0]
    total = sum(part.shape[1] for part in kv)
    out = lambda kind: jax.ShapeDtypeStruct((count, query.shape[1]), kind)
    given = 3 + len(kv)
    return pl.pallas_call(
        functools.partial(attend_kernel, len(kv), largest_block(count, 256)),
        grid=(width // LANES,),
        in_specs=[columns(count, at // LANES), whole((count, LANES)), whole((total, LANES))]
        + [pair_columns(part.shape[1], 0) for part in kv]
        + [pl.BlockSpec(memory_space=pl.ANY)] * len(earlier),
        out_specs=[columns(count, at // LANES)] * 2,
        out_shape=[out(bf16), out(f32)],
        scratch_shapes=[pltpu.VMEM((total, LANES), bf16)] * 4,
        input_output_aliases={given + i: i for i in range(len(earlier))},
        compiler_params=pltpu.CompilerParams(vmem_limit_bytes=40 << 20),
        cost_estimate=pl.CostEstimate(
            flops=16 * count * total * width,
            bytes_accessed=width * (count * 8 + total * 4),
            transcendentals=count * total * width // HALF,
        ),
        name="attend",
    )(query, mask_q, mask_k, *kv, *earlier)


def three(value):
    first = value.astype(bf16)
    rest = value - first.astype(f32)
    second = rest.astype(bf16)
    return first, second, (rest - second.astype(f32)).astype(bf16)


def attend_back_kernel(parts, block, *refs):
    q_ref, do_ref, o_ref, l_ref, mq_ref, mk_ref = refs[:6]
    kv_refs = refs[6 : 6 + parts]
    dq_ref, keep_ref, send_ref, keys_at, values_at = refs[6 + parts :]
    count = q_ref.shape[0]
    first = 0
    for kv_ref in kv_refs:
        here = pl.ds(first, kv_ref.shape[1])
        keys_at[here, :] = kv_ref[0]
        values_at[here, :] = kv_ref[1]
        first += kv_ref.shape[1]
    lane = lax.broadcasted_iota(jnp.int32, (count, LANES), 1)
    low = lane < HALF
    spot = lane % HALF
    query, grad, mask = q_ref[...], do_ref[...], mq_ref[...]
    zero = jnp.zeros_like(query)
    product = grad.astype(f32) * o_ref[...].astype(f32)
    delta0 = jnp.sum(jnp.where(low, product, 0.0), axis=1, keepdims=True)
    delta1 = jnp.sum(jnp.where(low, 0.0, product), axis=1, keepdims=True)
    delta = jnp.where(low, delta1, delta0)

    def beside(base, value):
        a, b, c = three(-value)
        return jnp.where(spot == 4, a, jnp.where(spot == 5, b, jnp.where(spot == 6, c, base)))

    query_side = beside(mask, l_ref[...])
    grad_side = beside(zero, delta)
    query_a = (jnp.where(low, query, query_side), jnp.where(low, query_side, query))
    grad_a = (jnp.where(low, grad, grad_side), jnp.where(low, grad_side, grad))
    query_m = (jnp.where(low, query, zero), jnp.where(low, zero, query))
    grad_m = (jnp.where(low, grad, zero), jnp.where(low, zero, grad))
    lane_k = lax.broadcasted_iota(jnp.int32, (block, LANES), 1)
    low_k = lane_k < HALF
    spot_k = lane_k % HALF
    one = jnp.where((spot_k >= 4) & (spot_k < 7), 1.0, 0.0).astype(bf16)
    dq = jnp.zeros((count, LANES), f32)
    for number in range(first // block):
        here = pl.ds(number * block, block)
        keys, values = keys_at[here, :], values_at[here, :]
        side = mk_ref[here, :] + one
        nought = jnp.zeros_like(keys)
        dk = jnp.zeros((block, LANES), f32)
        dv = jnp.zeros((block, LANES), f32)
        for head in (0, 1):
            pick = lambda a, b: jnp.where(low_k, a, b) if head == 0 else jnp.where(low_k, b, a)
            prob = jnp.exp2(dot(query_a[head], pick(keys, side), NT))
            change = dot(grad_a[head], pick(values, one), NT)
            score_grad = (prob * change).astype(bf16)
            dv += dot(prob.astype(bf16), grad_m[head], TN)
            dk += dot(score_grad, query_m[head], TN)
            dq += dot(score_grad, pick(keys, nought))
        out_ref = keep_ref if number * block < first // 2 else send_ref
        there = pl.ds(number * block % (first // 2), block)
        out_ref[0, there, :] = (dk * LN2).astype(bf16)
        out_ref[1, there, :] = dv.astype(bf16)
    dq_ref[...] = (dq * HALF**-0.5).astype(bf16)


def attend_back(query, kv, grad, out, logsum, mask_q, mask_k, at, at_out, at_kv, width):
    count = query.shape[0]
    total = sum(part.shape[1] for part in kv)
    return pl.pallas_call(
        functools.partial(attend_back_kernel, len(kv), largest_block(total // 2, 512)),
        grid=(width // LANES,),
        in_specs=[columns(count, at // LANES)] * 2
        + [columns(count, at_out // LANES)] * 2
        + [whole((count, LANES)), whole((total, LANES))]
        + [pair_columns(part.shape[1], at_kv // LANES) for part in kv],
        out_specs=[columns(count, 0)] + [pair_columns(total // 2, 0)] * 2,
        out_shape=[jax.ShapeDtypeStruct((count, width), bf16)]
        + [jax.ShapeDtypeStruct((2, total // 2, width), bf16)] * 2,
        scratch_shapes=[pltpu.VMEM((total, LANES), bf16)] * 2,
        compiler_params=pltpu.CompilerParams(vmem_limit_bytes=40 << 20),
        cost_estimate=pl.CostEstimate(
            flops=20 * count * total * width,
            bytes_accessed=width * (count * 12 + total * 8),
            transcendentals=count * total * width // HALF,
        ),
        name="attend_back",
    )(query, grad, out, logsum, mask_q, mask_k, *kv)


def norm_stats(value):
    mean = jnp.mean(value, axis=-1, keepdims=True)
    centred = value - mean
    spread = jnp.mean(centred * centred, axis=-1, keepdims=True)
    return centred, lax.rsqrt(spread + EPS)


def norm(value, gain):
    centred, scale = norm_stats(value)
    return (centred * scale * gain).astype(bf16)


def norm_back(grad, value, gain):
    centred, scale = norm_stats(value)
    unit = centred * scale
    gain_grad = jnp.sum(grad * unit, axis=0, keepdims=True)
    grad = grad * gain
    extra = scale * (
        grad
        - jnp.mean(grad, axis=-1, keepdims=True)
        - unit * jnp.mean(grad * unit, axis=-1, keepdims=True)
    )
    return extra, gain_grad


Q_SCALE = LOG2E * HALF**-0.5


def front_kernel(x_ref, gain_ref, wq_ref, wk_ref, wv_ref, n_ref, q_ref, *kv_refs):
    normed = norm(x_ref[...].astype(f32), gain_ref[...])
    n_ref[...] = normed
    width = kv_refs[0].shape[2]
    keys = dot(normed, wk_ref[...]).astype(bf16)
    values = dot(normed, wv_ref[...]).astype(bf16)
    for group, kv_ref in enumerate(kv_refs):
        kv_ref[0] = keys[:, group * width : (group + 1) * width]
        kv_ref[1] = values[:, group * width : (group + 1) * width]
    q_ref[...] = (dot(normed, wq_ref[...]) * Q_SCALE).astype(bf16)


def front(view, gain, wq, wk, wv, groups):
    rows, width = view.shape
    part = width // groups
    result = pl.pallas_call(
        front_kernel,
        out_shape=[jax.ShapeDtypeStruct((rows, width), bf16)] * 2
        + [jax.ShapeDtypeStruct((2, rows, part), bf16)] * groups,
        compiler_params=pltpu.CompilerParams(vmem_limit_bytes=40 << 20),
        cost_estimate=pl.CostEstimate(
            flops=6 * rows * width * width,
            bytes_accessed=6 * width * width + 10 * rows * width,
            transcendentals=0,
        ),
        name="front",
    )(view, gain, wq, wk, wv)
    return result[0], result[1], result[2:]


GELU_A = 0.7978845608028654
GELU_B = 0.044715


def gelu_both(value):
    square = value * value
    bent = jnp.tanh(GELU_A * value * (1.0 + GELU_B * square))
    half = 0.5 * (1.0 + bent)
    slope = half + 0.5 * value * (1.0 - bent * bent) * (
        GELU_A * (1.0 + 3.0 * GELU_B * square)
    )
    return value * half, slope


def fill_wide(wide, refs, rows, first):
    at, there = 0, pl.ds(first, rows)
    for ref in refs:
        if len(ref.shape) == 3:
            for pair in range(ref.shape[0]):
                wide[there, at : at + LANES] = ref[pair]
                at += LANES
        else:
            wide[there, at : at + ref.shape[1]] = ref[...]
            at += ref.shape[1]


def rest_kernel(steps, mixes, is_query, *refs):
    x_ref = refs[0]
    mixed_refs = refs[1 : 1 + mixes]
    wo_ref, gain_ref, up_ref, down_ref, next_gain_ref = refs[1 + mixes : 6 + mixes]
    next_refs = refs[6 + mixes : -9]
    merged_ref, hidden_ref, second_ref, active_ref, slope_ref = refs[-9:-4]
    asked_ref, out_ref, total, scratch = refs[-4:]
    step = pl.program_id(0)

    @pl.when(step == 0)
    def _():
        hidden = x_ref[...].astype(f32)
        fill_wide(scratch, mixed_refs, scratch.shape[0], 0)
        hidden = hidden + dot(scratch[...], wo_ref[...])
        hidden_ref[...] = hidden
        second_ref[...] = norm(hidden, gain_ref[...])
        total[...] = hidden

    inner = dot(second_ref[...], up_ref[...])
    active, slope = gelu_both(inner)
    active = active.astype(bf16)
    active_ref[...] = active
    slope_ref[...] = slope.astype(bf16)
    total[...] += dot(active, down_ref[...])

    @pl.when(step == steps - 1)
    def _():
        merged = total[...]
        merged_ref[...] = merged
        asked = norm(merged, next_gain_ref[...])
        asked_ref[...] = asked
        if is_query:
            query = (dot(asked, next_refs[0][...]) * Q_SCALE).astype(bf16)
            if len(out_ref.shape) == 3:
                for pair in range(out_ref.shape[0]):
                    out_ref[pair] = query[:, pair * LANES : (pair + 1) * LANES]
            else:
                out_ref[...] = query
        else:
            out_ref[0] = dot(asked, next_refs[0][...]).astype(bf16)
            out_ref[1] = dot(asked, next_refs[1][...]).astype(bf16)


def rest(view, mixed, wo, gain, up, down, next_gain, next_weights):
    rows, width = view.shape
    steps = up.shape[1] // width
    is_query = len(next_weights) == 1
    flat = whole((rows, width))
    slab = pl.BlockSpec((rows, width), lambda i: (0, i))
    square = whole((width, width))
    shape = lambda kind: jax.ShapeDtypeStruct((rows, width), kind)
    wide = jax.ShapeDtypeStruct((rows, up.shape[1]), bf16)
    last = (rows, width) if is_query else (2, rows, width)
    if len(mixed[0].shape) == 3:
        last = (width // LANES, rows, LANES)
    return pl.pallas_call(
        functools.partial(rest_kernel, steps, len(mixed), is_query),
        grid=(steps,),
        in_specs=[flat]
        + [whole(m.shape) for m in mixed]
        + [square, whole((1, width))]
        + [slab_of(width, width), pl.BlockSpec((width, width), lambda i: (i, 0))]
        + [whole((1, width))]
        + [square] * len(next_weights),
        out_specs=[flat, flat, flat, slab, slab, flat, whole(last)],
        out_shape=[shape(f32), shape(f32), shape(bf16), wide, wide, shape(bf16)]
        + [jax.ShapeDtypeStruct(last, bf16)],
        scratch_shapes=[pltpu.VMEM((rows, width), f32), pltpu.VMEM((rows, width), bf16)],
        compiler_params=pltpu.CompilerParams(vmem_limit_bytes=48 << 20),
        cost_estimate=pl.CostEstimate(
            flops=2 * rows * width * (4 * up.shape[1] // 2 + 2 * width),
            bytes_accessed=width * width * 22 + rows * width * 32,
            transcendentals=rows * up.shape[1],
        ),
        name="rest",
    )(view, *mixed, wo, gain, up, down, next_gain, *next_weights)


def slab_of(rows, width):
    return pl.BlockSpec((rows, width), lambda i: (0, i))


def back_kernel(steps, mixes, sizes, laid, orders, *refs):
    gl_ref, gs_ref, al_ref, as_ref, sl_ref, ss_ref = refs[:6]
    cl_ref, cs_ref, hl_ref, hs_ref = refs[6:10]
    mixed_refs = refs[10 : 10 + mixes]
    mixed_s_ref, wo_ref, gain_ref, up_ref, down_ref = refs[10 + mixes : 15 + mixes]
    flows = len(orders)
    locals_, outs = refs[15 + mixes : 15 + mixes + flows], refs[15 + mixes + flows :]
    (hgl_ref, hgs_ref, ml_ref, ms_ref, dup_ref, ddown_ref, dwo_ref, dgain_ref) = outs[:8]
    sums, outs = outs[8 : 8 + flows], outs[8 + flows :]
    branch, second, total, active, inner_grad, mixed = outs[:6]
    large, small = sizes
    top, bottom = pl.ds(0, large), pl.ds(large, small)
    step = pl.program_id(0)
    if flows:
        here = Here()
        rest_refs = list(outs[6:])
        running = [
            Flow(here, order, local, rest_refs, True, False)
            for order, local in zip(orders, locals_)
        ]

        @pl.when(step == 0)
        def _():
            here.greet(ALL_PARTNERS)
            for flow in running:
                flow.act(0)

    @pl.when(step == 0)
    def _():
        branch[top, :] = gl_ref[...].astype(bf16)
        branch[bottom, :] = gs_ref[...].astype(bf16)
        second[top, :] = cl_ref[...]
        second[bottom, :] = cs_ref[...]
        total[...] = jnp.zeros_like(total)

    grad = dot(branch[...], down_ref[...], NT)
    inner_grad[top, :] = (grad[:large] * sl_ref[...].astype(f32)).astype(bf16)
    inner_grad[bottom, :] = (grad[large:] * ss_ref[...].astype(f32)).astype(bf16)
    active[top, :] = al_ref[...]
    active[bottom, :] = as_ref[...]
    down = dot(active[...], branch[...], TN).astype(bf16)
    upper = dot(second[...], inner_grad[...], TN).astype(bf16)
    if laid:
        rows = dup_ref.shape[1]
        for at in range(8):
            zl, x, zh = at // 4, at // 2 % 2, at % 2
            first = ((zh * 2 + zl) * 2 + x) * rows
            dup_ref[at] = upper[first : first + rows]
        for x, core, y in ((a, b, c) for a in (0, 1) for b in (0, 1) for c in (0, 1)):
            first = (x * 4 + core * 2 + y) * rows
            there = core * 16 + (step % 2) * 8 + y * 4 + x * 2 + step // 2
            ddown_ref[there] = down[first : first + rows]
    else:
        dup_ref[...] = upper
        ddown_ref[...] = down
    total[...] += dot(inner_grad[...], up_ref[...], NT)

    @pl.when(step == steps - 1)
    def _():
        extra, gain_l = norm_back(total[top, :], hl_ref[...], gain_ref[...])
        hidden_grad = gl_ref[...] + extra
        hgl_ref[...] = hidden_grad
        branch[top, :] = hidden_grad.astype(bf16)
        extra, gain_s = norm_back(total[bottom, :], hs_ref[...], gain_ref[...])
        hidden_grad = gs_ref[...] + extra
        hgs_ref[...] = hidden_grad
        branch[bottom, :] = hidden_grad.astype(bf16)
        dgain_ref[...] = gain_l + gain_s
        mixed_grad = dot(branch[...], wo_ref[...], NT).astype(bf16)
        ml_ref[...] = mixed_grad[:large]
        ms_ref[...] = mixed_grad[large:]
        fill_wide(mixed, mixed_refs, large, 0)
        fill_wide(mixed, [mixed_s_ref], small, large)
        value = dot(mixed[...], branch[...], TN).astype(bf16)
        if laid:
            rows, wide = dwo_ref.shape[1:]
            for at, (core, y, tm) in enumerate(spots(BY_X)):
                first = (tm * 2 + core) * rows
                dwo_ref[at] = value[first : first + rows, y * wide : (y + 1) * wide]
        else:
            dwo_ref[...] = value

    for flow in range(flows):
        for stage, when in enumerate((0, 2, steps - 1)):

            @pl.when(step == when)
            def _(flow=flow, stage=stage):
                running[flow].act(stage + 1)
                if stage == 2:
                    sums[flow][...] = running[flow].result()


def back(
    grad_l, grad_s, saved_l, saved_s, mixed_l, mixed_s, wo, gain, up, down, laid, flows=(), orders=()
):
    (hidden_l, second_l, active_l, slope_l) = saved_l
    (hidden_s, second_s, active_s, slope_s) = saved_s
    large, width = grad_l.shape
    small = grad_s.shape[0]
    rows = large + small
    hidden = up.shape[1]
    part = width
    steps = hidden // part
    fl, fs = whole((large, width)), whole((small, width))
    square = whole((width, width))
    up_slab = slab_of(width, part)
    down_slab = pl.BlockSpec((part, width), lambda i: (i, 0))
    shape = jax.ShapeDtypeStruct
    results = [flow_result(o, f.shape[1:], False) for o, f in zip(orders, flows)]
    scratch = [s for o, f in zip(orders, flows) for s in flow_scratch(o, f.shape[1:], True, False)]
    out_up, out_down, out_square = up_slab, down_slab, square
    up_shape, down_shape, square_shape = up.shape, down.shape, (width, width)
    if laid:
        block = (width // 8, width)
        up_shape = down_shape = (32,) + block
        square_shape = (32, width // 16, width // 2)
        out_up = pl.BlockSpec((8,) + block, lambda i: (i, 0, 0))
        out_down, out_square = whole(down_shape), whole(square_shape)
    return pl.pallas_call(
        functools.partial(back_kernel, steps, len(mixed_l), (large, small), laid, orders),
        grid=(steps,),
        in_specs=[fl, fs]
        + [slab_of(large, part), slab_of(small, part)] * 2
        + [fl, fs, fl, fs]
        + [whole(m.shape) for m in mixed_l]
        + [whole(mixed_s.shape), square, whole((1, width)), up_slab, down_slab]
        + [pl.BlockSpec(memory_space=pl.ANY)] * len(flows),
        out_specs=[fl, fs, fl, fs, out_up, out_down, out_square, whole((1, width))]
        + [whole(result.shape) for result in results],
        out_shape=[
            shape((large, width), f32),
            shape((small, width), f32),
            shape((large, width), bf16),
            shape((small, width), bf16),
            shape(up_shape, bf16),
            shape(down_shape, bf16),
            shape(square_shape, bf16),
            shape((1, width), f32),
        ]
        + results,
        scratch_shapes=[
            pltpu.VMEM((rows, width), bf16),
            pltpu.VMEM((rows, width), bf16),
            pltpu.VMEM((rows, width), f32),
            pltpu.VMEM((rows, part), bf16),
            pltpu.VMEM((rows, part), bf16),
            pltpu.VMEM((rows, width), bf16),
        ]
        + scratch,
        compiler_params=pltpu.CompilerParams(
            vmem_limit_bytes=60 << 20,
            has_side_effects=bool(flows),
            collective_id=0 if flows else None,
        ),
        cost_estimate=pl.CostEstimate(
            flops=2 * rows * width * (4 * hidden + 2 * width),
            bytes_accessed=width * width * 36 + rows * width * 40,
            transcendentals=0,
        ),
        name="back",
    )(
        grad_l, grad_s, active_l, active_s, slope_l, slope_s, second_l, second_s, hidden_l, hidden_s,
        *mixed_l, mixed_s, wo, gain, up, down, *flows,
    )


MESH = pl.DeviceIdType.MESH
BY_Y = ("core", "y", "zl", "x", "zh")
BY_ZL = ("core", "zl", "y", "x", "zh")
BY_X = ("core", "x", "zl", "y", "zh")
BY_YX = ("core", "y", "x", "zl", "zh")


def spots(order):
    out = []
    for at in range(32):
        bit = {name: (at >> (4 - i)) & 1 for i, name in enumerate(order)}
        out.append((bit["core"], bit["y"], (bit["zh"] * 2 + bit["zl"]) * 2 + bit["x"]))
    return out


class Here:
    def __init__(self):
        tm, seq = lax.axis_index("tm"), lax.axis_index("seq")
        self.tm, self.seq = tm, seq
        self.bit = {
            "zh": tm // 4,
            "zl": (tm // 2) % 2,
            "x": tm % 2,
            "y": seq // 2,
            "core": seq % 2,
        }

    def partner(self, *names):
        tm, seq = self.tm, self.seq
        for name in names:
            one = 1 - 2 * self.bit[name]
            if name in ("y", "core"):
                seq = seq + one * (2 if name == "y" else 1)
            else:
                tm = tm + one * {"zh": 4, "zl": 2, "x": 1}[name]
        return (tm, seq)

    def greet(self, partners):
        barrier = pltpu.get_barrier_semaphore()
        for names in partners:
            pl.semaphore_signal(
                barrier, inc=1, device_id=self.partner(*names), device_id_type=MESH
            )
        pl.semaphore_wait(barrier, len(partners))


ALL_PARTNERS = (("core",), ("y",), ("zl",), ("x",), ("zh",), ("y", "core"))


class Flow:
    def __init__(self, here, order, local, refs, keep, ends):
        self.here, self.order, self.local = here, order, local
        self.keep = refs.pop(0) if keep else None
        self.got = [refs.pop(0) for _ in order]
        self.out = refs.pop(0) if ends else None
        self.sem = refs.pop(0)
        self.last = len(order)
        self.ends = ends

    def copy(self, step):
        name = self.order[step]
        half = 1 << (self.last - 1 - step)
        source = self.local if step == 0 else self.got[step - 1]
        at = (1 - self.here.bit[name]) * half
        return pltpu.make_async_remote_copy(
            src_ref=source.at[pl.ds(at, half)],
            dst_ref=self.got[step],
            send_sem=self.sem.at[0, step],
            recv_sem=self.sem.at[1, step],
            device_id=self.here.partner(name),
            device_id_type=MESH,
        )

    def keep_copy(self):
        half = 1 << (self.last - 1)
        at = self.here.bit[self.order[0]] * half
        return pltpu.make_async_copy(
            self.local.at[pl.ds(at, half)], self.keep, self.sem.at[0, self.last + 2]
        )

    def start(self, step):
        self.copy(step).start()
        if step == 0 and self.keep is not None:
            self.keep_copy().start()

    def finish(self, step):
        half = 1 << (self.last - 1 - step)
        self.copy(step).wait()
        got = self.got[step]
        at = self.here.bit[self.order[step]] * half
        if step == 0 and self.keep is not None:
            self.keep_copy().wait()
            source, at = self.keep, 0
        else:
            source = self.local if step == 0 else self.got[step - 1]

        def body(i, carry):
            got[i] = got[i] + source[at + i]
            return carry

        if half == 1:
            got[0] = got[0] + source[at]
        else:
            lax.fori_loop(0, half, body, 0)

    def spread_copy(self, which):
        here = self.here
        own = here.bit["core"] * 2
        if which == 0:
            source, there = self.got[-1].at[0], self.out.at[own + here.bit["y"]]
        else:
            source = there = self.out.at[pl.ds(own, 2)]
        return pltpu.make_async_remote_copy(
            src_ref=source,
            dst_ref=there,
            send_sem=self.sem.at[0, self.last + which],
            recv_sem=self.sem.at[1, self.last + which],
            device_id=here.partner(("y", "core")[which]),
            device_id_type=MESH,
        )

    def act(self, stage):
        if stage == 0:
            self.start(0)
        elif stage < self.last:
            self.finish(stage - 1)
            self.start(stage)
        elif stage == self.last:
            self.finish(stage - 1)
            if self.ends:
                self.spread_copy(0).start()
                self.out[self.here.bit["core"] * 2 + self.here.bit["y"]] = self.got[-1][0]
        elif stage == self.last + 1 and self.ends:
            self.spread_copy(0).wait()
            self.spread_copy(1).start()
        elif stage == self.last + 2 and self.ends:
            self.spread_copy(1).wait()

    def result(self):
        return self.out[...] if self.ends else self.got[-1][...]


def flow_scratch(order, block, keep, ends):
    steps = len(order)
    blocks = [pltpu.VMEM((1 << (steps - 1),) + block, bf16)] if keep else []
    for step in range(steps):
        blocks.append(pltpu.VMEM((1 << (steps - 1 - step),) + block, bf16))
    if ends:
        blocks.append(pltpu.VMEM((4,) + block, bf16))
    return blocks + [pltpu.SemaphoreType.DMA((2, steps + 3))]


def flow_result(order, block, ends):
    left = 4 if ends else 1
    return jax.ShapeDtypeStruct((left,) + block, bf16)


def pair_back(query, grad, out, logsum, mask, keys_at, values_at, mk_ref, block, store):
    count = query.shape[0]
    total = keys_at.shape[0]
    lane = lax.broadcasted_iota(jnp.int32, (count, LANES), 1)
    low = lane < HALF
    spot = lane % HALF
    zero = jnp.zeros_like(query)
    product = grad.astype(f32) * out.astype(f32)
    delta0 = jnp.sum(jnp.where(low, product, 0.0), axis=1, keepdims=True)
    delta1 = jnp.sum(jnp.where(low, 0.0, product), axis=1, keepdims=True)
    delta = jnp.where(low, delta1, delta0)

    def beside(base, value):
        a, b, c = three(-value)
        return jnp.where(spot == 4, a, jnp.where(spot == 5, b, jnp.where(spot == 6, c, base)))

    query_side = beside(mask, logsum)
    grad_side = beside(zero, delta)
    query_a = (jnp.where(low, query, query_side), jnp.where(low, query_side, query))
    grad_a = (jnp.where(low, grad, grad_side), jnp.where(low, grad_side, grad))
    query_m = (jnp.where(low, query, zero), jnp.where(low, zero, query))
    grad_m = (jnp.where(low, grad, zero), jnp.where(low, zero, grad))
    lane_k = lax.broadcasted_iota(jnp.int32, (block, LANES), 1)
    low_k = lane_k < HALF
    spot_k = lane_k % HALF
    one = jnp.where((spot_k >= 4) & (spot_k < 7), 1.0, 0.0).astype(bf16)
    dq = jnp.zeros((count, LANES), f32)
    for number in range(total // block):
        here = pl.ds(number * block, block)
        keys, values = keys_at[here, :], values_at[here, :]
        side = mk_ref[here, :] + one
        nought = jnp.zeros_like(keys)
        dk = jnp.zeros((block, LANES), f32)
        dv = jnp.zeros((block, LANES), f32)
        for head in (0, 1):
            pick = lambda a, b: jnp.where(low_k, a, b) if head == 0 else jnp.where(low_k, b, a)
            prob = jnp.exp2(dot(query_a[head], pick(keys, side), NT))
            change = dot(grad_a[head], pick(values, one), NT)
            score_grad = (prob * change).astype(bf16)
            dv += dot(prob.astype(bf16), grad_m[head], TN)
            dk += dot(score_grad, query_m[head], TN)
            dq += dot(score_grad, pick(keys, nought))
        store(number, (dk * LN2).astype(bf16), dv.astype(bf16))
    return (dq * HALF**-0.5).astype(bf16)


class Exchange:
    def __init__(self, here, rows, refs):
        self.here, self.rows = here, rows
        self.sums, self.send, self.got_core, self.across, self.got_x = refs[:5]
        self.sems = refs[5]

    def copy_core(self, pair):
        return pltpu.make_async_remote_copy(
            src_ref=self.send.at[pair % 2],
            dst_ref=self.got_core.at[pair],
            send_sem=self.sems.at[0, pair],
            recv_sem=self.sems.at[1, pair],
            device_id=self.here.partner("core"),
            device_id_type=MESH,
        )

    def copy_x(self, pair):
        return pltpu.make_async_remote_copy(
            src_ref=self.across.at[pair % 2],
            dst_ref=self.got_x.at[pair],
            send_sem=self.sems.at[2, pair],
            recv_sem=self.sems.at[3, pair],
            device_id=self.here.partner("x"),
            device_id_type=MESH,
        )

    def free(self, pair):
        self.copy_core(pair).wait_send()

    def put(self, pair, total, block):
        half = total // 2

        def store(number, dk, dv):
            there = pl.ds(number * block % half, block)
            if number * block < half:
                self.sums[pair % 3, 0, there, :] = dk
                self.sums[pair % 3, 1, there, :] = dv
            else:
                self.send[pair % 2, 0, there, :] = dk
                self.send[pair % 2, 1, there, :] = dv

        return store

    def pass_on(self, pair, wait_before):
        rows = self.rows
        self.copy_core(pair).wait_recv()
        if wait_before:
            self.copy_x(pair - 2).wait_send()
        far = pl.ds(rows, rows)
        for i in (0, 1):
            self.across[pair % 2, i] = (
                self.sums[pair % 3, i, far, :] + self.got_core[pair, i, far, :]
            )
        self.copy_x(pair).start()

    def take(self, pair, out_ref):
        near = pl.ds(0, self.rows)
        self.copy_x(pair).wait_recv()
        for i in (0, 1):
            out_ref[pair, i] = (
                self.sums[pair % 3, i, near, :].astype(f32)
                + self.got_core[pair, i, near, :].astype(f32)
                + self.got_x[pair, i].astype(f32)
            ).astype(bf16)


def exchange_scratch(pairs, rows):
    return [
        pltpu.VMEM((3, 2, 2 * rows, LANES), bf16),
        pltpu.VMEM((2, 2, 2 * rows, LANES), bf16),
        pltpu.VMEM((pairs, 2, 2 * rows, LANES), bf16),
        pltpu.VMEM((2, 2, rows, LANES), bf16),
        pltpu.VMEM((pairs, 2, rows, LANES), bf16),
        pltpu.SemaphoreType.DMA((4, pairs)),
    ]


def fill_keys(keys_at, values_at, kv_ref):
    rows = kv_ref.shape[3]
    for part in range(kv_ref.shape[0]):
        there = pl.ds(part * rows, rows)
        keys_at[there, :] = kv_ref[part, 0, 0]
        values_at[there, :] = kv_ref[part, 0, 1]


def selves_kernel(pairs, plan, blocks, *refs):
    orders, ends, stages = plan
    large_refs, kv_large, refs = refs[:6], refs[6], refs[7:]
    small_refs, kv_small, refs = refs[:6], refs[6], refs[7:]
    flows = len(orders)
    locals_, refs = refs[:flows], refs[flows:]
    dq_l, dkv_l, dq_s, dkv_s = refs[:4]
    sums, refs = refs[4 : 4 + flows], refs[4 + flows :]
    keys_l, values_l, keys_s, values_s = refs[:4]
    ex_l, ex_s, refs = refs[4:10], refs[10:16], refs[16:]
    here = Here()
    rows_l, rows_s = keys_l.shape[0] // 4, keys_s.shape[0] // 4
    large, small = Exchange(here, rows_l, ex_l), Exchange(here, rows_s, ex_s)
    refs = list(refs)
    running = [
        Flow(here, orders[flow], locals_[flow], refs, True, ends[flow]) for flow in range(flows)
    ]
    step = pl.program_id(0)

    @pl.when(step == 0)
    def _():
        here.greet(ALL_PARTNERS)
        for flow in running:
            flow.act(0)

    def move(exchange, pair, out_ref):
        exchange.copy_core(pair).start()

        @pl.when((pair >= 1) & (pair < 3))
        def _():
            exchange.pass_on(pair - 1, False)

        @pl.when(pair >= 3)
        def _():
            exchange.pass_on(pair - 1, True)

        @pl.when(pair >= 2)
        def _():
            exchange.take(pair - 2, out_ref)

    def attention(exchange, pair, refs, kv_ref, keys_at, values_at, block, dq_ref):
        q_ref, do_ref, o_ref, l_ref, mq_ref, mk_ref = refs
        fill_keys(keys_at, values_at, kv_ref)

        @pl.when(pair >= 2)
        def _():
            exchange.free(pair - 2)

        dq_ref[...] = pair_back(
            q_ref[0], do_ref[...], o_ref[0], l_ref[0], mq_ref[...],
            keys_at, values_at, mk_ref, block, exchange.put(pair, keys_at.shape[0], block),
        )

    @pl.when(step < pairs)
    def _():
        attention(large, step, large_refs, kv_large, keys_l, values_l, blocks[0], dq_l)
        move(large, step, dkv_l)

    @pl.when(step >= pairs)
    def _():
        pair = step - pairs
        attention(small, pair, small_refs, kv_small, keys_s, values_s, blocks[1], dq_s)
        move(small, pair, dkv_s)

    @pl.when(step == pairs)
    def _():
        large.pass_on(pairs - 1, True)
        large.take(pairs - 2, dkv_l)

    @pl.when(step == pairs + 1)
    def _():
        large.take(pairs - 1, dkv_l)
        for pair in (pairs - 2, pairs - 1):
            large.free(pair)
            large.copy_x(pair).wait_send()

    @pl.when(step == 2 * pairs - 1)
    def _():
        small.pass_on(pairs - 1, True)

    for at in range(2 * pairs):
        todo = []
        for flow in range(flows):
            for stage, when in enumerate(stages[flow]):
                if when == at:
                    todo.append((running[flow], stage + 1))
        if todo:

            @pl.when(step == at)
            def _(todo=todo):
                for flow, stage in todo:
                    flow.act(stage)

    @pl.when(step == 2 * pairs - 1)
    def _():
        small.take(pairs - 2, dkv_s)
        small.take(pairs - 1, dkv_s)
        for pair in (pairs - 2, pairs - 1):
            small.free(pair)
            small.copy_x(pair).wait_send()
        for flow, sum_ref in zip(running, sums):
            sum_ref[...] = flow.result()


def selves_back(large, large_kv, small, small_kv, flows, orders, ends, stages):
    count, width = large[1].shape
    few = small[1].shape[0]
    pairs = width // LANES
    total, less = large[5].shape[0], small[5].shape[0]
    shapes = [flow.shape[1:] for flow in flows]
    results = [flow_result(*flow) for flow in zip(orders, shapes, ends)]
    blocks = (largest_block(total // 2, 512), largest_block(less // 2, 512))
    first = lambda i: jnp.minimum(i, pairs - 1)
    last = lambda i: jnp.maximum(i - pairs, 0)
    in_specs = []
    for rows, keys, at in ((count, total, first), (few, less, last)):
        major = pl.BlockSpec((1, rows, LANES), lambda i, at=at: (at(i), 0, 0))
        minor = pl.BlockSpec((rows, LANES), lambda i, at=at: (0, at(i)))
        in_specs += [major, minor, major, major, whole((rows, LANES)), whole((keys, LANES))]
        in_specs.append(
            pl.BlockSpec((4, 1, 2, rows, LANES), lambda i, at=at: (0, at(i), 0, 0, 0))
        )
    in_specs += [pl.BlockSpec(memory_space=pl.ANY)] * len(flows)
    shape = jax.ShapeDtypeStruct
    out_shape = [
        shape((count, width), bf16),
        shape((pairs, 2, count, LANES), bf16),
        shape((few, width), bf16),
        shape((pairs, 2, few, LANES), bf16),
    ] + results
    out_specs = [
        pl.BlockSpec((count, LANES), lambda i: (0, first(i))),
        whole((pairs, 2, count, LANES)),
        pl.BlockSpec((few, LANES), lambda i: (0, last(i))),
        whole((pairs, 2, few, LANES)),
    ] + [whole(result.shape) for result in results]
    scratch = [pltpu.VMEM((total, LANES), bf16)] * 2 + [pltpu.VMEM((less, LANES), bf16)] * 2
    scratch += exchange_scratch(pairs, count) + exchange_scratch(pairs, few)
    for flow in range(len(flows)):
        scratch += flow_scratch(orders[flow], shapes[flow], True, ends[flow])
    result = pl.pallas_call(
        functools.partial(selves_kernel, pairs, (orders, ends, stages), blocks),
        grid=(2 * pairs,),
        in_specs=in_specs,
        out_specs=out_specs,
        out_shape=out_shape,
        scratch_shapes=scratch,
        compiler_params=pltpu.CompilerParams(
            vmem_limit_bytes=60 << 20, collective_id=1, has_side_effects=True
        ),
        cost_estimate=pl.CostEstimate(
            flops=20 * width * (count * total + few * less),
            bytes_accessed=64 * count * width,
            transcendentals=count * total * width // HALF,
        ),
        name="selves_back",
    )(*large, large_kv, *small, small_kv, *flows)
    return result[:4], result[4:]


def view_kernel(pairs, sizes, *refs):
    (dql, dkvl, dqs, dkvs, xl, xs, hl, hs, gain, wq, wk, wv) = refs[:12]
    gl_ref, gs_ref, gain_ref, grads = refs[12:]
    large, small = sizes
    top, bottom = pl.ds(0, large), pl.ds(large, small)
    total = None
    for which, weight in enumerate((wq, wk, wv)):
        if which == 0:
            grads[top, :] = dql[...]
            grads[bottom, :] = dqs[...]
        else:
            for pair in range(pairs):
                lanes = pl.ds(pair * LANES, LANES)
                grads[top, lanes] = dkvl[pair, which - 1]
                grads[bottom, lanes] = dkvs[pair, which - 1]
        part = dot(grads[...], weight[...], NT)
        total = part if total is None else total + part
    extra, gain_l = norm_back(total[:large], xl[...].astype(f32), gain[...])
    gl_ref[...] = (hl[...] + extra).astype(bf16)
    extra, gain_s = norm_back(total[large:], xs[...].astype(f32), gain[...])
    gs_ref[...] = (hs[...] + extra).astype(bf16)
    gain_ref[...] = gain_l + gain_s


def view_grads(selves, large, small, hidden_l, hidden_s, gain, weights):
    count, width = large.shape
    few = small.shape[0]
    shape = jax.ShapeDtypeStruct
    return pl.pallas_call(
        functools.partial(view_kernel, width // LANES, (count, few)),
        out_shape=[
            shape((count, width), bf16),
            shape((few, width), bf16),
            shape((1, width), f32),
        ],
        scratch_shapes=[pltpu.VMEM((count + few, width), bf16)],
        compiler_params=pltpu.CompilerParams(vmem_limit_bytes=48 << 20),
        cost_estimate=pl.CostEstimate(
            flops=6 * (count + few) * width * width,
            bytes_accessed=6 * width * width + 20 * (count + few) * width,
            transcendentals=0,
        ),
        name="view_grads",
    )(*selves, large, small, hidden_l, hidden_s, gain, *weights)


LAST_ORDERS = (BY_YX, BY_X, BY_ZL)
GAIN_ORDER = ("core", "y", "x", "zl", "zh")
LATE_ORDER = ("x", "zh")
LATE_STAGES = {2: 1, 4: 2, 5: 3, 6: 4}


def last_kernel(pairs, sizes, late, *refs):
    dql, dkvl, dqs, dkvs, nl, ns, gains = refs[:7]
    late_refs, refs = refs[7 : 7 + late], list(refs[7 + late :])
    sum_refs = [refs.pop(0) for _ in range(3 + late)]
    gain_ref, normed, grads = refs.pop(0), refs.pop(0), refs.pop(0)
    here = Here()
    flows = []
    for order in LAST_ORDERS:
        flows.append(Flow(here, order, refs.pop(0), refs, False, True))
    late_flows = [Flow(here, LATE_ORDER, ref, refs, False, True) for ref in late_refs]
    state, got, gain_sems = refs
    large, small = sizes
    top, bottom = pl.ds(0, large), pl.ds(large, small)
    here.greet(ALL_PARTNERS)
    for flow in late_flows:
        flow.act(0)

    def gain_copy(step):
        return pltpu.make_async_remote_copy(
            src_ref=state.at[step],
            dst_ref=got.at[step],
            send_sem=gain_sems.at[0, step],
            recv_sem=gain_sems.at[1, step],
            device_id=here.partner(GAIN_ORDER[step]),
            device_id_type=MESH,
        )

    state[0] = gains[...]
    gain_copy(0).start()
    normed[top, :] = nl[...]
    normed[bottom, :] = ns[...]
    for which, flow in enumerate(flows):
        if which == 0:
            grads[top, :] = dql[...]
            grads[bottom, :] = dqs[...]
        else:
            for pair in range(pairs):
                lanes = pl.ds(pair * LANES, LANES)
                grads[top, lanes] = dkvl[pair, which - 1]
                grads[bottom, lanes] = dkvs[pair, which - 1]
        value = dot(normed[...], grads[...], TN).astype(bf16)
        rows, wide = flow.local.shape[1:]
        for at, (core, y, tm) in enumerate(spots(flow.order)):
            first = tm * 2 * rows + core * rows
            flow.local[at] = value[first : first + rows, y * wide : (y + 1) * wide]
        flow.act(0)
    for stage in range(1, 8):
        for flow in flows:
            flow.act(stage)
        if stage in LATE_STAGES:
            for flow in late_flows:
                flow.act(LATE_STAGES[stage])
        if stage <= 5:
            gain_copy(stage - 1).wait()
            total = state[stage - 1] + got[stage - 1]
            if stage < 5:
                state[stage] = total
                gain_copy(stage).start()
            else:
                gain_ref[...] = total
    for flow, sum_ref in zip(flows + late_flows, sum_refs):
        sum_ref[...] = flow.result()


def last_sums(selves, normed_l, normed_s, gains, late):
    count, width = normed_l.shape
    few = normed_s.shape[0]
    block = (width // 16, width // 2)
    shape = jax.ShapeDtypeStruct
    scratch = [pltpu.VMEM((count + few, width), bf16), pltpu.VMEM((count + few, width), bf16)]
    for order in LAST_ORDERS:
        scratch.append(pltpu.VMEM((32,) + block, bf16))
        scratch += flow_scratch(order, block, False, True)
    for local in late:
        scratch += flow_scratch(LATE_ORDER, local.shape[1:], False, True)
    scratch += [
        pltpu.VMEM((5,) + gains.shape, f32),
        pltpu.VMEM((5,) + gains.shape, f32),
        pltpu.SemaphoreType.DMA((2, 5)),
    ]
    result = pl.pallas_call(
        functools.partial(last_kernel, width // LANES, (count, few), len(late)),
        out_shape=[shape((4,) + block, bf16)] * 3
        + [shape((4,) + local.shape[1:], bf16) for local in late]
        + [shape(gains.shape, f32)],
        scratch_shapes=scratch,
        compiler_params=pltpu.CompilerParams(
            vmem_limit_bytes=48 << 20, collective_id=2, has_side_effects=True
        ),
        cost_estimate=pl.CostEstimate(
            flops=40 * (count + few) * width * width,
            bytes_accessed=40 * (count + few) * width,
            transcendentals=0,
        ),
        name="last_sums",
    )(*selves, normed_l, normed_s, gains, *late)
    return result[:3], result[3:-1], result[-1]


def cross_kernel(pairs, block, *refs):
    (q_ref, do_ref, o_ref, l_ref, mq_ref, mk_ref), refs = refs[:6], refs[6:]
    kv_ref, given, gains, refs = refs[0], refs[1:10], refs[10:12], refs[12:]
    gl_ref, gs_ref, a_ref, b_ref, gain_l_ref, gain_s_ref = refs[:6]
    keys_at, values_at, exchange_refs, refs = refs[6], refs[7], refs[8:14], refs[14:]
    dkv, dq, dk, dv = refs[:4]
    held, sems = refs[4:13], refs[13]
    asked, context, united, grad_out, merged_l, merged_s, wq, wk, wv = held
    here = Here()
    exchange = Exchange(here, keys_at.shape[0] // 4, exchange_refs)
    step = pl.program_id(0)
    loads = [
        pltpu.make_async_copy(source, there, sems.at[i])
        for i, (source, there) in enumerate(zip(given, held))
    ]

    @pl.when(step == 0)
    def _():
        here.greet((("core",), ("x",)))
        for load in loads:
            load.start()

    fill_keys(keys_at, values_at, kv_ref)

    @pl.when(step >= 2)
    def _():
        exchange.free(step - 2)

    dq[step] = pair_back(
        q_ref[0], do_ref[...], o_ref[0], l_ref[0], mq_ref[...],
        keys_at, values_at, mk_ref, block, exchange.put(step, keys_at.shape[0], block),
    )
    exchange.copy_core(step).start()

    @pl.when((step >= 1) & (step < 3))
    def _():
        exchange.pass_on(step - 1, False)

    @pl.when(step >= 3)
    def _():
        exchange.pass_on(step - 1, True)

    @pl.when(step >= 2)
    def _():
        exchange.take(step - 2, dkv)

    def lay(out_ref, which, value, order):
        rows = out_ref.shape[1] // 4
        for at, (core, y, tm) in enumerate(spots(order)):
            if core == which:
                first = (tm * 2 + y) * rows
                out_ref[at // 4, at % 4 * rows : (at % 4 + 1) * rows, :] = value[
                    first : first + rows
                ]

    @pl.when(step == pairs - 1)
    def _():
        exchange.pass_on(pairs - 1, True)
        for load in loads:
            load.wait()
        grads = jnp.concatenate([united[i] for i in range(pairs)], axis=1)
        lay(a_ref, 0, dot(grads, grad_out[...], TN).astype(bf16), BY_Y)
        grads = jnp.concatenate([dq[i] for i in range(pairs)], axis=1)
        lay(a_ref, 1, dot(asked[...], grads, TN).astype(bf16), BY_Y)
        extra, gain_l_ref[...] = norm_back(dot(grads, wq[...], NT), merged_l[...], gains[0][...])
        gl_ref[...] = grad_out[...].astype(f32) + extra
        exchange.take(pairs - 2, dkv)
        exchange.take(pairs - 1, dkv)
        for pair in range(pairs):
            lanes = pl.ds(pair * LANES, LANES)
            dk[:, lanes] = dkv[pair, 0]
            dv[:, lanes] = dkv[pair, 1]
        lay(b_ref, 0, dot(context[...], dk[...], TN).astype(bf16), BY_ZL)
        lay(b_ref, 1, dot(context[...], dv[...], TN).astype(bf16), BY_ZL)
        grad = dot(dk[...], wk[...], NT) + dot(dv[...], wv[...], NT)
        gs_ref[...], gain_s_ref[...] = norm_back(grad, merged_s[...], gains[1][...])
        for pair in (pairs - 2, pairs - 1):
            exchange.free(pair)
            exchange.copy_x(pair).wait_send()


def cross_back(attention, kv, given, gains):
    count, width = attention[1].shape
    few = kv.shape[3]
    major = pl.BlockSpec((1, count, LANES), lambda i: (i, 0, 0))
    pairs = width // LANES
    total = attention[5].shape[0]
    block = largest_block(total // 2, 512)
    shape = jax.ShapeDtypeStruct
    laid = (8, 4 * width // 16, width)
    return pl.pallas_call(
        functools.partial(cross_kernel, pairs, block),
        grid=(pairs,),
        in_specs=[major, columns(count, 0), major, major]
        + [whole((count, LANES)), whole((total, LANES))]
        + [pl.BlockSpec((4, 1, 2, few, LANES), lambda i: (0, i, 0, 0, 0))]
        + [pl.BlockSpec(memory_space=pl.ANY)] * 9
        + [whole((1, width))] * 2,
        out_specs=[
            whole((count, width)), whole((few, width)), whole(laid), whole(laid),
            whole((1, width)), whole((1, width)),
        ],
        out_shape=[
            shape((count, width), f32), shape((few, width), f32), shape(laid, bf16), shape(laid, bf16),
            shape((1, width), f32), shape((1, width), f32),
        ],
        scratch_shapes=[pltpu.VMEM((total, LANES), bf16)] * 2
        + exchange_scratch(pairs, few)
        + [pltpu.VMEM((pairs, 2, few, LANES), bf16), pltpu.VMEM((pairs, count, LANES), bf16)]
        + [pltpu.VMEM((few, width), bf16)] * 2
        + [pltpu.VMEM(value.shape, value.dtype) for value in given]
        + [pltpu.SemaphoreType.DMA((len(given),))],
        compiler_params=pltpu.CompilerParams(
            vmem_limit_bytes=56 << 20, collective_id=3, has_side_effects=True
        ),
        cost_estimate=pl.CostEstimate(
            flops=20 * width * count * total,
            bytes_accessed=64 * count * width,
            transcendentals=count * total * width // HALF,
        ),
        name="cross_back",
    )(*attention, kv, *given, *gains)


def attend_pair(pair, q_ref, kv, mq_ref, mk_ref, spaces, o_ref, l_ref):
    parts, rows = kv.shape[0], kv.shape[3]
    total = parts * rows
    ka0, ka1, va0, va1 = (space.at[pl.ds(0, total), :] for space in spaces)
    low = lax.broadcasted_iota(jnp.int32, (rows, LANES), 1) < HALF
    for part in range(parts):
        here = pl.ds(part * rows, rows)
        keys, values, mask = kv[part, pair, 0], kv[part, pair, 1], mk_ref[here, :]
        one = jnp.ones_like(values)
        ka0[here, :] = jnp.where(low, keys, mask)
        ka1[here, :] = jnp.where(low, mask, keys)
        va0[here, :] = jnp.where(low, values, one)
        va1[here, :] = jnp.where(low, one, values)
    count = q_ref.shape[1]
    block = largest_block(count, 256)
    low = lax.broadcasted_iota(jnp.int32, (block, LANES), 1) < HALF
    for number in range(count // block):
        here = pl.ds(number * block, block)
        query, mask = q_ref[pair, here, :], mq_ref[here, :]
        tops, sums = [], []
        for head, keys, values in ((0, ka0, va0), (1, ka1, va1)):
            mine = jnp.where(low, query, mask) if head == 0 else jnp.where(low, mask, query)
            score = dot(mine, keys[...], NT)
            top = jnp.max(score, axis=1, keepdims=True)
            weight = jnp.exp2(score - top).astype(bf16)
            sums.append(dot(weight, values[...]))
            tops.append(jnp.broadcast_to(top, (block, LANES)))
        total = jnp.where(low, sums[1], sums[0])
        top = jnp.where(low, tops[1], tops[0])
        out = jnp.where(low, sums[0], sums[1])
        o_ref[pair, here, :] = (out / pltpu.roll(total, HALF, 1)).astype(bf16)
        l_ref[pair, here, :] = top + jnp.log2(total)


class Gather:
    def __init__(self, here, kv, sems):
        self.here, self.kv, self.sems = here, kv, sems

    def copy(self, kind, at, size, sem):
        source, there = ((0, 1), (0, 2), (1, 3))[kind]
        pairs = pl.ds(at, size)
        return pltpu.make_async_remote_copy(
            src_ref=self.kv.at[source, pairs],
            dst_ref=self.kv.at[there, pairs],
            send_sem=self.sems.at[0, 3 * sem + kind],
            recv_sem=self.sems.at[1, 3 * sem + kind],
            device_id=self.here.partner(("x", "core", "core")[kind]),
            device_id_type=MESH,
        )


def begin_kernel(pairs, *refs):
    refs = list(refs)
    take = lambda count: [refs.pop(0) for _ in range(count)]
    large_ref, small_ref, cot_ref, clip_ref = take(4)
    weight_refs = take(8)
    first_gain, second_gain, context_gain = take(3)
    xl_out, xs_out, cot_out, kvl_out, kvs_out, ckv_out = take(6)
    nl_ref, ns_ref, ql_ref, qs_ref, ol_ref, ll_ref, os_ref, ls_ref = take(8)
    merged_ref, hidden_ref, second_ref, active_ref, slope_ref, context_ref = take(6)
    mql_ref, mkl_ref, mqs_ref, mks_ref = take(4)
    xl, xs, cot, clip, kvl, kvs, ckv = take(7)
    wq, wk, wv, wo, up, down, wck, wcv = weights = take(8)
    spaces = take(4)
    wide, total = take(2)
    move_sems, gather_l, gather_s, gather_c, gather_clip, load_sems, out_sems = take(7)
    here = Here()
    z, core = here.tm // 2, here.bit["core"]
    stay = core == z // 2

    barrier = pltpu.get_barrier_semaphore()
    for dz in range(4):
        for dc in range(2):
            if dz or dc:
                place = (
                    lax.rem(z + dz, 4) * 2 + here.bit["x"],
                    here.bit["y"] * 2 + lax.rem(core + dc, 2),
                )
                pl.semaphore_signal(barrier, inc=1, device_id=place, device_id_type=MESH)
    pl.semaphore_signal(barrier, inc=1, device_id=here.partner("x"), device_id_type=MESH)
    pl.semaphore_wait(barrier, 8)

    odd = lax.rem(z, 2)
    from_seq = (odd, 1 - odd)

    def far(which, turn, source, there):
        rows = source.shape[1]
        place = (
            (2 * core + from_seq[turn]) * 2 + here.bit["x"],
            here.bit["y"] * 2 + z // 2,
        )
        return pltpu.make_async_remote_copy(
            src_ref=source.at[from_seq[turn]],
            dst_ref=there.at[pl.ds(turn * rows, rows)],
            send_sem=move_sems.at[0, 2 * which + turn],
            recv_sem=move_sems.at[1, 2 * which + turn],
            device_id=place,
            device_id_type=MESH,
        )

    def near(which, source, there):
        return pltpu.make_async_copy(
            source.at[from_seq[0]],
            there.at[pl.ds(0, source.shape[1])],
            move_sems.at[1, 2 * which],
        )

    def move(which, source, there):
        far(which, 1, source, there).start()

        @pl.when(stay)
        def _():
            near(which, source, there).start()

        @pl.when(jnp.logical_not(stay))
        def _():
            far(which, 0, source, there).start()

    def moved_out(which, source, there):
        far(which, 1, source, there).wait_send()

        @pl.when(jnp.logical_not(stay))
        def _():
            far(which, 0, source, there).wait_send()

    def moved_in(which, source, there):
        far(which, 1, source, there).wait_recv()

        @pl.when(stay)
        def _():
            near(which, source, there).wait()

        @pl.when(jnp.logical_not(stay))
        def _():
            far(which, 0, source, there).wait_recv()

    moves = ((0, clip_ref, clip.at[0, 0]), (1, small_ref, xs), (2, large_ref, xl), (3, cot_ref, cot))
    move(*moves[0])
    move(*moves[1])
    loads = [
        pltpu.make_async_copy(source, there, load_sems.at[i])
        for i, (source, there) in enumerate(zip(weight_refs, weights))
    ]
    for load in loads:
        load.start()
    moved_out(*moves[0])
    moved_out(*moves[1])
    move(*moves[2])
    outs = []

    def keep(source, there):
        copy = pltpu.make_async_copy(source, there, out_sems.at[len(outs)])
        copy.start()
        outs.append(copy)

    def front_into(x, n_ref, q_ref, kv):
        normed = norm(x[...].astype(f32), first_gain[...])
        n_ref[...] = normed
        keys = dot(normed, wk[...]).astype(bf16)
        values = dot(normed, wv[...]).astype(bf16)
        for pair in range(pairs):
            lanes = slice(pair * LANES, (pair + 1) * LANES)
            kv[0, pair, 0] = keys[:, lanes]
            kv[0, pair, 1] = values[:, lanes]

    def query_into(n_ref, q_ref):
        query = (dot(n_ref[...], wq[...]) * Q_SCALE).astype(bf16)
        for pair in range(pairs):
            q_ref[pair] = query[:, pair * LANES : (pair + 1) * LANES]

    large, small = Gather(here, kvl, gather_l), Gather(here, kvs, gather_s)
    cross, clips = Gather(here, ckv, gather_c), Gather(here, clip, gather_clip)

    moved_in(*moves[0])
    for kind in (0, 1):
        clips.copy(kind, 0, 1, 0).start()
    moved_in(*moves[1])
    keep(xs, xs_out)
    for i in (0, 1, 2):
        loads[i].wait()
    front_into(xs, ns_ref, qs_ref, kvs)
    for kind in (0, 1):
        small.copy(kind, 0, pairs, 0).start()
    query_into(ns_ref, qs_ref)
    clips.copy(0, 0, 1, 0).wait_recv()
    clips.copy(2, 0, 1, 0).start()
    for kind in (1, 2):
        clips.copy(kind, 0, 1, 0).wait_recv()

    few = clip.shape[2]
    spot = lax.broadcasted_iota(jnp.int32, (1, LANES), 1) % HALF
    number = spot.astype(f32)
    some = spot < 4
    row = lax.broadcasted_iota(jnp.int32, (2 * few, few), 0) // 2
    twice = jnp.where(row == lax.broadcasted_iota(jnp.int32, (2 * few, few), 1), 1.0, 0.0)
    twice = twice.astype(bf16)
    for part in range(4):
        mine = clip[part, 0]
        for value, mk_ref, mq_ref in (
            (mine.astype(f32), mks_ref, mqs_ref),
            (dot(twice, mine), mkl_ref, mql_ref),
        ):
            rows = value.shape[0]
            mk_ref[pl.ds(part * rows, rows), :] = jnp.where(
                some & (value != number), NEGATIVE, 0.0
            ).astype(bf16)
            if part == 0:
                mq_ref[...] = jnp.where(some & (value == number), 1.0, 0.0).astype(bf16)

    moved_in(*moves[2])
    moved_out(*moves[2])
    move(*moves[3])
    keep(xl, xl_out)
    front_into(xl, nl_ref, ql_ref, kvl)
    third = pairs // 3
    small.copy(0, 0, pairs, 0).wait_send()
    large.copy(0, 0, third, 0).start()
    for group in range(3):
        large.copy(1, group * third, third, group).start()
    query_into(nl_ref, ql_ref)

    small.copy(0, 0, pairs, 0).wait_recv()
    small.copy(2, 0, pairs, 0).start()
    small.copy(1, 0, pairs, 0).wait_recv()
    small.copy(2, 0, pairs, 0).wait_recv()
    keep(kvs, kvs_out)

    def small_pair(pair, carry):
        attend_pair(pair, qs_ref, kvs, mqs_ref, mks_ref, spaces, os_ref, ls_ref)
        return carry

    lax.fori_loop(0, pairs, small_pair, 0)
    loads[3].wait()
    for pair in range(pairs):
        wide[:, pair * LANES : (pair + 1) * LANES] = os_ref[pair]
    hidden = xs[...].astype(f32) + dot(wide[...], wo[...])
    hidden_ref[...] = hidden
    second_ref[...] = norm(hidden, second_gain[...])
    total[...] = hidden
    loads[4].wait()
    loads[5].wait()
    width = wide.shape[1]
    steps = up.shape[1] // width
    for step in range(steps):
        lanes = slice(step * width, (step + 1) * width)
        active, slope = gelu_both(dot(second_ref[...], up[:, lanes]))
        active = active.astype(bf16)
        active_ref[:, lanes] = active
        slope_ref[:, lanes] = slope.astype(bf16)
        total[...] += dot(active, down[lanes, :])
        if step == steps // 2:
            large.copy(0, 0, third, 0).wait_send()
            large.copy(0, third, third, 1).start()
    merged = total[...]
    merged_ref[...] = merged
    context = norm(merged, context_gain[...])
    context_ref[...] = context
    loads[6].wait()
    loads[7].wait()
    keys = dot(context, wck[...]).astype(bf16)
    values = dot(context, wcv[...]).astype(bf16)
    for pair in range(pairs):
        lanes = slice(pair * LANES, (pair + 1) * LANES)
        ckv[0, pair, 0] = keys[:, lanes]
        ckv[0, pair, 1] = values[:, lanes]
    cross.copy(1, 0, pairs, 0).start()

    def large_pair(pair, carry):
        attend_pair(pair, ql_ref, kvl, mql_ref, mkl_ref, spaces, ol_ref, ll_ref)
        return carry

    for group in range(3):
        at = group * third
        large.copy(0, at, third, group).wait_recv()
        large.copy(2, at, third, group).start()
        if group == 0:
            large.copy(0, third, third, 1).wait_send()
            large.copy(0, 2 * third, third, 2).start()
        if group == 2:
            large.copy(0, 2 * third, third, 2).wait_send()
            cross.copy(0, 0, pairs, 0).start()
        large.copy(1, at, third, group).wait_recv()
        large.copy(2, at, third, group).wait_recv()
        if group == 2:
            keep(kvl, kvl_out)
        lax.fori_loop(at, at + third, large_pair, 0)
    moved_in(*moves[3])
    moved_out(*moves[3])
    keep(cot, cot_out)
    cross.copy(0, 0, pairs, 0).wait_recv()
    cross.copy(2, 0, pairs, 0).start()
    cross.copy(1, 0, pairs, 0).wait_recv()
    cross.copy(2, 0, pairs, 0).wait_recv()
    keep(ckv, ckv_out)
    for copy in [small.copy(1, 0, pairs, 0), small.copy(2, 0, pairs, 0)]:
        copy.wait_send()
    for kind in (0, 1, 2):
        clips.copy(kind, 0, 1, 0).wait_send()
        cross.copy(kind, 0, pairs, 0).wait_send()
        if kind:
            for group in range(3):
                large.copy(kind, group * third, third, group).wait_send()
    for copy in outs:
        copy.wait()


def begin(large, small, cotangent, clip, weights, gains):
    seqs, count, width = large.shape
    few = small.shape[1]
    count, few = 2 * count, 2 * few
    pairs = width // LANES
    hidden = weights[4].shape[1]
    shape = jax.ShapeDtypeStruct
    kv_l, kv_s = (4, pairs, 2, count, LANES), (4, pairs, 2, few, LANES)
    anywhere = pl.BlockSpec(memory_space=pl.ANY)
    vmem = pl.BlockSpec(memory_space=pltpu.VMEM)
    out_shape = [
        shape((count, width), bf16),
        shape((few, width), bf16),
        shape((count, width), bf16),
        shape(kv_l, bf16),
        shape(kv_s, bf16),
        shape(kv_s, bf16),
        shape((count, width), bf16),
        shape((few, width), bf16),
        shape((pairs, count, LANES), bf16),
        shape((pairs, few, LANES), bf16),
        shape((pairs, count, LANES), bf16),
        shape((pairs, count, LANES), f32),
        shape((pairs, few, LANES), bf16),
        shape((pairs, few, LANES), f32),
        shape((few, width), f32),
        shape((few, width), f32),
        shape((few, width), bf16),
        shape((few, hidden), bf16),
        shape((few, hidden), bf16),
        shape((few, width), bf16),
        shape((count, LANES), bf16),
        shape((4 * count, LANES), bf16),
        shape((few, LANES), bf16),
        shape((4 * few, LANES), bf16),
    ]
    dma = pltpu.SemaphoreType.DMA
    scratch = [
        pltpu.VMEM((count, width), bf16),
        pltpu.VMEM((few, width), bf16),
        pltpu.VMEM((count, width), bf16),
        pltpu.VMEM((4, 1, few, LANES), bf16),
        pltpu.VMEM(kv_l, bf16),
        pltpu.VMEM(kv_s, bf16),
        pltpu.VMEM(kv_s, bf16),
    ]
    scratch += [pltpu.VMEM(weight.shape, bf16) for weight in weights]
    scratch += [pltpu.VMEM((4 * count, LANES), bf16)] * 4
    scratch += [pltpu.VMEM((few, width), bf16), pltpu.VMEM((few, width), f32)]
    scratch += [dma((2, 8)), dma((2, 9)), dma((2, 3)), dma((2, 3)), dma((2, 3)), dma((8,)), dma((6,))]
    return pl.pallas_call(
        functools.partial(begin_kernel, pairs),
        in_specs=[anywhere] * 12 + [vmem] * 3,
        out_specs=[anywhere] * 6 + [vmem] * 18,
        out_shape=out_shape,
        scratch_shapes=scratch,
        compiler_params=pltpu.CompilerParams(
            vmem_limit_bytes=62 << 20, collective_id=4, has_side_effects=True
        ),
        cost_estimate=pl.CostEstimate(
            flops=16 * count * 4 * count * width + 18 * few * width * hidden,
            bytes_accessed=40 << 20,
            transcendentals=count * count * 4 * width // HALF,
        ),
        name="begin",
    )(large, small, cotangent, clip, *weights, *gains)


def cross_attend_kernel(q_ref, kv_ref, mq_ref, mk_ref, o_ref, l_ref, *spaces):
    attend_pair(0, q_ref, kv_ref, mq_ref, mk_ref, spaces, o_ref, l_ref)


def cross_attend(query, kv, mask_q, mask_k):
    pairs, count = query.shape[:2]
    rows = kv.shape[3]
    one = pl.BlockSpec((1, count, LANES), lambda i: (i, 0, 0))
    return pl.pallas_call(
        cross_attend_kernel,
        grid=(pairs,),
        in_specs=[
            one,
            pl.BlockSpec((4, 1, 2, rows, LANES), lambda i: (0, i, 0, 0, 0)),
            whole((count, LANES)),
            whole((4 * rows, LANES)),
        ],
        out_specs=[one, one],
        out_shape=[
            jax.ShapeDtypeStruct(query.shape, bf16),
            jax.ShapeDtypeStruct(query.shape, f32),
        ],
        scratch_shapes=[pltpu.VMEM((4 * rows, LANES), bf16)] * 4,
        compiler_params=pltpu.CompilerParams(vmem_limit_bytes=40 << 20),
        cost_estimate=pl.CostEstimate(
            flops=64 * count * rows * pairs * LANES,
            bytes_accessed=32 * count * pairs * LANES,
            transcendentals=8 * count * rows * pairs,
        ),
        name="cross_attend",
    )(query, kv, mask_q, mask_k)


def after(value, *needed):
    return lax.optimization_barrier((value, needed))[0]


CROSS_ORDERS = (BY_Y[:3], BY_ZL[:3])
SELVES_ORDERS = (BY_Y[:3], BY_ZL[:3], BY_X, LATE_ORDER, LATE_ORDER)
SELVES_ENDS = (False, False, True, True, True)
SELVES_STAGES = (
    (0, 4, 11),
    (0, 5, 11),
    (0, 2, 4, 6, 8, 9, 10),
    (2, 4, 6, 7),
    (2, 4, 6, 7),
)


def paired_end(views, normed, large, small, cross, merged, weights, crosses, gains, united_view, restore):
    large_view, small_view = views
    large_normed, small_normed, asked, context = normed
    large_q, large_mixed, large_logsum, large_mask_q, large_mask_k, large_kv = large
    small_q, small_mixed, small_logsum, small_mask_q, small_mask_k, small_kv = small
    cross_q, united, cross_logsum, cross_kv, united_grad, grad_out = cross
    large_merged, large_saved, small_merged, small_saved = merged
    query_weight, key_weight, value_weight, output_weight, up_weight, down_weight = weights
    first_gain, second_gain, query_gain, context_gain = gains
    width = large_view.shape[1]
    rows = width // 8
    large_grad, small_grad, first, other, query_gain_grad, context_gain_grad = cross_back(
        (cross_q, united_grad, united, cross_logsum, large_mask_q, small_mask_k),
        cross_kv,
        (asked, context, united, grad_out, large_merged, small_merged) + crosses,
        (query_gain, context_gain),
    )
    (
        large_hidden, small_hidden, large_mixed_grad, small_mixed_grad, up_grad, down_grad,
        output_grad, second_gain_grad, first, other,
    ) = back(
        large_grad, small_grad, large_saved, small_saved, [large_mixed], small_mixed, output_weight,
        second_gain, up_weight, down_weight, True, (first, other), CROSS_ORDERS,
    )
    eight = (8, 4 * rows, width)
    four = (4, rows // 2, width)
    selves, sums = selves_back(
        (large_q, large_mixed_grad, large_mixed, large_logsum, large_mask_q, large_mask_k),
        large_kv,
        (small_q, small_mixed_grad, small_mixed, small_logsum, small_mask_q, small_mask_k),
        small_kv,
        (
            up_grad.reshape(eight), down_grad.reshape(eight), output_grad,
            first.reshape(four), other.reshape(four),
        ),
        SELVES_ORDERS, SELVES_ENDS, SELVES_STAGES,
    )
    up, down, output, first, other = sums
    large_grad, small_grad, gain = view_grads(
        selves, large_view, small_view, large_hidden, small_hidden, first_gain,
        (query_weight, key_weight, value_weight),
    )
    large_grad, small_grad = restore(large_grad), restore(small_grad)
    gains = jnp.concatenate(
        (gain, second_gain_grad, query_gain_grad, context_gain_grad, jnp.zeros((4, width), f32)),
        axis=0,
    )
    last, late, gains = last_sums(
        selves, large_normed, small_normed, gains,
        (up.reshape(4, rows, width), down.reshape(4, rows, width)),
    )
    up, down = (total.astype(f32) for total in late)

    def square(total):
        total = total.astype(f32).reshape(2, 2, width // 16, width // 2)
        return jnp.transpose(total, (0, 2, 1, 3)).reshape(rows, width)

    first = first.astype(f32).reshape(2, rows, width)
    other = other.astype(f32).reshape(2, rows, width)
    at = lax.axis_index("tm") * rows
    gains = [lax.dynamic_slice(gains, (i, at), (1, rows))[0] for i in range(4)]
    return (
        united_view,
        large_grad.astype(f32),
        small_grad.astype(f32),
        gains[0],
        square(last[0]),
        square(last[1]),
        square(last[2]),
        square(output),
        gains[1],
        jnp.transpose(up, (1, 0, 2)).reshape(rows, 4 * width),
        down.reshape(4 * rows, width),
        gains[2],
        gains[3],
        first[1],
        other[0],
        other[1],
        first[0],
    )


def per_device(tm, seq_size, *args):
    (
        large_view,
        small_view,
        clip_ids,
        first_gain,
        query_weight,
        key_weight,
        value_weight,
        output_weight,
        second_gain,
        up_weight,
        down_weight,
        query_gain,
        context_gain,
        cross_query,
        cross_key,
        cross_value,
        cross_output,
        cotangent,
    ) = args
    seqs, count, width = large_view.shape
    side = tm // 4
    gains = [
        g.astype(f32).reshape(1, width)
        for g in (first_gain, second_gain, query_gain, context_gain)
    ]
    first_gain, second_gain, query_gain, context_gain = gains

    tm_at = lax.axis_index("tm")
    seq_at = lax.axis_index("seq")
    z, x = tm_at // side, tm_at % side
    y, core = seq_at // 2, seq_at % 2
    places = [
        (pz, px, py, pc)
        for pz in range(4)
        for px in range(side)
        for py in range(2)
        for pc in range(2)
    ]

    def number(place):
        return (place[0] * side + place[1]) * seq_size + place[2] * 2 + place[3]

    def permute(value, place):
        pairs = [(number(at), number(place(*at))) for at in places]
        return lax.ppermute(value, ("tm", "seq"), pairs)

    def inverse(place):
        table = {place(*at): at for at in places}
        return lambda *at: table[at]

    go = (
        lambda z, x, y, c: (2 * c + z % 2, x, y, z // 2),
        lambda z, x, y, c: (2 * c + 1 - z % 2, x, y, z // 2),
    )
    back_home = tuple(inverse(place) for place in go)
    other_core = lambda value: permute(value, lambda z, x, y, c: (z, x, y, 1 - c))
    other_y = lambda value: permute(value, lambda z, x, y, c: (z, x, 1 - y, c))
    by_x = lambda value, d: permute(value, lambda z, x, y, c: (z, (x + d) % side, y, c))
    odd = z % 2 == 1

    def relocate(value):
        near = jnp.where(odd, value[1], value[0])
        far = jnp.where(odd, value[0], value[1])
        return jnp.concatenate([permute(near, go[0]), permute(far, go[1])], axis=0)

    def restore(value):
        rows = value.shape[0] // 2
        near, far = permute(value[:rows], back_home[0]), permute(value[rows:], back_home[1])
        return jnp.where(odd, jnp.stack([far, near]), jnp.stack([near, far]))

    def join(parts, axis):
        return parts[0] if len(parts) == 1 else jnp.concatenate(parts, axis=axis)

    def gather(value, axis=1):
        across = join([by_x(value, d) for d in range(1, side)], axis)
        return (value, across, other_core(value), other_core(across))

    def add(a, b):
        return (a.astype(f32) + b.astype(f32)).astype(bf16)

    def scatter_core(keep, send):
        return add(keep, other_core(send))

    def scatter_x(sums):
        rows = sums.shape[1] // side
        total = sums[:, :rows].astype(f32)
        for d in range(1, side):
            total = total + by_x(sums[:, d * rows : (d + 1) * rows], -d).astype(f32)
        return total.astype(bf16)

    if side == 2:
        clip = jnp.broadcast_to(
            clip_ids[:, ::2].astype(bf16)[:, :, None], (seqs, count // 2, LANES)
        )
        (
            large, small, grad_out, large_kv, small_kv, cross_kv, large_normed, small_normed,
            large_q, small_q, large_mixed, large_logsum, small_mixed, small_logsum, small_merged,
            *small_saved, context, large_mask_q, large_mask_k, small_mask_q, small_mask_k,
        ) = begin(
            large_view, small_view, cotangent, clip,
            (query_weight, key_weight, value_weight, output_weight, up_weight, down_weight,
             cross_key, cross_value),
            (first_gain, second_gain, context_gain),
        )
        united_grad = dot(grad_out, cross_output, NT).astype(bf16)
        large_merged, *large_saved, asked, cross_q = rest(
            large, [large_mixed], output_weight, second_gain, up_weight, down_weight,
            query_gain, (cross_query,),
        )
        united, cross_logsum = cross_attend(cross_q, cross_kv, large_mask_q, small_mask_k)
        flat = jnp.transpose(united, (1, 0, 2)).reshape(2 * count, width)
        united_view = restore((large_merged + dot(flat, cross_output)).astype(bf16))
        return paired_end(
            (large, small),
            (large_normed, small_normed, asked, context),
            (large_q, large_mixed, large_logsum, large_mask_q, large_mask_k, large_kv),
            (small_q, small_mixed, small_logsum, small_mask_q, small_mask_k, small_kv),
            (cross_q, united, cross_logsum, cross_kv, united_grad, grad_out),
            (large_merged, large_saved, small_merged, small_saved),
            (query_weight, key_weight, value_weight, output_weight, up_weight, down_weight),
            (cross_query, cross_key, cross_value),
            (first_gain, second_gain, query_gain, context_gain),
            united_view,
            restore,
        )

    groups = 3
    part = width // groups
    short_clips = gather(relocate(clip_ids[:, ::2].astype(f32)), 0)
    small = relocate(small_view)
    large = relocate(large_view)
    grad_out = relocate(after(cotangent, large))
    spot = lax.broadcasted_iota(jnp.int32, (1, LANES), 1) % HALF

    def mask_of_keys(numbers):
        away = numbers.astype(jnp.int32)[:, None] != spot
        return jnp.where((spot < 4) & away, NEGATIVE, 0.0).astype(bf16)

    def mask_of_queries(numbers):
        same = numbers.astype(jnp.int32)[:, None] == spot
        return jnp.where((spot < 4) & same, 1.0, 0.0).astype(bf16)

    short = jnp.concatenate(short_clips)
    small_mask_k = mask_of_keys(short)
    large_mask_k = mask_of_keys(jnp.repeat(short, 2))
    small_mask_q = mask_of_queries(short_clips[0])
    large_mask_q = mask_of_queries(jnp.repeat(short_clips[0], 2))

    small_normed, small_q, small_kv = front(
        small, first_gain, query_weight, key_weight, value_weight, 1
    )
    small_kv = gather(small_kv[0])
    large_normed, large_q, large_kv = front(
        large, first_gain, query_weight, key_weight, value_weight, groups
    )
    large_kv = [gather(kv) for kv in large_kv]
    small_mixed, small_logsum = attend(small_q, small_kv, small_mask_q, small_mask_k, 0, width)
    small_merged, *small_saved, context, cross_kv = rest(
        small, [small_mixed], output_weight, second_gain, up_weight, down_weight,
        context_gain, (cross_key, cross_value),
    )
    cross_kv = gather(cross_kv)
    united_grad = dot(grad_out, cross_output, NT).astype(bf16)
    large_out = ()
    for group, kv in enumerate(large_kv):
        large_out = attend(large_q, kv, large_mask_q, large_mask_k, group * part, part, large_out)
    large_mixed, large_logsum = large_out
    large_merged, *large_saved, asked, cross_q = rest(
        large, [large_mixed], output_weight, second_gain, up_weight, down_weight,
        query_gain, (cross_query,),
    )
    united, cross_logsum = attend(cross_q, cross_kv, large_mask_q, small_mask_k, 0, width)
    united_view = restore((large_merged + dot(united, cross_output)).astype(bf16))

    bits = side.bit_length() - 1
    moves = {"zh": lambda z, x, y, c: (z ^ 2, x, y, c), "zl": lambda z, x, y, c: (z ^ 1, x, y, c)}
    mine = {"zh": z // 2, "zl": z % 2}
    axes = {"zh": 0, "zl": 1}
    for bit in range(bits):
        flip = 1 << (bits - 1 - bit)
        moves[f"x{bit}"] = lambda z, x, y, c, flip=flip: (z, x ^ flip, y, c)
        mine[f"x{bit}"] = (x // flip) % 2
        axes[f"x{bit}"] = 2 + bit
    moves["core"] = lambda z, x, y, c: (z, x, y, 1 - c)
    moves["y"] = lambda z, x, y, c: (z, x, 1 - y, c)
    mine["core"], mine["y"] = core, y
    axes["core"], axes["y"] = 2 + bits, 3 + bits
    by_y = ["core", "y", "zl"] + [f"x{bit}" for bit in range(bits)] + ["zh"]
    by_zl = ["core", "zl", "y"] + [f"x{bit}" for bit in range(bits)] + ["zh"]
    by_yx = ["core", "y"] + [f"x{bit}" for bit in range(bits)] + ["zl", "zh"]

    class Sum:
        def __init__(self, local, order):
            rows, wide = local.shape
            self.value = local.reshape((2,) * (2 + bits) + (rows // tm, wide))
            self.todo = list(order)
            self.rows, self.wide = rows // tm, wide

        def step(self, *needed):
            name = self.todo.pop(0)
            axis = axes[name]
            size = self.value.shape[axis] // 2
            at = mine[name]
            keep = lax.dynamic_slice_in_dim(self.value, at * size, size, axis)
            send = lax.dynamic_slice_in_dim(self.value, (1 - at) * size, size, axis)
            self.value = add(keep, permute(send, moves[name]))
            return self.value

        def finish(self):
            while self.todo:
                self.step()
            value = self.value.reshape(self.rows // 2, self.wide // 2)
            other = other_y(value)
            value = jnp.where(
                y == 0,
                jnp.concatenate([value, other], axis=1),
                jnp.concatenate([other, value], axis=1),
            )
            other = other_core(value)
            return jnp.where(
                core == 0,
                jnp.concatenate([value, other], axis=0),
                jnp.concatenate([other, value], axis=0),
            ).astype(f32)

    cross_groups = 2
    cross_part = width // cross_groups
    dcq, dckv = [], []
    for group in range(cross_groups):
        query = after(cross_q, *dcq[-1:])
        at = group * cross_part
        dq, keep, send = attend_back(
            query, cross_kv, united_grad, united, cross_logsum,
            large_mask_q, small_mask_k, at, at, at, cross_part,
        )
        dcq.append(dq)
        dckv.append(scatter_x(scatter_core(keep, send)))
    dcq = jnp.concatenate(dcq, axis=1)
    dck = jnp.concatenate([kv[0] for kv in dckv], axis=1)
    dcv = jnp.concatenate([kv[1] for kv in dckv], axis=1)
    extra, query_gain_grad = norm_back(dot(dcq, cross_query, NT), large_merged, query_gain)
    large_merged_grad = grad_out.astype(f32) + extra
    small_merged_grad, context_gain_grad = norm_back(
        dot(dck, cross_key, NT) + dot(dcv, cross_value, NT), small_merged, context_gain
    )
    cross_parts = [
        dot(united, grad_out, TN).astype(bf16),
        dot(asked, dcq, TN).astype(bf16),
        dot(context, dck, TN).astype(bf16),
        dot(context, dcv, TN).astype(bf16),
    ]
    (
        large_hidden_grad,
        small_hidden_grad,
        large_mixed_grad,
        small_mixed_grad,
        up_grad,
        down_grad,
        output_grad,
        second_gain_grad,
    ) = back(
        large_merged_grad, small_merged_grad, large_saved, small_saved, [large_mixed], small_mixed,
        output_weight, second_gain, up_weight, down_weight, False,
    )
    cross_sum = Sum(jnp.concatenate(cross_parts, axis=1), by_y)
    up_sum = Sum(up_grad, by_y)
    down_sum = Sum(down_grad, by_zl)
    cross_sum.step()
    small_dq, keep, send = attend_back(
        after(small_q, cross_sum.value), small_kv, small_mixed_grad, small_mixed, small_logsum,
        small_mask_q, small_mask_k, 0, 0, 0, width,
    )
    small_sums = scatter_core(keep, send)
    up_sum.step()
    down_sum.step()
    cross_sum.step()
    needed = [small_dq, up_sum.value, down_sum.value]
    normed = jnp.concatenate([large_normed, small_normed], axis=0)
    last_sums, dqs, dkvs = [], [], []
    pending = None
    for group in range(groups):
        at = group * part
        dq, keep, send = attend_back(
            after(large_q, *needed), large_kv[group], large_mixed_grad, large_mixed, large_logsum,
            large_mask_q, large_mask_k, at, at, 0, part,
        )
        sums = scatter_core(keep, send)
        dqs.append(dq)
        needed = [dq]
        if group == 0:
            small_dkv = scatter_x(small_sums)
            needed += [cross_sum.value, small_sums]
        if group == 1:
            needed += [small_dkv, up_sum.step(), down_sum.step(), cross_sum.step()]
        if pending is not None:
            needed.append(pending.step())
        dkv = scatter_x(sums)
        dkvs.append(dkv)
        local = jnp.concatenate(
            [
                jnp.concatenate([dq, dkv[0], dkv[1]], axis=1),
                jnp.concatenate(
                    [
                        small_dq[:, at : at + part],
                        small_dkv[0, :, at : at + part],
                        small_dkv[1, :, at : at + part],
                    ],
                    axis=1,
                ),
            ],
            axis=0,
        )
        local = dot(normed, local, TN).astype(bf16)
        pending = Sum(local, by_yx)
        last_sums.append(pending)

    def front_back(view, hidden_grad, dq, dk, dv):
        grad = (
            dot(dq, query_weight, NT) + dot(dk, key_weight, NT) + dot(dv, value_weight, NT)
        )
        extra, gain_part = norm_back(grad, view.astype(f32), first_gain)
        return (hidden_grad + extra).astype(bf16), gain_part

    small_grad, small_gain = front_back(
        small, small_hidden_grad, small_dq, small_dkv[0], small_dkv[1]
    )
    large_grad, large_gain = front_back(
        large,
        large_hidden_grad,
        jnp.concatenate(dqs, axis=1),
        jnp.concatenate([kv[0] for kv in dkvs], axis=1),
        jnp.concatenate([kv[1] for kv in dkvs], axis=1),
    )
    small_grad = restore(small_grad).astype(f32)
    large_grad = restore(large_grad).astype(f32)
    output_sum = Sum(output_grad, by_yx)
    gain_rows = jnp.concatenate(
        [large_gain + small_gain, second_gain_grad, query_gain_grad, context_gain_grad], axis=0
    )
    wide = width // tm
    gain_rows = jnp.transpose(gain_rows.reshape(4, tm, wide), (1, 0, 2)).astype(bf16)
    gain_rows = jnp.pad(gain_rows, ((0, 0), (0, 28), (0, 2 * LANES - wide)))
    gain_sum = Sum(gain_rows.reshape(tm * 32, 2 * LANES), by_yx)

    cross_total = cross_sum.finish()
    up_total = up_sum.finish()
    down_total = down_sum.finish()
    output_total = output_sum.finish()
    last_totals = [total.finish() for total in last_sums]
    gain_total = gain_sum.finish()
    cross_grads = [cross_total[:, i * width : (i + 1) * width] for i in range(4)]
    last_grads = [
        jnp.concatenate([total[:, i * part : (i + 1) * part] for total in last_totals], axis=1)
        for i in range(3)
    ]
    gain_grads = [gain_total[i, :wide] for i in range(4)]
    return (
        united_view,
        large_grad,
        small_grad,
        gain_grads[0],
        last_grads[0],
        last_grads[1],
        last_grads[2],
        output_total,
        gain_grads[1],
        up_total,
        down_total,
        gain_grads[2],
        gain_grads[3],
        cross_grads[1],
        cross_grads[2],
        cross_grads[3],
        cross_grads[0],
    )


def solution(mesh):
    token = P("seq", "tm", None)
    in_specs = (token, token, P("seq", "tm")) + (P(),) * 14 + (token,)
    vector, matrix = P("tm"), P("tm", None)
    out_specs = (
        (token, token, token, vector)
        + (matrix,) * 4
        + (vector, matrix, matrix, vector, vector)
        + (matrix,) * 4
    )
    return jax.shard_map(
        functools.partial(per_device, mesh.shape["tm"], mesh.shape["seq"]),
        mesh=mesh,
        in_specs=in_specs,
        out_specs=out_specs,
        check_vma=False,
    )
```

```python
import functools

import jax
import jax.numpy as jnp
from jax import lax
from jax.experimental import pallas as pl
from jax.experimental.pallas import tpu as pltpu
from jax.sharding import PartitionSpec as P

HEADS = 12
EPS = 1e-05
NEGATIVE = -1e30
LOG2E = 1.4426950408889634
LN2 = 0.6931471805599453
LANES = 128
HALF = 64

bf16 = jnp.bfloat16
f32 = jnp.float32
NT = (((1,), (1,)), ((), ()))
NN = (((1,), (0,)), ((), ()))
TN = (((0,), (0,)), ((), ()))


def dot(a, b, dims=NN):
    return lax.dot_general(a, b, dims, preferred_element_type=f32)


def largest_block(rows, most):
    block = min(rows, most)
    while rows % block or block % 16:
        block -= 1
    return block


def columns(rows, at):
    return pl.BlockSpec((rows, LANES), lambda i: (0, i + at))


def pair_columns(rows, at):
    return pl.BlockSpec((2, rows, LANES), lambda i: (0, 0, i + at))


def whole(shape):
    return pl.BlockSpec(shape, lambda i: (0,) * len(shape))


def attend_kernel(parts, block, *refs):
    q_ref, mq_ref, mk_ref = refs[:3]
    kv_refs = refs[3 : 3 + parts]
    o_ref, l_ref, ka0, ka1, va0, va1 = refs[-6:]
    count = q_ref.shape[0]
    first = 0
    for kv_ref in kv_refs:
        rows = kv_ref.shape[1]
        low = lax.broadcasted_iota(jnp.int32, (rows, LANES), 1) < HALF
        here = pl.ds(first, rows)
        keys, values, mask = kv_ref[0], kv_ref[1], mk_ref[here, :]
        one = jnp.ones_like(values)
        ka0[here, :] = jnp.where(low, keys, mask)
        ka1[here, :] = jnp.where(low, mask, keys)
        va0[here, :] = jnp.where(low, values, one)
        va1[here, :] = jnp.where(low, one, values)
        first += rows
    low = lax.broadcasted_iota(jnp.int32, (block, LANES), 1) < HALF
    for number in range(count // block):
        here = pl.ds(number * block, block)
        query, mask = q_ref[here, :], mq_ref[here, :]
        tops, sums = [], []
        for head, keys, values in ((0, ka0, va0), (1, ka1, va1)):
            mine = jnp.where(low, query, mask) if head == 0 else jnp.where(low, mask, query)
            score = dot(mine, keys[...], NT)
            top = jnp.max(score, axis=1, keepdims=True)
            weight = jnp.exp2(score - top).astype(bf16)
            sums.append(dot(weight, values[...]))
            tops.append(jnp.broadcast_to(top, (block, LANES)))
        total = jnp.where(low, sums[1], sums[0])
        top = jnp.where(low, tops[1], tops[0])
        out = jnp.where(low, sums[0], sums[1])
        o_ref[here, :] = (out / pltpu.roll(total, HALF, 1)).astype(bf16)
        l_ref[here, :] = top + jnp.log2(total)


def attend(query, kv, mask_q, mask_k, at, width, earlier=()):
    count = query.shape[0]
    total = sum(part.shape[1] for part in kv)
    out = lambda kind: jax.ShapeDtypeStruct((count, query.shape[1]), kind)
    given = 3 + len(kv)
    return pl.pallas_call(
        functools.partial(attend_kernel, len(kv), largest_block(count, 256)),
        grid=(width // LANES,),
        in_specs=[columns(count, at // LANES), whole((count, LANES)), whole((total, LANES))]
        + [pair_columns(part.shape[1], 0) for part in kv]
        + [pl.BlockSpec(memory_space=pl.ANY)] * len(earlier),
        out_specs=[columns(count, at // LANES)] * 2,
        out_shape=[out(bf16), out(f32)],
        scratch_shapes=[pltpu.VMEM((total, LANES), bf16)] * 4,
        input_output_aliases={given + i: i for i in range(len(earlier))},
        compiler_params=pltpu.CompilerParams(vmem_limit_bytes=40 << 20),
        cost_estimate=pl.CostEstimate(
            flops=16 * count * total * width,
            bytes_accessed=width * (count * 8 + total * 4),
            transcendentals=count * total * width // HALF,
        ),
        name="attend",
    )(query, mask_q, mask_k, *kv, *earlier)


def three(value):
    first = value.astype(bf16)
    rest = value - first.astype(f32)
    second = rest.astype(bf16)
    return first, second, (rest - second.astype(f32)).astype(bf16)


def attend_back_kernel(parts, block, *refs):
    q_ref, do_ref, o_ref, l_ref, mq_ref, mk_ref = refs[:6]
    kv_refs = refs[6 : 6 + parts]
    dq_ref, keep_ref, send_ref, keys_at, values_at = refs[6 + parts :]
    count = q_ref.shape[0]
    first = 0
    for kv_ref in kv_refs:
        here = pl.ds(first, kv_ref.shape[1])
        keys_at[here, :] = kv_ref[0]
        values_at[here, :] = kv_ref[1]
        first += kv_ref.shape[1]
    lane = lax.broadcasted_iota(jnp.int32, (count, LANES), 1)
    low = lane < HALF
    spot = lane % HALF
    query, grad, mask = q_ref[...], do_ref[...], mq_ref[...]
    zero = jnp.zeros_like(query)
    product = grad.astype(f32) * o_ref[...].astype(f32)
    delta0 = jnp.sum(jnp.where(low, product, 0.0), axis=1, keepdims=True)
    delta1 = jnp.sum(jnp.where(low, 0.0, product), axis=1, keepdims=True)
    delta = jnp.where(low, delta1, delta0)

    def beside(base, value):
        a, b, c = three(-value)
        return jnp.where(spot == 4, a, jnp.where(spot == 5, b, jnp.where(spot == 6, c, base)))

    query_side = beside(mask, l_ref[...])
    grad_side = beside(zero, delta)
    query_a = (jnp.where(low, query, query_side), jnp.where(low, query_side, query))
    grad_a = (jnp.where(low, grad, grad_side), jnp.where(low, grad_side, grad))
    query_m = (jnp.where(low, query, zero), jnp.where(low, zero, query))
    grad_m = (jnp.where(low, grad, zero), jnp.where(low, zero, grad))
    lane_k = lax.broadcasted_iota(jnp.int32, (block, LANES), 1)
    low_k = lane_k < HALF
    spot_k = lane_k % HALF
    one = jnp.where((spot_k >= 4) & (spot_k < 7), 1.0, 0.0).astype(bf16)
    dq = jnp.zeros((count, LANES), f32)
    for number in range(first // block):
        here = pl.ds(number * block, block)
        keys, values = keys_at[here, :], values_at[here, :]
        side = mk_ref[here, :] + one
        nought = jnp.zeros_like(keys)
        dk = jnp.zeros((block, LANES), f32)
        dv = jnp.zeros((block, LANES), f32)
        for head in (0, 1):
            pick = lambda a, b: jnp.where(low_k, a, b) if head == 0 else jnp.where(low_k, b, a)
            prob = jnp.exp2(dot(query_a[head], pick(keys, side), NT))
            change = dot(grad_a[head], pick(values, one), NT)
            score_grad = (prob * change).astype(bf16)
            dv += dot(prob.astype(bf16), grad_m[head], TN)
            dk += dot(score_grad, query_m[head], TN)
            dq += dot(score_grad, pick(keys, nought))
        out_ref = keep_ref if number * block < first // 2 else send_ref
        there = pl.ds(number * block % (first // 2), block)
        out_ref[0, there, :] = (dk * LN2).astype(bf16)
        out_ref[1, there, :] = dv.astype(bf16)
    dq_ref[...] = (dq * HALF**-0.5).astype(bf16)


def attend_back(query, kv, grad, out, logsum, mask_q, mask_k, at, at_out, at_kv, width):
    count = query.shape[0]
    total = sum(part.shape[1] for part in kv)
    return pl.pallas_call(
        functools.partial(attend_back_kernel, len(kv), largest_block(total // 2, 512)),
        grid=(width // LANES,),
        in_specs=[columns(count, at // LANES)] * 2
        + [columns(count, at_out // LANES)] * 2
        + [whole((count, LANES)), whole((total, LANES))]
        + [pair_columns(part.shape[1], at_kv // LANES) for part in kv],
        out_specs=[columns(count, 0)] + [pair_columns(total // 2, 0)] * 2,
        out_shape=[jax.ShapeDtypeStruct((count, width), bf16)]
        + [jax.ShapeDtypeStruct((2, total // 2, width), bf16)] * 2,
        scratch_shapes=[pltpu.VMEM((total, LANES), bf16)] * 2,
        compiler_params=pltpu.CompilerParams(vmem_limit_bytes=40 << 20),
        cost_estimate=pl.CostEstimate(
            flops=20 * count * total * width,
            bytes_accessed=width * (count * 12 + total * 8),
            transcendentals=count * total * width // HALF,
        ),
        name="attend_back",
    )(query, grad, out, logsum, mask_q, mask_k, *kv)


def norm_stats(value):
    mean = jnp.mean(value, axis=-1, keepdims=True)
    centred = value - mean
    spread = jnp.mean(centred * centred, axis=-1, keepdims=True)
    return centred, lax.rsqrt(spread + EPS)


def norm(value, gain):
    centred, scale = norm_stats(value)
    return (centred * scale * gain).astype(bf16)


def norm_back(grad, value, gain):
    centred, scale = norm_stats(value)
    unit = centred * scale
    gain_grad = jnp.sum(grad * unit, axis=0, keepdims=True)
    grad = grad * gain
    extra = scale * (
        grad
        - jnp.mean(grad, axis=-1, keepdims=True)
        - unit * jnp.mean(grad * unit, axis=-1, keepdims=True)
    )
    return extra, gain_grad


Q_SCALE = LOG2E * HALF**-0.5


def front_kernel(x_ref, gain_ref, wq_ref, wk_ref, wv_ref, n_ref, q_ref, *kv_refs):
    normed = norm(x_ref[...].astype(f32), gain_ref[...])
    n_ref[...] = normed
    width = kv_refs[0].shape[2]
    keys = dot(normed, wk_ref[...]).astype(bf16)
    values = dot(normed, wv_ref[...]).astype(bf16)
    for group, kv_ref in enumerate(kv_refs):
        kv_ref[0] = keys[:, group * width : (group + 1) * width]
        kv_ref[1] = values[:, group * width : (group + 1) * width]
    q_ref[...] = (dot(normed, wq_ref[...]) * Q_SCALE).astype(bf16)


def front(view, gain, wq, wk, wv, groups):
    rows, width = view.shape
    part = width // groups
    result = pl.pallas_call(
        front_kernel,
        out_shape=[jax.ShapeDtypeStruct((rows, width), bf16)] * 2
        + [jax.ShapeDtypeStruct((2, rows, part), bf16)] * groups,
        compiler_params=pltpu.CompilerParams(vmem_limit_bytes=40 << 20),
        cost_estimate=pl.CostEstimate(
            flops=6 * rows * width * width,
            bytes_accessed=6 * width * width + 10 * rows * width,
            transcendentals=0,
        ),
        name="front",
    )(view, gain, wq, wk, wv)
    return result[0], result[1], result[2:]


GELU_A = 0.7978845608028654
GELU_B = 0.044715


def gelu_both(value):
    square = value * value
    bent = jnp.tanh(GELU_A * value * (1.0 + GELU_B * square))
    half = 0.5 * (1.0 + bent)
    slope = half + 0.5 * value * (1.0 - bent * bent) * (
        GELU_A * (1.0 + 3.0 * GELU_B * square)
    )
    return value * half, slope


def fill_wide(wide, refs, rows, first):
    at, there = 0, pl.ds(first, rows)
    for ref in refs:
        if len(ref.shape) == 3:
            for pair in range(ref.shape[0]):
                wide[there, at : at + LANES] = ref[pair]
                at += LANES
        else:
            wide[there, at : at + ref.shape[1]] = ref[...]
            at += ref.shape[1]


def rest_kernel(steps, mixes, is_query, *refs):
    x_ref = refs[0]
    mixed_refs = refs[1 : 1 + mixes]
    wo_ref, gain_ref, up_ref, down_ref, next_gain_ref = refs[1 + mixes : 6 + mixes]
    next_refs = refs[6 + mixes : -9]
    merged_ref, hidden_ref, second_ref, active_ref, slope_ref = refs[-9:-4]
    asked_ref, out_ref, total, scratch = refs[-4:]
    step = pl.program_id(0)

    @pl.when(step == 0)
    def _():
        hidden = x_ref[...].astype(f32)
        fill_wide(scratch, mixed_refs, scratch.shape[0], 0)
        hidden = hidden + dot(scratch[...], wo_ref[...])
        hidden_ref[...] = hidden
        second_ref[...] = norm(hidden, gain_ref[...])
        total[...] = hidden

    inner = dot(second_ref[...], up_ref[...])
    active, slope = gelu_both(inner)
    active = active.astype(bf16)
    active_ref[...] = active
    slope_ref[...] = slope.astype(bf16)
    total[...] += dot(active, down_ref[...])

    @pl.when(step == steps - 1)
    def _():
        merged = total[...]
        merged_ref[...] = merged
        asked = norm(merged, next_gain_ref[...])
        asked_ref[...] = asked
        if is_query:
            query = (dot(asked, next_refs[0][...]) * Q_SCALE).astype(bf16)
            if len(out_ref.shape) == 3:
                for pair in range(out_ref.shape[0]):
                    out_ref[pair] = query[:, pair * LANES : (pair + 1) * LANES]
            else:
                out_ref[...] = query
        else:
            out_ref[0] = dot(asked, next_refs[0][...]).astype(bf16)
            out_ref[1] = dot(asked, next_refs[1][...]).astype(bf16)


def rest(view, mixed, wo, gain, up, down, next_gain, next_weights):
    rows, width = view.shape
    steps = up.shape[1] // width
    is_query = len(next_weights) == 1
    flat = whole((rows, width))
    slab = pl.BlockSpec((rows, width), lambda i: (0, i))
    square = whole((width, width))
    shape = lambda kind: jax.ShapeDtypeStruct((rows, width), kind)
    wide = jax.ShapeDtypeStruct((rows, up.shape[1]), bf16)
    last = (rows, width) if is_query else (2, rows, width)
    if len(mixed[0].shape) == 3:
        last = (width // LANES, rows, LANES)
    return pl.pallas_call(
        functools.partial(rest_kernel, steps, len(mixed), is_query),
        grid=(steps,),
        in_specs=[flat]
        + [whole(m.shape) for m in mixed]
        + [square, whole((1, width))]
        + [slab_of(width, width), pl.BlockSpec((width, width), lambda i: (i, 0))]
        + [whole((1, width))]
        + [square] * len(next_weights),
        out_specs=[flat, flat, flat, slab, slab, flat, whole(last)],
        out_shape=[shape(f32), shape(f32), shape(bf16), wide, wide, shape(bf16)]
        + [jax.ShapeDtypeStruct(last, bf16)],
        scratch_shapes=[pltpu.VMEM((rows, width), f32), pltpu.VMEM((rows, width), bf16)],
        compiler_params=pltpu.CompilerParams(vmem_limit_bytes=48 << 20),
        cost_estimate=pl.CostEstimate(
            flops=2 * rows * width * (4 * up.shape[1] // 2 + 2 * width),
            bytes_accessed=width * width * 22 + rows * width * 32,
            transcendentals=rows * up.shape[1],
        ),
        name="rest",
    )(view, *mixed, wo, gain, up, down, next_gain, *next_weights)


def slab_of(rows, width):
    return pl.BlockSpec((rows, width), lambda i: (0, i))


def back_kernel(steps, mixes, sizes, laid, orders, *refs):
    gl_ref, gs_ref, al_ref, as_ref, sl_ref, ss_ref = refs[:6]
    cl_ref, cs_ref, hl_ref, hs_ref = refs[6:10]
    mixed_refs = refs[10 : 10 + mixes]
    mixed_s_ref, wo_ref, gain_ref, up_ref, down_ref = refs[10 + mixes : 15 + mixes]
    flows = len(orders)
    locals_, outs = refs[15 + mixes : 15 + mixes + flows], refs[15 + mixes + flows :]
    (hgl_ref, hgs_ref, ml_ref, ms_ref, dup_ref, ddown_ref, dwo_ref, dgain_ref) = outs[:8]
    sums, outs = outs[8 : 8 + flows], outs[8 + flows :]
    branch, second, total, active, inner_grad, mixed = outs[:6]
    large, small = sizes
    top, bottom = pl.ds(0, large), pl.ds(large, small)
    step = pl.program_id(0)
    if flows:
        here = Here()
        rest_refs = list(outs[6:])
        running = [
            Flow(here, order, local, rest_refs, True, False)
            for order, local in zip(orders, locals_)
        ]

        @pl.when(step == 0)
        def _():
            here.greet(ALL_PARTNERS)
            for flow in running:
                flow.act(0)

    @pl.when(step == 0)
    def _():
        branch[top, :] = gl_ref[...].astype(bf16)
        branch[bottom, :] = gs_ref[...].astype(bf16)
        second[top, :] = cl_ref[...]
        second[bottom, :] = cs_ref[...]
        total[...] = jnp.zeros_like(total)

    grad = dot(branch[...], down_ref[...], NT)
    inner_grad[top, :] = (grad[:large] * sl_ref[...].astype(f32)).astype(bf16)
    inner_grad[bottom, :] = (grad[large:] * ss_ref[...].astype(f32)).astype(bf16)
    active[top, :] = al_ref[...]
    active[bottom, :] = as_ref[...]
    down = dot(active[...], branch[...], TN).astype(bf16)
    upper = dot(second[...], inner_grad[...], TN).astype(bf16)
    if laid:
        rows = dup_ref.shape[1]
        for at in range(8):
            zl, x, zh = at // 4, at // 2 % 2, at % 2
            first = ((zh * 2 + zl) * 2 + x) * rows
            dup_ref[at] = upper[first : first + rows]
        for x, core, y in ((a, b, c) for a in (0, 1) for b in (0, 1) for c in (0, 1)):
            first = (x * 4 + core * 2 + y) * rows
            there = core * 16 + (step % 2) * 8 + y * 4 + x * 2 + step // 2
            ddown_ref[there] = down[first : first + rows]
    else:
        dup_ref[...] = upper
        ddown_ref[...] = down
    total[...] += dot(inner_grad[...], up_ref[...], NT)

    @pl.when(step == steps - 1)
    def _():
        extra, gain_l = norm_back(total[top, :], hl_ref[...], gain_ref[...])
        hidden_grad = gl_ref[...] + extra
        hgl_ref[...] = hidden_grad
        branch[top, :] = hidden_grad.astype(bf16)
        extra, gain_s = norm_back(total[bottom, :], hs_ref[...], gain_ref[...])
        hidden_grad = gs_ref[...] + extra
        hgs_ref[...] = hidden_grad
        branch[bottom, :] = hidden_grad.astype(bf16)
        dgain_ref[...] = gain_l + gain_s
        mixed_grad = dot(branch[...], wo_ref[...], NT).astype(bf16)
        ml_ref[...] = mixed_grad[:large]
        ms_ref[...] = mixed_grad[large:]
        fill_wide(mixed, mixed_refs, large, 0)
        fill_wide(mixed, [mixed_s_ref], small, large)
        value = dot(mixed[...], branch[...], TN).astype(bf16)
        if laid:
            rows, wide = dwo_ref.shape[1:]
            for at, (core, y, tm) in enumerate(spots(BY_Y)):
                first = (tm * 2 + core) * rows
                dwo_ref[at] = value[first : first + rows, y * wide : (y + 1) * wide]
        else:
            dwo_ref[...] = value

    for flow in range(flows):
        for stage, when in enumerate((0, steps - 1)):

            @pl.when(step == when)
            def _(flow=flow, stage=stage):
                running[flow].act(stage + 1)
                if stage == 1:
                    sums[flow][...] = running[flow].result()


def back(
    grad_l, grad_s, saved_l, saved_s, mixed_l, mixed_s, wo, gain, up, down, laid, flows=(), orders=()
):
    (hidden_l, second_l, active_l, slope_l) = saved_l
    (hidden_s, second_s, active_s, slope_s) = saved_s
    large, width = grad_l.shape
    small = grad_s.shape[0]
    rows = large + small
    hidden = up.shape[1]
    part = width
    steps = hidden // part
    fl, fs = whole((large, width)), whole((small, width))
    square = whole((width, width))
    up_slab = slab_of(width, part)
    down_slab = pl.BlockSpec((part, width), lambda i: (i, 0))
    shape = jax.ShapeDtypeStruct
    results = [flow_result(o, f.shape[1:], False) for o, f in zip(orders, flows)]
    scratch = [s for o, f in zip(orders, flows) for s in flow_scratch(o, f.shape[1:], True, False)]
    out_up, out_down, out_square = up_slab, down_slab, square
    up_shape, down_shape, square_shape = up.shape, down.shape, (width, width)
    if laid:
        block = (width // 8, width)
        up_shape = down_shape = (32,) + block
        square_shape = (32, width // 16, width // 2)
        out_up = pl.BlockSpec((8,) + block, lambda i: (i, 0, 0))
        out_down, out_square = whole(down_shape), whole(square_shape)
    return pl.pallas_call(
        functools.partial(back_kernel, steps, len(mixed_l), (large, small), laid, orders),
        grid=(steps,),
        in_specs=[fl, fs]
        + [slab_of(large, part), slab_of(small, part)] * 2
        + [fl, fs, fl, fs]
        + [whole(m.shape) for m in mixed_l]
        + [whole(mixed_s.shape), square, whole((1, width)), up_slab, down_slab]
        + [pl.BlockSpec(memory_space=pl.ANY)] * len(flows),
        out_specs=[fl, fs, fl, fs, out_up, out_down, out_square, whole((1, width))]
        + [whole(result.shape) for result in results],
        out_shape=[
            shape((large, width), f32),
            shape((small, width), f32),
            shape((large, width), bf16),
            shape((small, width), bf16),
            shape(up_shape, bf16),
            shape(down_shape, bf16),
            shape(square_shape, bf16),
            shape((1, width), f32),
        ]
        + results,
        scratch_shapes=[
            pltpu.VMEM((rows, width), bf16),
            pltpu.VMEM((rows, width), bf16),
            pltpu.VMEM((rows, width), f32),
            pltpu.VMEM((rows, part), bf16),
            pltpu.VMEM((rows, part), bf16),
            pltpu.VMEM((rows, width), bf16),
        ]
        + scratch,
        compiler_params=pltpu.CompilerParams(
            vmem_limit_bytes=60 << 20,
            has_side_effects=bool(flows),
            collective_id=0 if flows else None,
        ),
        cost_estimate=pl.CostEstimate(
            flops=2 * rows * width * (4 * hidden + 2 * width),
            bytes_accessed=width * width * 36 + rows * width * 40,
            transcendentals=0,
        ),
        name="back",
    )(
        grad_l, grad_s, active_l, active_s, slope_l, slope_s, second_l, second_s, hidden_l, hidden_s,
        *mixed_l, mixed_s, wo, gain, up, down, *flows,
    )


MESH = pl.DeviceIdType.MESH
BY_Y = ("core", "y", "zl", "x", "zh")
BY_ZL = ("core", "zl", "y", "x", "zh")
BY_X = ("core", "x", "zl", "y", "zh")
BY_YX = ("core", "y", "x", "zl", "zh")


def spots(order):
    out = []
    for at in range(32):
        bit = {name: (at >> (4 - i)) & 1 for i, name in enumerate(order)}
        out.append((bit["core"], bit["y"], (bit["zh"] * 2 + bit["zl"]) * 2 + bit["x"]))
    return out


class Here:
    def __init__(self):
        tm, seq = lax.axis_index("tm"), lax.axis_index("seq")
        self.tm, self.seq = tm, seq
        self.bit = {
            "zh": tm // 4,
            "zl": (tm // 2) % 2,
            "x": tm % 2,
            "y": seq // 2,
            "core": seq % 2,
        }

    def partner(self, *names):
        tm, seq = self.tm, self.seq
        for name in names:
            one = 1 - 2 * self.bit[name]
            if name in ("y", "core"):
                seq = seq + one * (2 if name == "y" else 1)
            else:
                tm = tm + one * {"zh": 4, "zl": 2, "x": 1}[name]
        return (tm, seq)

    def greet(self, partners):
        barrier = pltpu.get_barrier_semaphore()
        for names in partners:
            pl.semaphore_signal(
                barrier, inc=1, device_id=self.partner(*names), device_id_type=MESH
            )
        pl.semaphore_wait(barrier, len(partners))


    def greet_line(self, *more):
        barrier = pltpu.get_barrier_semaphore()
        z, core = self.tm // 2, self.bit["core"]
        places = [
            (
                lax.rem(z + dz, 4) * 2 + self.bit["x"],
                self.bit["y"] * 2 + lax.rem(core + dc, 2),
            )
            for dz in range(4)
            for dc in range(2)
            if dz or dc
        ] + [self.partner(name) for name in more]
        for place in places:
            pl.semaphore_signal(barrier, inc=1, device_id=place, device_id_type=MESH)
        pl.semaphore_wait(barrier, len(places))


ALL_PARTNERS = (("core",), ("y",), ("zl",), ("x",), ("zh",))


class Restore:
    def __init__(self, here, held, got, sems):
        self.held, self.got, self.sems = held, got, sems
        self.rows = got.shape[1]
        z, core = here.tm // 2, here.bit["core"]
        self.odd = lax.rem(z, 2)
        self.stay = core == z // 2
        turns = (self.odd, 1 - self.odd)
        self.places = [
            ((2 * core + turn) * 2 + here.bit["x"], here.bit["y"] * 2 + z // 2) for turn in turns
        ]

    def far(self, turn, arriving=False):
        at = 1 - self.odd if arriving and turn else self.odd
        return pltpu.make_async_remote_copy(
            src_ref=self.held.at[pl.ds(turn * self.rows, self.rows)],
            dst_ref=self.got.at[at],
            send_sem=self.sems.at[0, turn],
            recv_sem=self.sems.at[1, turn],
            device_id=self.places[turn],
            device_id_type=MESH,
        )

    def near(self):
        return pltpu.make_async_copy(
            self.held.at[pl.ds(0, self.rows)], self.got.at[self.odd], self.sems.at[1, 0]
        )

    def start(self):
        self.far(1).start()

        @pl.when(self.stay)
        def _():
            self.near().start()

        @pl.when(jnp.logical_not(self.stay))
        def _():
            self.far(0).start()

    def finish(self):
        self.far(1).wait_send()
        self.far(1, True).wait_recv()

        @pl.when(self.stay)
        def _():
            self.near().wait()

        @pl.when(jnp.logical_not(self.stay))
        def _():
            self.far(0).wait_send()
            self.far(0).wait_recv()


def restore_scratch(rows, width):
    return [
        pltpu.VMEM((2 * rows, width), bf16),
        pltpu.VMEM((2, rows, width), bf16),
        pltpu.SemaphoreType.DMA((2, 2)),
    ]


class Flow:
    def __init__(self, here, order, local, refs, keep, ends):
        self.here, self.order, self.local = here, order, local
        self.keep = refs.pop(0) if keep else None
        self.got = [refs.pop(0) for _ in order]
        self.out = refs.pop(0) if ends else None
        self.sem = refs.pop(0)
        self.last = len(order)
        self.ends = ends

    def copy(self, step):
        name = self.order[step]
        half = 1 << (self.last - 1 - step)
        source = self.local if step == 0 else self.got[step - 1]
        at = (1 - self.here.bit[name]) * half
        return pltpu.make_async_remote_copy(
            src_ref=source.at[pl.ds(at, half)],
            dst_ref=self.got[step],
            send_sem=self.sem.at[0, step],
            recv_sem=self.sem.at[1, step],
            device_id=self.here.partner(name),
            device_id_type=MESH,
        )

    def keep_copy(self):
        half = 1 << (self.last - 1)
        at = self.here.bit[self.order[0]] * half
        return pltpu.make_async_copy(
            self.local.at[pl.ds(at, half)], self.keep, self.sem.at[0, self.last + 2]
        )

    def start(self, step):
        self.copy(step).start()
        if step == 0 and self.keep is not None:
            self.keep_copy().start()

    def finish(self, step):
        half = 1 << (self.last - 1 - step)
        self.copy(step).wait()
        got = self.got[step]
        at = self.here.bit[self.order[step]] * half
        if step == 0 and self.keep is not None:
            self.keep_copy().wait()
            source, at = self.keep, 0
        else:
            source = self.local if step == 0 else self.got[step - 1]

        def body(i, carry):
            got[i] = got[i] + source[at + i]
            return carry

        if half == 1:
            got[0] = got[0] + source[at]
        else:
            lax.fori_loop(0, half, body, 0)

    def spread_copy(self, which):
        here = self.here
        own = here.bit["core"] * 2
        if which == 0:
            source, there = self.got[-1].at[0], self.out.at[own + here.bit["y"]]
        else:
            source = there = self.out.at[pl.ds(own, 2)]
        return pltpu.make_async_remote_copy(
            src_ref=source,
            dst_ref=there,
            send_sem=self.sem.at[0, self.last + which],
            recv_sem=self.sem.at[1, self.last + which],
            device_id=here.partner(("y", "core")[which]),
            device_id_type=MESH,
        )

    def act(self, stage):
        if stage == 0:
            self.start(0)
        elif stage < self.last:
            self.finish(stage - 1)
            self.start(stage)
        elif stage == self.last:
            self.finish(stage - 1)
            if self.ends:
                self.spread_copy(0).start()
                self.out[self.here.bit["core"] * 2 + self.here.bit["y"]] = self.got[-1][0]
        elif stage == self.last + 1 and self.ends:
            self.spread_copy(0).wait()
            self.spread_copy(1).start()
        elif stage == self.last + 2 and self.ends:
            self.spread_copy(1).wait()

    def result(self):
        return self.out[...] if self.ends else self.got[-1][...]


def flow_scratch(order, block, keep, ends):
    steps = len(order)
    blocks = [pltpu.VMEM((1 << (steps - 1),) + block, bf16)] if keep else []
    for step in range(steps):
        blocks.append(pltpu.VMEM((1 << (steps - 1 - step),) + block, bf16))
    if ends:
        blocks.append(pltpu.VMEM((4,) + block, bf16))
    return blocks + [pltpu.SemaphoreType.DMA((2, steps + 3))]


def flow_result(order, block, ends):
    left = 4 if ends else 1
    return jax.ShapeDtypeStruct((left,) + block, bf16)


def pair_back(query, grad, out, logsum, mask, keys_at, values_at, mk_ref, block, exchange, pair):
    count = query.shape[0]
    total = keys_at.shape[0]
    lane = lax.broadcasted_iota(jnp.int32, (count, LANES), 1)
    low = lane < HALF
    spot = lane % HALF
    zero = jnp.zeros_like(query)
    product = grad.astype(f32) * out.astype(f32)
    delta0 = jnp.sum(jnp.where(low, product, 0.0), axis=1, keepdims=True)
    delta1 = jnp.sum(jnp.where(low, 0.0, product), axis=1, keepdims=True)
    delta = jnp.where(low, delta1, delta0)

    def beside(base, value):
        a, b, c = three(-value)
        return jnp.where(spot == 4, a, jnp.where(spot == 5, b, jnp.where(spot == 6, c, base)))

    query_side = beside(mask, logsum)
    grad_side = beside(zero, delta)
    query_a = (jnp.where(low, query, query_side), jnp.where(low, query_side, query))
    grad_a = (jnp.where(low, grad, grad_side), jnp.where(low, grad_side, grad))
    query_m = (jnp.where(low, query, zero), jnp.where(low, zero, query))
    grad_m = (jnp.where(low, grad, zero), jnp.where(low, zero, grad))
    lane_k = lax.broadcasted_iota(jnp.int32, (block, LANES), 1)
    low_k = lane_k < HALF
    spot_k = lane_k % HALF
    one = jnp.where((spot_k >= 4) & (spot_k < 7), 1.0, 0.0).astype(bf16)
    dq = jnp.zeros((count, LANES), f32)
    for number in exchange.turns(total // block):
        here = pl.ds(number * block, block)
        keys, values = keys_at[here, :], values_at[here, :]
        side = mk_ref[here, :] + one
        nought = jnp.zeros_like(keys)
        dk = jnp.zeros((block, LANES), f32)
        dv = jnp.zeros((block, LANES), f32)
        for head in (0, 1):
            pick = lambda a, b: jnp.where(low_k, a, b) if head == 0 else jnp.where(low_k, b, a)
            prob = jnp.exp2(dot(query_a[head], pick(keys, side), NT))
            change = dot(grad_a[head], pick(values, one), NT)
            score_grad = (prob * change).astype(bf16)
            dv += dot(prob.astype(bf16), grad_m[head], TN)
            dk += dot(score_grad, query_m[head], TN)
            dq += dot(score_grad, pick(keys, nought))
        exchange.put(pair, number, block, (dk * LN2).astype(bf16), dv.astype(bf16))
    return (dq * HALF**-0.5).astype(bf16)


class Exchange:
    def __init__(self, here, rows, refs):
        self.here, self.rows = here, rows
        self.sums, self.send, self.got_core, self.across, self.got_x = refs[:5]
        self.sems = refs[5]

    def turns(self, blocks):
        return (3, 1, 0, 2) if blocks == 4 else tuple(reversed(range(blocks)))

    def copy_core(self, pair, far):
        rows = pl.ds(far * self.rows, self.rows)
        return pltpu.make_async_remote_copy(
            src_ref=self.send.at[pair % 2, :, rows, :],
            dst_ref=self.got_core.at[pair, :, rows, :],
            send_sem=self.sems.at[2 * far, pair],
            recv_sem=self.sems.at[2 * far + 1, pair],
            device_id=self.here.partner("core"),
            device_id_type=MESH,
        )

    def copy_x(self, pair):
        return pltpu.make_async_remote_copy(
            src_ref=self.across.at[pair],
            dst_ref=self.got_x.at[pair],
            send_sem=self.sems.at[4, pair],
            recv_sem=self.sems.at[5, pair],
            device_id=self.here.partner("x"),
            device_id_type=MESH,
        )

    def end(self):
        pairs = self.got_x.shape[0]
        for pair in range(pairs):
            if pair >= pairs - 2:
                self.free(pair)
            self.copy_x(pair).wait_send()

    def free(self, pair):
        for far in (0, 1):
            self.copy_core(pair, far).wait_send()

    def put(self, pair, number, block, dk, dv):
        half = 2 * self.rows
        there = pl.ds(number * block % half, block)
        ref, slot = (self.sums, pair) if number * block < half else (self.send, pair % 2)
        ref[slot, 0, there, :] = dk
        ref[slot, 1, there, :] = dv
        if 2 * half == 4 * block:
            if number == 3:
                self.copy_core(pair, 1).start()
            elif number == 2:
                self.copy_core(pair, 0).start()
            elif number == 0:
                self.pass_on(pair)
        elif number == 1:
            for far in (1, 0):
                self.copy_core(pair, far).start()
        else:
            self.pass_on(pair)

    def pass_on(self, pair):
        rows = self.rows
        self.copy_core(pair, 1).wait_recv()
        far = pl.ds(rows, rows)
        for i in (0, 1):
            self.across[pair, i] = self.sums[pair, i, far, :] + self.got_core[pair, i, far, :]
        self.copy_x(pair).start()

    def take(self, pair, out_ref):
        near = pl.ds(0, self.rows)
        self.copy_core(pair, 0).wait_recv()
        self.copy_x(pair).wait_recv()
        for i in (0, 1):
            out_ref[pair, i] = (
                self.sums[pair, i, near, :].astype(f32)
                + self.got_core[pair, i, near, :].astype(f32)
                + self.got_x[pair, i].astype(f32)
            ).astype(bf16)


def exchange_scratch(pairs, rows):
    return [
        pltpu.VMEM((pairs, 2, 2 * rows, LANES), bf16),
        pltpu.VMEM((2, 2, 2 * rows, LANES), bf16),
        pltpu.VMEM((pairs, 2, 2 * rows, LANES), bf16),
        pltpu.VMEM((pairs, 2, rows, LANES), bf16),
        pltpu.VMEM((pairs, 2, rows, LANES), bf16),
        pltpu.SemaphoreType.DMA((6, pairs)),
    ]


def fill_keys(keys_at, values_at, kv_ref):
    rows = kv_ref.shape[3]
    for part in range(kv_ref.shape[0]):
        there = pl.ds(part * rows, rows)
        keys_at[there, :] = kv_ref[part, 0, 0]
        values_at[there, :] = kv_ref[part, 0, 1]


def selves_kernel(pairs, plan, blocks, *refs):
    orders, ends, stages = plan
    large_refs, kv_large, refs = refs[:6], refs[6], refs[7:]
    small_refs, kv_small, refs = refs[:6], refs[6], refs[7:]
    flows = len(orders)
    locals_, refs = refs[:flows], refs[flows:]
    dq_l, dkv_l, dq_s, dkv_s = refs[:4]
    sums, refs = refs[4 : 4 + flows], refs[4 + flows :]
    keys_l, values_l, keys_s, values_s = refs[:4]
    ex_l, ex_s, refs = refs[4:10], refs[10:16], refs[16:]
    here = Here()
    rows_l, rows_s = keys_l.shape[0] // 4, keys_s.shape[0] // 4
    large, small = Exchange(here, rows_l, ex_l), Exchange(here, rows_s, ex_s)
    refs = list(refs)
    running = [
        Flow(here, orders[flow], locals_[flow], refs, True, ends[flow]) for flow in range(flows)
    ]
    step = pl.program_id(0)

    @pl.when(step == 0)
    def _():
        here.greet(ALL_PARTNERS)
        for flow in running:
            flow.act(0)

    def attention(exchange, pair, refs, kv_ref, keys_at, values_at, block, dq_ref):
        q_ref, do_ref, o_ref, l_ref, mq_ref, mk_ref = refs
        fill_keys(keys_at, values_at, kv_ref)

        @pl.when(pair >= 2)
        def _():
            exchange.free(pair - 2)

        dq_ref[...] = pair_back(
            q_ref[0], do_ref[...], o_ref[0], l_ref[0], mq_ref[...], keys_at, values_at, mk_ref,
            block, exchange, pair,
        )

    half = pairs // 2
    late = step >= half + pairs

    @pl.when((step >= half) & (step < half + pairs))
    def _():
        pair = step - half
        attention(large, pair, large_refs, kv_large, keys_l, values_l, blocks[0], dq_l)

    @pl.when((step < half) | late)
    def _():
        pair = jnp.where(late, step - pairs, step)
        attention(small, pair, small_refs, kv_small, keys_s, values_s, blocks[1], dq_s)

    takes = [(half + 1 + i, small, i, dkv_s) for i in range(half)]
    takes += [(half + 3 + i, large, i, dkv_l) for i in range(pairs - 1)]
    for when, exchange, pair, out_ref in takes:

        @pl.when(step == when)
        def _(exchange=exchange, pair=pair, out_ref=out_ref):
            exchange.take(pair, out_ref)

    for at in range(2 * pairs):
        todo = []
        for flow in range(flows):
            for stage, when in enumerate(stages[flow]):
                if when == at:
                    todo.append((running[flow], stage + 1))
        if todo:

            @pl.when(step == at)
            def _(todo=todo):
                for flow, stage in todo:
                    flow.act(stage)

    @pl.when(step == 2 * pairs - 1)
    def _():
        large.take(pairs - 1, dkv_l)
        for pair in range(half, pairs):
            small.take(pair, dkv_s)
        small.end()
        large.end()
        for flow, sum_ref in zip(running, sums):
            sum_ref[...] = flow.result()


def selves_back(large, large_kv, small, small_kv, flows, orders, ends, stages):
    count, width = large[1].shape
    few = small[1].shape[0]
    pairs = width // LANES
    total, less = large[5].shape[0], small[5].shape[0]
    shapes = [flow.shape[1:] for flow in flows]
    results = [flow_result(*flow) for flow in zip(orders, shapes, ends)]
    blocks = (largest_block(total // 2, 512), largest_block(less // 2, 512))
    half = pairs // 2
    first = lambda i: jnp.clip(i - half, 0, pairs - 1)
    last = lambda i: jnp.where(i < half, i, jnp.maximum(i - pairs, half))
    in_specs = []
    for rows, keys, at in ((count, total, first), (few, less, last)):
        major = pl.BlockSpec((1, rows, LANES), lambda i, at=at: (at(i), 0, 0))
        minor = pl.BlockSpec((rows, LANES), lambda i, at=at: (0, at(i)))
        in_specs += [major, minor, major, major, whole((rows, LANES)), whole((keys, LANES))]
        in_specs.append(
            pl.BlockSpec((4, 1, 2, rows, LANES), lambda i, at=at: (0, at(i), 0, 0, 0))
        )
    in_specs += [pl.BlockSpec(memory_space=pl.ANY)] * len(flows)
    shape = jax.ShapeDtypeStruct
    out_shape = [
        shape((count, width), bf16),
        shape((pairs, 2, count, LANES), bf16),
        shape((few, width), bf16),
        shape((pairs, 2, few, LANES), bf16),
    ] + results
    out_specs = [
        pl.BlockSpec((count, LANES), lambda i: (0, first(i))),
        whole((pairs, 2, count, LANES)),
        pl.BlockSpec((few, LANES), lambda i: (0, last(i))),
        whole((pairs, 2, few, LANES)),
    ] + [whole(result.shape) for result in results]
    scratch = [pltpu.VMEM((total, LANES), bf16)] * 2 + [pltpu.VMEM((less, LANES), bf16)] * 2
    scratch += exchange_scratch(pairs, count) + exchange_scratch(pairs, few)
    for flow in range(len(flows)):
        scratch += flow_scratch(orders[flow], shapes[flow], True, ends[flow])
    result = pl.pallas_call(
        functools.partial(selves_kernel, pairs, (orders, ends, stages), blocks),
        grid=(2 * pairs,),
        in_specs=in_specs,
        out_specs=out_specs,
        out_shape=out_shape,
        scratch_shapes=scratch,
        compiler_params=pltpu.CompilerParams(
            vmem_limit_bytes=60 << 20, collective_id=1, has_side_effects=True
        ),
        cost_estimate=pl.CostEstimate(
            flops=20 * width * (count * total + few * less),
            bytes_accessed=64 * count * width,
            transcendentals=count * total * width // HALF,
        ),
        name="selves_back",
    )(*large, large_kv, *small, small_kv, *flows)
    return result[:4], result[4:]


LAST_ORDERS = (BY_YX, BY_X, BY_YX)
GAIN_ORDER = ("core", "y", "x", "zl", "zh")
LATE_ORDER = ("x", "zh")
LATE_STAGES = {1: 1, 4: 2, 5: 3, 6: 4}


def last_kernel(pairs, sizes, late, *refs):
    refs = list(refs)
    take = lambda count: [refs.pop(0) for _ in range(count)]
    given, late_refs = take(13), take(late)
    gain, second_gain, query_gain, context_gain = take(4)
    gl_ref, gs_ref = take(2)
    sum_refs = take(3 + late)
    (gain_ref,) = take(1)
    held = take(13)
    dql, dkvl, dqs, dkvs, wq, wk, wv, xl, xs, hl, hs, nl, ns = held
    load_sems, normed, *grads = take(5)
    large_back, small_back = take(3), take(3)
    here = Here()
    flows = []
    for order in LAST_ORDERS:
        flows.append(Flow(here, order, refs.pop(0), refs, False, True))
    late_flows = [Flow(here, LATE_ORDER, ref, refs, True, True) for ref in late_refs]
    state, got, gain_sems = refs
    large, small = sizes
    top, bottom = pl.ds(0, large), pl.ds(large, small)
    loads = [
        pltpu.make_async_copy(source, there, load_sems.at[i])
        for i, (source, there) in enumerate(zip(given, held))
    ]
    for load in loads:
        load.start()
    here.greet_line("x", "y")
    for flow in late_flows:
        flow.act(0)
    homes = [Restore(here, *large_back), Restore(here, *small_back)]

    def gain_copy(step):
        return pltpu.make_async_remote_copy(
            src_ref=state.at[step],
            dst_ref=got.at[step],
            send_sem=gain_sems.at[0, step],
            recv_sem=gain_sems.at[1, step],
            device_id=here.partner(GAIN_ORDER[step]),
            device_id_type=MESH,
        )

    for load in loads[:4]:
        load.wait()
    total = None
    for which, weight in enumerate((wq, wk, wv)):
        if which == 0:
            grads[0][top, :] = dql[...]
            grads[0][bottom, :] = dqs[...]
        else:
            for pair in range(pairs):
                lanes = pl.ds(pair * LANES, LANES)
                grads[which][top, lanes] = dkvl[pair, which - 1]
                grads[which][bottom, lanes] = dkvs[pair, which - 1]
        loads[4 + which].wait()
        part = dot(grads[which][...], weight[...], NT)
        total = part if total is None else total + part
    for load in loads[7:]:
        load.wait()
    extra, gain_l = norm_back(total[:large], xl[...].astype(f32), gain[...])
    large_back[0][...] = (hl[...] + extra).astype(bf16)
    homes[0].start()
    extra, gain_s = norm_back(total[large:], xs[...].astype(f32), gain[...])
    small_back[0][...] = (hs[...] + extra).astype(bf16)
    homes[1].start()
    state[0] = jnp.zeros(state.shape[1:], f32)
    for row, value in enumerate(
        (gain_l + gain_s, second_gain[...], query_gain[...], context_gain[...])
    ):
        state[0, row : row + 1, :] = value
    gain_copy(0).start()
    normed[top, :] = nl[...]
    normed[bottom, :] = ns[...]
    for which, flow in enumerate(flows):
        value = dot(normed[...], grads[which][...], TN).astype(bf16)
        rows, wide = flow.local.shape[1:]
        for at, (core, y, tm) in enumerate(spots(flow.order)):
            first = tm * 2 * rows + core * rows
            flow.local[at] = value[first : first + rows, y * wide : (y + 1) * wide]
        flow.act(0)
    for stage in range(1, 8):
        for flow in flows:
            flow.act(stage)
        if stage in LATE_STAGES:
            for flow in late_flows:
                flow.act(LATE_STAGES[stage])
        if stage <= 5:
            gain_copy(stage - 1).wait()
            total = state[stage - 1] + got[stage - 1]
            if stage < 5:
                state[stage] = total
                gain_copy(stage).start()
            else:
                gain_ref[...] = total
    for flow, sum_ref in zip(flows + late_flows, sum_refs):
        sum_ref[...] = flow.result()
    homes[0].finish()
    gl_ref[...] = large_back[1][...].astype(f32)
    homes[1].finish()
    gs_ref[...] = small_back[1][...].astype(f32)


def last_sums(given, late, gains):
    count, width = given[0].shape
    few = given[2].shape[0]
    block = (width // 16, width // 2)
    shape = jax.ShapeDtypeStruct
    tokens = count + few
    scratch = [pltpu.VMEM(value.shape, value.dtype) for value in given]
    scratch += [pltpu.SemaphoreType.DMA((len(given),))]
    scratch += [pltpu.VMEM((tokens, width), bf16)] * 4
    scratch += restore_scratch(count // 2, width) + restore_scratch(few // 2, width)
    for order in LAST_ORDERS:
        scratch.append(pltpu.VMEM((32,) + block, bf16))
        scratch += flow_scratch(order, block, False, True)
    for local in late:
        scratch += flow_scratch(LATE_ORDER, local.shape[1:], True, True)
    scratch += [
        pltpu.VMEM((5, 8, width), f32),
        pltpu.VMEM((5, 8, width), f32),
        pltpu.SemaphoreType.DMA((2, 5)),
    ]
    anywhere = pl.BlockSpec(memory_space=pl.ANY)
    vmem = pl.BlockSpec(memory_space=pltpu.VMEM)
    result = pl.pallas_call(
        functools.partial(last_kernel, width // LANES, (count, few), len(late)),
        in_specs=[anywhere] * (len(given) + len(late)) + [vmem] * 4,
        out_shape=[
            shape((2, count // 2, width), f32),
            shape((2, few // 2, width), f32),
        ]
        + [shape((4,) + block, bf16)] * 3
        + [shape((4,) + local.shape[1:], bf16) for local in late]
        + [shape((8, width), f32)],
        scratch_shapes=scratch,
        compiler_params=pltpu.CompilerParams(
            vmem_limit_bytes=60 << 20, collective_id=2, has_side_effects=True
        ),
        cost_estimate=pl.CostEstimate(
            flops=40 * tokens * width * width,
            bytes_accessed=40 * tokens * width,
            transcendentals=0,
        ),
        name="last_sums",
    )(*given, *late, *gains)
    return result[:2], result[2:5], result[5:-1], result[-1]


def cross_kernel(pairs, block, *refs):
    (q_ref, do_ref, o_ref, l_ref, mq_ref, mk_ref), refs = refs[:6], refs[6:]
    kv_ref, given, gains, refs = refs[0], refs[1:11], refs[11:13], refs[13:]
    view_ref, gl_ref, gs_ref, a_ref, b_ref, gain_l_ref, gain_s_ref = refs[:7]
    keys_at, values_at, exchange_refs, refs = refs[7], refs[8], refs[9:15], refs[15:]
    dkv, dq, dk, dv = refs[:4]
    held, sems, home_refs = refs[4:14], refs[14], refs[15:18]
    united, wo, merged_l, asked, context, grad_out, merged_s, wq, wk, wv = held
    here = Here()
    exchange = Exchange(here, keys_at.shape[0] // 4, exchange_refs)
    step = pl.program_id(0)
    loads = [
        pltpu.make_async_copy(source, there, sems.at[i])
        for i, (source, there) in enumerate(zip(given, held))
    ]

    @pl.when(step == 0)
    def _():
        for load in loads:
            load.start()
        here.greet_line("x")

    home = Restore(here, *home_refs)

    @pl.when(step == 1)
    def _():
        for load in loads[:3]:
            load.wait()
        wide = jnp.concatenate([united[i] for i in range(pairs)], axis=1)
        home_refs[0][...] = (merged_l[...] + dot(wide, wo[...])).astype(bf16)
        home.start()

    fill_keys(keys_at, values_at, kv_ref)

    @pl.when(step >= 2)
    def _():
        exchange.free(step - 2)

    dq[step] = pair_back(
        q_ref[0], do_ref[...], o_ref[0], l_ref[0], mq_ref[...], keys_at, values_at, mk_ref,
        block, exchange, step,
    )

    @pl.when(step >= 3)
    def _():
        exchange.take(step - 3, dkv)

    def lay(out_ref, which, value, order):
        left = 32 // out_ref.shape[0]
        rows = out_ref.shape[1] // left
        for at, (core, y, tm) in enumerate(spots(order)):
            if core == which:
                first, there = (tm * 2 + y) * rows, at % left * rows
                out_ref[at // left, there : there + rows, :] = value[first : first + rows]

    @pl.when(step == pairs - 1)
    def _():
        for load in loads[3:]:
            load.wait()
        grads = jnp.concatenate([united[i] for i in range(pairs)], axis=1)
        lay(a_ref, 0, dot(grads, grad_out[...], TN).astype(bf16), BY_Y)
        grads = jnp.concatenate([dq[i] for i in range(pairs)], axis=1)
        lay(a_ref, 1, dot(asked[...], grads, TN).astype(bf16), BY_Y)
        extra, gain_l_ref[...] = norm_back(dot(grads, wq[...], NT), merged_l[...], gains[0][...])
        gl_ref[...] = grad_out[...].astype(f32) + extra
        for pair in range(pairs - 3, pairs):
            exchange.take(pair, dkv)
        for pair in range(pairs):
            lanes = pl.ds(pair * LANES, LANES)
            dk[:, lanes] = dkv[pair, 0]
            dv[:, lanes] = dkv[pair, 1]
        lay(b_ref, 0, dot(context[...], dk[...], TN).astype(bf16), BY_ZL)
        lay(b_ref, 1, dot(context[...], dv[...], TN).astype(bf16), BY_ZL)
        grad = dot(dk[...], wk[...], NT) + dot(dv[...], wv[...], NT)
        gs_ref[...], gain_s_ref[...] = norm_back(grad, merged_s[...], gains[1][...])
        exchange.end()
        home.finish()
        view_ref[...] = home_refs[1][...]


def cross_back(attention, kv, given, gains):
    count, width = attention[1].shape
    few = kv.shape[3]
    major = pl.BlockSpec((1, count, LANES), lambda i: (i, 0, 0))
    pairs = width // LANES
    total = attention[5].shape[0]
    block = largest_block(total // 2, 512)
    shape = jax.ShapeDtypeStruct
    laid = (4, 8 * width // 16, width)
    return pl.pallas_call(
        functools.partial(cross_kernel, pairs, block),
        grid=(pairs,),
        in_specs=[major, columns(count, 0), major, major]
        + [whole((count, LANES)), whole((total, LANES))]
        + [pl.BlockSpec((4, 1, 2, few, LANES), lambda i: (0, i, 0, 0, 0))]
        + [pl.BlockSpec(memory_space=pl.ANY)] * len(given)
        + [whole((1, width))] * 2,
        out_specs=[
            whole((2, count // 2, width)), whole((count, width)), whole((few, width)), whole(laid), whole(laid),
            whole((1, width)), whole((1, width)),
        ],
        out_shape=[
            shape((2, count // 2, width), bf16),
            shape((count, width), f32), shape((few, width), f32), shape(laid, bf16), shape(laid, bf16),
            shape((1, width), f32), shape((1, width), f32),
        ],
        scratch_shapes=[pltpu.VMEM((total, LANES), bf16)] * 2
        + exchange_scratch(pairs, few)
        + [pltpu.VMEM((pairs, 2, few, LANES), bf16), pltpu.VMEM((pairs, count, LANES), bf16)]
        + [pltpu.VMEM((few, width), bf16)] * 2
        + [pltpu.VMEM(value.shape, value.dtype) for value in given]
        + [pltpu.SemaphoreType.DMA((len(given),))]
        + restore_scratch(count // 2, width),
        compiler_params=pltpu.CompilerParams(
            vmem_limit_bytes=60 << 20, collective_id=3, has_side_effects=True
        ),
        cost_estimate=pl.CostEstimate(
            flops=20 * width * count * total,
            bytes_accessed=64 * count * width,
            transcendentals=count * total * width // HALF,
        ),
        name="cross_back",
    )(*attention, kv, *given, *gains)


def attend_pair(pair, q_ref, kv, mq_ref, mk_ref, spaces, o_ref, l_ref):
    parts, rows = kv.shape[0], kv.shape[3]
    total = parts * rows
    ka0, ka1, va0, va1 = (space.at[pl.ds(0, total), :] for space in spaces)
    low = lax.broadcasted_iota(jnp.int32, (rows, LANES), 1) < HALF
    for part in range(parts):
        here = pl.ds(part * rows, rows)
        keys, values, mask = kv[part, pair, 0], kv[part, pair, 1], mk_ref[here, :]
        one = jnp.ones_like(values)
        ka0[here, :] = jnp.where(low, keys, mask)
        ka1[here, :] = jnp.where(low, mask, keys)
        va0[here, :] = jnp.where(low, values, one)
        va1[here, :] = jnp.where(low, one, values)
    count = q_ref.shape[1]
    block = largest_block(count, 256)
    low = lax.broadcasted_iota(jnp.int32, (block, LANES), 1) < HALF
    for number in range(count // block):
        here = pl.ds(number * block, block)
        query, mask = q_ref[pair, here, :], mq_ref[here, :]
        tops, sums = [], []
        for head, keys, values in ((0, ka0, va0), (1, ka1, va1)):
            mine = jnp.where(low, query, mask) if head == 0 else jnp.where(low, mask, query)
            score = dot(mine, keys[...], NT)
            top = jnp.max(score, axis=1, keepdims=True)
            weight = jnp.exp2(score - top).astype(bf16)
            sums.append(dot(weight, values[...]))
            tops.append(jnp.broadcast_to(top, (block, LANES)))
        total = jnp.where(low, sums[1], sums[0])
        top = jnp.where(low, tops[1], tops[0])
        out = jnp.where(low, sums[0], sums[1])
        o_ref[pair, here, :] = (out / pltpu.roll(total, HALF, 1)).astype(bf16)
        l_ref[pair, here, :] = top + jnp.log2(total)


class Gather:
    def __init__(self, here, kv, sems):
        self.here, self.kv, self.sems = here, kv, sems

    def copy(self, kind, at, size, sem):
        source, there = ((0, 1), (0, 2), (1, 3))[kind]
        pairs = pl.ds(at, size)
        return pltpu.make_async_remote_copy(
            src_ref=self.kv.at[source, pairs],
            dst_ref=self.kv.at[there, pairs],
            send_sem=self.sems.at[0, 3 * sem + kind],
            recv_sem=self.sems.at[1, 3 * sem + kind],
            device_id=self.here.partner(("x", "core", "core")[kind]),
            device_id_type=MESH,
        )


def begin_kernel(pairs, *refs):
    refs = list(refs)
    take = lambda count: [refs.pop(0) for _ in range(count)]
    large_ref, small_ref, cot_ref, clip_ref = take(4)
    weight_refs = take(8)
    first_gain, second_gain, context_gain = take(3)
    xl_out, xs_out, cot_out, kvl_out, kvs_out, ckv_out = take(6)
    nl_ref, ns_ref, ql_ref, qs_ref, ol_ref, ll_ref, os_ref, ls_ref = take(8)
    merged_ref, hidden_ref, second_ref, active_ref, slope_ref, context_ref = take(6)
    mql_ref, mkl_ref, mqs_ref, mks_ref = take(4)
    xl, xs, cot, clip, kvl, kvs, ckv = take(7)
    wq, wk, wv, wo, up, down, wck, wcv = weights = take(8)
    spaces = take(4)
    wide, total = take(2)
    move_sems, gather_l, gather_s, gather_c, gather_clip, load_sems, out_sems = take(7)
    here = Here()
    z, core = here.tm // 2, here.bit["core"]
    stay = core == z // 2

    here.greet_line("x")

    odd = lax.rem(z, 2)
    from_seq = (odd, 1 - odd)

    def far(which, turn, source, there):
        rows = source.shape[1]
        place = (
            (2 * core + from_seq[turn]) * 2 + here.bit["x"],
            here.bit["y"] * 2 + z // 2,
        )
        return pltpu.make_async_remote_copy(
            src_ref=source.at[from_seq[turn]],
            dst_ref=there.at[pl.ds(turn * rows, rows)],
            send_sem=move_sems.at[0, 2 * which + turn],
            recv_sem=move_sems.at[1, 2 * which + turn],
            device_id=place,
            device_id_type=MESH,
        )

    def near(which, source, there):
        return pltpu.make_async_copy(
            source.at[from_seq[0]],
            there.at[pl.ds(0, source.shape[1])],
            move_sems.at[1, 2 * which],
        )

    def move(which, source, there):
        far(which, 1, source, there).start()

        @pl.when(stay)
        def _():
            near(which, source, there).start()

        @pl.when(jnp.logical_not(stay))
        def _():
            far(which, 0, source, there).start()

    def moved_out(which, source, there):
        far(which, 1, source, there).wait_send()

        @pl.when(jnp.logical_not(stay))
        def _():
            far(which, 0, source, there).wait_send()

    def moved_in(which, source, there):
        far(which, 1, source, there).wait_recv()

        @pl.when(stay)
        def _():
            near(which, source, there).wait()

        @pl.when(jnp.logical_not(stay))
        def _():
            far(which, 0, source, there).wait_recv()

    moves = ((0, clip_ref, clip.at[0, 0]), (1, small_ref, xs), (2, large_ref, xl), (3, cot_ref, cot))
    move(*moves[0])
    move(*moves[1])
    loads = [
        pltpu.make_async_copy(source, there, load_sems.at[i])
        for i, (source, there) in enumerate(zip(weight_refs, weights))
    ]
    for load in loads:
        load.start()
    moved_out(*moves[0])
    moved_out(*moves[1])
    move(*moves[2])
    outs = []

    def keep(source, there):
        copy = pltpu.make_async_copy(source, there, out_sems.at[len(outs)])
        copy.start()
        outs.append(copy)

    def front_into(x, n_ref, q_ref, kv):
        normed = norm(x[...].astype(f32), first_gain[...])
        n_ref[...] = normed
        keys = dot(normed, wk[...]).astype(bf16)
        values = dot(normed, wv[...]).astype(bf16)
        for pair in range(pairs):
            lanes = slice(pair * LANES, (pair + 1) * LANES)
            kv[0, pair, 0] = keys[:, lanes]
            kv[0, pair, 1] = values[:, lanes]

    def query_into(n_ref, q_ref):
        query = (dot(n_ref[...], wq[...]) * Q_SCALE).astype(bf16)
        for pair in range(pairs):
            q_ref[pair] = query[:, pair * LANES : (pair + 1) * LANES]

    large, small = Gather(here, kvl, gather_l), Gather(here, kvs, gather_s)
    cross, clips = Gather(here, ckv, gather_c), Gather(here, clip, gather_clip)

    moved_in(*moves[0])
    for kind in (0, 1):
        clips.copy(kind, 0, 1, 0).start()
    moved_in(*moves[1])
    keep(xs, xs_out)
    for i in (0, 1, 2):
        loads[i].wait()
    front_into(xs, ns_ref, qs_ref, kvs)
    for kind in (0, 1):
        small.copy(kind, 0, pairs, 0).start()
    query_into(ns_ref, qs_ref)
    clips.copy(0, 0, 1, 0).wait_recv()
    clips.copy(2, 0, 1, 0).start()
    for kind in (1, 2):
        clips.copy(kind, 0, 1, 0).wait_recv()

    few = clip.shape[2]
    spot = lax.broadcasted_iota(jnp.int32, (1, LANES), 1) % HALF
    number = spot.astype(f32)
    some = spot < 4
    row = lax.broadcasted_iota(jnp.int32, (2 * few, few), 0) // 2
    twice = jnp.where(row == lax.broadcasted_iota(jnp.int32, (2 * few, few), 1), 1.0, 0.0)
    twice = twice.astype(bf16)
    for part in range(4):
        mine = clip[part, 0]
        for value, mk_ref, mq_ref in (
            (mine.astype(f32), mks_ref, mqs_ref),
            (dot(twice, mine), mkl_ref, mql_ref),
        ):
            rows = value.shape[0]
            mk_ref[pl.ds(part * rows, rows), :] = jnp.where(
                some & (value != number), NEGATIVE, 0.0
            ).astype(bf16)
            if part == 0:
                mq_ref[...] = jnp.where(some & (value == number), 1.0, 0.0).astype(bf16)

    moved_in(*moves[2])
    moved_out(*moves[2])
    move(*moves[3])
    keep(xl, xl_out)
    front_into(xl, nl_ref, ql_ref, kvl)
    third = pairs // 3
    small.copy(0, 0, pairs, 0).wait_send()
    large.copy(0, 0, third, 0).start()
    for group in range(3):
        large.copy(1, group * third, third, group).start()
    query_into(nl_ref, ql_ref)

    small.copy(0, 0, pairs, 0).wait_recv()
    small.copy(2, 0, pairs, 0).start()
    small.copy(1, 0, pairs, 0).wait_recv()
    small.copy(2, 0, pairs, 0).wait_recv()
    keep(kvs, kvs_out)

    def small_pair(pair, carry):
        attend_pair(pair, qs_ref, kvs, mqs_ref, mks_ref, spaces, os_ref, ls_ref)
        return carry

    lax.fori_loop(0, pairs, small_pair, 0)
    loads[3].wait()
    for pair in range(pairs):
        wide[:, pair * LANES : (pair + 1) * LANES] = os_ref[pair]
    hidden = xs[...].astype(f32) + dot(wide[...], wo[...])
    hidden_ref[...] = hidden
    second_ref[...] = norm(hidden, second_gain[...])
    total[...] = hidden
    loads[4].wait()
    loads[5].wait()
    width = wide.shape[1]
    steps = up.shape[1] // width
    for step in range(steps):
        lanes = slice(step * width, (step + 1) * width)
        active, slope = gelu_both(dot(second_ref[...], up[:, lanes]))
        active = active.astype(bf16)
        active_ref[:, lanes] = active
        slope_ref[:, lanes] = slope.astype(bf16)
        total[...] += dot(active, down[lanes, :])
        if step == steps // 2:
            large.copy(0, 0, third, 0).wait_send()
            large.copy(0, third, third, 1).start()
    merged = total[...]
    merged_ref[...] = merged
    context = norm(merged, context_gain[...])
    context_ref[...] = context
    loads[6].wait()
    loads[7].wait()
    keys = dot(context, wck[...]).astype(bf16)
    values = dot(context, wcv[...]).astype(bf16)
    for pair in range(pairs):
        lanes = slice(pair * LANES, (pair + 1) * LANES)
        ckv[0, pair, 0] = keys[:, lanes]
        ckv[0, pair, 1] = values[:, lanes]
    cross.copy(1, 0, pairs, 0).start()

    def large_pair(pair, carry):
        attend_pair(pair, ql_ref, kvl, mql_ref, mkl_ref, spaces, ol_ref, ll_ref)
        return carry

    for group in range(3):
        at = group * third
        large.copy(0, at, third, group).wait_recv()
        large.copy(2, at, third, group).start()
        if group == 0:
            large.copy(0, third, third, 1).wait_send()
            large.copy(0, 2 * third, third, 2).start()
        if group == 2:
            large.copy(0, 2 * third, third, 2).wait_send()
            cross.copy(0, 0, pairs, 0).start()
        large.copy(1, at, third, group).wait_recv()
        large.copy(2, at, third, group).wait_recv()
        if group == 2:
            keep(kvl, kvl_out)
        lax.fori_loop(at, at + third, large_pair, 0)
    moved_in(*moves[3])
    moved_out(*moves[3])
    keep(cot, cot_out)
    cross.copy(0, 0, pairs, 0).wait_recv()
    cross.copy(2, 0, pairs, 0).start()
    cross.copy(1, 0, pairs, 0).wait_recv()
    cross.copy(2, 0, pairs, 0).wait_recv()
    keep(ckv, ckv_out)
    for copy in [small.copy(1, 0, pairs, 0), small.copy(2, 0, pairs, 0)]:
        copy.wait_send()
    for kind in (0, 1, 2):
        clips.copy(kind, 0, 1, 0).wait_send()
        cross.copy(kind, 0, pairs, 0).wait_send()
        if kind:
            for group in range(3):
                large.copy(kind, group * third, third, group).wait_send()
    for copy in outs:
        copy.wait()


def begin(large, small, cotangent, clip, weights, gains):
    seqs, count, width = large.shape
    few = small.shape[1]
    count, few = 2 * count, 2 * few
    pairs = width // LANES
    hidden = weights[4].shape[1]
    shape = jax.ShapeDtypeStruct
    kv_l, kv_s = (4, pairs, 2, count, LANES), (4, pairs, 2, few, LANES)
    anywhere = pl.BlockSpec(memory_space=pl.ANY)
    vmem = pl.BlockSpec(memory_space=pltpu.VMEM)
    out_shape = [
        shape((count, width), bf16),
        shape((few, width), bf16),
        shape((count, width), bf16),
        shape(kv_l, bf16),
        shape(kv_s, bf16),
        shape(kv_s, bf16),
        shape((count, width), bf16),
        shape((few, width), bf16),
        shape((pairs, count, LANES), bf16),
        shape((pairs, few, LANES), bf16),
        shape((pairs, count, LANES), bf16),
        shape((pairs, count, LANES), f32),
        shape((pairs, few, LANES), bf16),
        shape((pairs, few, LANES), f32),
        shape((few, width), f32),
        shape((few, width), f32),
        shape((few, width), bf16),
        shape((few, hidden), bf16),
        shape((few, hidden), bf16),
        shape((few, width), bf16),
        shape((count, LANES), bf16),
        shape((4 * count, LANES), bf16),
        shape((few, LANES), bf16),
        shape((4 * few, LANES), bf16),
    ]
    dma = pltpu.SemaphoreType.DMA
    scratch = [
        pltpu.VMEM((count, width), bf16),
        pltpu.VMEM((few, width), bf16),
        pltpu.VMEM((count, width), bf16),
        pltpu.VMEM((4, 1, few, LANES), bf16),
        pltpu.VMEM(kv_l, bf16),
        pltpu.VMEM(kv_s, bf16),
        pltpu.VMEM(kv_s, bf16),
    ]
    scratch += [pltpu.VMEM(weight.shape, bf16) for weight in weights]
    scratch += [pltpu.VMEM((4 * count, LANES), bf16)] * 4
    scratch += [pltpu.VMEM((few, width), bf16), pltpu.VMEM((few, width), f32)]
    scratch += [dma((2, 8)), dma((2, 9)), dma((2, 3)), dma((2, 3)), dma((2, 3)), dma((8,)), dma((6,))]
    return pl.pallas_call(
        functools.partial(begin_kernel, pairs),
        in_specs=[anywhere] * 12 + [vmem] * 3,
        out_specs=[anywhere] * 6 + [vmem] * 18,
        out_shape=out_shape,
        scratch_shapes=scratch,
        compiler_params=pltpu.CompilerParams(
            vmem_limit_bytes=62 << 20, collective_id=4, has_side_effects=True
        ),
        cost_estimate=pl.CostEstimate(
            flops=16 * count * 4 * count * width + 18 * few * width * hidden,
            bytes_accessed=40 << 20,
            transcendentals=count * count * 4 * width // HALF,
        ),
        name="begin",
    )(large, small, cotangent, clip, *weights, *gains)


def cross_attend_kernel(q_ref, kv_ref, mq_ref, mk_ref, o_ref, l_ref, *spaces):
    attend_pair(0, q_ref, kv_ref, mq_ref, mk_ref, spaces, o_ref, l_ref)


def cross_attend(query, kv, mask_q, mask_k):
    pairs, count = query.shape[:2]
    rows = kv.shape[3]
    one = pl.BlockSpec((1, count, LANES), lambda i: (i, 0, 0))
    return pl.pallas_call(
        cross_attend_kernel,
        grid=(pairs,),
        in_specs=[
            one,
            pl.BlockSpec((4, 1, 2, rows, LANES), lambda i: (0, i, 0, 0, 0)),
            whole((count, LANES)),
            whole((4 * rows, LANES)),
        ],
        out_specs=[one, one],
        out_shape=[
            jax.ShapeDtypeStruct(query.shape, bf16),
            jax.ShapeDtypeStruct(query.shape, f32),
        ],
        scratch_shapes=[pltpu.VMEM((4 * rows, LANES), bf16)] * 4,
        compiler_params=pltpu.CompilerParams(vmem_limit_bytes=40 << 20),
        cost_estimate=pl.CostEstimate(
            flops=64 * count * rows * pairs * LANES,
            bytes_accessed=32 * count * pairs * LANES,
            transcendentals=8 * count * rows * pairs,
        ),
        name="cross_attend",
    )(query, kv, mask_q, mask_k)


def after(value, *needed):
    return lax.optimization_barrier((value, needed))[0]


CROSS_ORDERS = (BY_Y[:2], BY_ZL[:2])
SELVES_ORDERS = (BY_Y[:3], BY_ZL[:3], BY_Y[:3], BY_Y[2:], BY_ZL[2:])
SELVES_ENDS = (False, False, False, True, True)
SELVES_STAGES = (
    (1, 6, 11),
    (1, 7, 11),
    (1, 7, 11),
    (4, 6, 8, 9, 10),
    (4, 6, 8, 9, 10),
)


def paired_end(views, normed, large, small, cross, merged, weights, crosses, gains):
    large_view, small_view = views
    large_normed, small_normed, asked, context = normed
    large_q, large_mixed, large_logsum, large_mask_q, large_mask_k, large_kv = large
    small_q, small_mixed, small_logsum, small_mask_q, small_mask_k, small_kv = small
    cross_q, united, cross_logsum, cross_kv, united_grad, grad_out = cross
    large_merged, large_saved, small_merged, small_saved = merged
    query_weight, key_weight, value_weight, output_weight, up_weight, down_weight = weights
    first_gain, second_gain, query_gain, context_gain = gains
    width = large_view.shape[1]
    rows = width // 8
    (
        united_view, large_grad, small_grad, first, other, query_gain_grad, context_gain_grad,
    ) = cross_back(
        (cross_q, united_grad, united, cross_logsum, large_mask_q, small_mask_k),
        cross_kv,
        (united, crosses[3], large_merged, asked, context, grad_out, small_merged) + crosses[:3],
        (query_gain, context_gain),
    )
    (
        large_hidden, small_hidden, large_mixed_grad, small_mixed_grad, up_grad, down_grad,
        output_grad, second_gain_grad, first, other,
    ) = back(
        large_grad, small_grad, large_saved, small_saved, [large_mixed], small_mixed, output_weight,
        second_gain, up_weight, down_weight, True, (first, other), CROSS_ORDERS,
    )
    eight = (8, 4 * rows, width)
    still = (8, rows // 2, width)
    selves, sums = selves_back(
        (large_q, large_mixed_grad, large_mixed, large_logsum, large_mask_q, large_mask_k),
        large_kv,
        (small_q, small_mixed_grad, small_mixed, small_logsum, small_mask_q, small_mask_k),
        small_kv,
        (
            up_grad.reshape(eight), down_grad.reshape(eight),
            output_grad.reshape(8, 2 * rows, width // 2),
            first.reshape(still), other.reshape(still),
        ),
        SELVES_ORDERS, SELVES_ENDS, SELVES_STAGES,
    )
    up, down, output, first, other = sums
    (large_grad, small_grad), last, late, gains = last_sums(
        tuple(selves) + (query_weight, key_weight, value_weight, large_view, small_view)
        + (large_hidden, small_hidden, large_normed, small_normed),
        (
            up.reshape(4, rows, width), down.reshape(4, rows, width),
            output.reshape(4, rows // 2, width // 2),
        ),
        (first_gain, second_gain_grad, query_gain_grad, context_gain_grad),
    )
    up, down, output = (total.astype(f32) for total in late)

    def square(total):
        total = total.astype(f32).reshape(2, 2, width // 16, width // 2)
        return jnp.transpose(total, (0, 2, 1, 3)).reshape(rows, width)

    first = first.astype(f32).reshape(2, rows, width)
    other = other.astype(f32).reshape(2, rows, width)
    at = lax.axis_index("tm") * rows
    gains = [lax.dynamic_slice(gains, (i, at), (1, rows))[0] for i in range(4)]
    return (
        united_view,
        large_grad,
        small_grad,
        gains[0],
        square(last[0]),
        square(last[1]),
        square(last[2]),
        square(output),
        gains[1],
        jnp.transpose(up, (1, 0, 2)).reshape(rows, 4 * width),
        down.reshape(4 * rows, width),
        gains[2],
        gains[3],
        first[1],
        other[0],
        other[1],
        first[0],
    )


def per_device(tm, seq_size, *args):
    (
        large_view,
        small_view,
        clip_ids,
        first_gain,
        query_weight,
        key_weight,
        value_weight,
        output_weight,
        second_gain,
        up_weight,
        down_weight,
        query_gain,
        context_gain,
        cross_query,
        cross_key,
        cross_value,
        cross_output,
        cotangent,
    ) = args
    seqs, count, width = large_view.shape
    side = tm // 4
    gains = jnp.stack((first_gain, second_gain, query_gain, context_gain)).astype(f32)
    first_gain, second_gain, query_gain, context_gain = (gains[i : i + 1] for i in range(4))

    tm_at = lax.axis_index("tm")
    seq_at = lax.axis_index("seq")
    z, x = tm_at // side, tm_at % side
    y, core = seq_at // 2, seq_at % 2
    places = [
        (pz, px, py, pc)
        for pz in range(4)
        for px in range(side)
        for py in range(2)
        for pc in range(2)
    ]

    def number(place):
        return (place[0] * side + place[1]) * seq_size + place[2] * 2 + place[3]

    def permute(value, place):
        pairs = [(number(at), number(place(*at))) for at in places]
        return lax.ppermute(value, ("tm", "seq"), pairs)

    def inverse(place):
        table = {place(*at): at for at in places}
        return lambda *at: table[at]

    go = (
        lambda z, x, y, c: (2 * c + z % 2, x, y, z // 2),
        lambda z, x, y, c: (2 * c + 1 - z % 2, x, y, z // 2),
    )
    back_home = tuple(inverse(place) for place in go)
    other_core = lambda value: permute(value, lambda z, x, y, c: (z, x, y, 1 - c))
    other_y = lambda value: permute(value, lambda z, x, y, c: (z, x, 1 - y, c))
    by_x = lambda value, d: permute(value, lambda z, x, y, c: (z, (x + d) % side, y, c))
    odd = z % 2 == 1

    def relocate(value):
        near = jnp.where(odd, value[1], value[0])
        far = jnp.where(odd, value[0], value[1])
        return jnp.concatenate([permute(near, go[0]), permute(far, go[1])], axis=0)

    def restore(value):
        rows = value.shape[0] // 2
        near, far = permute(value[:rows], back_home[0]), permute(value[rows:], back_home[1])
        return jnp.where(odd, jnp.stack([far, near]), jnp.stack([near, far]))

    def join(parts, axis):
        return parts[0] if len(parts) == 1 else jnp.concatenate(parts, axis=axis)

    def gather(value, axis=1):
        across = join([by_x(value, d) for d in range(1, side)], axis)
        return (value, across, other_core(value), other_core(across))

    def add(a, b):
        return (a.astype(f32) + b.astype(f32)).astype(bf16)

    def scatter_core(keep, send):
        return add(keep, other_core(send))

    def scatter_x(sums):
        rows = sums.shape[1] // side
        total = sums[:, :rows].astype(f32)
        for d in range(1, side):
            total = total + by_x(sums[:, d * rows : (d + 1) * rows], -d).astype(f32)
        return total.astype(bf16)

    if side == 2:
        clip = jnp.broadcast_to(
            clip_ids[:, ::2].astype(bf16)[:, :, None], (seqs, count // 2, LANES)
        )
        (
            large, small, grad_out, large_kv, small_kv, cross_kv, large_normed, small_normed,
            large_q, small_q, large_mixed, large_logsum, small_mixed, small_logsum, small_merged,
            *small_saved, context, large_mask_q, large_mask_k, small_mask_q, small_mask_k,
        ) = begin(
            large_view, small_view, cotangent, clip,
            (query_weight, key_weight, value_weight, output_weight, up_weight, down_weight,
             cross_key, cross_value),
            (first_gain, second_gain, context_gain),
        )
        united_grad = dot(grad_out, cross_output, NT).astype(bf16)
        large_merged, *large_saved, asked, cross_q = rest(
            large, [large_mixed], output_weight, second_gain, up_weight, down_weight,
            query_gain, (cross_query,),
        )
        united, cross_logsum = cross_attend(cross_q, cross_kv, large_mask_q, small_mask_k)
        return paired_end(
            (large, small),
            (large_normed, small_normed, asked, context),
            (large_q, large_mixed, large_logsum, large_mask_q, large_mask_k, large_kv),
            (small_q, small_mixed, small_logsum, small_mask_q, small_mask_k, small_kv),
            (cross_q, united, cross_logsum, cross_kv, united_grad, grad_out),
            (large_merged, large_saved, small_merged, small_saved),
            (query_weight, key_weight, value_weight, output_weight, up_weight, down_weight),
            (cross_query, cross_key, cross_value, cross_output),
            (first_gain, second_gain, query_gain, context_gain),
        )

    groups = 3
    part = width // groups
    short_clips = gather(relocate(clip_ids[:, ::2].astype(f32)), 0)
    small = relocate(small_view)
    large = relocate(large_view)
    grad_out = relocate(after(cotangent, large))
    spot = lax.broadcasted_iota(jnp.int32, (1, LANES), 1) % HALF

    def mask_of_keys(numbers):
        away = numbers.astype(jnp.int32)[:, None] != spot
        return jnp.where((spot < 4) & away, NEGATIVE, 0.0).astype(bf16)

    def mask_of_queries(numbers):
        same = numbers.astype(jnp.int32)[:, None] == spot
        return jnp.where((spot < 4) & same, 1.0, 0.0).astype(bf16)

    short = jnp.concatenate(short_clips)
    small_mask_k = mask_of_keys(short)
    large_mask_k = mask_of_keys(jnp.repeat(short, 2))
    small_mask_q = mask_of_queries(short_clips[0])
    large_mask_q = mask_of_queries(jnp.repeat(short_clips[0], 2))

    small_normed, small_q, small_kv = front(
        small, first_gain, query_weight, key_weight, value_weight, 1
    )
    small_kv = gather(small_kv[0])
    large_normed, large_q, large_kv = front(
        large, first_gain, query_weight, key_weight, value_weight, groups
    )
    large_kv = [gather(kv) for kv in large_kv]
    small_mixed, small_logsum = attend(small_q, small_kv, small_mask_q, small_mask_k, 0, width)
    small_merged, *small_saved, context, cross_kv = rest(
        small, [small_mixed], output_weight, second_gain, up_weight, down_weight,
        context_gain, (cross_key, cross_value),
    )
    cross_kv = gather(cross_kv)
    united_grad = dot(grad_out, cross_output, NT).astype(bf16)
    large_out = ()
    for group, kv in enumerate(large_kv):
        large_out = attend(large_q, kv, large_mask_q, large_mask_k, group * part, part, large_out)
    large_mixed, large_logsum = large_out
    large_merged, *large_saved, asked, cross_q = rest(
        large, [large_mixed], output_weight, second_gain, up_weight, down_weight,
        query_gain, (cross_query,),
    )
    united, cross_logsum = attend(cross_q, cross_kv, large_mask_q, small_mask_k, 0, width)
    united_view = restore((large_merged + dot(united, cross_output)).astype(bf16))

    bits = side.bit_length() - 1
    moves = {"zh": lambda z, x, y, c: (z ^ 2, x, y, c), "zl": lambda z, x, y, c: (z ^ 1, x, y, c)}
    mine = {"zh": z // 2, "zl": z % 2}
    axes = {"zh": 0, "zl": 1}
    for bit in range(bits):
        flip = 1 << (bits - 1 - bit)
        moves[f"x{bit}"] = lambda z, x, y, c, flip=flip: (z, x ^ flip, y, c)
        mine[f"x{bit}"] = (x // flip) % 2
        axes[f"x{bit}"] = 2 + bit
    moves["core"] = lambda z, x, y, c: (z, x, y, 1 - c)
    moves["y"] = lambda z, x, y, c: (z, x, 1 - y, c)
    mine["core"], mine["y"] = core, y
    axes["core"], axes["y"] = 2 + bits, 3 + bits
    by_y = ["core", "y", "zl"] + [f"x{bit}" for bit in range(bits)] + ["zh"]
    by_zl = ["core", "zl", "y"] + [f"x{bit}" for bit in range(bits)] + ["zh"]
    by_yx = ["core", "y"] + [f"x{bit}" for bit in range(bits)] + ["zl", "zh"]

    class Sum:
        def __init__(self, local, order):
            rows, wide = local.shape
            self.value = local.reshape((2,) * (2 + bits) + (rows // tm, wide))
            self.todo = list(order)
            self.rows, self.wide = rows // tm, wide

        def step(self, *needed):
            name = self.todo.pop(0)
            axis = axes[name]
            size = self.value.shape[axis] // 2
            at = mine[name]
            keep = lax.dynamic_slice_in_dim(self.value, at * size, size, axis)
            send = lax.dynamic_slice_in_dim(self.value, (1 - at) * size, size, axis)
            self.value = add(keep, permute(send, moves[name]))
            return self.value

        def finish(self):
            while self.todo:
                self.step()
            value = self.value.reshape(self.rows // 2, self.wide // 2)
            other = other_y(value)
            value = jnp.where(
                y == 0,
                jnp.concatenate([value, other], axis=1),
                jnp.concatenate([other, value], axis=1),
            )
            other = other_core(value)
            return jnp.where(
                core == 0,
                jnp.concatenate([value, other], axis=0),
                jnp.concatenate([other, value], axis=0),
            ).astype(f32)

    cross_groups = 2
    cross_part = width // cross_groups
    dcq, dckv = [], []
    for group in range(cross_groups):
        query = after(cross_q, *dcq[-1:])
        at = group * cross_part
        dq, keep, send = attend_back(
            query, cross_kv, united_grad, united, cross_logsum,
            large_mask_q, small_mask_k, at, at, at, cross_part,
        )
        dcq.append(dq)
        dckv.append(scatter_x(scatter_core(keep, send)))
    dcq = jnp.concatenate(dcq, axis=1)
    dck = jnp.concatenate([kv[0] for kv in dckv], axis=1)
    dcv = jnp.concatenate([kv[1] for kv in dckv], axis=1)
    extra, query_gain_grad = norm_back(dot(dcq, cross_query, NT), large_merged, query_gain)
    large_merged_grad = grad_out.astype(f32) + extra
    small_merged_grad, context_gain_grad = norm_back(
        dot(dck, cross_key, NT) + dot(dcv, cross_value, NT), small_merged, context_gain
    )
    cross_parts = [
        dot(united, grad_out, TN).astype(bf16),
        dot(asked, dcq, TN).astype(bf16),
        dot(context, dck, TN).astype(bf16),
        dot(context, dcv, TN).astype(bf16),
    ]
    (
        large_hidden_grad,
        small_hidden_grad,
        large_mixed_grad,
        small_mixed_grad,
        up_grad,
        down_grad,
        output_grad,
        second_gain_grad,
    ) = back(
        large_merged_grad, small_merged_grad, large_saved, small_saved, [large_mixed], small_mixed,
        output_weight, second_gain, up_weight, down_weight, False,
    )
    cross_sum = Sum(jnp.concatenate(cross_parts, axis=1), by_y)
    up_sum = Sum(up_grad, by_y)
    down_sum = Sum(down_grad, by_zl)
    cross_sum.step()
    small_dq, keep, send = attend_back(
        after(small_q, cross_sum.value), small_kv, small_mixed_grad, small_mixed, small_logsum,
        small_mask_q, small_mask_k, 0, 0, 0, width,
    )
    small_sums = scatter_core(keep, send)
    up_sum.step()
    down_sum.step()
    cross_sum.step()
    needed = [small_dq, up_sum.value, down_sum.value]
    normed = jnp.concatenate([large_normed, small_normed], axis=0)
    last_sums, dqs, dkvs = [], [], []
    pending = None
    for group in range(groups):
        at = group * part
        dq, keep, send = attend_back(
            after(large_q, *needed), large_kv[group], large_mixed_grad, large_mixed, large_logsum,
            large_mask_q, large_mask_k, at, at, 0, part,
        )
        sums = scatter_core(keep, send)
        dqs.append(dq)
        needed = [dq]
        if group == 0:
            small_dkv = scatter_x(small_sums)
            needed += [cross_sum.value, small_sums]
        if group == 1:
            needed += [small_dkv, up_sum.step(), down_sum.step(), cross_sum.step()]
        if pending is not None:
            needed.append(pending.step())
        dkv = scatter_x(sums)
        dkvs.append(dkv)
        local = jnp.concatenate(
            [
                jnp.concatenate([dq, dkv[0], dkv[1]], axis=1),
                jnp.concatenate(
                    [
                        small_dq[:, at : at + part],
                        small_dkv[0, :, at : at + part],
                        small_dkv[1, :, at : at + part],
                    ],
                    axis=1,
                ),
            ],
            axis=0,
        )
        local = dot(normed, local, TN).astype(bf16)
        pending = Sum(local, by_yx)
        last_sums.append(pending)

    def front_back(view, hidden_grad, dq, dk, dv):
        grad = (
            dot(dq, query_weight, NT) + dot(dk, key_weight, NT) + dot(dv, value_weight, NT)
        )
        extra, gain_part = norm_back(grad, view.astype(f32), first_gain)
        return (hidden_grad + extra).astype(bf16), gain_part

    small_grad, small_gain = front_back(
        small, small_hidden_grad, small_dq, small_dkv[0], small_dkv[1]
    )
    large_grad, large_gain = front_back(
        large,
        large_hidden_grad,
        jnp.concatenate(dqs, axis=1),
        jnp.concatenate([kv[0] for kv in dkvs], axis=1),
        jnp.concatenate([kv[1] for kv in dkvs], axis=1),
    )
    small_grad = restore(small_grad).astype(f32)
    large_grad = restore(large_grad).astype(f32)
    output_sum = Sum(output_grad, by_yx)
    gain_rows = jnp.concatenate(
        [large_gain + small_gain, second_gain_grad, query_gain_grad, context_gain_grad], axis=0
    )
    wide = width // tm
    gain_rows = jnp.transpose(gain_rows.reshape(4, tm, wide), (1, 0, 2)).astype(bf16)
    gain_rows = jnp.pad(gain_rows, ((0, 0), (0, 28), (0, 2 * LANES - wide)))
    gain_sum = Sum(gain_rows.reshape(tm * 32, 2 * LANES), by_yx)

    cross_total = cross_sum.finish()
    up_total = up_sum.finish()
    down_total = down_sum.finish()
    output_total = output_sum.finish()
    last_totals = [total.finish() for total in last_sums]
    gain_total = gain_sum.finish()
    cross_grads = [cross_total[:, i * width : (i + 1) * width] for i in range(4)]
    last_grads = [
        jnp.concatenate([total[:, i * part : (i + 1) * part] for total in last_totals], axis=1)
        for i in range(3)
    ]
    gain_grads = [gain_total[i, :wide] for i in range(4)]
    return (
        united_view,
        large_grad,
        small_grad,
        gain_grads[0],
        last_grads[0],
        last_grads[1],
        last_grads[2],
        output_total,
        gain_grads[1],
        up_total,
        down_total,
        gain_grads[2],
        gain_grads[3],
        cross_grads[1],
        cross_grads[2],
        cross_grads[3],
        cross_grads[0],
    )


def solution(mesh):
    token = P("seq", "tm", None)
    in_specs = (token, token, P("seq", "tm")) + (P(),) * 14 + (token,)
    vector, matrix = P("tm"), P("tm", None)
    out_specs = (
        (token, token, token, vector)
        + (matrix,) * 4
        + (vector, matrix, matrix, vector, vector)
        + (matrix,) * 4
    )
    return jax.shard_map(
        functools.partial(per_device, mesh.shape["tm"], mesh.shape["seq"]),
        mesh=mesh,
        in_specs=in_specs,
        out_specs=out_specs,
        check_vma=False,
    )
```

```python
import functools

import jax
import jax.numpy as jnp
from jax import lax
from jax.experimental import pallas as pl
from jax.experimental.pallas import tpu as pltpu
from jax.sharding import PartitionSpec as P

HEADS = 12
EPS = 1e-05
NEGATIVE = -1e30
LOG2E = 1.4426950408889634
LN2 = 0.6931471805599453
LANES = 128
HALF = 64

bf16 = jnp.bfloat16
f32 = jnp.float32
NT = (((1,), (1,)), ((), ()))
NN = (((1,), (0,)), ((), ()))
TN = (((0,), (0,)), ((), ()))


def dot(a, b, dims=NN):
    return lax.dot_general(a, b, dims, preferred_element_type=f32)


def largest_block(rows, most):
    block = min(rows, most)
    while rows % block or block % 16:
        block -= 1
    return block


def columns(rows, at):
    return pl.BlockSpec((rows, LANES), lambda i: (0, i + at))


def pair_columns(rows, at):
    return pl.BlockSpec((2, rows, LANES), lambda i: (0, 0, i + at))


def whole(shape):
    return pl.BlockSpec(shape, lambda i: (0,) * len(shape))


def attend_kernel(parts, block, *refs):
    q_ref, mq_ref, mk_ref = refs[:3]
    kv_refs = refs[3 : 3 + parts]
    o_ref, l_ref, ka0, ka1, va0, va1 = refs[-6:]
    count = q_ref.shape[0]
    first = 0
    for kv_ref in kv_refs:
        rows = kv_ref.shape[1]
        low = lax.broadcasted_iota(jnp.int32, (rows, LANES), 1) < HALF
        here = pl.ds(first, rows)
        keys, values, mask = kv_ref[0], kv_ref[1], mk_ref[here, :]
        one = jnp.ones_like(values)
        ka0[here, :] = jnp.where(low, keys, mask)
        ka1[here, :] = jnp.where(low, mask, keys)
        va0[here, :] = jnp.where(low, values, one)
        va1[here, :] = jnp.where(low, one, values)
        first += rows
    low = lax.broadcasted_iota(jnp.int32, (block, LANES), 1) < HALF
    for number in range(count // block):
        here = pl.ds(number * block, block)
        query, mask = q_ref[here, :], mq_ref[here, :]
        tops, sums = [], []
        for head, keys, values in ((0, ka0, va0), (1, ka1, va1)):
            mine = jnp.where(low, query, mask) if head == 0 else jnp.where(low, mask, query)
            score = dot(mine, keys[...], NT)
            top = jnp.max(score, axis=1, keepdims=True)
            weight = jnp.exp2(score - top).astype(bf16)
            sums.append(dot(weight, values[...]))
            tops.append(jnp.broadcast_to(top, (block, LANES)))
        total = jnp.where(low, sums[1], sums[0])
        top = jnp.where(low, tops[1], tops[0])
        out = jnp.where(low, sums[0], sums[1])
        o_ref[here, :] = (out / pltpu.roll(total, HALF, 1)).astype(bf16)
        l_ref[here, :] = top + jnp.log2(total)


def attend(query, kv, mask_q, mask_k, at, width, earlier=()):
    count = query.shape[0]
    total = sum(part.shape[1] for part in kv)
    out = lambda kind: jax.ShapeDtypeStruct((count, query.shape[1]), kind)
    given = 3 + len(kv)
    return pl.pallas_call(
        functools.partial(attend_kernel, len(kv), largest_block(count, 256)),
        grid=(width // LANES,),
        in_specs=[columns(count, at // LANES), whole((count, LANES)), whole((total, LANES))]
        + [pair_columns(part.shape[1], 0) for part in kv]
        + [pl.BlockSpec(memory_space=pl.ANY)] * len(earlier),
        out_specs=[columns(count, at // LANES)] * 2,
        out_shape=[out(bf16), out(f32)],
        scratch_shapes=[pltpu.VMEM((total, LANES), bf16)] * 4,
        input_output_aliases={given + i: i for i in range(len(earlier))},
        compiler_params=pltpu.CompilerParams(vmem_limit_bytes=40 << 20),
        cost_estimate=pl.CostEstimate(
            flops=16 * count * total * width,
            bytes_accessed=width * (count * 8 + total * 4),
            transcendentals=count * total * width // HALF,
        ),
        name="attend",
    )(query, mask_q, mask_k, *kv, *earlier)


def three(value):
    first = value.astype(bf16)
    rest = value - first.astype(f32)
    second = rest.astype(bf16)
    return first, second, (rest - second.astype(f32)).astype(bf16)


def attend_back_kernel(parts, block, *refs):
    q_ref, do_ref, o_ref, l_ref, mq_ref, mk_ref = refs[:6]
    kv_refs = refs[6 : 6 + parts]
    dq_ref, keep_ref, send_ref, keys_at, values_at = refs[6 + parts :]
    count = q_ref.shape[0]
    first = 0
    for kv_ref in kv_refs:
        here = pl.ds(first, kv_ref.shape[1])
        keys_at[here, :] = kv_ref[0]
        values_at[here, :] = kv_ref[1]
        first += kv_ref.shape[1]
    lane = lax.broadcasted_iota(jnp.int32, (count, LANES), 1)
    low = lane < HALF
    spot = lane % HALF
    query, grad, mask = q_ref[...], do_ref[...], mq_ref[...]
    zero = jnp.zeros_like(query)
    product = grad.astype(f32) * o_ref[...].astype(f32)
    delta0 = jnp.sum(jnp.where(low, product, 0.0), axis=1, keepdims=True)
    delta1 = jnp.sum(jnp.where(low, 0.0, product), axis=1, keepdims=True)
    delta = jnp.where(low, delta1, delta0)

    def beside(base, value):
        a, b, c = three(-value)
        return jnp.where(spot == 4, a, jnp.where(spot == 5, b, jnp.where(spot == 6, c, base)))

    query_side = beside(mask, l_ref[...])
    grad_side = beside(zero, delta)
    query_a = (jnp.where(low, query, query_side), jnp.where(low, query_side, query))
    grad_a = (jnp.where(low, grad, grad_side), jnp.where(low, grad_side, grad))
    query_m = (jnp.where(low, query, zero), jnp.where(low, zero, query))
    grad_m = (jnp.where(low, grad, zero), jnp.where(low, zero, grad))
    lane_k = lax.broadcasted_iota(jnp.int32, (block, LANES), 1)
    low_k = lane_k < HALF
    spot_k = lane_k % HALF
    one = jnp.where((spot_k >= 4) & (spot_k < 7), 1.0, 0.0).astype(bf16)
    dq = jnp.zeros((count, LANES), f32)
    for number in range(first // block):
        here = pl.ds(number * block, block)
        keys, values = keys_at[here, :], values_at[here, :]
        side = mk_ref[here, :] + one
        nought = jnp.zeros_like(keys)
        dk = jnp.zeros((block, LANES), f32)
        dv = jnp.zeros((block, LANES), f32)
        for head in (0, 1):
            pick = lambda a, b: jnp.where(low_k, a, b) if head == 0 else jnp.where(low_k, b, a)
            prob = jnp.exp2(dot(query_a[head], pick(keys, side), NT))
            change = dot(grad_a[head], pick(values, one), NT)
            score_grad = (prob * change).astype(bf16)
            dv += dot(prob.astype(bf16), grad_m[head], TN)
            dk += dot(score_grad, query_m[head], TN)
            dq += dot(score_grad, pick(keys, nought))
        out_ref = keep_ref if number * block < first // 2 else send_ref
        there = pl.ds(number * block % (first // 2), block)
        out_ref[0, there, :] = (dk * LN2).astype(bf16)
        out_ref[1, there, :] = dv.astype(bf16)
    dq_ref[...] = (dq * HALF**-0.5).astype(bf16)


def attend_back(query, kv, grad, out, logsum, mask_q, mask_k, at, at_out, at_kv, width):
    count = query.shape[0]
    total = sum(part.shape[1] for part in kv)
    return pl.pallas_call(
        functools.partial(attend_back_kernel, len(kv), largest_block(total // 2, 512)),
        grid=(width // LANES,),
        in_specs=[columns(count, at // LANES)] * 2
        + [columns(count, at_out // LANES)] * 2
        + [whole((count, LANES)), whole((total, LANES))]
        + [pair_columns(part.shape[1], at_kv // LANES) for part in kv],
        out_specs=[columns(count, 0)] + [pair_columns(total // 2, 0)] * 2,
        out_shape=[jax.ShapeDtypeStruct((count, width), bf16)]
        + [jax.ShapeDtypeStruct((2, total // 2, width), bf16)] * 2,
        scratch_shapes=[pltpu.VMEM((total, LANES), bf16)] * 2,
        compiler_params=pltpu.CompilerParams(vmem_limit_bytes=40 << 20),
        cost_estimate=pl.CostEstimate(
            flops=20 * count * total * width,
            bytes_accessed=width * (count * 12 + total * 8),
            transcendentals=count * total * width // HALF,
        ),
        name="attend_back",
    )(query, grad, out, logsum, mask_q, mask_k, *kv)


def norm_stats(value):
    mean = jnp.mean(value, axis=-1, keepdims=True)
    centred = value - mean
    spread = jnp.mean(centred * centred, axis=-1, keepdims=True)
    return centred, lax.rsqrt(spread + EPS)


def norm(value, gain):
    centred, scale = norm_stats(value)
    return (centred * scale * gain).astype(bf16)


def norm_back(grad, value, gain):
    centred, scale = norm_stats(value)
    unit = centred * scale
    gain_grad = jnp.sum(grad * unit, axis=0, keepdims=True)
    grad = grad * gain
    extra = scale * (
        grad
        - jnp.mean(grad, axis=-1, keepdims=True)
        - unit * jnp.mean(grad * unit, axis=-1, keepdims=True)
    )
    return extra, gain_grad


Q_SCALE = LOG2E * HALF**-0.5


def front_kernel(x_ref, gain_ref, wq_ref, wk_ref, wv_ref, n_ref, q_ref, *kv_refs):
    normed = norm(x_ref[...].astype(f32), gain_ref[...])
    n_ref[...] = normed
    width = kv_refs[0].shape[2]
    keys = dot(normed, wk_ref[...]).astype(bf16)
    values = dot(normed, wv_ref[...]).astype(bf16)
    for group, kv_ref in enumerate(kv_refs):
        kv_ref[0] = keys[:, group * width : (group + 1) * width]
        kv_ref[1] = values[:, group * width : (group + 1) * width]
    q_ref[...] = (dot(normed, wq_ref[...]) * Q_SCALE).astype(bf16)


def front(view, gain, wq, wk, wv, groups):
    rows, width = view.shape
    part = width // groups
    result = pl.pallas_call(
        front_kernel,
        out_shape=[jax.ShapeDtypeStruct((rows, width), bf16)] * 2
        + [jax.ShapeDtypeStruct((2, rows, part), bf16)] * groups,
        compiler_params=pltpu.CompilerParams(vmem_limit_bytes=40 << 20),
        cost_estimate=pl.CostEstimate(
            flops=6 * rows * width * width,
            bytes_accessed=6 * width * width + 10 * rows * width,
            transcendentals=0,
        ),
        name="front",
    )(view, gain, wq, wk, wv)
    return result[0], result[1], result[2:]


GELU_A = 0.7978845608028654
GELU_B = 0.044715


def gelu_both(value):
    square = value * value
    bent = jnp.tanh(GELU_A * value * (1.0 + GELU_B * square))
    half = 0.5 * (1.0 + bent)
    slope = half + 0.5 * value * (1.0 - bent * bent) * (
        GELU_A * (1.0 + 3.0 * GELU_B * square)
    )
    return value * half, slope


def fill_wide(wide, refs, rows, first):
    at, there = 0, pl.ds(first, rows)
    for ref in refs:
        if len(ref.shape) == 3:
            for pair in range(ref.shape[0]):
                wide[there, at : at + LANES] = ref[pair]
                at += LANES
        else:
            wide[there, at : at + ref.shape[1]] = ref[...]
            at += ref.shape[1]


def rest_kernel(steps, mixes, is_query, *refs):
    x_ref = refs[0]
    mixed_refs = refs[1 : 1 + mixes]
    wo_ref, gain_ref, up_ref, down_ref, next_gain_ref = refs[1 + mixes : 6 + mixes]
    next_refs = refs[6 + mixes : -9]
    merged_ref, hidden_ref, second_ref, active_ref, slope_ref = refs[-9:-4]
    asked_ref, out_ref, total, scratch = refs[-4:]
    step = pl.program_id(0)

    @pl.when(step == 0)
    def _():
        hidden = x_ref[...].astype(f32)
        fill_wide(scratch, mixed_refs, scratch.shape[0], 0)
        hidden = hidden + dot(scratch[...], wo_ref[...])
        hidden_ref[...] = hidden
        second_ref[...] = norm(hidden, gain_ref[...])
        total[...] = hidden

    inner = dot(second_ref[...], up_ref[...])
    active, slope = gelu_both(inner)
    active = active.astype(bf16)
    active_ref[...] = active
    slope_ref[...] = slope.astype(bf16)
    total[...] += dot(active, down_ref[...])

    @pl.when(step == steps - 1)
    def _():
        merged = total[...]
        merged_ref[...] = merged
        asked = norm(merged, next_gain_ref[...])
        asked_ref[...] = asked
        if is_query:
            query = (dot(asked, next_refs[0][...]) * Q_SCALE).astype(bf16)
            if len(out_ref.shape) == 3:
                for pair in range(out_ref.shape[0]):
                    out_ref[pair] = query[:, pair * LANES : (pair + 1) * LANES]
            else:
                out_ref[...] = query
        else:
            out_ref[0] = dot(asked, next_refs[0][...]).astype(bf16)
            out_ref[1] = dot(asked, next_refs[1][...]).astype(bf16)


def rest(view, mixed, wo, gain, up, down, next_gain, next_weights):
    rows, width = view.shape
    steps = up.shape[1] // width
    is_query = len(next_weights) == 1
    flat = whole((rows, width))
    slab = pl.BlockSpec((rows, width), lambda i: (0, i))
    square = whole((width, width))
    shape = lambda kind: jax.ShapeDtypeStruct((rows, width), kind)
    wide = jax.ShapeDtypeStruct((rows, up.shape[1]), bf16)
    last = (rows, width) if is_query else (2, rows, width)
    if len(mixed[0].shape) == 3:
        last = (width // LANES, rows, LANES)
    return pl.pallas_call(
        functools.partial(rest_kernel, steps, len(mixed), is_query),
        grid=(steps,),
        in_specs=[flat]
        + [whole(m.shape) for m in mixed]
        + [square, whole((1, width))]
        + [slab_of(width, width), pl.BlockSpec((width, width), lambda i: (i, 0))]
        + [whole((1, width))]
        + [square] * len(next_weights),
        out_specs=[flat, flat, flat, slab, slab, flat, whole(last)],
        out_shape=[shape(f32), shape(f32), shape(bf16), wide, wide, shape(bf16)]
        + [jax.ShapeDtypeStruct(last, bf16)],
        scratch_shapes=[pltpu.VMEM((rows, width), f32), pltpu.VMEM((rows, width), bf16)],
        compiler_params=pltpu.CompilerParams(vmem_limit_bytes=48 << 20),
        cost_estimate=pl.CostEstimate(
            flops=2 * rows * width * (4 * up.shape[1] // 2 + 2 * width),
            bytes_accessed=width * width * 22 + rows * width * 32,
            transcendentals=rows * up.shape[1],
        ),
        name="rest",
    )(view, *mixed, wo, gain, up, down, next_gain, *next_weights)


def slab_of(rows, width):
    return pl.BlockSpec((rows, width), lambda i: (0, i))


def back_kernel(steps, mixes, sizes, laid, orders, *refs):
    gl_ref, gs_ref, al_ref, as_ref, sl_ref, ss_ref = refs[:6]
    cl_ref, cs_ref, hl_ref, hs_ref = refs[6:10]
    mixed_refs = refs[10 : 10 + mixes]
    mixed_s_ref, wo_ref, gain_ref, up_ref, down_ref = refs[10 + mixes : 15 + mixes]
    flows = len(orders)
    locals_, outs = refs[15 + mixes : 15 + mixes + flows], refs[15 + mixes + flows :]
    (hgl_ref, hgs_ref, ml_ref, ms_ref, dup_ref, ddown_ref, dwo_ref, dgain_ref) = outs[:8]
    sums, outs = outs[8 : 8 + flows], outs[8 + flows :]
    branch, second, total, active, inner_grad, mixed = outs[:6]
    large, small = sizes
    top, bottom = pl.ds(0, large), pl.ds(large, small)
    step = pl.program_id(0)
    if flows:
        here = Here()
        rest_refs = list(outs[6:])
        running = [
            Flow(here, order, local, rest_refs, True, False)
            for order, local in zip(orders, locals_)
        ]

        @pl.when(step == 0)
        def _():
            here.greet(ALL_PARTNERS)
            for flow in running:
                flow.act(0)

    @pl.when(step == 0)
    def _():
        branch[top, :] = gl_ref[...].astype(bf16)
        branch[bottom, :] = gs_ref[...].astype(bf16)
        second[top, :] = cl_ref[...]
        second[bottom, :] = cs_ref[...]
        total[...] = jnp.zeros_like(total)

    grad = dot(branch[...], down_ref[...], NT)
    inner_grad[top, :] = (grad[:large] * sl_ref[...].astype(f32)).astype(bf16)
    inner_grad[bottom, :] = (grad[large:] * ss_ref[...].astype(f32)).astype(bf16)
    active[top, :] = al_ref[...]
    active[bottom, :] = as_ref[...]
    down = dot(active[...], branch[...], TN).astype(bf16)
    upper = dot(second[...], inner_grad[...], TN).astype(bf16)
    if laid:
        rows = dup_ref.shape[1]
        for at in range(8):
            zl, zh, x = at // 4, at // 2 % 2, at % 2
            first = ((zh * 2 + zl) * 2 + x) * rows
            dup_ref[at] = upper[first : first + rows]
        for x, core, y in ((a, b, c) for a in (0, 1) for b in (0, 1) for c in (0, 1)):
            first = (x * 4 + core * 2 + y) * rows
            there = core * 16 + (step % 2) * 8 + y * 4 + x * 2 + step // 2
            ddown_ref[there] = down[first : first + rows]
    else:
        dup_ref[...] = upper
        ddown_ref[...] = down
    total[...] += dot(inner_grad[...], up_ref[...], NT)

    @pl.when(step == steps - 1)
    def _():
        extra, gain_l = norm_back(total[top, :], hl_ref[...], gain_ref[...])
        hidden_grad = gl_ref[...] + extra
        hgl_ref[...] = hidden_grad
        branch[top, :] = hidden_grad.astype(bf16)
        extra, gain_s = norm_back(total[bottom, :], hs_ref[...], gain_ref[...])
        hidden_grad = gs_ref[...] + extra
        hgs_ref[...] = hidden_grad
        branch[bottom, :] = hidden_grad.astype(bf16)
        dgain_ref[...] = gain_l + gain_s
        mixed_grad = dot(branch[...], wo_ref[...], NT).astype(bf16)
        ml_ref[...] = mixed_grad[:large]
        ms_ref[...] = mixed_grad[large:]
        fill_wide(mixed, mixed_refs, large, 0)
        fill_wide(mixed, [mixed_s_ref], small, large)
        value = dot(mixed[...], branch[...], TN).astype(bf16)
        if laid:
            rows, wide = dwo_ref.shape[1:]
            for at, (core, y, tm) in enumerate(spots(BY_Y_LATE)):
                first = (tm * 2 + core) * rows
                dwo_ref[at] = value[first : first + rows, y * wide : (y + 1) * wide]
        else:
            dwo_ref[...] = value

    for flow in range(flows):
        for stage, when in enumerate((0, steps - 1)):

            @pl.when(step == when)
            def _(flow=flow, stage=stage):
                running[flow].act(stage + 1)
                if stage == 1:
                    sums[flow][...] = running[flow].result()


def back(
    grad_l, grad_s, saved_l, saved_s, mixed_l, mixed_s, wo, gain, up, down, laid, flows=(), orders=()
):
    (hidden_l, second_l, active_l, slope_l) = saved_l
    (hidden_s, second_s, active_s, slope_s) = saved_s
    large, width = grad_l.shape
    small = grad_s.shape[0]
    rows = large + small
    hidden = up.shape[1]
    part = width
    steps = hidden // part
    fl, fs = whole((large, width)), whole((small, width))
    square = whole((width, width))
    up_slab = slab_of(width, part)
    down_slab = pl.BlockSpec((part, width), lambda i: (i, 0))
    shape = jax.ShapeDtypeStruct
    results = [flow_result(o, f.shape[1:], False) for o, f in zip(orders, flows)]
    scratch = [s for o, f in zip(orders, flows) for s in flow_scratch(o, f.shape[1:], True, False)]
    out_up, out_down, out_square = up_slab, down_slab, square
    up_shape, down_shape, square_shape = up.shape, down.shape, (width, width)
    if laid:
        block = (width // 8, width)
        up_shape = down_shape = (32,) + block
        square_shape = (32, width // 16, width // 2)
        out_up = pl.BlockSpec((8,) + block, lambda i: (i, 0, 0))
        out_down, out_square = whole(down_shape), whole(square_shape)
    return pl.pallas_call(
        functools.partial(back_kernel, steps, len(mixed_l), (large, small), laid, orders),
        grid=(steps,),
        in_specs=[fl, fs]
        + [slab_of(large, part), slab_of(small, part)] * 2
        + [fl, fs, fl, fs]
        + [whole(m.shape) for m in mixed_l]
        + [whole(mixed_s.shape), square, whole((1, width)), up_slab, down_slab]
        + [pl.BlockSpec(memory_space=pl.ANY)] * len(flows),
        out_specs=[fl, fs, fl, fs, out_up, out_down, out_square, whole((1, width))]
        + [whole(result.shape) for result in results],
        out_shape=[
            shape((large, width), f32),
            shape((small, width), f32),
            shape((large, width), bf16),
            shape((small, width), bf16),
            shape(up_shape, bf16),
            shape(down_shape, bf16),
            shape(square_shape, bf16),
            shape((1, width), f32),
        ]
        + results,
        scratch_shapes=[
            pltpu.VMEM((rows, width), bf16),
            pltpu.VMEM((rows, width), bf16),
            pltpu.VMEM((rows, width), f32),
            pltpu.VMEM((rows, part), bf16),
            pltpu.VMEM((rows, part), bf16),
            pltpu.VMEM((rows, width), bf16),
        ]
        + scratch,
        compiler_params=pltpu.CompilerParams(
            vmem_limit_bytes=60 << 20,
            has_side_effects=bool(flows),
            collective_id=0 if flows else None,
        ),
        cost_estimate=pl.CostEstimate(
            flops=2 * rows * width * (4 * hidden + 2 * width),
            bytes_accessed=width * width * 36 + rows * width * 40,
            transcendentals=0,
        ),
        name="back",
    )(
        grad_l, grad_s, active_l, active_s, slope_l, slope_s, second_l, second_s, hidden_l, hidden_s,
        *mixed_l, mixed_s, wo, gain, up, down, *flows,
    )


MESH = pl.DeviceIdType.MESH
BY_Y = ("core", "y", "zl", "x", "zh")
BY_Y_LATE = ("core", "y", "zl", "zh", "x")
BY_ZL = ("core", "zl", "y", "x", "zh")
BY_X = ("core", "x", "zl", "y", "zh")
BY_YX = ("core", "y", "x", "zl", "zh")


def spots(order):
    out = []
    for at in range(32):
        bit = {name: (at >> (4 - i)) & 1 for i, name in enumerate(order)}
        out.append((bit["core"], bit["y"], (bit["zh"] * 2 + bit["zl"]) * 2 + bit["x"]))
    return out


class Here:
    def __init__(self):
        tm, seq = lax.axis_index("tm"), lax.axis_index("seq")
        self.tm, self.seq = tm, seq
        self.bit = {
            "zh": tm // 4,
            "zl": (tm // 2) % 2,
            "x": tm % 2,
            "y": seq // 2,
            "core": seq % 2,
        }

    def partner(self, *names):
        tm, seq = self.tm, self.seq
        for name in names:
            one = 1 - 2 * self.bit[name]
            if name in ("y", "core"):
                seq = seq + one * (2 if name == "y" else 1)
            else:
                tm = tm + one * {"zh": 4, "zl": 2, "x": 1}[name]
        return (tm, seq)

    def greet(self, partners):
        barrier = pltpu.get_barrier_semaphore()
        for names in partners:
            pl.semaphore_signal(
                barrier, inc=1, device_id=self.partner(*names), device_id_type=MESH
            )
        pl.semaphore_wait(barrier, len(partners))


    def greet_line(self, *more):
        barrier = pltpu.get_barrier_semaphore()
        z, core = self.tm // 2, self.bit["core"]
        places = [
            (
                lax.rem(z + dz, 4) * 2 + self.bit["x"],
                self.bit["y"] * 2 + lax.rem(core + dc, 2),
            )
            for dz in range(4)
            for dc in range(2)
            if dz or dc
        ] + [self.partner(name) for name in more]
        for place in places:
            pl.semaphore_signal(barrier, inc=1, device_id=place, device_id_type=MESH)
        pl.semaphore_wait(barrier, len(places))


ALL_PARTNERS = (("core",), ("y",), ("zl",), ("x",), ("zh",))


class Restore:
    def __init__(self, here, held, got, sems):
        self.held, self.got, self.sems = held, got, sems
        self.rows = got.shape[1]
        z, core = here.tm // 2, here.bit["core"]
        self.odd = lax.rem(z, 2)
        self.stay = core == z // 2
        turns = (self.odd, 1 - self.odd)
        self.places = [
            ((2 * core + turn) * 2 + here.bit["x"], here.bit["y"] * 2 + z // 2) for turn in turns
        ]

    def far(self, turn, arriving=False):
        at = 1 - self.odd if arriving and turn else self.odd
        return pltpu.make_async_remote_copy(
            src_ref=self.held.at[pl.ds(turn * self.rows, self.rows)],
            dst_ref=self.got.at[at],
            send_sem=self.sems.at[0, turn],
            recv_sem=self.sems.at[1, turn],
            device_id=self.places[turn],
            device_id_type=MESH,
        )

    def near(self):
        return pltpu.make_async_copy(
            self.held.at[pl.ds(0, self.rows)], self.got.at[self.odd], self.sems.at[1, 0]
        )

    def start(self):
        self.far(1).start()

        @pl.when(self.stay)
        def _():
            self.near().start()

        @pl.when(jnp.logical_not(self.stay))
        def _():
            self.far(0).start()

    def finish(self):
        self.far(1).wait_send()
        self.far(1, True).wait_recv()

        @pl.when(self.stay)
        def _():
            self.near().wait()

        @pl.when(jnp.logical_not(self.stay))
        def _():
            self.far(0).wait_send()
            self.far(0).wait_recv()


def restore_scratch(rows, width):
    return [
        pltpu.VMEM((2 * rows, width), bf16),
        pltpu.VMEM((2, rows, width), bf16),
        pltpu.SemaphoreType.DMA((2, 2)),
    ]


class Flow:
    def __init__(self, here, order, local, refs, keep, ends):
        self.here, self.order, self.local = here, order, local
        self.keep = refs.pop(0) if keep else None
        self.got = [refs.pop(0) for _ in order]
        self.out = refs.pop(0) if ends else None
        self.sem = refs.pop(0)
        self.last = len(order)
        self.ends = ends

    def copy(self, step):
        name = self.order[step]
        half = 1 << (self.last - 1 - step)
        source = self.local if step == 0 else self.got[step - 1]
        at = (1 - self.here.bit[name]) * half
        return pltpu.make_async_remote_copy(
            src_ref=source.at[pl.ds(at, half)],
            dst_ref=self.got[step],
            send_sem=self.sem.at[0, step],
            recv_sem=self.sem.at[1, step],
            device_id=self.here.partner(name),
            device_id_type=MESH,
        )

    def keep_copy(self):
        half = 1 << (self.last - 1)
        at = self.here.bit[self.order[0]] * half
        return pltpu.make_async_copy(
            self.local.at[pl.ds(at, half)], self.keep, self.sem.at[0, self.last + 2]
        )

    def start(self, step):
        self.copy(step).start()
        if step == 0 and self.keep is not None:
            self.keep_copy().start()

    def finish(self, step):
        half = 1 << (self.last - 1 - step)
        self.copy(step).wait()
        got = self.got[step]
        at = self.here.bit[self.order[step]] * half
        if step == 0 and self.keep is not None:
            self.keep_copy().wait()
            source, at = self.keep, 0
        else:
            source = self.local if step == 0 else self.got[step - 1]

        def body(i, carry):
            got[i] = got[i] + source[at + i]
            return carry

        if half == 1:
            got[0] = got[0] + source[at]
        else:
            lax.fori_loop(0, half, body, 0)

    def spread_copy(self, which):
        here = self.here
        own = here.bit["core"] * 2
        if which == 0:
            source, there = self.got[-1].at[0], self.out.at[own + here.bit["y"]]
        else:
            source = there = self.out.at[pl.ds(own, 2)]
        return pltpu.make_async_remote_copy(
            src_ref=source,
            dst_ref=there,
            send_sem=self.sem.at[0, self.last + which],
            recv_sem=self.sem.at[1, self.last + which],
            device_id=here.partner(("y", "core")[which]),
            device_id_type=MESH,
        )

    def act(self, stage):
        if stage == 0:
            self.start(0)
        elif stage < self.last:
            self.finish(stage - 1)
            self.start(stage)
        elif stage == self.last:
            self.finish(stage - 1)
            if self.ends:
                self.spread_copy(0).start()
                self.out[self.here.bit["core"] * 2 + self.here.bit["y"]] = self.got[-1][0]
        elif stage == self.last + 1 and self.ends:
            self.spread_copy(0).wait()
            self.spread_copy(1).start()
        elif stage == self.last + 2 and self.ends:
            self.spread_copy(1).wait()

    def result(self):
        return self.out[...] if self.ends else self.got[-1][...]


def flow_scratch(order, block, keep, ends):
    steps = len(order)
    blocks = [pltpu.VMEM((1 << (steps - 1),) + block, bf16)] if keep else []
    for step in range(steps):
        blocks.append(pltpu.VMEM((1 << (steps - 1 - step),) + block, bf16))
    if ends:
        blocks.append(pltpu.VMEM((4,) + block, bf16))
    return blocks + [pltpu.SemaphoreType.DMA((2, steps + 3))]


def flow_result(order, block, ends):
    left = 4 if ends else 1
    return jax.ShapeDtypeStruct((left,) + block, bf16)


def pair_back(query, grad, out, logsum, mask, keys_at, values_at, mk_ref, block, exchange, pair):
    count = query.shape[0]
    total = keys_at.shape[0]
    lane = lax.broadcasted_iota(jnp.int32, (count, LANES), 1)
    low = lane < HALF
    spot = lane % HALF
    zero = jnp.zeros_like(query)
    product = grad.astype(f32) * out.astype(f32)
    delta0 = jnp.sum(jnp.where(low, product, 0.0), axis=1, keepdims=True)
    delta1 = jnp.sum(jnp.where(low, 0.0, product), axis=1, keepdims=True)
    delta = jnp.where(low, delta1, delta0)

    def beside(base, value):
        a, b, c = three(-value)
        return jnp.where(spot == 4, a, jnp.where(spot == 5, b, jnp.where(spot == 6, c, base)))

    query_side = beside(mask, logsum)
    grad_side = beside(zero, delta)
    query_a = (jnp.where(low, query, query_side), jnp.where(low, query_side, query))
    grad_a = (jnp.where(low, grad, grad_side), jnp.where(low, grad_side, grad))
    query_m = (jnp.where(low, query, zero), jnp.where(low, zero, query))
    grad_m = (jnp.where(low, grad, zero), jnp.where(low, zero, grad))
    lane_k = lax.broadcasted_iota(jnp.int32, (block, LANES), 1)
    low_k = lane_k < HALF
    spot_k = lane_k % HALF
    one = jnp.where((spot_k >= 4) & (spot_k < 7), 1.0, 0.0).astype(bf16)
    dq = jnp.zeros((count, LANES), f32)
    for number in exchange.turns(total // block):
        here = pl.ds(number * block, block)
        keys, values = keys_at[here, :], values_at[here, :]
        side = mk_ref[here, :] + one
        nought = jnp.zeros_like(keys)
        dk = jnp.zeros((block, LANES), f32)
        dv = jnp.zeros((block, LANES), f32)
        for head in (0, 1):
            pick = lambda a, b: jnp.where(low_k, a, b) if head == 0 else jnp.where(low_k, b, a)
            prob = jnp.exp2(dot(query_a[head], pick(keys, side), NT))
            change = dot(grad_a[head], pick(values, one), NT)
            score_grad = (prob * change).astype(bf16)
            dv += dot(prob.astype(bf16), grad_m[head], TN)
            dk += dot(score_grad, query_m[head], TN)
            dq += dot(score_grad, pick(keys, nought))
        exchange.put(pair, number, block, (dk * LN2).astype(bf16), dv.astype(bf16))
    return (dq * HALF**-0.5).astype(bf16)


class Exchange:
    def __init__(self, here, rows, refs):
        self.here, self.rows = here, rows
        self.sums, self.send, self.got_core, self.across, self.got_x = refs[:5]
        self.sems = refs[5]

    def turns(self, blocks):
        return (3, 1, 0, 2) if blocks == 4 else tuple(reversed(range(blocks)))

    def copy_core(self, pair, far):
        rows = pl.ds(far * self.rows, self.rows)
        return pltpu.make_async_remote_copy(
            src_ref=self.send.at[pair % 2, :, rows, :],
            dst_ref=self.got_core.at[pair, :, rows, :],
            send_sem=self.sems.at[2 * far, pair],
            recv_sem=self.sems.at[2 * far + 1, pair],
            device_id=self.here.partner("core"),
            device_id_type=MESH,
        )

    def copy_x(self, pair):
        return pltpu.make_async_remote_copy(
            src_ref=self.across.at[pair],
            dst_ref=self.got_x.at[pair],
            send_sem=self.sems.at[4, pair],
            recv_sem=self.sems.at[5, pair],
            device_id=self.here.partner("x"),
            device_id_type=MESH,
        )

    def end(self):
        pairs = self.got_x.shape[0]
        for pair in range(pairs):
            if pair >= pairs - 2:
                self.free(pair)
            self.copy_x(pair).wait_send()

    def free(self, pair):
        for far in (0, 1):
            self.copy_core(pair, far).wait_send()

    def put(self, pair, number, block, dk, dv):
        half = 2 * self.rows
        there = pl.ds(number * block % half, block)
        ref, slot = (self.sums, pair) if number * block < half else (self.send, pair % 2)
        ref[slot, 0, there, :] = dk
        ref[slot, 1, there, :] = dv
        if 2 * half == 4 * block:
            if number == 3:
                self.copy_core(pair, 1).start()
            elif number == 2:
                self.copy_core(pair, 0).start()
            elif number == 0:
                self.pass_on(pair)
        elif number == 1:
            for far in (1, 0):
                self.copy_core(pair, far).start()
        else:
            self.pass_on(pair)

    def pass_on(self, pair):
        rows = self.rows
        self.copy_core(pair, 1).wait_recv()
        far = pl.ds(rows, rows)
        for i in (0, 1):
            self.across[pair, i] = self.sums[pair, i, far, :] + self.got_core[pair, i, far, :]
        self.copy_x(pair).start()

    def take(self, pair, out_ref):
        near = pl.ds(0, self.rows)
        self.copy_core(pair, 0).wait_recv()
        self.copy_x(pair).wait_recv()
        for i in (0, 1):
            out_ref[pair, i] = (
                self.sums[pair, i, near, :].astype(f32)
                + self.got_core[pair, i, near, :].astype(f32)
                + self.got_x[pair, i].astype(f32)
            ).astype(bf16)


def exchange_scratch(pairs, rows):
    return [
        pltpu.VMEM((pairs, 2, 2 * rows, LANES), bf16),
        pltpu.VMEM((2, 2, 2 * rows, LANES), bf16),
        pltpu.VMEM((pairs, 2, 2 * rows, LANES), bf16),
        pltpu.VMEM((pairs, 2, rows, LANES), bf16),
        pltpu.VMEM((pairs, 2, rows, LANES), bf16),
        pltpu.SemaphoreType.DMA((6, pairs)),
    ]


def fill_keys(keys_at, values_at, kv_ref):
    rows = kv_ref.shape[3]
    for part in range(kv_ref.shape[0]):
        there = pl.ds(part * rows, rows)
        keys_at[there, :] = kv_ref[part, 0, 0]
        values_at[there, :] = kv_ref[part, 0, 1]


def selves_kernel(pairs, plan, blocks, *refs):
    orders, ends, stages = plan
    large_refs, kv_large, refs = refs[:6], refs[6], refs[7:]
    small_refs, kv_small, refs = refs[:6], refs[6], refs[7:]
    flows = len(orders)
    locals_, refs = refs[:flows], refs[flows:]
    dq_l, dkv_l, dq_s, dkv_s = refs[:4]
    sums, refs = refs[4 : 4 + flows], refs[4 + flows :]
    keys_l, values_l, keys_s, values_s = refs[:4]
    ex_l, ex_s, refs = refs[4:10], refs[10:16], refs[16:]
    here = Here()
    rows_l, rows_s = keys_l.shape[0] // 4, keys_s.shape[0] // 4
    large, small = Exchange(here, rows_l, ex_l), Exchange(here, rows_s, ex_s)
    refs = list(refs)
    running = [
        Flow(here, orders[flow], locals_[flow], refs, True, ends[flow]) for flow in range(flows)
    ]
    step = pl.program_id(0)

    @pl.when(step == 0)
    def _():
        here.greet(ALL_PARTNERS)
        for flow in running:
            flow.act(0)

    def attention(exchange, pair, refs, kv_ref, keys_at, values_at, block, dq_ref):
        q_ref, do_ref, o_ref, l_ref, mq_ref, mk_ref = refs
        fill_keys(keys_at, values_at, kv_ref)

        @pl.when(pair >= 2)
        def _():
            exchange.free(pair - 2)

        dq_ref[...] = pair_back(
            q_ref[0], do_ref[...], o_ref[0], l_ref[0], mq_ref[...], keys_at, values_at, mk_ref,
            block, exchange, pair,
        )

    half = pairs // 2
    late = step >= half + pairs

    @pl.when((step >= half) & (step < half + pairs))
    def _():
        pair = step - half
        attention(large, pair, large_refs, kv_large, keys_l, values_l, blocks[0], dq_l)

    @pl.when((step < half) | late)
    def _():
        pair = jnp.where(late, step - pairs, step)
        attention(small, pair, small_refs, kv_small, keys_s, values_s, blocks[1], dq_s)

    takes = [(half + 1 + i, small, i, dkv_s) for i in range(half)]
    takes += [(half + 3 + i, large, i, dkv_l) for i in range(pairs - 1)]
    for when, exchange, pair, out_ref in takes:

        @pl.when(step == when)
        def _(exchange=exchange, pair=pair, out_ref=out_ref):
            exchange.take(pair, out_ref)

    for at in range(2 * pairs):
        todo = []
        for flow in range(flows):
            for stage, when in enumerate(stages[flow]):
                if when == at:
                    todo.append((running[flow], stage + 1))
        if todo:

            @pl.when(step == at)
            def _(todo=todo):
                for flow, stage in todo:
                    flow.act(stage)

    @pl.when(step == 2 * pairs - 1)
    def _():
        large.take(pairs - 1, dkv_l)
        for pair in range(half, pairs):
            small.take(pair, dkv_s)
        small.end()
        large.end()
        for flow, sum_ref in zip(running, sums):
            sum_ref[...] = flow.result()


def selves_back(large, large_kv, small, small_kv, flows, orders, ends, stages):
    count, width = large[1].shape
    few = small[1].shape[0]
    pairs = width // LANES
    total, less = large[5].shape[0], small[5].shape[0]
    shapes = [flow.shape[1:] for flow in flows]
    results = [flow_result(*flow) for flow in zip(orders, shapes, ends)]
    blocks = (largest_block(total // 2, 512), largest_block(less // 2, 512))
    half = pairs // 2
    first = lambda i: jnp.clip(i - half, 0, pairs - 1)
    last = lambda i: jnp.where(i < half, i, jnp.maximum(i - pairs, half))
    in_specs = []
    for rows, keys, at in ((count, total, first), (few, less, last)):
        major = pl.BlockSpec((1, rows, LANES), lambda i, at=at: (at(i), 0, 0))
        minor = pl.BlockSpec((rows, LANES), lambda i, at=at: (0, at(i)))
        in_specs += [major, minor, major, major, whole((rows, LANES)), whole((keys, LANES))]
        in_specs.append(
            pl.BlockSpec((4, 1, 2, rows, LANES), lambda i, at=at: (0, at(i), 0, 0, 0))
        )
    in_specs += [pl.BlockSpec(memory_space=pl.ANY)] * len(flows)
    shape = jax.ShapeDtypeStruct
    out_shape = [
        shape((count, width), bf16),
        shape((pairs, 2, count, LANES), bf16),
        shape((few, width), bf16),
        shape((pairs, 2, few, LANES), bf16),
    ] + results
    out_specs = [
        pl.BlockSpec((count, LANES), lambda i: (0, first(i))),
        whole((pairs, 2, count, LANES)),
        pl.BlockSpec((few, LANES), lambda i: (0, last(i))),
        whole((pairs, 2, few, LANES)),
    ] + [whole(result.shape) for result in results]
    scratch = [pltpu.VMEM((total, LANES), bf16)] * 2 + [pltpu.VMEM((less, LANES), bf16)] * 2
    scratch += exchange_scratch(pairs, count) + exchange_scratch(pairs, few)
    for flow in range(len(flows)):
        scratch += flow_scratch(orders[flow], shapes[flow], True, ends[flow])
    result = pl.pallas_call(
        functools.partial(selves_kernel, pairs, (orders, ends, stages), blocks),
        grid=(2 * pairs,),
        in_specs=in_specs,
        out_specs=out_specs,
        out_shape=out_shape,
        scratch_shapes=scratch,
        compiler_params=pltpu.CompilerParams(
            vmem_limit_bytes=60 << 20, collective_id=1, has_side_effects=True
        ),
        cost_estimate=pl.CostEstimate(
            flops=20 * width * (count * total + few * less),
            bytes_accessed=64 * count * width,
            transcendentals=count * total * width // HALF,
        ),
        name="selves_back",
    )(*large, large_kv, *small, small_kv, *flows)
    return result[:4], result[4:]


LAST_ORDERS = (BY_YX, BY_X, BY_ZL)
GAIN_ORDER = ("core", "y", "x", "zl", "zh")
LATE_ORDERS = (("x",), ("x", "zh"), ("x",))
LATE_STAGES = (
    {2: 2, 4: 3},
    {2: 2, 3: 3, 4: 4},
    {2: 2, 4: 3},
)


def last_kernel(pairs, sizes, late, *refs):
    refs = list(refs)
    take = lambda count: [refs.pop(0) for _ in range(count)]
    given, late_refs = take(13), take(late)
    gain, second_gain, query_gain, context_gain = take(4)
    gl_ref, gs_ref = take(2)
    sum_refs = take(3 + late)
    (gain_ref,) = take(1)
    held = take(13)
    dql, dkvl, dqs, dkvs, nl, ns, wq, wk, wv, xl, xs, hl, hs = held
    load_sems, normed, *grads = take(5)
    large_back, small_back = take(3), take(3)
    here = Here()
    flows = []
    for order in LAST_ORDERS:
        flows.append(Flow(here, order, refs.pop(0), refs, False, True))
    late_flows = [
        Flow(here, order, ref, refs, True, True) for order, ref in zip(LATE_ORDERS, late_refs)
    ]
    state, got, gain_sems = refs
    large, small = sizes
    top, bottom = pl.ds(0, large), pl.ds(large, small)
    loads = [
        pltpu.make_async_copy(source, there, load_sems.at[i])
        for i, (source, there) in enumerate(zip(given, held))
    ]
    for load in loads:
        load.start()
    here.greet_line("x", "y")
    for flow in late_flows:
        flow.act(0)
    homes = [Restore(here, *large_back), Restore(here, *small_back)]

    def gain_copy(step):
        return pltpu.make_async_remote_copy(
            src_ref=state.at[step],
            dst_ref=got.at[step],
            send_sem=gain_sems.at[0, step],
            recv_sem=gain_sems.at[1, step],
            device_id=here.partner(GAIN_ORDER[step]),
            device_id_type=MESH,
        )

    for load in loads[:6]:
        load.wait()
    normed[top, :] = nl[...]
    normed[bottom, :] = ns[...]
    for which, flow in enumerate(flows):
        if which == 0:
            grads[0][top, :] = dql[...]
            grads[0][bottom, :] = dqs[...]
        else:
            for pair in range(pairs):
                lanes = pl.ds(pair * LANES, LANES)
                grads[which][top, lanes] = dkvl[pair, which - 1]
                grads[which][bottom, lanes] = dkvs[pair, which - 1]
        value = dot(normed[...], grads[which][...], TN).astype(bf16)
        rows, wide = flow.local.shape[1:]
        for at, (core, y, tm) in enumerate(spots(flow.order)):
            first = tm * 2 * rows + core * rows
            flow.local[at] = value[first : first + rows, y * wide : (y + 1) * wide]
        flow.act(0)
    total = None
    for which, weight in enumerate((wq, wk, wv)):
        loads[6 + which].wait()
        part = dot(grads[which][...], weight[...], NT)
        total = part if total is None else total + part
    for load in loads[9:]:
        load.wait()
    for flow in late_flows:
        flow.act(1)
    extra, gain_l = norm_back(total[:large], xl[...].astype(f32), gain[...])
    large_back[0][...] = (hl[...] + extra).astype(bf16)
    homes[0].start()
    for flow in flows:
        flow.act(1)
    extra, gain_s = norm_back(total[large:], xs[...].astype(f32), gain[...])
    small_back[0][...] = (hs[...] + extra).astype(bf16)
    homes[1].start()
    state[0] = jnp.zeros(state.shape[1:], f32)
    for row, value in enumerate(
        (gain_l + gain_s, second_gain[...], query_gain[...], context_gain[...])
    ):
        state[0, row : row + 1, :] = value
    gain_copy(0).start()
    for stage in range(1, 8):
        if stage > 1:
            for flow in flows:
                flow.act(stage)
        for flow, stages in zip(late_flows, LATE_STAGES):
            if stage in stages:
                flow.act(stages[stage])
        if stage <= 5:
            gain_copy(stage - 1).wait()
            total = state[stage - 1] + got[stage - 1]
            if stage < 5:
                state[stage] = total
                gain_copy(stage).start()
            else:
                wide = total.shape[1]
                turned = pltpu.roll(total, lax.rem(wide - here.tm * (wide // 8), wide), 1)
                gain_ref[...] = turned[:, : gain_ref.shape[1]]
    for flow, sum_ref in zip(flows + late_flows, sum_refs):
        sum_ref[...] = flow.result()
    homes[0].finish()
    gl_ref[...] = large_back[1][...]
    homes[1].finish()
    gs_ref[...] = small_back[1][...]


def last_sums(given, late, gains):
    count, width = given[0].shape
    few = given[2].shape[0]
    block = (width // 16, width // 2)
    shape = jax.ShapeDtypeStruct
    tokens = count + few
    scratch = [pltpu.VMEM(value.shape, value.dtype) for value in given]
    scratch += [pltpu.SemaphoreType.DMA((len(given),))]
    scratch += [pltpu.VMEM((tokens, width), bf16)] * 4
    scratch += restore_scratch(count // 2, width) + restore_scratch(few // 2, width)
    for order in LAST_ORDERS:
        scratch.append(pltpu.VMEM((32,) + block, bf16))
        scratch += flow_scratch(order, block, False, True)
    for order, local in zip(LATE_ORDERS, late):
        scratch += flow_scratch(order, local.shape[1:], True, True)
    scratch += [
        pltpu.VMEM((5, 8, width), f32),
        pltpu.VMEM((5, 8, width), f32),
        pltpu.SemaphoreType.DMA((2, 5)),
    ]
    anywhere = pl.BlockSpec(memory_space=pl.ANY)
    vmem = pl.BlockSpec(memory_space=pltpu.VMEM)
    result = pl.pallas_call(
        functools.partial(last_kernel, width // LANES, (count, few), len(late)),
        in_specs=[anywhere] * (len(given) + len(late)) + [vmem] * 4,
        out_shape=[
            shape((2, count // 2, width), bf16),
            shape((2, few // 2, width), bf16),
        ]
        + [shape((4,) + block, bf16)] * 3
        + [shape((4,) + local.shape[1:], bf16) for local in late]
        + [shape((8, LANES), f32)],
        scratch_shapes=scratch,
        compiler_params=pltpu.CompilerParams(
            vmem_limit_bytes=60 << 20, collective_id=2, has_side_effects=True
        ),
        cost_estimate=pl.CostEstimate(
            flops=40 * tokens * width * width,
            bytes_accessed=40 * tokens * width,
            transcendentals=0,
        ),
        name="last_sums",
    )(*given, *late, *gains)
    return result[:2], result[2:5], result[5:-1], result[-1]


def results_kernel(*refs):
    outs, given, sems = refs[12:29], refs[29:41], refs[41]
    loads = [
        pltpu.make_async_copy(source, there, sems.at[i])
        for i, (source, there) in enumerate(zip(refs, given))
    ]
    for load in loads:
        load.start()
    for load in loads:
        load.wait()
    united, large, small, q, k, v, up, down, output, first, other, gains = given
    for source, there in zip((united, large, small), outs[:3]):
        there[...] = source[...].astype(there.dtype)
    for source, there in zip((q, k, v, output), (outs[4], outs[5], outs[6], outs[7])):
        rows, wide = source.shape[1:]
        for at in range(4):
            core, y = at // 2, at % 2
            there[core * rows : (core + 1) * rows, y * wide : (y + 1) * wide] = source[at].astype(f32)
    rows, wide = up.shape[1:]
    for at in range(4):
        outs[9][:, at * wide : (at + 1) * wide] = up[at].astype(f32)
        outs[10][at * rows : (at + 1) * rows, :] = down[at].astype(f32)
        half = rows // 2
        there = slice(at % 2 * half, (at % 2 + 1) * half)
        (outs[16] if at < 2 else outs[13])[there, :] = first[at].astype(f32)
        (outs[14] if at < 2 else outs[15])[there, :] = other[at].astype(f32)
    for row, at in enumerate((3, 8, 11, 12)):
        outs[at][...] = gains[row : row + 1, : outs[at].shape[1]]


def results(united, large, small, last, late, first, other, gains):
    shape = jax.ShapeDtypeStruct
    rows, width = late[0].shape[1:]
    square, vector = shape((rows, width), f32), shape((1, rows), f32)
    given = (united, large, small, *last, *late, first, other, gains)
    out = pl.pallas_call(
        results_kernel,
        in_specs=[pl.BlockSpec(memory_space=pl.ANY)] * len(given),
        scratch_shapes=[pltpu.VMEM(value.shape, value.dtype) for value in given]
        + [pltpu.SemaphoreType.DMA((len(given),))],
        out_shape=[
            shape(united.shape, bf16), shape(large.shape, f32), shape(small.shape, f32), vector,
            square, square, square, square, vector,
            shape((rows, 4 * width), f32), shape((4 * rows, width), f32), vector, vector,
            square, square, square, square,
        ],
        compiler_params=pltpu.CompilerParams(vmem_limit_bytes=60 << 20),
        cost_estimate=pl.CostEstimate(flops=0, bytes_accessed=14 << 20, transcendentals=0),
        name="results",
    )(*given)
    return tuple(value.reshape(rows) if value.shape == (1, rows) else value for value in out)


def cross_kernel(pairs, block, *refs):
    (q_ref, do_ref, o_ref, l_ref, mq_ref, mk_ref), refs = refs[:6], refs[6:]
    kv_ref, given, gains, refs = refs[0], refs[1:11], refs[11:13], refs[13:]
    view_ref, gl_ref, gs_ref, a_ref, b_ref, gain_l_ref, gain_s_ref = refs[:7]
    keys_at, values_at, exchange_refs, refs = refs[7], refs[8], refs[9:15], refs[15:]
    dkv, dq, dk, dv = refs[:4]
    held, sems, home_refs = refs[4:14], refs[14], refs[15:18]
    united, wo, merged_l, asked, context, grad_out, merged_s, wq, wk, wv = held
    here = Here()
    exchange = Exchange(here, keys_at.shape[0] // 4, exchange_refs)
    step = pl.program_id(0)
    loads = [
        pltpu.make_async_copy(source, there, sems.at[i])
        for i, (source, there) in enumerate(zip(given, held))
    ]

    @pl.when(step == 0)
    def _():
        for load in loads:
            load.start()
        here.greet_line("x")

    home = Restore(here, *home_refs)

    @pl.when(step == 1)
    def _():
        for load in loads[:3]:
            load.wait()
        wide = jnp.concatenate([united[i] for i in range(pairs)], axis=1)
        home_refs[0][...] = (merged_l[...] + dot(wide, wo[...])).astype(bf16)
        home.start()

    fill_keys(keys_at, values_at, kv_ref)

    @pl.when(step >= 2)
    def _():
        exchange.free(step - 2)

    dq[step] = pair_back(
        q_ref[0], do_ref[...], o_ref[0], l_ref[0], mq_ref[...], keys_at, values_at, mk_ref,
        block, exchange, step,
    )

    @pl.when(step >= 3)
    def _():
        exchange.take(step - 3, dkv)

    def lay(out_ref, which, value, order):
        left = 32 // out_ref.shape[0]
        rows = out_ref.shape[1] // left
        for at, (core, y, tm) in enumerate(spots(order)):
            if core == which:
                first, there = (tm * 2 + y) * rows, at % left * rows
                out_ref[at // left, there : there + rows, :] = value[first : first + rows]

    @pl.when(step == pairs - 1)
    def _():
        for load in loads[3:]:
            load.wait()
        grads = jnp.concatenate([united[i] for i in range(pairs)], axis=1)
        lay(a_ref, 0, dot(grads, grad_out[...], TN).astype(bf16), BY_Y)
        grads = jnp.concatenate([dq[i] for i in range(pairs)], axis=1)
        lay(a_ref, 1, dot(asked[...], grads, TN).astype(bf16), BY_Y)
        extra, gain_l_ref[...] = norm_back(dot(grads, wq[...], NT), merged_l[...], gains[0][...])
        gl_ref[...] = grad_out[...].astype(f32) + extra
        for pair in range(pairs - 3, pairs):
            exchange.take(pair, dkv)
        for pair in range(pairs):
            lanes = pl.ds(pair * LANES, LANES)
            dk[:, lanes] = dkv[pair, 0]
            dv[:, lanes] = dkv[pair, 1]
        lay(b_ref, 0, dot(context[...], dk[...], TN).astype(bf16), BY_ZL)
        lay(b_ref, 1, dot(context[...], dv[...], TN).astype(bf16), BY_ZL)
        grad = dot(dk[...], wk[...], NT) + dot(dv[...], wv[...], NT)
        gs_ref[...], gain_s_ref[...] = norm_back(grad, merged_s[...], gains[1][...])
        exchange.end()
        home.finish()
        view_ref[...] = home_refs[1][...]


def cross_back(attention, kv, given, gains):
    count, width = attention[1].shape
    few = kv.shape[3]
    major = pl.BlockSpec((1, count, LANES), lambda i: (i, 0, 0))
    pairs = width // LANES
    total = attention[5].shape[0]
    block = largest_block(total // 2, 512)
    shape = jax.ShapeDtypeStruct
    laid = (4, 8 * width // 16, width)
    return pl.pallas_call(
        functools.partial(cross_kernel, pairs, block),
        grid=(pairs,),
        in_specs=[major, columns(count, 0), major, major]
        + [whole((count, LANES)), whole((total, LANES))]
        + [pl.BlockSpec((4, 1, 2, few, LANES), lambda i: (0, i, 0, 0, 0))]
        + [pl.BlockSpec(memory_space=pl.ANY)] * len(given)
        + [whole((1, width))] * 2,
        out_specs=[
            whole((2, count // 2, width)), whole((count, width)), whole((few, width)), whole(laid), whole(laid),
            whole((1, width)), whole((1, width)),
        ],
        out_shape=[
            shape((2, count // 2, width), bf16),
            shape((count, width), f32), shape((few, width), f32), shape(laid, bf16), shape(laid, bf16),
            shape((1, width), f32), shape((1, width), f32),
        ],
        scratch_shapes=[pltpu.VMEM((total, LANES), bf16)] * 2
        + exchange_scratch(pairs, few)
        + [pltpu.VMEM((pairs, 2, few, LANES), bf16), pltpu.VMEM((pairs, count, LANES), bf16)]
        + [pltpu.VMEM((few, width), bf16)] * 2
        + [pltpu.VMEM(value.shape, value.dtype) for value in given]
        + [pltpu.SemaphoreType.DMA((len(given),))]
        + restore_scratch(count // 2, width),
        compiler_params=pltpu.CompilerParams(
            vmem_limit_bytes=60 << 20, collective_id=3, has_side_effects=True
        ),
        cost_estimate=pl.CostEstimate(
            flops=20 * width * count * total,
            bytes_accessed=64 * count * width,
            transcendentals=count * total * width // HALF,
        ),
        name="cross_back",
    )(*attention, kv, *given, *gains)


def attend_pair(pair, q_ref, kv, mq_ref, mk_ref, spaces, o_ref, l_ref):
    parts, rows = kv.shape[0], kv.shape[3]
    total = parts * rows
    ka0, ka1, va0, va1 = (space.at[pl.ds(0, total), :] for space in spaces)
    low = lax.broadcasted_iota(jnp.int32, (rows, LANES), 1) < HALF
    for part in range(parts):
        here = pl.ds(part * rows, rows)
        keys, values, mask = kv[part, pair, 0], kv[part, pair, 1], mk_ref[here, :]
        one = jnp.ones_like(values)
        ka0[here, :] = jnp.where(low, keys, mask)
        ka1[here, :] = jnp.where(low, mask, keys)
        va0[here, :] = jnp.where(low, values, one)
        va1[here, :] = jnp.where(low, one, values)
    count = q_ref.shape[1]
    block = largest_block(count, 256)
    low = lax.broadcasted_iota(jnp.int32, (block, LANES), 1) < HALF
    for number in range(count // block):
        here = pl.ds(number * block, block)
        query, mask = q_ref[pair, here, :], mq_ref[here, :]
        tops, sums = [], []
        for head, keys, values in ((0, ka0, va0), (1, ka1, va1)):
            mine = jnp.where(low, query, mask) if head == 0 else jnp.where(low, mask, query)
            score = dot(mine, keys[...], NT)
            top = jnp.max(score, axis=1, keepdims=True)
            weight = jnp.exp2(score - top).astype(bf16)
            sums.append(dot(weight, values[...]))
            tops.append(jnp.broadcast_to(top, (block, LANES)))
        total = jnp.where(low, sums[1], sums[0])
        top = jnp.where(low, tops[1], tops[0])
        out = jnp.where(low, sums[0], sums[1])
        o_ref[pair, here, :] = (out / pltpu.roll(total, HALF, 1)).astype(bf16)
        l_ref[pair, here, :] = top + jnp.log2(total)


class Gather:
    def __init__(self, here, kv, sems):
        self.here, self.kv, self.sems = here, kv, sems

    def copy(self, kind, at, size, sem):
        source, there = ((0, 1), (0, 2), (1, 3))[kind]
        pairs = pl.ds(at, size)
        return pltpu.make_async_remote_copy(
            src_ref=self.kv.at[source, pairs],
            dst_ref=self.kv.at[there, pairs],
            send_sem=self.sems.at[0, 3 * sem + kind],
            recv_sem=self.sems.at[1, 3 * sem + kind],
            device_id=self.here.partner(("x", "core", "core")[kind]),
            device_id_type=MESH,
        )


def begin_kernel(pairs, *refs):
    refs = list(refs)
    take = lambda count: [refs.pop(0) for _ in range(count)]
    large_ref, small_ref, cot_ref, clip_ref = take(4)
    weight_refs = take(9)
    (gains,) = take(1)
    first_gain, second_gain, query_gain, context_gain = (
        gains.at[i : i + 1, :] for i in range(4)
    )
    xl_out, xs_out, cot_out, kvl_out, kvs_out, ckv_out = take(6)
    nl_ref, ns_ref, ql_ref, qs_ref, ol_ref, ll_ref, os_ref, ls_ref = take(8)
    merged_ref, hidden_ref, second_ref, active_ref, slope_ref, context_ref = take(6)
    mql_ref, mkl_ref, mqs_ref, mks_ref = take(4)
    for gain, gain_out in zip((first_gain, second_gain, query_gain, context_gain), take(4)):
        gain_out[...] = gain[...]
    (grad_ref,) = take(1)
    xl, xs, cot, clip, kvl, kvs, ckv = take(7)
    wq, wk, wv, wo, up, down, wck, wcv, wco = weights = take(9)
    spaces = take(4)
    wide, total = take(2)
    move_sems, gather_l, gather_s, gather_c, gather_clip, load_sems, out_sems = take(7)
    near_l, near_s, near_c, x_sems = take(4)
    here = Here()
    z, core = here.tm // 2, here.bit["core"]
    stay = core == z // 2

    here.greet_line("x")

    odd = lax.rem(z, 2)
    from_seq = (odd, 1 - odd)

    def far(which, turn, source, there):
        rows = source.shape[1]
        place = (
            (2 * core + from_seq[turn]) * 2 + here.bit["x"],
            here.bit["y"] * 2 + z // 2,
        )
        return pltpu.make_async_remote_copy(
            src_ref=source.at[from_seq[turn]],
            dst_ref=there.at[pl.ds(turn * rows, rows)],
            send_sem=move_sems.at[0, 2 * which + turn],
            recv_sem=move_sems.at[1, 2 * which + turn],
            device_id=place,
            device_id_type=MESH,
        )

    def near(which, source, there):
        return pltpu.make_async_copy(
            source.at[from_seq[0]],
            there.at[pl.ds(0, source.shape[1])],
            move_sems.at[1, 2 * which],
        )

    def move(which, source, there):
        far(which, 1, source, there).start()

        @pl.when(stay)
        def _():
            near(which, source, there).start()

        @pl.when(jnp.logical_not(stay))
        def _():
            far(which, 0, source, there).start()

    def moved_out(which, source, there):
        far(which, 1, source, there).wait_send()

        @pl.when(jnp.logical_not(stay))
        def _():
            far(which, 0, source, there).wait_send()

    def moved_in(which, source, there):
        far(which, 1, source, there).wait_recv()

        @pl.when(stay)
        def _():
            near(which, source, there).wait()

        @pl.when(jnp.logical_not(stay))
        def _():
            far(which, 0, source, there).wait_recv()

    moves = ((0, clip_ref, clip.at[0, 0]), (1, small_ref, xs), (2, large_ref, xl), (3, cot_ref, cot))
    move(*moves[0])
    move(*moves[1])
    loads = [
        pltpu.make_async_copy(source, there, load_sems.at[i])
        for i, (source, there) in enumerate(zip(weight_refs, weights))
    ]
    for load in loads:
        load.start()
    moved_out(*moves[0])
    moved_out(*moves[1])
    move(*moves[2])
    outs = []

    def keep(source, there):
        copy = pltpu.make_async_copy(source, there, out_sems.at[len(outs)])
        copy.start()
        outs.append(copy)

    def split(kv, part, value, key_weight, value_weight):
        keys = dot(value, key_weight[...]).astype(bf16)
        values = dot(value, value_weight[...]).astype(bf16)
        for pair in range(pairs):
            lanes = slice(pair * LANES, (pair + 1) * LANES)
            kv[part, pair, 0] = keys[:, lanes]
            kv[part, pair, 1] = values[:, lanes]

    def to_x(which, source, there):
        return pltpu.make_async_remote_copy(
            src_ref=source,
            dst_ref=there,
            send_sem=x_sems.at[0, which],
            recv_sem=x_sems.at[1, which],
            device_id=here.partner("x"),
            device_id_type=MESH,
        )

    x_small, x_large, x_cross = (
        to_x(0, ns_ref, near_s), to_x(1, nl_ref, near_l), to_x(2, context_ref, near_c)
    )

    def query_into(n_ref, q_ref):
        query = (dot(n_ref[...], wq[...]) * Q_SCALE).astype(bf16)
        for pair in range(pairs):
            q_ref[pair] = query[:, pair * LANES : (pair + 1) * LANES]

    large, small = Gather(here, kvl, gather_l), Gather(here, kvs, gather_s)
    cross, clips = Gather(here, ckv, gather_c), Gather(here, clip, gather_clip)

    moved_in(*moves[0])
    for kind in (0, 1):
        clips.copy(kind, 0, 1, 0).start()
    moved_in(*moves[1])
    keep(xs, xs_out)
    ns_ref[...] = norm(xs[...].astype(f32), first_gain[...])
    x_small.start()
    for i in (0, 1, 2):
        loads[i].wait()
    split(kvs, 0, ns_ref[...], wk, wv)
    small.copy(1, 0, pairs, 0).start()
    query_into(ns_ref, qs_ref)
    clips.copy(0, 0, 1, 0).wait_recv()
    clips.copy(2, 0, 1, 0).start()
    for kind in (1, 2):
        clips.copy(kind, 0, 1, 0).wait_recv()

    few = clip.shape[2]
    spot = lax.broadcasted_iota(jnp.int32, (1, LANES), 1) % HALF
    number = spot.astype(f32)
    some = spot < 4
    row = lax.broadcasted_iota(jnp.int32, (2 * few, few), 0) // 2
    twice = jnp.where(row == lax.broadcasted_iota(jnp.int32, (2 * few, few), 1), 1.0, 0.0)
    twice = twice.astype(bf16)
    for part in range(4):
        mine = clip[part, 0]
        for value, mk_ref, mq_ref in (
            (mine.astype(f32), mks_ref, mqs_ref),
            (dot(twice, mine), mkl_ref, mql_ref),
        ):
            rows = value.shape[0]
            mk_ref[pl.ds(part * rows, rows), :] = jnp.where(
                some & (value != number), NEGATIVE, 0.0
            ).astype(bf16)
            if part == 0:
                mq_ref[...] = jnp.where(some & (value == number), 1.0, 0.0).astype(bf16)

    x_small.wait_recv()
    split(kvs, 1, near_s[...], wk, wv)
    small.copy(2, 0, pairs, 0).start()
    moved_in(*moves[2])
    moved_out(*moves[2])
    move(*moves[3])
    keep(xl, xl_out)
    nl_ref[...] = norm(xl[...].astype(f32), first_gain[...])
    x_large.start()
    split(kvl, 0, nl_ref[...], wk, wv)
    large.copy(1, 0, pairs, 0).start()
    query_into(nl_ref, ql_ref)

    small.copy(1, 0, pairs, 0).wait_recv()
    small.copy(2, 0, pairs, 0).wait_recv()
    keep(kvs, kvs_out)

    def small_pair(pair, carry):
        attend_pair(pair, qs_ref, kvs, mqs_ref, mks_ref, spaces, os_ref, ls_ref)
        return carry

    lax.fori_loop(0, pairs, small_pair, 0)
    loads[3].wait()
    for pair in range(pairs):
        wide[:, pair * LANES : (pair + 1) * LANES] = os_ref[pair]
    hidden = xs[...].astype(f32) + dot(wide[...], wo[...])
    hidden_ref[...] = hidden
    second_ref[...] = norm(hidden, second_gain[...])
    total[...] = hidden
    loads[4].wait()
    loads[5].wait()
    width = wide.shape[1]
    steps = up.shape[1] // width
    for step in range(steps):
        lanes = slice(step * width, (step + 1) * width)
        active, slope = gelu_both(dot(second_ref[...], up[:, lanes]))
        active = active.astype(bf16)
        active_ref[:, lanes] = active
        slope_ref[:, lanes] = slope.astype(bf16)
        total[...] += dot(active, down[lanes, :])
    merged = total[...]
    merged_ref[...] = merged
    context = norm(merged, context_gain[...])
    context_ref[...] = context
    x_cross.start()
    x_large.wait_recv()
    split(kvl, 1, near_l[...], wk, wv)
    large.copy(2, 0, pairs, 0).start()
    loads[6].wait()
    loads[7].wait()
    split(ckv, 0, context, wck, wcv)
    cross.copy(1, 0, pairs, 0).start()

    def large_pair(pair, carry):
        attend_pair(pair, ql_ref, kvl, mql_ref, mkl_ref, spaces, ol_ref, ll_ref)
        return carry

    large.copy(1, 0, pairs, 0).wait_recv()
    large.copy(2, 0, pairs, 0).wait_recv()
    keep(kvl, kvl_out)
    lax.fori_loop(0, pairs // 2, large_pair, 0)
    x_cross.wait_recv()
    split(ckv, 1, near_c[...], wck, wcv)
    cross.copy(2, 0, pairs, 0).start()
    moved_in(*moves[3])
    moved_out(*moves[3])
    keep(cot, cot_out)
    loads[8].wait()
    grad_ref[...] = dot(cot[...], wco[...], NT).astype(bf16)
    lax.fori_loop(pairs // 2, pairs, large_pair, 0)
    cross.copy(1, 0, pairs, 0).wait_recv()
    cross.copy(2, 0, pairs, 0).wait_recv()
    keep(ckv, ckv_out)
    for kind in (0, 1, 2):
        clips.copy(kind, 0, 1, 0).wait_send()
        if kind:
            for gathered in (small, large, cross):
                gathered.copy(kind, 0, pairs, 0).wait_send()
    for copy in (x_small, x_large, x_cross):
        copy.wait_send()
    for copy in outs:
        copy.wait()


def begin(large, small, cotangent, clip, weights, gains):
    seqs, count, width = large.shape
    few = small.shape[1]
    count, few = 2 * count, 2 * few
    pairs = width // LANES
    hidden = weights[4].shape[1]
    shape = jax.ShapeDtypeStruct
    kv_l, kv_s = (4, pairs, 2, count, LANES), (4, pairs, 2, few, LANES)
    anywhere = pl.BlockSpec(memory_space=pl.ANY)
    vmem = pl.BlockSpec(memory_space=pltpu.VMEM)
    out_shape = [
        shape((count, width), bf16),
        shape((few, width), bf16),
        shape((count, width), bf16),
        shape(kv_l, bf16),
        shape(kv_s, bf16),
        shape(kv_s, bf16),
        shape((count, width), bf16),
        shape((few, width), bf16),
        shape((pairs, count, LANES), bf16),
        shape((pairs, few, LANES), bf16),
        shape((pairs, count, LANES), bf16),
        shape((pairs, count, LANES), f32),
        shape((pairs, few, LANES), bf16),
        shape((pairs, few, LANES), f32),
        shape((few, width), f32),
        shape((few, width), f32),
        shape((few, width), bf16),
        shape((few, hidden), bf16),
        shape((few, hidden), bf16),
        shape((few, width), bf16),
        shape((count, LANES), bf16),
        shape((4 * count, LANES), bf16),
        shape((few, LANES), bf16),
        shape((4 * few, LANES), bf16),
        *[shape((1, width), f32)] * 4,
        shape((count, width), bf16),
    ]
    dma = pltpu.SemaphoreType.DMA
    scratch = [
        pltpu.VMEM((count, width), bf16),
        pltpu.VMEM((few, width), bf16),
        pltpu.VMEM((count, width), bf16),
        pltpu.VMEM((4, 1, few, LANES), bf16),
        pltpu.VMEM(kv_l, bf16),
        pltpu.VMEM(kv_s, bf16),
        pltpu.VMEM(kv_s, bf16),
    ]
    scratch += [pltpu.VMEM(weight.shape, bf16) for weight in weights]
    scratch += [pltpu.VMEM((4 * count, LANES), bf16)] * 4
    scratch += [pltpu.VMEM((few, width), bf16), pltpu.VMEM((few, width), f32)]
    scratch += [dma((2, 8))] + [dma((2, 3))] * 4 + [dma((9,)), dma((6,))]
    scratch += [
        pltpu.VMEM((count, width), bf16),
        pltpu.VMEM((few, width), bf16),
        pltpu.VMEM((few, width), bf16),
        dma((2, 3)),
    ]
    return pl.pallas_call(
        functools.partial(begin_kernel, pairs),
        in_specs=[anywhere] * 13 + [vmem],
        out_specs=[anywhere] * 6 + [vmem] * 23,
        out_shape=out_shape,
        scratch_shapes=scratch,
        compiler_params=pltpu.CompilerParams(
            vmem_limit_bytes=62 << 20, collective_id=4, has_side_effects=True
        ),
        cost_estimate=pl.CostEstimate(
            flops=16 * count * 4 * count * width + 18 * few * width * hidden,
            bytes_accessed=40 << 20,
            transcendentals=count * count * 4 * width // HALF,
        ),
        name="begin",
    )(large, small, cotangent, clip, *weights, gains)


def cross_attend_kernel(q_ref, kv_ref, mq_ref, mk_ref, o_ref, l_ref, *spaces):
    attend_pair(0, q_ref, kv_ref, mq_ref, mk_ref, spaces, o_ref, l_ref)


def cross_attend(query, kv, mask_q, mask_k):
    pairs, count = query.shape[:2]
    rows = kv.shape[3]
    one = pl.BlockSpec((1, count, LANES), lambda i: (i, 0, 0))
    return pl.pallas_call(
        cross_attend_kernel,
        grid=(pairs,),
        in_specs=[
            one,
            pl.BlockSpec((4, 1, 2, rows, LANES), lambda i: (0, i, 0, 0, 0)),
            whole((count, LANES)),
            whole((4 * rows, LANES)),
        ],
        out_specs=[one, one],
        out_shape=[
            jax.ShapeDtypeStruct(query.shape, bf16),
            jax.ShapeDtypeStruct(query.shape, f32),
        ],
        scratch_shapes=[pltpu.VMEM((4 * rows, LANES), bf16)] * 4,
        compiler_params=pltpu.CompilerParams(vmem_limit_bytes=40 << 20),
        cost_estimate=pl.CostEstimate(
            flops=64 * count * rows * pairs * LANES,
            bytes_accessed=32 * count * pairs * LANES,
            transcendentals=8 * count * rows * pairs,
        ),
        name="cross_attend",
    )(query, kv, mask_q, mask_k)


def after(value, *needed):
    return lax.optimization_barrier((value, needed))[0]


CROSS_ORDERS = (BY_Y[:2], BY_ZL[:2])
SELVES_ORDERS = (BY_Y_LATE[:4], BY_ZL[:3], BY_Y_LATE[:4], BY_Y[2:], BY_ZL[2:])
SELVES_ENDS = (False, False, False, True, True)
SELVES_STAGES = (
    (1, 6, 8, 11),
    (1, 6, 11),
    (1, 6, 8, 11),
    (3, 5, 7, 8, 9),
    (3, 5, 7, 8, 9),
)


def paired_end(views, normed, large, small, cross, merged, weights, crosses, gains):
    large_view, small_view = views
    large_normed, small_normed, asked, context = normed
    large_q, large_mixed, large_logsum, large_mask_q, large_mask_k, large_kv = large
    small_q, small_mixed, small_logsum, small_mask_q, small_mask_k, small_kv = small
    cross_q, united, cross_logsum, cross_kv, united_grad, grad_out = cross
    large_merged, large_saved, small_merged, small_saved = merged
    query_weight, key_weight, value_weight, output_weight, up_weight, down_weight = weights
    first_gain, second_gain, query_gain, context_gain = gains
    width = large_view.shape[1]
    rows = width // 8
    (
        united_view, large_grad, small_grad, first, other, query_gain_grad, context_gain_grad,
    ) = cross_back(
        (cross_q, united_grad, united, cross_logsum, large_mask_q, small_mask_k),
        cross_kv,
        (united, crosses[3], large_merged, asked, context, grad_out, small_merged) + crosses[:3],
        (query_gain, context_gain),
    )
    (
        large_hidden, small_hidden, large_mixed_grad, small_mixed_grad, up_grad, down_grad,
        output_grad, second_gain_grad, first, other,
    ) = back(
        large_grad, small_grad, large_saved, small_saved, [large_mixed], small_mixed, output_weight,
        second_gain, up_weight, down_weight, True, (first, other), CROSS_ORDERS,
    )
    still = (8, rows // 2, width)
    selves, sums = selves_back(
        (large_q, large_mixed_grad, large_mixed, large_logsum, large_mask_q, large_mask_k),
        large_kv,
        (small_q, small_mixed_grad, small_mixed, small_logsum, small_mask_q, small_mask_k),
        small_kv,
        (
            up_grad.reshape(16, 2 * rows, width), down_grad.reshape(8, 4 * rows, width),
            output_grad.reshape(16, rows, width // 2),
            first.reshape(still), other.reshape(still),
        ),
        SELVES_ORDERS, SELVES_ENDS, SELVES_STAGES,
    )
    up, down, output, first, other = sums
    (large_grad, small_grad), last, late, gains = last_sums(
        tuple(selves) + (large_normed, small_normed, query_weight, key_weight, value_weight)
        + (large_view, small_view, large_hidden, small_hidden),
        (
            up.reshape(2, rows, width), down.reshape(4, rows, width),
            output.reshape(2, rows // 2, width // 2),
        ),
        (first_gain, second_gain_grad, query_gain_grad, context_gain_grad),
    )
    return results(united_view, large_grad, small_grad, last, late, first, other, gains)


def per_device(tm, seq_size, *args):
    (
        large_view,
        small_view,
        clip_ids,
        first_gain,
        query_weight,
        key_weight,
        value_weight,
        output_weight,
        second_gain,
        up_weight,
        down_weight,
        query_gain,
        context_gain,
        cross_query,
        cross_key,
        cross_value,
        cross_output,
        cotangent,
    ) = args
    seqs, count, width = large_view.shape
    side = tm // 4
    gains = jnp.concatenate((first_gain, second_gain, query_gain, context_gain))
    gains = gains.astype(f32).reshape(4, width)
    first_gain, second_gain, query_gain, context_gain = (gains[i : i + 1] for i in range(4))

    tm_at = lax.axis_index("tm")
    seq_at = lax.axis_index("seq")
    z, x = tm_at // side, tm_at % side
    y, core = seq_at // 2, seq_at % 2
    places = [
        (pz, px, py, pc)
        for pz in range(4)
        for px in range(side)
        for py in range(2)
        for pc in range(2)
    ]

    def number(place):
        return (place[0] * side + place[1]) * seq_size + place[2] * 2 + place[3]

    def permute(value, place):
        pairs = [(number(at), number(place(*at))) for at in places]
        return lax.ppermute(value, ("tm", "seq"), pairs)

    def inverse(place):
        table = {place(*at): at for at in places}
        return lambda *at: table[at]

    go = (
        lambda z, x, y, c: (2 * c + z % 2, x, y, z // 2),
        lambda z, x, y, c: (2 * c + 1 - z % 2, x, y, z // 2),
    )
    back_home = tuple(inverse(place) for place in go)
    other_core = lambda value: permute(value, lambda z, x, y, c: (z, x, y, 1 - c))
    other_y = lambda value: permute(value, lambda z, x, y, c: (z, x, 1 - y, c))
    by_x = lambda value, d: permute(value, lambda z, x, y, c: (z, (x + d) % side, y, c))
    odd = z % 2 == 1

    def relocate(value):
        near = jnp.where(odd, value[1], value[0])
        far = jnp.where(odd, value[0], value[1])
        return jnp.concatenate([permute(near, go[0]), permute(far, go[1])], axis=0)

    def restore(value):
        rows = value.shape[0] // 2
        near, far = permute(value[:rows], back_home[0]), permute(value[rows:], back_home[1])
        return jnp.where(odd, jnp.stack([far, near]), jnp.stack([near, far]))

    def join(parts, axis):
        return parts[0] if len(parts) == 1 else jnp.concatenate(parts, axis=axis)

    def gather(value, axis=1):
        across = join([by_x(value, d) for d in range(1, side)], axis)
        return (value, across, other_core(value), other_core(across))

    def add(a, b):
        return (a.astype(f32) + b.astype(f32)).astype(bf16)

    def scatter_core(keep, send):
        return add(keep, other_core(send))

    def scatter_x(sums):
        rows = sums.shape[1] // side
        total = sums[:, :rows].astype(f32)
        for d in range(1, side):
            total = total + by_x(sums[:, d * rows : (d + 1) * rows], -d).astype(f32)
        return total.astype(bf16)

    if side == 2:
        clip = jnp.broadcast_to(
            clip_ids[:, ::2].astype(bf16)[:, :, None], (seqs, count // 2, LANES)
        )
        (
            large, small, grad_out, large_kv, small_kv, cross_kv, large_normed, small_normed,
            large_q, small_q, large_mixed, large_logsum, small_mixed, small_logsum, small_merged,
            *small_saved, context, large_mask_q, large_mask_k, small_mask_q, small_mask_k,
            first_gain, second_gain, query_gain, context_gain, united_grad,
        ) = begin(
            large_view, small_view, cotangent, clip,
            (query_weight, key_weight, value_weight, output_weight, up_weight, down_weight,
             cross_key, cross_value, cross_output),
            gains,
        )
        large_merged, *large_saved, asked, cross_q = rest(
            large, [large_mixed], output_weight, second_gain, up_weight, down_weight,
            query_gain, (cross_query,),
        )
        united, cross_logsum = cross_attend(cross_q, cross_kv, large_mask_q, small_mask_k)
        return paired_end(
            (large, small),
            (large_normed, small_normed, asked, context),
            (large_q, large_mixed, large_logsum, large_mask_q, large_mask_k, large_kv),
            (small_q, small_mixed, small_logsum, small_mask_q, small_mask_k, small_kv),
            (cross_q, united, cross_logsum, cross_kv, united_grad, grad_out),
            (large_merged, large_saved, small_merged, small_saved),
            (query_weight, key_weight, value_weight, output_weight, up_weight, down_weight),
            (cross_query, cross_key, cross_value, cross_output),
            (first_gain, second_gain, query_gain, context_gain),
        )

    groups = 3
    part = width // groups
    short_clips = gather(relocate(clip_ids[:, ::2].astype(f32)), 0)
    small = relocate(small_view)
    large = relocate(large_view)
    grad_out = relocate(after(cotangent, large))
    spot = lax.broadcasted_iota(jnp.int32, (1, LANES), 1) % HALF

    def mask_of_keys(numbers):
        away = numbers.astype(jnp.int32)[:, None] != spot
        return jnp.where((spot < 4) & away, NEGATIVE, 0.0).astype(bf16)

    def mask_of_queries(numbers):
        same = numbers.astype(jnp.int32)[:, None] == spot
        return jnp.where((spot < 4) & same, 1.0, 0.0).astype(bf16)

    short = jnp.concatenate(short_clips)
    small_mask_k = mask_of_keys(short)
    large_mask_k = mask_of_keys(jnp.repeat(short, 2))
    small_mask_q = mask_of_queries(short_clips[0])
    large_mask_q = mask_of_queries(jnp.repeat(short_clips[0], 2))

    small_normed, small_q, small_kv = front(
        small, first_gain, query_weight, key_weight, value_weight, 1
    )
    small_kv = gather(small_kv[0])
    large_normed, large_q, large_kv = front(
        large, first_gain, query_weight, key_weight, value_weight, groups
    )
    large_kv = [gather(kv) for kv in large_kv]
    small_mixed, small_logsum = attend(small_q, small_kv, small_mask_q, small_mask_k, 0, width)
    small_merged, *small_saved, context, cross_kv = rest(
        small, [small_mixed], output_weight, second_gain, up_weight, down_weight,
        context_gain, (cross_key, cross_value),
    )
    cross_kv = gather(cross_kv)
    united_grad = dot(grad_out, cross_output, NT).astype(bf16)
    large_out = ()
    for group, kv in enumerate(large_kv):
        large_out = attend(large_q, kv, large_mask_q, large_mask_k, group * part, part, large_out)
    large_mixed, large_logsum = large_out
    large_merged, *large_saved, asked, cross_q = rest(
        large, [large_mixed], output_weight, second_gain, up_weight, down_weight,
        query_gain, (cross_query,),
    )
    united, cross_logsum = attend(cross_q, cross_kv, large_mask_q, small_mask_k, 0, width)
    united_view = restore((large_merged + dot(united, cross_output)).astype(bf16))

    bits = side.bit_length() - 1
    moves = {"zh": lambda z, x, y, c: (z ^ 2, x, y, c), "zl": lambda z, x, y, c: (z ^ 1, x, y, c)}
    mine = {"zh": z // 2, "zl": z % 2}
    axes = {"zh": 0, "zl": 1}
    for bit in range(bits):
        flip = 1 << (bits - 1 - bit)
        moves[f"x{bit}"] = lambda z, x, y, c, flip=flip: (z, x ^ flip, y, c)
        mine[f"x{bit}"] = (x // flip) % 2
        axes[f"x{bit}"] = 2 + bit
    moves["core"] = lambda z, x, y, c: (z, x, y, 1 - c)
    moves["y"] = lambda z, x, y, c: (z, x, 1 - y, c)
    mine["core"], mine["y"] = core, y
    axes["core"], axes["y"] = 2 + bits, 3 + bits
    by_y = ["core", "y", "zl"] + [f"x{bit}" for bit in range(bits)] + ["zh"]
    by_zl = ["core", "zl", "y"] + [f"x{bit}" for bit in range(bits)] + ["zh"]
    by_yx = ["core", "y"] + [f"x{bit}" for bit in range(bits)] + ["zl", "zh"]

    class Sum:
        def __init__(self, local, order):
            rows, wide = local.shape
            self.value = local.reshape((2,) * (2 + bits) + (rows // tm, wide))
            self.todo = list(order)
            self.rows, self.wide = rows // tm, wide

        def step(self, *needed):
            name = self.todo.pop(0)
            axis = axes[name]
            size = self.value.shape[axis] // 2
            at = mine[name]
            keep = lax.dynamic_slice_in_dim(self.value, at * size, size, axis)
            send = lax.dynamic_slice_in_dim(self.value, (1 - at) * size, size, axis)
            self.value = add(keep, permute(send, moves[name]))
            return self.value

        def finish(self):
            while self.todo:
                self.step()
            value = self.value.reshape(self.rows // 2, self.wide // 2)
            other = other_y(value)
            value = jnp.where(
                y == 0,
                jnp.concatenate([value, other], axis=1),
                jnp.concatenate([other, value], axis=1),
            )
            other = other_core(value)
            return jnp.where(
                core == 0,
                jnp.concatenate([value, other], axis=0),
                jnp.concatenate([other, value], axis=0),
            ).astype(f32)

    cross_groups = 2
    cross_part = width // cross_groups
    dcq, dckv = [], []
    for group in range(cross_groups):
        query = after(cross_q, *dcq[-1:])
        at = group * cross_part
        dq, keep, send = attend_back(
            query, cross_kv, united_grad, united, cross_logsum,
            large_mask_q, small_mask_k, at, at, at, cross_part,
        )
        dcq.append(dq)
        dckv.append(scatter_x(scatter_core(keep, send)))
    dcq = jnp.concatenate(dcq, axis=1)
    dck = jnp.concatenate([kv[0] for kv in dckv], axis=1)
    dcv = jnp.concatenate([kv[1] for kv in dckv], axis=1)
    extra, query_gain_grad = norm_back(dot(dcq, cross_query, NT), large_merged, query_gain)
    large_merged_grad = grad_out.astype(f32) + extra
    small_merged_grad, context_gain_grad = norm_back(
        dot(dck, cross_key, NT) + dot(dcv, cross_value, NT), small_merged, context_gain
    )
    cross_parts = [
        dot(united, grad_out, TN).astype(bf16),
        dot(asked, dcq, TN).astype(bf16),
        dot(context, dck, TN).astype(bf16),
        dot(context, dcv, TN).astype(bf16),
    ]
    (
        large_hidden_grad,
        small_hidden_grad,
        large_mixed_grad,
        small_mixed_grad,
        up_grad,
        down_grad,
        output_grad,
        second_gain_grad,
    ) = back(
        large_merged_grad, small_merged_grad, large_saved, small_saved, [large_mixed], small_mixed,
        output_weight, second_gain, up_weight, down_weight, False,
    )
    cross_sum = Sum(jnp.concatenate(cross_parts, axis=1), by_y)
    up_sum = Sum(up_grad, by_y)
    down_sum = Sum(down_grad, by_zl)
    cross_sum.step()
    small_dq, keep, send = attend_back(
        after(small_q, cross_sum.value), small_kv, small_mixed_grad, small_mixed, small_logsum,
        small_mask_q, small_mask_k, 0, 0, 0, width,
    )
    small_sums = scatter_core(keep, send)
    up_sum.step()
    down_sum.step()
    cross_sum.step()
    needed = [small_dq, up_sum.value, down_sum.value]
    normed = jnp.concatenate([large_normed, small_normed], axis=0)
    last_sums, dqs, dkvs = [], [], []
    pending = None
    for group in range(groups):
        at = group * part
        dq, keep, send = attend_back(
            after(large_q, *needed), large_kv[group], large_mixed_grad, large_mixed, large_logsum,
            large_mask_q, large_mask_k, at, at, 0, part,
        )
        sums = scatter_core(keep, send)
        dqs.append(dq)
        needed = [dq]
        if group == 0:
            small_dkv = scatter_x(small_sums)
            needed += [cross_sum.value, small_sums]
        if group == 1:
            needed += [small_dkv, up_sum.step(), down_sum.step(), cross_sum.step()]
        if pending is not None:
            needed.append(pending.step())
        dkv = scatter_x(sums)
        dkvs.append(dkv)
        local = jnp.concatenate(
            [
                jnp.concatenate([dq, dkv[0], dkv[1]], axis=1),
                jnp.concatenate(
                    [
                        small_dq[:, at : at + part],
                        small_dkv[0, :, at : at + part],
                        small_dkv[1, :, at : at + part],
                    ],
                    axis=1,
                ),
            ],
            axis=0,
        )
        local = dot(normed, local, TN).astype(bf16)
        pending = Sum(local, by_yx)
        last_sums.append(pending)

    def front_back(view, hidden_grad, dq, dk, dv):
        grad = (
            dot(dq, query_weight, NT) + dot(dk, key_weight, NT) + dot(dv, value_weight, NT)
        )
        extra, gain_part = norm_back(grad, view.astype(f32), first_gain)
        return (hidden_grad + extra).astype(bf16), gain_part

    small_grad, small_gain = front_back(
        small, small_hidden_grad, small_dq, small_dkv[0], small_dkv[1]
    )
    large_grad, large_gain = front_back(
        large,
        large_hidden_grad,
        jnp.concatenate(dqs, axis=1),
        jnp.concatenate([kv[0] for kv in dkvs], axis=1),
        jnp.concatenate([kv[1] for kv in dkvs], axis=1),
    )
    small_grad = restore(small_grad).astype(f32)
    large_grad = restore(large_grad).astype(f32)
    output_sum = Sum(output_grad, by_yx)
    gain_rows = jnp.concatenate(
        [large_gain + small_gain, second_gain_grad, query_gain_grad, context_gain_grad], axis=0
    )
    wide = width // tm
    gain_rows = jnp.transpose(gain_rows.reshape(4, tm, wide), (1, 0, 2)).astype(bf16)
    gain_rows = jnp.pad(gain_rows, ((0, 0), (0, 28), (0, 2 * LANES - wide)))
    gain_sum = Sum(gain_rows.reshape(tm * 32, 2 * LANES), by_yx)

    cross_total = cross_sum.finish()
    up_total = up_sum.finish()
    down_total = down_sum.finish()
    output_total = output_sum.finish()
    last_totals = [total.finish() for total in last_sums]
    gain_total = gain_sum.finish()
    cross_grads = [cross_total[:, i * width : (i + 1) * width] for i in range(4)]
    last_grads = [
        jnp.concatenate([total[:, i * part : (i + 1) * part] for total in last_totals], axis=1)
        for i in range(3)
    ]
    gain_grads = [gain_total[i, :wide] for i in range(4)]
    return (
        united_view,
        large_grad,
        small_grad,
        gain_grads[0],
        last_grads[0],
        last_grads[1],
        last_grads[2],
        output_total,
        gain_grads[1],
        up_total,
        down_total,
        gain_grads[2],
        gain_grads[3],
        cross_grads[1],
        cross_grads[2],
        cross_grads[3],
        cross_grads[0],
    )


def solution(mesh):
    token = P("seq", "tm", None)
    in_specs = (token, token, P("seq", "tm")) + (P(),) * 14 + (token,)
    vector, matrix = P("tm"), P("tm", None)
    out_specs = (
        (token, token, token, vector)
        + (matrix,) * 4
        + (vector, matrix, matrix, vector, vector)
        + (matrix,) * 4
    )
    return jax.shard_map(
        functools.partial(per_device, mesh.shape["tm"], mesh.shape["seq"]),
        mesh=mesh,
        in_specs=in_specs,
        out_specs=out_specs,
        check_vma=False,
    )
```

```python
import functools

import jax
import jax.numpy as jnp
from jax import lax
from jax.experimental import pallas as pl
from jax.experimental.pallas import tpu as pltpu
from jax.sharding import PartitionSpec as P

HEADS = 12
EPS = 1e-05
NEGATIVE = -1e30
LOG2E = 1.4426950408889634
LN2 = 0.6931471805599453
LANES = 128
HALF = 64

bf16 = jnp.bfloat16
f32 = jnp.float32
NT = (((1,), (1,)), ((), ()))
NN = (((1,), (0,)), ((), ()))
TN = (((0,), (0,)), ((), ()))


def dot(a, b, dims=NN):
    return lax.dot_general(a, b, dims, preferred_element_type=f32)


def largest_block(rows, most):
    block = min(rows, most)
    while rows % block or block % 16:
        block -= 1
    return block


def columns(rows, at):
    return pl.BlockSpec((rows, LANES), lambda i: (0, i + at))


def pair_columns(rows, at):
    return pl.BlockSpec((2, rows, LANES), lambda i: (0, 0, i + at))


def whole(shape):
    return pl.BlockSpec(shape, lambda i: (0,) * len(shape))


def attend_kernel(parts, block, *refs):
    q_ref, mq_ref, mk_ref = refs[:3]
    kv_refs = refs[3 : 3 + parts]
    o_ref, l_ref, ka0, ka1, va0, va1 = refs[-6:]
    count = q_ref.shape[0]
    first = 0
    for kv_ref in kv_refs:
        rows = kv_ref.shape[1]
        low = lax.broadcasted_iota(jnp.int32, (rows, LANES), 1) < HALF
        here = pl.ds(first, rows)
        keys, values, mask = kv_ref[0], kv_ref[1], mk_ref[here, :]
        one = jnp.ones_like(values)
        ka0[here, :] = jnp.where(low, keys, mask)
        ka1[here, :] = jnp.where(low, mask, keys)
        va0[here, :] = jnp.where(low, values, one)
        va1[here, :] = jnp.where(low, one, values)
        first += rows
    low = lax.broadcasted_iota(jnp.int32, (block, LANES), 1) < HALF
    for number in range(count // block):
        here = pl.ds(number * block, block)
        query, mask = q_ref[here, :], mq_ref[here, :]
        tops, sums = [], []
        for head, keys, values in ((0, ka0, va0), (1, ka1, va1)):
            mine = jnp.where(low, query, mask) if head == 0 else jnp.where(low, mask, query)
            score = dot(mine, keys[...], NT)
            top = jnp.max(score, axis=1, keepdims=True)
            weight = jnp.exp2(score - top).astype(bf16)
            sums.append(dot(weight, values[...]))
            tops.append(jnp.broadcast_to(top, (block, LANES)))
        total = jnp.where(low, sums[1], sums[0])
        top = jnp.where(low, tops[1], tops[0])
        out = jnp.where(low, sums[0], sums[1])
        o_ref[here, :] = (out / pltpu.roll(total, HALF, 1)).astype(bf16)
        l_ref[here, :] = top + jnp.log2(total)


def attend(query, kv, mask_q, mask_k, at, width, earlier=()):
    count = query.shape[0]
    total = sum(part.shape[1] for part in kv)
    out = lambda kind: jax.ShapeDtypeStruct((count, query.shape[1]), kind)
    given = 3 + len(kv)
    return pl.pallas_call(
        functools.partial(attend_kernel, len(kv), largest_block(count, 256)),
        grid=(width // LANES,),
        in_specs=[columns(count, at // LANES), whole((count, LANES)), whole((total, LANES))]
        + [pair_columns(part.shape[1], 0) for part in kv]
        + [pl.BlockSpec(memory_space=pl.ANY)] * len(earlier),
        out_specs=[columns(count, at // LANES)] * 2,
        out_shape=[out(bf16), out(f32)],
        scratch_shapes=[pltpu.VMEM((total, LANES), bf16)] * 4,
        input_output_aliases={given + i: i for i in range(len(earlier))},
        compiler_params=pltpu.CompilerParams(vmem_limit_bytes=40 << 20),
        cost_estimate=pl.CostEstimate(
            flops=16 * count * total * width,
            bytes_accessed=width * (count * 8 + total * 4),
            transcendentals=count * total * width // HALF,
        ),
        name="attend",
    )(query, mask_q, mask_k, *kv, *earlier)


def three(value):
    first = value.astype(bf16)
    rest = value - first.astype(f32)
    second = rest.astype(bf16)
    return first, second, (rest - second.astype(f32)).astype(bf16)


def attend_back_kernel(parts, block, *refs):
    q_ref, do_ref, o_ref, l_ref, mq_ref, mk_ref = refs[:6]
    kv_refs = refs[6 : 6 + parts]
    dq_ref, keep_ref, send_ref, keys_at, values_at = refs[6 + parts :]
    count = q_ref.shape[0]
    first = 0
    for kv_ref in kv_refs:
        here = pl.ds(first, kv_ref.shape[1])
        keys_at[here, :] = kv_ref[0]
        values_at[here, :] = kv_ref[1]
        first += kv_ref.shape[1]
    lane = lax.broadcasted_iota(jnp.int32, (count, LANES), 1)
    low = lane < HALF
    spot = lane % HALF
    query, grad, mask = q_ref[...], do_ref[...], mq_ref[...]
    zero = jnp.zeros_like(query)
    product = grad.astype(f32) * o_ref[...].astype(f32)
    delta0 = jnp.sum(jnp.where(low, product, 0.0), axis=1, keepdims=True)
    delta1 = jnp.sum(jnp.where(low, 0.0, product), axis=1, keepdims=True)
    delta = jnp.where(low, delta1, delta0)

    def beside(base, value):
        a, b, c = three(-value)
        return jnp.where(spot == 4, a, jnp.where(spot == 5, b, jnp.where(spot == 6, c, base)))

    query_side = beside(mask, l_ref[...])
    grad_side = beside(zero, delta)
    query_a = (jnp.where(low, query, query_side), jnp.where(low, query_side, query))
    grad_a = (jnp.where(low, grad, grad_side), jnp.where(low, grad_side, grad))
    query_m = (jnp.where(low, query, zero), jnp.where(low, zero, query))
    grad_m = (jnp.where(low, grad, zero), jnp.where(low, zero, grad))
    lane_k = lax.broadcasted_iota(jnp.int32, (block, LANES), 1)
    low_k = lane_k < HALF
    spot_k = lane_k % HALF
    one = jnp.where((spot_k >= 4) & (spot_k < 7), 1.0, 0.0).astype(bf16)
    dq = jnp.zeros((count, LANES), f32)
    for number in range(first // block):
        here = pl.ds(number * block, block)
        keys, values = keys_at[here, :], values_at[here, :]
        side = mk_ref[here, :] + one
        nought = jnp.zeros_like(keys)
        dk = jnp.zeros((block, LANES), f32)
        dv = jnp.zeros((block, LANES), f32)
        for head in (0, 1):
            pick = lambda a, b: jnp.where(low_k, a, b) if head == 0 else jnp.where(low_k, b, a)
            prob = jnp.exp2(dot(query_a[head], pick(keys, side), NT))
            change = dot(grad_a[head], pick(values, one), NT)
            score_grad = (prob * change).astype(bf16)
            dv += dot(prob.astype(bf16), grad_m[head], TN)
            dk += dot(score_grad, query_m[head], TN)
            dq += dot(score_grad, pick(keys, nought))
        out_ref = keep_ref if number * block < first // 2 else send_ref
        there = pl.ds(number * block % (first // 2), block)
        out_ref[0, there, :] = (dk * LN2).astype(bf16)
        out_ref[1, there, :] = dv.astype(bf16)
    dq_ref[...] = (dq * HALF**-0.5).astype(bf16)


def attend_back(query, kv, grad, out, logsum, mask_q, mask_k, at, at_out, at_kv, width):
    count = query.shape[0]
    total = sum(part.shape[1] for part in kv)
    return pl.pallas_call(
        functools.partial(attend_back_kernel, len(kv), largest_block(total // 2, 512)),
        grid=(width // LANES,),
        in_specs=[columns(count, at // LANES)] * 2
        + [columns(count, at_out // LANES)] * 2
        + [whole((count, LANES)), whole((total, LANES))]
        + [pair_columns(part.shape[1], at_kv // LANES) for part in kv],
        out_specs=[columns(count, 0)] + [pair_columns(total // 2, 0)] * 2,
        out_shape=[jax.ShapeDtypeStruct((count, width), bf16)]
        + [jax.ShapeDtypeStruct((2, total // 2, width), bf16)] * 2,
        scratch_shapes=[pltpu.VMEM((total, LANES), bf16)] * 2,
        compiler_params=pltpu.CompilerParams(vmem_limit_bytes=40 << 20),
        cost_estimate=pl.CostEstimate(
            flops=20 * count * total * width,
            bytes_accessed=width * (count * 12 + total * 8),
            transcendentals=count * total * width // HALF,
        ),
        name="attend_back",
    )(query, grad, out, logsum, mask_q, mask_k, *kv)


def norm_stats(value):
    mean = jnp.mean(value, axis=-1, keepdims=True)
    centred = value - mean
    spread = jnp.mean(centred * centred, axis=-1, keepdims=True)
    return centred, lax.rsqrt(spread + EPS)


def norm(value, gain):
    centred, scale = norm_stats(value)
    return (centred * scale * gain).astype(bf16)


def norm_back(grad, value, gain):
    centred, scale = norm_stats(value)
    unit = centred * scale
    gain_grad = jnp.sum(grad * unit, axis=0, keepdims=True)
    grad = grad * gain
    extra = scale * (
        grad
        - jnp.mean(grad, axis=-1, keepdims=True)
        - unit * jnp.mean(grad * unit, axis=-1, keepdims=True)
    )
    return extra, gain_grad


Q_SCALE = LOG2E * HALF**-0.5


def front_kernel(x_ref, gain_ref, wq_ref, wk_ref, wv_ref, n_ref, q_ref, *kv_refs):
    normed = norm(x_ref[...].astype(f32), gain_ref[...])
    n_ref[...] = normed
    width = kv_refs[0].shape[2]
    keys = dot(normed, wk_ref[...]).astype(bf16)
    values = dot(normed, wv_ref[...]).astype(bf16)
    for group, kv_ref in enumerate(kv_refs):
        kv_ref[0] = keys[:, group * width : (group + 1) * width]
        kv_ref[1] = values[:, group * width : (group + 1) * width]
    q_ref[...] = (dot(normed, wq_ref[...]) * Q_SCALE).astype(bf16)


def front(view, gain, wq, wk, wv, groups):
    rows, width = view.shape
    part = width // groups
    result = pl.pallas_call(
        front_kernel,
        out_shape=[jax.ShapeDtypeStruct((rows, width), bf16)] * 2
        + [jax.ShapeDtypeStruct((2, rows, part), bf16)] * groups,
        compiler_params=pltpu.CompilerParams(vmem_limit_bytes=40 << 20),
        cost_estimate=pl.CostEstimate(
            flops=6 * rows * width * width,
            bytes_accessed=6 * width * width + 10 * rows * width,
            transcendentals=0,
        ),
        name="front",
    )(view, gain, wq, wk, wv)
    return result[0], result[1], result[2:]


GELU_A = 0.7978845608028654
GELU_B = 0.044715


def gelu_both(value):
    square = value * value
    bent = jnp.tanh(GELU_A * value * (1.0 + GELU_B * square))
    half = 0.5 * (1.0 + bent)
    slope = half + 0.5 * value * (1.0 - bent * bent) * (
        GELU_A * (1.0 + 3.0 * GELU_B * square)
    )
    return value * half, slope


def fill_wide(wide, refs, rows, first):
    at, there = 0, pl.ds(first, rows)
    for ref in refs:
        if len(ref.shape) == 3:
            for pair in range(ref.shape[0]):
                wide[there, at : at + LANES] = ref[pair]
                at += LANES
        else:
            wide[there, at : at + ref.shape[1]] = ref[...]
            at += ref.shape[1]


def rest_kernel(steps, mixes, is_query, *refs):
    x_ref = refs[0]
    mixed_refs = refs[1 : 1 + mixes]
    wo_ref, gain_ref, up_ref, down_ref, next_gain_ref = refs[1 + mixes : 6 + mixes]
    next_refs = refs[6 + mixes : -9]
    merged_ref, hidden_ref, second_ref, active_ref, slope_ref = refs[-9:-4]
    asked_ref, out_ref, total, scratch = refs[-4:]
    step = pl.program_id(0)

    @pl.when(step == 0)
    def _():
        hidden = x_ref[...].astype(f32)
        fill_wide(scratch, mixed_refs, scratch.shape[0], 0)
        hidden = hidden + dot(scratch[...], wo_ref[...])
        hidden_ref[...] = hidden
        second_ref[...] = norm(hidden, gain_ref[...])
        total[...] = hidden

    rows = total.shape[0] // 2
    halves = [pl.ds(at * rows, rows) for at in (0, 1)]
    inners = [dot(second_ref[half, :], up_ref[...]) for half in halves]
    for half, inner in zip(halves, inners):
        active, slope = gelu_both(inner)
        active = active.astype(bf16)
        active_ref[half, :] = active
        slope_ref[half, :] = slope.astype(bf16)
        total[half, :] += dot(active, down_ref[...])

    @pl.when(step == steps - 1)
    def _():
        merged = total[...]
        merged_ref[...] = merged
        asked = norm(merged, next_gain_ref[...])
        asked_ref[...] = asked
        if is_query:
            query = (dot(asked, next_refs[0][...]) * Q_SCALE).astype(bf16)
            if len(out_ref.shape) == 3:
                for pair in range(out_ref.shape[0]):
                    out_ref[pair] = query[:, pair * LANES : (pair + 1) * LANES]
            else:
                out_ref[...] = query
        else:
            out_ref[0] = dot(asked, next_refs[0][...]).astype(bf16)
            out_ref[1] = dot(asked, next_refs[1][...]).astype(bf16)


def rest(view, mixed, wo, gain, up, down, next_gain, next_weights):
    rows, width = view.shape
    steps = up.shape[1] // width
    is_query = len(next_weights) == 1
    flat = whole((rows, width))
    slab = pl.BlockSpec((rows, width), lambda i: (0, i))
    square = whole((width, width))
    shape = lambda kind: jax.ShapeDtypeStruct((rows, width), kind)
    wide = jax.ShapeDtypeStruct((rows, up.shape[1]), bf16)
    last = (rows, width) if is_query else (2, rows, width)
    if len(mixed[0].shape) == 3:
        last = (width // LANES, rows, LANES)
    return pl.pallas_call(
        functools.partial(rest_kernel, steps, len(mixed), is_query),
        grid=(steps,),
        in_specs=[flat]
        + [whole(m.shape) for m in mixed]
        + [square, whole((1, width))]
        + [slab_of(width, width), pl.BlockSpec((width, width), lambda i: (i, 0))]
        + [whole((1, width))]
        + [square] * len(next_weights),
        out_specs=[flat, flat, flat, slab, slab, flat, whole(last)],
        out_shape=[shape(f32), shape(f32), shape(bf16), wide, wide, shape(bf16)]
        + [jax.ShapeDtypeStruct(last, bf16)],
        scratch_shapes=[pltpu.VMEM((rows, width), f32), pltpu.VMEM((rows, width), bf16)],
        compiler_params=pltpu.CompilerParams(vmem_limit_bytes=62 << 20),
        cost_estimate=pl.CostEstimate(
            flops=2 * rows * width * (4 * up.shape[1] // 2 + 2 * width),
            bytes_accessed=width * width * 22 + rows * width * 32,
            transcendentals=rows * up.shape[1],
        ),
        name="rest",
    )(view, *mixed, wo, gain, up, down, next_gain, *next_weights)


def slab_of(rows, width):
    return pl.BlockSpec((rows, width), lambda i: (0, i))


def back_kernel(steps, mixes, sizes, laid, orders, *refs):
    gl_ref, gs_ref, al_ref, as_ref, sl_ref, ss_ref = refs[:6]
    cl_ref, cs_ref, hl_ref, hs_ref = refs[6:10]
    mixed_refs = refs[10 : 10 + mixes]
    mixed_s_ref, wo_ref, gain_ref, up_ref, down_ref = refs[10 + mixes : 15 + mixes]
    flows = len(orders)
    locals_, outs = refs[15 + mixes : 15 + mixes + flows], refs[15 + mixes + flows :]
    (hgl_ref, hgs_ref, ml_ref, ms_ref, dup_ref, ddown_ref, dwo_ref, dgain_ref) = outs[:8]
    sums, outs = outs[8 : 8 + flows], outs[8 + flows :]
    branch, second, total, active, inner_grad, mixed = outs[:6]
    large, small = sizes
    top, bottom = pl.ds(0, large), pl.ds(large, small)
    step = pl.program_id(0)
    if flows:
        here = Here()
        rest_refs = list(outs[6:])
        running = [
            Flow(here, order, local, rest_refs, True, False)
            for order, local in zip(orders, locals_)
        ]

        @pl.when(step == 0)
        def _():
            here.hail(*ALL_PARTNERS)
            here.heard(len(ALL_PARTNERS))
            for flow in running:
                flow.act(0)

    @pl.when(step == 0)
    def _():
        branch[top, :] = gl_ref[...].astype(bf16)
        branch[bottom, :] = gs_ref[...].astype(bf16)
        second[top, :] = cl_ref[...]
        second[bottom, :] = cs_ref[...]
        total[...] = jnp.zeros_like(total)

    grad = dot(branch[...], down_ref[...], NT)
    inner_grad[top, :] = (grad[:large] * sl_ref[...].astype(f32)).astype(bf16)
    inner_grad[bottom, :] = (grad[large:] * ss_ref[...].astype(f32)).astype(bf16)
    active[top, :] = al_ref[...]
    active[bottom, :] = as_ref[...]
    down = dot(active[...], branch[...], TN).astype(bf16)
    upper = dot(second[...], inner_grad[...], TN).astype(bf16)
    if laid:
        rows = dup_ref.shape[1]
        for at in range(8):
            zl, x, zh = at // 4, at // 2 % 2, at % 2
            first = ((zh * 2 + zl) * 2 + x) * rows
            dup_ref[at] = upper[first : first + rows]
        for x, core, y in ((a, b, c) for a in (0, 1) for b in (0, 1) for c in (0, 1)):
            first = (x * 4 + core * 2 + y) * rows
            there = core * 16 + (step % 2) * 8 + y * 4 + x * 2 + step // 2
            ddown_ref[there] = down[first : first + rows]
    else:
        dup_ref[...] = upper
        ddown_ref[...] = down
    total[...] += dot(inner_grad[...], up_ref[...], NT)

    @pl.when(step == steps - 1)
    def _():
        extra, gain_l = norm_back(total[top, :], hl_ref[...], gain_ref[...])
        hidden_grad = gl_ref[...] + extra
        hgl_ref[...] = hidden_grad
        branch[top, :] = hidden_grad.astype(bf16)
        extra, gain_s = norm_back(total[bottom, :], hs_ref[...], gain_ref[...])
        hidden_grad = gs_ref[...] + extra
        hgs_ref[...] = hidden_grad
        branch[bottom, :] = hidden_grad.astype(bf16)
        dgain_ref[...] = gain_l + gain_s
        mixed_grad = dot(branch[...], wo_ref[...], NT).astype(bf16)
        ml_ref[...] = mixed_grad[:large]
        ms_ref[...] = mixed_grad[large:]
        fill_wide(mixed, mixed_refs, large, 0)
        fill_wide(mixed, [mixed_s_ref], small, large)
        value = dot(mixed[...], branch[...], TN).astype(bf16)
        if laid:
            rows, wide = dwo_ref.shape[1:]
            for at, (core, y, tm) in enumerate(spots(BY_Y)):
                first = (tm * 2 + core) * rows
                dwo_ref[at] = value[first : first + rows, y * wide : (y + 1) * wide]
        else:
            dwo_ref[...] = value

    for flow in range(flows):
        for stage, when in enumerate((0, steps - 1)):

            @pl.when(step == when)
            def _(flow=flow, stage=stage):
                running[flow].act(stage + 1)
                if stage == 1:
                    sums[flow][...] = running[flow].result()


def back(
    grad_l, grad_s, saved_l, saved_s, mixed_l, mixed_s, wo, gain, up, down, laid, flows=(), orders=()
):
    (hidden_l, second_l, active_l, slope_l) = saved_l
    (hidden_s, second_s, active_s, slope_s) = saved_s
    large, width = grad_l.shape
    small = grad_s.shape[0]
    rows = large + small
    hidden = up.shape[1]
    part = width
    steps = hidden // part
    fl, fs = whole((large, width)), whole((small, width))
    square = whole((width, width))
    up_slab = slab_of(width, part)
    down_slab = pl.BlockSpec((part, width), lambda i: (i, 0))
    shape = jax.ShapeDtypeStruct
    results = [flow_result(o, f.shape[1:], False) for o, f in zip(orders, flows)]
    scratch = [s for o, f in zip(orders, flows) for s in flow_scratch(o, f.shape[1:], True, False)]
    out_up, out_down, out_square = up_slab, down_slab, square
    up_shape, down_shape, square_shape = up.shape, down.shape, (width, width)
    if laid:
        block = (width // 8, width)
        up_shape = down_shape = (32,) + block
        square_shape = (32, width // 16, width // 2)
        out_up = pl.BlockSpec((8,) + block, lambda i: (i, 0, 0))
        out_down, out_square = whole(down_shape), whole(square_shape)
    return pl.pallas_call(
        functools.partial(back_kernel, steps, len(mixed_l), (large, small), laid, orders),
        grid=(steps,),
        in_specs=[fl, fs]
        + [slab_of(large, part), slab_of(small, part)] * 2
        + [fl, fs, fl, fs]
        + [whole(m.shape) for m in mixed_l]
        + [whole(mixed_s.shape), square, whole((1, width)), up_slab, down_slab]
        + [pl.BlockSpec(memory_space=pl.ANY)] * len(flows),
        out_specs=[fl, fs, fl, fs, out_up, out_down, out_square, whole((1, width))]
        + [whole(result.shape) for result in results],
        out_shape=[
            shape((large, width), f32),
            shape((small, width), f32),
            shape((large, width), bf16),
            shape((small, width), bf16),
            shape(up_shape, bf16),
            shape(down_shape, bf16),
            shape(square_shape, bf16),
            shape((1, width), f32),
        ]
        + results,
        scratch_shapes=[
            pltpu.VMEM((rows, width), bf16),
            pltpu.VMEM((rows, width), bf16),
            pltpu.VMEM((rows, width), f32),
            pltpu.VMEM((rows, part), bf16),
            pltpu.VMEM((rows, part), bf16),
            pltpu.VMEM((rows, width), bf16),
        ]
        + scratch,
        compiler_params=pltpu.CompilerParams(
            vmem_limit_bytes=60 << 20,
            has_side_effects=bool(flows),
            collective_id=0 if flows else None,
        ),
        cost_estimate=pl.CostEstimate(
            flops=2 * rows * width * (4 * hidden + 2 * width),
            bytes_accessed=width * width * 36 + rows * width * 40,
            transcendentals=0,
        ),
        name="back",
    )(
        grad_l, grad_s, active_l, active_s, slope_l, slope_s, second_l, second_s, hidden_l, hidden_s,
        *mixed_l, mixed_s, wo, gain, up, down, *flows,
    )


MESH = pl.DeviceIdType.MESH
BY_Y = ("core", "y", "zl", "x", "zh")
BY_ZL = ("core", "zl", "y", "x", "zh")
BY_X = ("core", "x", "zl", "y", "zh")
BY_YX = ("core", "y", "x", "zl", "zh")


def spots(order):
    out = []
    for at in range(32):
        bit = {name: (at >> (4 - i)) & 1 for i, name in enumerate(order)}
        out.append((bit["core"], bit["y"], (bit["zh"] * 2 + bit["zl"]) * 2 + bit["x"]))
    return out


class Here:
    def __init__(self):
        tm, seq = lax.axis_index("tm"), lax.axis_index("seq")
        self.tm, self.seq = tm, seq
        self.bit = {
            "zh": tm // 4,
            "zl": (tm // 2) % 2,
            "x": tm % 2,
            "y": seq // 2,
            "core": seq % 2,
        }

    def partner(self, *names):
        tm, seq = self.tm, self.seq
        for name in names:
            one = 1 - 2 * self.bit[name]
            if name in ("y", "core"):
                seq = seq + one * (2 if name == "y" else 1)
            else:
                tm = tm + one * {"zh": 4, "zl": 2, "x": 1}[name]
        return (tm, seq)

    def hail(self, *partners):
        self.hail_all([self.partner(*names) for names in partners])

    def hail_line(self, *more):
        z, core = self.tm // 2, self.bit["core"]
        self.hail_all(
            [
                (
                    lax.rem(z + dz, 4) * 2 + self.bit["x"],
                    self.bit["y"] * 2 + lax.rem(core + dc, 2),
                )
                for dz in range(4)
                for dc in range(2)
                if dz or dc
            ]
            + [self.partner(name) for name in more]
        )

    def hail_all(self, places):
        barrier = pltpu.get_barrier_semaphore()
        for place in places:
            pl.semaphore_signal(barrier, inc=1, device_id=place, device_id_type=MESH)

    def heard(self, count):
        pl.semaphore_wait(pltpu.get_barrier_semaphore(), count)


ALL_PARTNERS = (("core",), ("y",), ("zl",), ("x",), ("zh",))


class Restore:
    def __init__(self, here, held, got, sems):
        self.held, self.got, self.sems = held, got, sems
        self.rows = got.shape[1]
        z, core = here.tm // 2, here.bit["core"]
        self.odd = lax.rem(z, 2)
        self.stay = core == z // 2
        turns = (self.odd, 1 - self.odd)
        self.places = [
            ((2 * core + turn) * 2 + here.bit["x"], here.bit["y"] * 2 + z // 2) for turn in turns
        ]

    def far(self, turn, arriving=False):
        at = 1 - self.odd if arriving and turn else self.odd
        return pltpu.make_async_remote_copy(
            src_ref=self.held.at[pl.ds(turn * self.rows, self.rows)],
            dst_ref=self.got.at[at],
            send_sem=self.sems.at[0, turn],
            recv_sem=self.sems.at[1, turn],
            device_id=self.places[turn],
            device_id_type=MESH,
        )

    def near(self):
        return pltpu.make_async_copy(
            self.held.at[pl.ds(0, self.rows)], self.got.at[self.odd], self.sems.at[1, 0]
        )

    def start(self):
        self.far(1).start()

        @pl.when(self.stay)
        def _():
            self.near().start()

        @pl.when(jnp.logical_not(self.stay))
        def _():
            self.far(0).start()

    def finish(self):
        self.far(1).wait_send()
        self.far(1, True).wait_recv()

        @pl.when(self.stay)
        def _():
            self.near().wait()

        @pl.when(jnp.logical_not(self.stay))
        def _():
            self.far(0).wait_send()
            self.far(0).wait_recv()


def restore_scratch(rows, width):
    return [
        pltpu.VMEM((2 * rows, width), bf16),
        pltpu.VMEM((2, rows, width), bf16),
        pltpu.SemaphoreType.DMA((2, 2)),
    ]


class Flow:
    def __init__(self, here, order, local, refs, keep, ends):
        self.here, self.order, self.local = here, order, local
        self.keep = refs.pop(0) if keep else None
        self.got = [refs.pop(0) for _ in order]
        self.out = refs.pop(0) if ends else None
        self.sem = refs.pop(0)
        self.last = len(order)
        self.ends = ends

    def copy(self, step):
        name = self.order[step]
        half = 1 << (self.last - 1 - step)
        source = self.local if step == 0 else self.got[step - 1]
        at = (1 - self.here.bit[name]) * half
        return pltpu.make_async_remote_copy(
            src_ref=source.at[pl.ds(at, half)],
            dst_ref=self.got[step],
            send_sem=self.sem.at[0, step],
            recv_sem=self.sem.at[1, step],
            device_id=self.here.partner(name),
            device_id_type=MESH,
        )

    def keep_copy(self):
        half = 1 << (self.last - 1)
        at = self.here.bit[self.order[0]] * half
        return pltpu.make_async_copy(
            self.local.at[pl.ds(at, half)], self.keep, self.sem.at[0, self.last + 2]
        )

    def start(self, step):
        self.copy(step).start()
        if step == 0 and self.keep is not None:
            self.keep_copy().start()

    def finish(self, step):
        half = 1 << (self.last - 1 - step)
        self.copy(step).wait()
        got = self.got[step]
        at = self.here.bit[self.order[step]] * half
        if step == 0 and self.keep is not None:
            self.keep_copy().wait()
            source, at = self.keep, 0
        else:
            source = self.local if step == 0 else self.got[step - 1]

        def body(i, carry):
            got[i] = got[i] + source[at + i]
            return carry

        if half == 1:
            got[0] = got[0] + source[at]
        else:
            lax.fori_loop(0, half, body, 0)

    def spread_copy(self, which):
        here = self.here
        own = here.bit["core"] * 2
        if which == 0:
            source, there = self.got[-1].at[0], self.out.at[own + here.bit["y"]]
        else:
            source = there = self.out.at[pl.ds(own, 2)]
        return pltpu.make_async_remote_copy(
            src_ref=source,
            dst_ref=there,
            send_sem=self.sem.at[0, self.last + which],
            recv_sem=self.sem.at[1, self.last + which],
            device_id=here.partner(("y", "core")[which]),
            device_id_type=MESH,
        )

    def act(self, stage):
        if stage == 0:
            self.start(0)
        elif stage < self.last:
            self.finish(stage - 1)
            self.start(stage)
        elif stage == self.last:
            self.finish(stage - 1)
            if self.ends:
                self.spread_copy(0).start()
                self.out[self.here.bit["core"] * 2 + self.here.bit["y"]] = self.got[-1][0]
        elif stage == self.last + 1 and self.ends:
            self.spread_copy(0).wait()
            self.spread_copy(1).start()
        elif stage == self.last + 2 and self.ends:
            self.spread_copy(1).wait()

    def result(self):
        return self.out[...] if self.ends else self.got[-1][...]


def flow_scratch(order, block, keep, ends):
    steps = len(order)
    blocks = [pltpu.VMEM((1 << (steps - 1),) + block, bf16)] if keep else []
    for step in range(steps):
        blocks.append(pltpu.VMEM((1 << (steps - 1 - step),) + block, bf16))
    if ends:
        blocks.append(pltpu.VMEM((4,) + block, bf16))
    return blocks + [pltpu.SemaphoreType.DMA((2, steps + 3))]


def flow_result(order, block, ends):
    left = 4 if ends else 1
    return jax.ShapeDtypeStruct((left,) + block, bf16)


def pair_back(query, grad, out, logsum, mask, keys_at, values_at, mk_ref, block, exchange, pair):
    count = query.shape[0]
    total = keys_at.shape[0]
    lane = lax.broadcasted_iota(jnp.int32, (count, LANES), 1)
    low = lane < HALF
    spot = lane % HALF
    zero = jnp.zeros_like(query)
    product = grad.astype(f32) * out.astype(f32)
    delta0 = jnp.sum(jnp.where(low, product, 0.0), axis=1, keepdims=True)
    delta1 = jnp.sum(jnp.where(low, 0.0, product), axis=1, keepdims=True)
    delta = jnp.where(low, delta1, delta0)

    def beside(base, value):
        a, b, c = three(-value)
        return jnp.where(spot == 4, a, jnp.where(spot == 5, b, jnp.where(spot == 6, c, base)))

    query_side = beside(mask, logsum)
    grad_side = beside(zero, delta)
    query_a = (jnp.where(low, query, query_side), jnp.where(low, query_side, query))
    grad_a = (jnp.where(low, grad, grad_side), jnp.where(low, grad_side, grad))
    query_m = (jnp.where(low, query, zero), jnp.where(low, zero, query))
    grad_m = (jnp.where(low, grad, zero), jnp.where(low, zero, grad))
    lane_k = lax.broadcasted_iota(jnp.int32, (block, LANES), 1)
    low_k = lane_k < HALF
    spot_k = lane_k % HALF
    one = jnp.where((spot_k >= 4) & (spot_k < 7), 1.0, 0.0).astype(bf16)
    dq = jnp.zeros((count, LANES), f32)
    for number in exchange.turns(total // block):
        here = pl.ds(number * block, block)
        keys, values = keys_at[here, :], values_at[here, :]
        side = mk_ref[here, :] + one
        nought = jnp.zeros_like(keys)
        dk = jnp.zeros((block, LANES), f32)
        dv = jnp.zeros((block, LANES), f32)
        for head in (0, 1):
            pick = lambda a, b: jnp.where(low_k, a, b) if head == 0 else jnp.where(low_k, b, a)
            prob = jnp.exp2(dot(query_a[head], pick(keys, side), NT))
            change = dot(grad_a[head], pick(values, one), NT)
            score_grad = (prob * change).astype(bf16)
            dv += dot(prob.astype(bf16), grad_m[head], TN)
            dk += dot(score_grad, query_m[head], TN)
            dq += dot(score_grad, pick(keys, nought))
        exchange.put(pair, number, block, (dk * LN2).astype(bf16), dv.astype(bf16))
    return (dq * HALF**-0.5).astype(bf16)


class Exchange:
    def __init__(self, here, rows, refs):
        self.here, self.rows = here, rows
        self.sums, self.send, self.got_core, self.across, self.got_x = refs[:5]
        self.sems = refs[5]
        self.before = None

    def turns(self, blocks):
        return (3, 1, 0, 2) if blocks == 4 else tuple(reversed(range(blocks)))

    def copy_core(self, pair, far):
        rows = pl.ds(far * self.rows, self.rows)
        return pltpu.make_async_remote_copy(
            src_ref=self.send.at[pair % 2, :, rows, :],
            dst_ref=self.got_core.at[pair, :, rows, :],
            send_sem=self.sems.at[2 * far, pair],
            recv_sem=self.sems.at[2 * far + 1, pair],
            device_id=self.here.partner("core"),
            device_id_type=MESH,
        )

    def copy_x(self, pair):
        return pltpu.make_async_remote_copy(
            src_ref=self.across.at[pair],
            dst_ref=self.got_x.at[pair],
            send_sem=self.sems.at[4, pair],
            recv_sem=self.sems.at[5, pair],
            device_id=self.here.partner("x"),
            device_id_type=MESH,
        )

    def end(self):
        pairs = self.got_x.shape[0]
        for pair in range(pairs):
            if pair >= pairs - 2:
                self.free(pair)
            self.copy_x(pair).wait_send()

    def free(self, pair):
        for far in (0, 1):
            self.copy_core(pair, far).wait_send()

    def put(self, pair, number, block, dk, dv):
        half = 2 * self.rows
        there = pl.ds(number * block % half, block)
        ref, slot = (self.sums, pair) if number * block < half else (self.send, pair % 2)
        ref[slot, 0, there, :] = dk
        ref[slot, 1, there, :] = dv
        if 2 * half == 4 * block:
            if number == 3:
                if self.before is not None:
                    self.before()
                self.copy_core(pair, 1).start()
            elif number == 2:
                self.copy_core(pair, 0).start()
            elif number == 0:
                self.pass_on(pair)
        elif number == 1:
            if self.before is not None:
                self.before()
            for far in (1, 0):
                self.copy_core(pair, far).start()
        else:
            self.pass_on(pair)

    def pass_on(self, pair):
        rows = self.rows
        self.copy_core(pair, 1).wait_recv()
        far = pl.ds(rows, rows)
        for i in (0, 1):
            self.across[pair, i] = self.sums[pair, i, far, :] + self.got_core[pair, i, far, :]
        self.copy_x(pair).start()

    def take(self, pair, out_ref):
        near = pl.ds(0, self.rows)
        self.copy_core(pair, 0).wait_recv()
        self.copy_x(pair).wait_recv()
        for i in (0, 1):
            out_ref[pair, i] = (
                self.sums[pair, i, near, :].astype(f32)
                + self.got_core[pair, i, near, :].astype(f32)
                + self.got_x[pair, i].astype(f32)
            ).astype(bf16)


def exchange_scratch(pairs, rows):
    return [
        pltpu.VMEM((pairs, 2, 2 * rows, LANES), bf16),
        pltpu.VMEM((2, 2, 2 * rows, LANES), bf16),
        pltpu.VMEM((pairs, 2, 2 * rows, LANES), bf16),
        pltpu.VMEM((pairs, 2, rows, LANES), bf16),
        pltpu.VMEM((pairs, 2, rows, LANES), bf16),
        pltpu.SemaphoreType.DMA((6, pairs)),
    ]


def fill_keys(keys_at, values_at, kv_ref):
    rows = kv_ref.shape[3]
    for part in range(kv_ref.shape[0]):
        there = pl.ds(part * rows, rows)
        keys_at[there, :] = kv_ref[part, 0, 0]
        values_at[there, :] = kv_ref[part, 0, 1]


def selves_kernel(pairs, plan, blocks, *refs):
    orders, ends, stages = plan
    large_refs, kv_large, refs = refs[:6], refs[6], refs[7:]
    small_refs, kv_small, refs = refs[:6], refs[6], refs[7:]
    flows = len(orders)
    locals_, refs = refs[:flows], refs[flows:]
    given, gain, refs = refs[:5], refs[5], refs[6:]
    dq_l, dkv_l, dq_s, dkv_s, view_ref, gain_ref = refs[:6]
    sums, refs = refs[6 : 6 + flows], refs[6 + flows :]
    held, load_sems, dq_all, grads, home_refs, refs = refs[:5], refs[5], refs[6], refs[7], refs[8:11], refs[11:]
    keys_l, values_l, keys_s, values_s = refs[:4]
    ex_l, ex_s, refs = refs[4:10], refs[10:16], refs[16:]
    here = Here()
    rows_l, rows_s = keys_l.shape[0] // 4, keys_s.shape[0] // 4
    large, small = Exchange(here, rows_l, ex_l), Exchange(here, rows_s, ex_s)
    refs = list(refs)
    running = [
        Flow(here, orders[flow], locals_[flow], refs, True, ends[flow]) for flow in range(flows)
    ]
    step = pl.program_id(0)
    home = Restore(here, *home_refs)
    loads = [
        pltpu.make_async_copy(source, there, load_sems.at[i])
        for i, (source, there) in enumerate(zip(given, held))
    ]

    @pl.when(step == 0)
    def _():
        here.hail_line("x", "y")
        for load in loads:
            load.start()

    def before():
        @pl.when(step == 0)
        def _():
            here.heard(9)
            for flow in running:
                flow.act(0)

    large.before = before

    def attention(exchange, pair, refs, kv_ref, keys_at, values_at, block, dq_ref):
        q_ref, do_ref, o_ref, l_ref, mq_ref, mk_ref = refs
        fill_keys(keys_at, values_at, kv_ref)

        @pl.when(pair >= 2)
        def _():
            exchange.free(pair - 2)

        dq_ref[...] = pair_back(
            q_ref[0], do_ref[...], o_ref[0], l_ref[0], mq_ref[...], keys_at, values_at, mk_ref,
            block, exchange, pair,
        )

    @pl.when(step < pairs)
    def _():
        attention(large, step, large_refs, kv_large, keys_l, values_l, blocks[0], dq_l)
        dq_all[step] = dq_l[...]

    @pl.when(step >= pairs)
    def _():
        attention(small, step - pairs, small_refs, kv_small, keys_s, values_s, blocks[1], dq_s)

    for pair in range(pairs):

        @pl.when(step == pair + 2 + pair // (pairs - 1))
        def _(pair=pair):
            large.take(pair, dkv_l)

    @pl.when(step == pairs + 2)
    def _():
        *weights, hidden_grad, view = held
        for load in loads:
            load.wait()
        total = None
        for which, weight in enumerate(weights):
            for pair in range(pairs):
                lanes = slice(pair * LANES, (pair + 1) * LANES)
                grads[:, lanes] = dkv_l[pair, which - 1] if which else dq_all[pair]
            product = dot(grads[...], weight[...], NT)
            total = product if total is None else total + product
        extra, gain_ref[...] = norm_back(total, view[...].astype(f32), gain[...])
        home_refs[0][...] = (hidden_grad[...] + extra).astype(bf16)
        home.start()

    for at in range(2 * pairs):
        todo = []
        for flow in range(flows):
            for stage, when in enumerate(stages[flow]):
                if when == at:
                    todo.append((running[flow], stage + 1))
        if todo:

            @pl.when(step == at)
            def _(todo=todo):
                for flow, stage in todo:
                    flow.act(stage)

    @pl.when(step == 2 * pairs - 1)
    def _():
        for pair in range(pairs):
            small.take(pair, dkv_s)
        small.end()
        large.end()
        for flow, sum_ref in zip(running, sums):
            sum_ref[...] = flow.result()
        home.finish()
        view_ref[...] = home_refs[1][...]


def selves_back(large, large_kv, small, small_kv, flows, view, gain, orders, ends, stages):
    count, width = large[1].shape
    few = small[1].shape[0]
    pairs = width // LANES
    total, less = large[5].shape[0], small[5].shape[0]
    shapes = [flow.shape[1:] for flow in flows]
    results = [flow_result(*flow) for flow in zip(orders, shapes, ends)]
    blocks = (largest_block(total // 2, 512), largest_block(less // 2, 512))
    first = lambda i: jnp.minimum(i, pairs - 1)
    last = lambda i: jnp.maximum(i - pairs, 0)
    in_specs = []
    for rows, keys, at in ((count, total, first), (few, less, last)):
        major = pl.BlockSpec((1, rows, LANES), lambda i, at=at: (at(i), 0, 0))
        minor = pl.BlockSpec((rows, LANES), lambda i, at=at: (0, at(i)))
        in_specs += [major, minor, major, major, whole((rows, LANES)), whole((keys, LANES))]
        in_specs.append(
            pl.BlockSpec((4, 1, 2, rows, LANES), lambda i, at=at: (0, at(i), 0, 0, 0))
        )
    in_specs += [pl.BlockSpec(memory_space=pl.ANY)] * (len(flows) + len(view))
    in_specs.append(whole((1, width)))
    shape = jax.ShapeDtypeStruct
    out_shape = [
        shape((count, width), bf16),
        shape((pairs, 2, count, LANES), bf16),
        shape((few, width), bf16),
        shape((pairs, 2, few, LANES), bf16),
        shape((2, count // 2, width), bf16),
        shape((1, width), f32),
    ] + results
    out_specs = [
        pl.BlockSpec((count, LANES), lambda i: (0, first(i))),
        whole((pairs, 2, count, LANES)),
        pl.BlockSpec((few, LANES), lambda i: (0, last(i))),
        whole((pairs, 2, few, LANES)),
        whole((2, count // 2, width)),
        whole((1, width)),
    ] + [whole(result.shape) for result in results]
    scratch = [pltpu.VMEM(value.shape, value.dtype) for value in view]
    scratch += [pltpu.SemaphoreType.DMA((len(view),)), pltpu.VMEM((pairs, count, LANES), bf16)]
    scratch += [pltpu.VMEM((count, width), bf16)] + restore_scratch(count // 2, width)
    scratch += [pltpu.VMEM((total, LANES), bf16)] * 2 + [pltpu.VMEM((less, LANES), bf16)] * 2
    scratch += exchange_scratch(pairs, count) + exchange_scratch(pairs, few)
    for flow in range(len(flows)):
        scratch += flow_scratch(orders[flow], shapes[flow], True, ends[flow])
    result = pl.pallas_call(
        functools.partial(selves_kernel, pairs, (orders, ends, stages), blocks),
        grid=(2 * pairs,),
        in_specs=in_specs,
        out_specs=out_specs,
        out_shape=out_shape,
        scratch_shapes=scratch,
        compiler_params=pltpu.CompilerParams(
            vmem_limit_bytes=60 << 20, collective_id=1, has_side_effects=True
        ),
        cost_estimate=pl.CostEstimate(
            flops=20 * width * (count * total + few * less),
            bytes_accessed=64 * count * width,
            transcendentals=count * total * width // HALF,
        ),
        name="selves_back",
    )(*large, large_kv, *small, small_kv, *flows, *view, gain)
    return result[:4], result[4:6], result[6:]


LAST_ORDERS = (BY_YX, BY_X, BY_YX)
GAIN_ORDER = ("core", "y", "x", "zl", "zh")
LATE_ORDER = ("x", "zh")
LATE_ORDERS = (LATE_ORDER,) * 3
LATE_STAGES = {3: 2, 5: 3, 6: 4}


def last_kernel(pairs, sizes, late, *refs):
    refs = list(refs)
    take = lambda count: [refs.pop(0) for _ in range(count)]
    given, late_refs = take(11), take(late)
    gain, gain_l, second_gain, query_gain, context_gain = take(5)
    (gs_ref,) = take(1)
    sum_refs = take(3 + late)
    (gain_ref,) = take(1)
    held = take(11)
    dql, dkvl, dqs, dkvs, nl, ns, wq, wk, wv, xs, hs = held
    load_sems, normed, *grads = take(5)
    small_back = take(3)
    here = Here()
    flows = []
    for order in LAST_ORDERS:
        flows.append(Flow(here, order, refs.pop(0), refs, False, True))
    late_flows = [
        Flow(here, order, ref, refs, True, True) for order, ref in zip(LATE_ORDERS, late_refs)
    ]
    state, got, gain_sems = refs
    large, small = sizes
    top, bottom = pl.ds(0, large), pl.ds(large, small)
    loads = [
        pltpu.make_async_copy(source, there, load_sems.at[i])
        for i, (source, there) in enumerate(zip(given, held))
    ]
    here.hail_line("x", "y")
    for load in loads:
        load.start()
    home = Restore(here, *small_back)

    def gain_copy(step):
        return pltpu.make_async_remote_copy(
            src_ref=state.at[step],
            dst_ref=got.at[step],
            send_sem=gain_sems.at[0, step],
            recv_sem=gain_sems.at[1, step],
            device_id=here.partner(GAIN_ORDER[step]),
            device_id_type=MESH,
        )

    for load in loads[:6]:
        load.wait()
    normed[top, :] = nl[...]
    normed[bottom, :] = ns[...]
    for which, flow in enumerate(flows):
        if which == 0:
            grads[0][top, :] = dql[...]
            grads[0][bottom, :] = dqs[...]
        else:
            for pair in range(pairs):
                lanes = pl.ds(pair * LANES, LANES)
                grads[which][top, lanes] = dkvl[pair, which - 1]
                grads[which][bottom, lanes] = dkvs[pair, which - 1]
        value = dot(normed[...], grads[which][...], TN).astype(bf16)
        if which == 0:
            here.heard(9)
            for late_flow in late_flows:
                late_flow.act(0)
        rows, wide = flow.local.shape[1:]
        for at, (core, y, tm) in enumerate(spots(flow.order)):
            first = tm * 2 * rows + core * rows
            flow.local[at] = value[first : first + rows, y * wide : (y + 1) * wide]
        flow.act(0)
    total = None
    for which, weight in enumerate((wq, wk, wv)):
        loads[6 + which].wait()
        part = dot(grads[which][bottom, :], weight[...], NT)
        total = part if total is None else total + part
    for load in loads[9:]:
        load.wait()
    for flow in late_flows:
        flow.act(1)
    extra, gain_s = norm_back(total, xs[...].astype(f32), gain[...])
    small_back[0][...] = (hs[...] + extra).astype(bf16)
    home.start()
    for flow in flows:
        flow.act(1)
    state[0] = jnp.zeros(state.shape[1:], f32)
    for row, value in enumerate(
        (gain_l[...] + gain_s, second_gain[...], query_gain[...], context_gain[...])
    ):
        state[0, row : row + 1, :] = value
    gain_copy(0).start()
    for stage in range(1, 8):
        if stage > 1:
            for flow in flows:
                flow.act(stage)
        if stage in LATE_STAGES:
            for flow in late_flows:
                flow.act(LATE_STAGES[stage])
        if stage <= 5:
            gain_copy(stage - 1).wait()
            total = state[stage - 1] + got[stage - 1]
            if stage < 5:
                state[stage] = total
                gain_copy(stage).start()
            else:
                wide = total.shape[1]
                turned = pltpu.roll(total, lax.rem(wide - here.tm * (wide // 8), wide), 1)
                gain_ref[...] = turned[:, : gain_ref.shape[1]]
    for flow, sum_ref in zip(flows + late_flows, sum_refs):
        sum_ref[...] = flow.result()
    home.finish()
    gs_ref[...] = small_back[1][...]


def last_sums(given, late, gains):
    count, width = given[0].shape
    few = given[2].shape[0]
    block = (width // 16, width // 2)
    shape = jax.ShapeDtypeStruct
    tokens = count + few
    scratch = [pltpu.VMEM(value.shape, value.dtype) for value in given]
    scratch += [pltpu.SemaphoreType.DMA((len(given),))]
    scratch += [pltpu.VMEM((tokens, width), bf16)] * 4
    scratch += restore_scratch(few // 2, width)
    for order in LAST_ORDERS:
        scratch.append(pltpu.VMEM((32,) + block, bf16))
        scratch += flow_scratch(order, block, False, True)
    for order, local in zip(LATE_ORDERS, late):
        scratch += flow_scratch(order, local.shape[1:], True, True)
    scratch += [
        pltpu.VMEM((5, 8, width), f32),
        pltpu.VMEM((5, 8, width), f32),
        pltpu.SemaphoreType.DMA((2, 5)),
    ]
    anywhere = pl.BlockSpec(memory_space=pl.ANY)
    vmem = pl.BlockSpec(memory_space=pltpu.VMEM)
    result = pl.pallas_call(
        functools.partial(last_kernel, width // LANES, (count, few), len(late)),
        in_specs=[anywhere] * (len(given) + len(late)) + [vmem] * 5,
        out_shape=[
            shape((2, few // 2, width), bf16),
        ]
        + [shape((4,) + block, bf16)] * 3
        + [shape((4,) + local.shape[1:], bf16) for local in late]
        + [shape((8, LANES), f32)],
        scratch_shapes=scratch,
        compiler_params=pltpu.CompilerParams(
            vmem_limit_bytes=60 << 20, collective_id=2, has_side_effects=True
        ),
        cost_estimate=pl.CostEstimate(
            flops=40 * tokens * width * width,
            bytes_accessed=40 * tokens * width,
            transcendentals=0,
        ),
        name="last_sums",
    )(*given, *late, *gains)
    return result[0], result[1:4], result[4:-1], result[-1]


def results_kernel(*refs):
    outs, given, sems = refs[12:29], refs[29:41], refs[41]
    loads = [
        pltpu.make_async_copy(source, there, sems.at[i])
        for i, (source, there) in enumerate(zip(refs, given))
    ]
    for load in loads:
        load.start()
    for load in loads:
        load.wait()
    united, large, small, q, k, v, up, down, output, first, other, gains = given
    for source, there in zip((united, large, small), outs[:3]):
        there[...] = source[...].astype(there.dtype)
    for source, there in zip((q, k, v, output), (outs[4], outs[5], outs[6], outs[7])):
        rows, wide = source.shape[1:]
        for at in range(4):
            core, y = at // 2, at % 2
            there[core * rows : (core + 1) * rows, y * wide : (y + 1) * wide] = source[at].astype(f32)
    rows, wide = up.shape[1:]
    for at in range(4):
        outs[9][:, at * wide : (at + 1) * wide] = up[at].astype(f32)
        outs[10][at * rows : (at + 1) * rows, :] = down[at].astype(f32)
        half = rows // 2
        there = slice(at % 2 * half, (at % 2 + 1) * half)
        (outs[16] if at < 2 else outs[13])[there, :] = first[at].astype(f32)
        (outs[14] if at < 2 else outs[15])[there, :] = other[at].astype(f32)
    for row, at in enumerate((3, 8, 11, 12)):
        outs[at][...] = gains[row : row + 1, : outs[at].shape[1]]


def results(united, large, small, last, late, first, other, gains):
    shape = jax.ShapeDtypeStruct
    rows, width = late[0].shape[1:]
    square, vector = shape((rows, width), f32), shape((1, rows), f32)
    given = (united, large, small, *last, *late, first, other, gains)
    out = pl.pallas_call(
        results_kernel,
        in_specs=[pl.BlockSpec(memory_space=pl.ANY)] * len(given),
        scratch_shapes=[pltpu.VMEM(value.shape, value.dtype) for value in given]
        + [pltpu.SemaphoreType.DMA((len(given),))],
        out_shape=[
            shape(united.shape, bf16), shape(large.shape, f32), shape(small.shape, f32), vector,
            square, square, square, square, vector,
            shape((rows, 4 * width), f32), shape((4 * rows, width), f32), vector, vector,
            square, square, square, square,
        ],
        compiler_params=pltpu.CompilerParams(vmem_limit_bytes=60 << 20),
        cost_estimate=pl.CostEstimate(flops=0, bytes_accessed=14 << 20, transcendentals=0),
        name="results",
    )(*given)
    return tuple(value.reshape(rows) if value.shape == (1, rows) else value for value in out)


def cross_kernel(pairs, block, *refs):
    (q_ref, do_ref, o_ref, l_ref, mq_ref, mk_ref), refs = refs[:6], refs[6:]
    kv_ref, given, gains, refs = refs[0], refs[1:11], refs[11:13], refs[13:]
    view_ref, gl_ref, gs_ref, a_ref, b_ref, gain_l_ref, gain_s_ref = refs[:7]
    keys_at, values_at, exchange_refs, refs = refs[7], refs[8], refs[9:15], refs[15:]
    dkv, dq, dk, dv = refs[:4]
    held, sems, home_refs = refs[4:14], refs[14], refs[15:18]
    united, wo, merged_l, asked, context, grad_out, merged_s, wq, wk, wv = held
    here = Here()
    exchange = Exchange(here, keys_at.shape[0] // 4, exchange_refs)
    step = pl.program_id(0)
    loads = [
        pltpu.make_async_copy(source, there, sems.at[i])
        for i, (source, there) in enumerate(zip(given, held))
    ]

    @pl.when(step == 0)
    def _():
        here.hail_line("x")
        for load in loads:
            load.start()

    def before():
        @pl.when(step == 0)
        def _():
            here.heard(8)

    exchange.before = before
    home = Restore(here, *home_refs)

    fill_keys(keys_at, values_at, kv_ref)

    @pl.when(step >= 2)
    def _():
        exchange.free(step - 2)

    dq[step] = pair_back(
        q_ref[0], do_ref[...], o_ref[0], l_ref[0], mq_ref[...], keys_at, values_at, mk_ref,
        block, exchange, step,
    )

    @pl.when(step == 1)
    def _():
        for load in loads[:3]:
            load.wait()
        wide = jnp.concatenate([united[i] for i in range(pairs)], axis=1)
        home_refs[0][...] = (merged_l[...] + dot(wide, wo[...])).astype(bf16)
        home.start()

    @pl.when(step >= 3)
    def _():
        exchange.take(step - 3, dkv)

    def lay(out_ref, which, value, order):
        left = 32 // out_ref.shape[0]
        rows = out_ref.shape[1] // left
        for at, (core, y, tm) in enumerate(spots(order)):
            if core == which:
                first, there = (tm * 2 + y) * rows, at % left * rows
                out_ref[at // left, there : there + rows, :] = value[first : first + rows]

    @pl.when(step == pairs - 1)
    def _():
        for load in loads[3:]:
            load.wait()
        grads = jnp.concatenate([united[i] for i in range(pairs)], axis=1)
        lay(a_ref, 0, dot(grads, grad_out[...], TN).astype(bf16), BY_Y)
        grads = jnp.concatenate([dq[i] for i in range(pairs)], axis=1)
        lay(a_ref, 1, dot(asked[...], grads, TN).astype(bf16), BY_Y)
        extra, gain_l_ref[...] = norm_back(dot(grads, wq[...], NT), merged_l[...], gains[0][...])
        gl_ref[...] = grad_out[...].astype(f32) + extra
        for pair in range(pairs - 3, pairs):
            exchange.take(pair, dkv)
        for pair in range(pairs):
            lanes = pl.ds(pair * LANES, LANES)
            dk[:, lanes] = dkv[pair, 0]
            dv[:, lanes] = dkv[pair, 1]
        lay(b_ref, 0, dot(context[...], dk[...], TN).astype(bf16), BY_ZL)
        lay(b_ref, 1, dot(context[...], dv[...], TN).astype(bf16), BY_ZL)
        grad = dot(dk[...], wk[...], NT) + dot(dv[...], wv[...], NT)
        gs_ref[...], gain_s_ref[...] = norm_back(grad, merged_s[...], gains[1][...])
        exchange.end()
        home.finish()
        view_ref[...] = home_refs[1][...]


def cross_back(attention, kv, given, gains):
    count, width = attention[1].shape
    few = kv.shape[3]
    major = pl.BlockSpec((1, count, LANES), lambda i: (i, 0, 0))
    pairs = width // LANES
    total = attention[5].shape[0]
    block = largest_block(total // 2, 512)
    shape = jax.ShapeDtypeStruct
    laid = (4, 8 * width // 16, width)
    return pl.pallas_call(
        functools.partial(cross_kernel, pairs, block),
        grid=(pairs,),
        in_specs=[major, columns(count, 0), major, major]
        + [whole((count, LANES)), whole((total, LANES))]
        + [pl.BlockSpec((4, 1, 2, few, LANES), lambda i: (0, i, 0, 0, 0))]
        + [pl.BlockSpec(memory_space=pl.ANY)] * len(given)
        + [whole((1, width))] * 2,
        out_specs=[
            whole((2, count // 2, width)), whole((count, width)), whole((few, width)), whole(laid), whole(laid),
            whole((1, width)), whole((1, width)),
        ],
        out_shape=[
            shape((2, count // 2, width), bf16),
            shape((count, width), f32), shape((few, width), f32), shape(laid, bf16), shape(laid, bf16),
            shape((1, width), f32), shape((1, width), f32),
        ],
        scratch_shapes=[pltpu.VMEM((total, LANES), bf16)] * 2
        + exchange_scratch(pairs, few)
        + [pltpu.VMEM((pairs, 2, few, LANES), bf16), pltpu.VMEM((pairs, count, LANES), bf16)]
        + [pltpu.VMEM((few, width), bf16)] * 2
        + [pltpu.VMEM(value.shape, value.dtype) for value in given]
        + [pltpu.SemaphoreType.DMA((len(given),))]
        + restore_scratch(count // 2, width),
        compiler_params=pltpu.CompilerParams(
            vmem_limit_bytes=60 << 20, collective_id=3, has_side_effects=True
        ),
        cost_estimate=pl.CostEstimate(
            flops=20 * width * count * total,
            bytes_accessed=64 * count * width,
            transcendentals=count * total * width // HALF,
        ),
        name="cross_back",
    )(*attention, kv, *given, *gains)


def attend_pair(pair, q_ref, kv, mq_ref, mk_ref, spaces, o_ref, l_ref):
    parts, rows = kv.shape[0], kv.shape[3]
    total = parts * rows
    ka0, ka1, va0, va1 = (space.at[pl.ds(0, total), :] for space in spaces)
    low = lax.broadcasted_iota(jnp.int32, (rows, LANES), 1) < HALF
    for part in range(parts):
        here = pl.ds(part * rows, rows)
        keys, values, mask = kv[part, pair, 0], kv[part, pair, 1], mk_ref[here, :]
        one = jnp.ones_like(values)
        ka0[here, :] = jnp.where(low, keys, mask)
        ka1[here, :] = jnp.where(low, mask, keys)
        va0[here, :] = jnp.where(low, values, one)
        va1[here, :] = jnp.where(low, one, values)
    count = q_ref.shape[1]
    block = largest_block(count, 256)
    low = lax.broadcasted_iota(jnp.int32, (block, LANES), 1) < HALF
    for number in range(count // block):
        here = pl.ds(number * block, block)
        query, mask = q_ref[pair, here, :], mq_ref[here, :]
        tops, sums = [], []
        for head, keys, values in ((0, ka0, va0), (1, ka1, va1)):
            mine = jnp.where(low, query, mask) if head == 0 else jnp.where(low, mask, query)
            score = dot(mine, keys[...], NT)
            top = jnp.max(score, axis=1, keepdims=True)
            weight = jnp.exp2(score - top).astype(bf16)
            sums.append(dot(weight, values[...]))
            tops.append(jnp.broadcast_to(top, (block, LANES)))
        total = jnp.where(low, sums[1], sums[0])
        top = jnp.where(low, tops[1], tops[0])
        out = jnp.where(low, sums[0], sums[1])
        o_ref[pair, here, :] = (out / pltpu.roll(total, HALF, 1)).astype(bf16)
        l_ref[pair, here, :] = top + jnp.log2(total)


class Gather:
    def __init__(self, here, kv, sems):
        self.here, self.kv, self.sems = here, kv, sems

    def copy(self, kind, at, size, sem):
        source, there = ((0, 1), (0, 2), (1, 3))[kind]
        pairs = pl.ds(at, size)
        return pltpu.make_async_remote_copy(
            src_ref=self.kv.at[source, pairs],
            dst_ref=self.kv.at[there, pairs],
            send_sem=self.sems.at[0, 3 * sem + kind],
            recv_sem=self.sems.at[1, 3 * sem + kind],
            device_id=self.here.partner(("x", "core", "core")[kind]),
            device_id_type=MESH,
        )


def begin_kernel(pairs, *refs):
    refs = list(refs)
    take = lambda count: [refs.pop(0) for _ in range(count)]
    large_ref, small_ref, cot_ref, clip_ref = take(4)
    weight_refs = take(9)
    (gains,) = take(1)
    first_gain, second_gain, query_gain, context_gain = (
        gains.at[i : i + 1, :] for i in range(4)
    )
    xl_out, xs_out, cot_out, kvl_out, kvs_out, ckv_out = take(6)
    nl_ref, ns_ref, ql_ref, qs_ref, ol_ref, ll_ref, os_ref, ls_ref = take(8)
    merged_ref, hidden_ref, second_ref, active_ref, slope_ref, context_ref = take(6)
    mql_ref, mkl_ref, mqs_ref, mks_ref = take(4)
    for gain, gain_out in zip((first_gain, second_gain, query_gain, context_gain), take(4)):
        gain_out[...] = gain[...]
    (grad_ref,) = take(1)
    xl, xs, cot, clip, kvl, kvs, ckv = take(7)
    wq, wk, wv, wo, up, down, wck, wcv, wco = weights = take(9)
    spaces = take(4)
    wide, total = take(2)
    move_sems, gather_l, gather_s, gather_c, gather_clip, load_sems, out_sems = take(7)
    near_l, near_s, near_c, x_sems = take(4)
    here = Here()
    z, core = here.tm // 2, here.bit["core"]
    stay = core == z // 2

    here.hail_line("x")

    odd = lax.rem(z, 2)
    from_seq = (odd, 1 - odd)

    def far(which, turn, source, there):
        rows = source.shape[1]
        place = (
            (2 * core + from_seq[turn]) * 2 + here.bit["x"],
            here.bit["y"] * 2 + z // 2,
        )
        return pltpu.make_async_remote_copy(
            src_ref=source.at[from_seq[turn]],
            dst_ref=there.at[pl.ds(turn * rows, rows)],
            send_sem=move_sems.at[0, 2 * which + turn],
            recv_sem=move_sems.at[1, 2 * which + turn],
            device_id=place,
            device_id_type=MESH,
        )

    def near(which, source, there):
        return pltpu.make_async_copy(
            source.at[from_seq[0]],
            there.at[pl.ds(0, source.shape[1])],
            move_sems.at[1, 2 * which],
        )

    def move(which, source, there):
        far(which, 1, source, there).start()

        @pl.when(stay)
        def _():
            near(which, source, there).start()

        @pl.when(jnp.logical_not(stay))
        def _():
            far(which, 0, source, there).start()

    def moved_out(which, source, there):
        far(which, 1, source, there).wait_send()

        @pl.when(jnp.logical_not(stay))
        def _():
            far(which, 0, source, there).wait_send()

    def moved_in(which, source, there):
        far(which, 1, source, there).wait_recv()

        @pl.when(stay)
        def _():
            near(which, source, there).wait()

        @pl.when(jnp.logical_not(stay))
        def _():
            far(which, 0, source, there).wait_recv()

    moves = ((0, clip_ref, clip.at[0, 0]), (1, small_ref, xs), (2, large_ref, xl), (3, cot_ref, cot))
    here.heard(8)
    move(*moves[0])
    move(*moves[1])
    loads = [
        pltpu.make_async_copy(source, there, load_sems.at[i])
        for i, (source, there) in enumerate(zip(weight_refs, weights))
    ]
    for load in loads:
        load.start()
    moved_out(*moves[0])
    moved_out(*moves[1])
    move(*moves[2])
    outs = []

    def keep(source, there):
        copy = pltpu.make_async_copy(source, there, out_sems.at[len(outs)])
        copy.start()
        outs.append(copy)

    def split(kv, part, value, key_weight, value_weight):
        keys = dot(value, key_weight[...]).astype(bf16)
        values = dot(value, value_weight[...]).astype(bf16)
        for pair in range(pairs):
            lanes = slice(pair * LANES, (pair + 1) * LANES)
            kv[part, pair, 0] = keys[:, lanes]
            kv[part, pair, 1] = values[:, lanes]

    def to_x(which, source, there):
        return pltpu.make_async_remote_copy(
            src_ref=source,
            dst_ref=there,
            send_sem=x_sems.at[0, which],
            recv_sem=x_sems.at[1, which],
            device_id=here.partner("x"),
            device_id_type=MESH,
        )

    x_small, x_large, x_cross = (
        to_x(0, ns_ref, near_s), to_x(1, nl_ref, near_l), to_x(2, context_ref, near_c)
    )

    def query_into(n_ref, q_ref):
        query = (dot(n_ref[...], wq[...]) * Q_SCALE).astype(bf16)
        for pair in range(pairs):
            q_ref[pair] = query[:, pair * LANES : (pair + 1) * LANES]

    large, small = Gather(here, kvl, gather_l), Gather(here, kvs, gather_s)
    cross, clips = Gather(here, ckv, gather_c), Gather(here, clip, gather_clip)

    moved_in(*moves[0])
    for kind in (0, 1):
        clips.copy(kind, 0, 1, 0).start()
    moved_in(*moves[1])
    keep(xs, xs_out)
    ns_ref[...] = norm(xs[...].astype(f32), first_gain[...])
    x_small.start()
    for i in (0, 1, 2):
        loads[i].wait()
    split(kvs, 0, ns_ref[...], wk, wv)
    small.copy(1, 0, pairs, 0).start()
    query_into(ns_ref, qs_ref)
    clips.copy(0, 0, 1, 0).wait_recv()
    clips.copy(2, 0, 1, 0).start()
    for kind in (1, 2):
        clips.copy(kind, 0, 1, 0).wait_recv()

    few = clip.shape[2]
    spot = lax.broadcasted_iota(jnp.int32, (1, LANES), 1) % HALF
    number = spot.astype(f32)
    some = spot < 4
    row = lax.broadcasted_iota(jnp.int32, (2 * few, few), 0) // 2
    twice = jnp.where(row == lax.broadcasted_iota(jnp.int32, (2 * few, few), 1), 1.0, 0.0)
    twice = twice.astype(bf16)
    for part in range(4):
        mine = clip[part, 0]
        for value, mk_ref, mq_ref in (
            (mine.astype(f32), mks_ref, mqs_ref),
            (dot(twice, mine), mkl_ref, mql_ref),
        ):
            rows = value.shape[0]
            mk_ref[pl.ds(part * rows, rows), :] = jnp.where(
                some & (value != number), NEGATIVE, 0.0
            ).astype(bf16)
            if part == 0:
                mq_ref[...] = jnp.where(some & (value == number), 1.0, 0.0).astype(bf16)

    x_small.wait_recv()
    split(kvs, 1, near_s[...], wk, wv)
    small.copy(2, 0, pairs, 0).start()
    moved_in(*moves[2])
    moved_out(*moves[2])
    move(*moves[3])
    keep(xl, xl_out)
    nl_ref[...] = norm(xl[...].astype(f32), first_gain[...])
    x_large.start()
    split(kvl, 0, nl_ref[...], wk, wv)
    large.copy(1, 0, pairs, 0).start()
    query_into(nl_ref, ql_ref)

    small.copy(1, 0, pairs, 0).wait_recv()
    small.copy(2, 0, pairs, 0).wait_recv()
    keep(kvs, kvs_out)

    def small_pair(pair, carry):
        attend_pair(pair, qs_ref, kvs, mqs_ref, mks_ref, spaces, os_ref, ls_ref)
        return carry

    lax.fori_loop(0, pairs, small_pair, 0)
    loads[3].wait()
    for pair in range(pairs):
        wide[:, pair * LANES : (pair + 1) * LANES] = os_ref[pair]
    hidden = xs[...].astype(f32) + dot(wide[...], wo[...])
    hidden_ref[...] = hidden
    second_ref[...] = norm(hidden, second_gain[...])
    total[...] = hidden
    loads[4].wait()
    loads[5].wait()
    width = wide.shape[1]
    steps = up.shape[1] // width
    for step in range(steps):
        lanes = slice(step * width, (step + 1) * width)
        active, slope = gelu_both(dot(second_ref[...], up[:, lanes]))
        active = active.astype(bf16)
        active_ref[:, lanes] = active
        slope_ref[:, lanes] = slope.astype(bf16)
        total[...] += dot(active, down[lanes, :])
    merged = total[...]
    merged_ref[...] = merged
    context = norm(merged, context_gain[...])
    context_ref[...] = context
    x_cross.start()
    x_large.wait_recv()
    split(kvl, 1, near_l[...], wk, wv)
    large.copy(2, 0, pairs, 0).start()
    loads[6].wait()
    loads[7].wait()
    split(ckv, 0, context, wck, wcv)
    cross.copy(1, 0, pairs, 0).start()

    def large_pair(pair, carry):
        attend_pair(pair, ql_ref, kvl, mql_ref, mkl_ref, spaces, ol_ref, ll_ref)
        return carry

    large.copy(1, 0, pairs, 0).wait_recv()
    large.copy(2, 0, pairs, 0).wait_recv()
    keep(kvl, kvl_out)
    lax.fori_loop(0, pairs // 2, large_pair, 0)
    x_cross.wait_recv()
    split(ckv, 1, near_c[...], wck, wcv)
    cross.copy(2, 0, pairs, 0).start()
    moved_in(*moves[3])
    moved_out(*moves[3])
    keep(cot, cot_out)
    loads[8].wait()
    grad_ref[...] = dot(cot[...], wco[...], NT).astype(bf16)
    lax.fori_loop(pairs // 2, pairs, large_pair, 0)
    cross.copy(1, 0, pairs, 0).wait_recv()
    cross.copy(2, 0, pairs, 0).wait_recv()
    keep(ckv, ckv_out)
    for kind in (0, 1, 2):
        clips.copy(kind, 0, 1, 0).wait_send()
        if kind:
            for gathered in (small, large, cross):
                gathered.copy(kind, 0, pairs, 0).wait_send()
    for copy in (x_small, x_large, x_cross):
        copy.wait_send()
    for copy in outs:
        copy.wait()


def begin(large, small, cotangent, clip, weights, gains):
    seqs, count, width = large.shape
    few = small.shape[1]
    count, few = 2 * count, 2 * few
    pairs = width // LANES
    hidden = weights[4].shape[1]
    shape = jax.ShapeDtypeStruct
    kv_l, kv_s = (4, pairs, 2, count, LANES), (4, pairs, 2, few, LANES)
    anywhere = pl.BlockSpec(memory_space=pl.ANY)
    vmem = pl.BlockSpec(memory_space=pltpu.VMEM)
    out_shape = [
        shape((count, width), bf16),
        shape((few, width), bf16),
        shape((count, width), bf16),
        shape(kv_l, bf16),
        shape(kv_s, bf16),
        shape(kv_s, bf16),
        shape((count, width), bf16),
        shape((few, width), bf16),
        shape((pairs, count, LANES), bf16),
        shape((pairs, few, LANES), bf16),
        shape((pairs, count, LANES), bf16),
        shape((pairs, count, LANES), f32),
        shape((pairs, few, LANES), bf16),
        shape((pairs, few, LANES), f32),
        shape((few, width), f32),
        shape((few, width), f32),
        shape((few, width), bf16),
        shape((few, hidden), bf16),
        shape((few, hidden), bf16),
        shape((few, width), bf16),
        shape((count, LANES), bf16),
        shape((4 * count, LANES), bf16),
        shape((few, LANES), bf16),
        shape((4 * few, LANES), bf16),
        *[shape((1, width), f32)] * 4,
        shape((count, width), bf16),
    ]
    dma = pltpu.SemaphoreType.DMA
    scratch = [
        pltpu.VMEM((count, width), bf16),
        pltpu.VMEM((few, width), bf16),
        pltpu.VMEM((count, width), bf16),
        pltpu.VMEM((4, 1, few, LANES), bf16),
        pltpu.VMEM(kv_l, bf16),
        pltpu.VMEM(kv_s, bf16),
        pltpu.VMEM(kv_s, bf16),
    ]
    scratch += [pltpu.VMEM(weight.shape, bf16) for weight in weights]
    scratch += [pltpu.VMEM((4 * count, LANES), bf16)] * 4
    scratch += [pltpu.VMEM((few, width), bf16), pltpu.VMEM((few, width), f32)]
    scratch += [dma((2, 8))] + [dma((2, 3))] * 4 + [dma((9,)), dma((6,))]
    scratch += [
        pltpu.VMEM((count, width), bf16),
        pltpu.VMEM((few, width), bf16),
        pltpu.VMEM((few, width), bf16),
        dma((2, 3)),
    ]
    return pl.pallas_call(
        functools.partial(begin_kernel, pairs),
        in_specs=[anywhere] * 13 + [vmem],
        out_specs=[anywhere] * 6 + [vmem] * 23,
        out_shape=out_shape,
        scratch_shapes=scratch,
        compiler_params=pltpu.CompilerParams(
            vmem_limit_bytes=62 << 20, collective_id=4, has_side_effects=True
        ),
        cost_estimate=pl.CostEstimate(
            flops=16 * count * 4 * count * width + 18 * few * width * hidden,
            bytes_accessed=40 << 20,
            transcendentals=count * count * 4 * width // HALF,
        ),
        name="begin",
    )(large, small, cotangent, clip, *weights, gains)


def cross_attend_kernel(q_ref, kv_ref, mq_ref, mk_ref, o_ref, l_ref, *spaces):
    attend_pair(0, q_ref, kv_ref, mq_ref, mk_ref, spaces, o_ref, l_ref)


def cross_attend(query, kv, mask_q, mask_k):
    pairs, count = query.shape[:2]
    rows = kv.shape[3]
    one = pl.BlockSpec((1, count, LANES), lambda i: (i, 0, 0))
    return pl.pallas_call(
        cross_attend_kernel,
        grid=(pairs,),
        in_specs=[
            one,
            pl.BlockSpec((4, 1, 2, rows, LANES), lambda i: (0, i, 0, 0, 0)),
            whole((count, LANES)),
            whole((4 * rows, LANES)),
        ],
        out_specs=[one, one],
        out_shape=[
            jax.ShapeDtypeStruct(query.shape, bf16),
            jax.ShapeDtypeStruct(query.shape, f32),
        ],
        scratch_shapes=[pltpu.VMEM((4 * rows, LANES), bf16)] * 4,
        compiler_params=pltpu.CompilerParams(vmem_limit_bytes=62 << 20),
        cost_estimate=pl.CostEstimate(
            flops=64 * count * rows * pairs * LANES,
            bytes_accessed=32 * count * pairs * LANES,
            transcendentals=8 * count * rows * pairs,
        ),
        name="cross_attend",
    )(query, kv, mask_q, mask_k)


def after(value, *needed):
    return lax.optimization_barrier((value, needed))[0]


CROSS_ORDERS = (BY_Y[:2], BY_ZL[:2])
SELVES_ORDERS = (BY_Y[:3], BY_ZL[:3], BY_Y[:3], BY_Y[2:], BY_ZL[2:])
SELVES_ENDS = (False, False, False, True, True)
SELVES_STAGES = (
    (0, 4, 11),
    (0, 4, 11),
    (0, 5, 11),
    (1, 3, 5, 7, 9),
    (1, 3, 5, 7, 9),
)


def paired_end(views, normed, large, small, cross, merged, weights, crosses, gains):
    large_view, small_view = views
    large_normed, small_normed, asked, context = normed
    large_q, large_mixed, large_logsum, large_mask_q, large_mask_k, large_kv = large
    small_q, small_mixed, small_logsum, small_mask_q, small_mask_k, small_kv = small
    cross_q, united, cross_logsum, cross_kv, united_grad, grad_out = cross
    large_merged, large_saved, small_merged, small_saved = merged
    query_weight, key_weight, value_weight, output_weight, up_weight, down_weight = weights
    first_gain, second_gain, query_gain, context_gain = gains
    width = large_view.shape[1]
    rows = width // 8
    (
        united_view, large_grad, small_grad, first, other, query_gain_grad, context_gain_grad,
    ) = cross_back(
        (cross_q, united_grad, united, cross_logsum, large_mask_q, small_mask_k),
        cross_kv,
        (united, crosses[3], large_merged, asked, context, grad_out, small_merged) + crosses[:3],
        (query_gain, context_gain),
    )
    (
        large_hidden, small_hidden, large_mixed_grad, small_mixed_grad, up_grad, down_grad,
        output_grad, second_gain_grad, first, other,
    ) = back(
        large_grad, small_grad, large_saved, small_saved, [large_mixed], small_mixed, output_weight,
        second_gain, up_weight, down_weight, True, (first, other), CROSS_ORDERS,
    )
    still = (8, rows // 2, width)
    selves, (large_grad, large_gain), sums = selves_back(
        (large_q, large_mixed_grad, large_mixed, large_logsum, large_mask_q, large_mask_k),
        large_kv,
        (small_q, small_mixed_grad, small_mixed, small_logsum, small_mask_q, small_mask_k),
        small_kv,
        (
            up_grad.reshape(8, 4 * rows, width), down_grad.reshape(8, 4 * rows, width),
            output_grad.reshape(8, 2 * rows, width // 2),
            first.reshape(still), other.reshape(still),
        ),
        (query_weight, key_weight, value_weight, large_hidden, large_view), first_gain,
        SELVES_ORDERS, SELVES_ENDS, SELVES_STAGES,
    )
    up, down, output, first, other = sums
    small_grad, last, late, gains = last_sums(
        tuple(selves) + (large_normed, small_normed, query_weight, key_weight, value_weight)
        + (small_view, small_hidden),
        (
            up.reshape(4, rows, width), down.reshape(4, rows, width),
            output.reshape(4, rows // 2, width // 2),
        ),
        (first_gain, large_gain, second_gain_grad, query_gain_grad, context_gain_grad),
    )
    return results(united_view, large_grad, small_grad, last, late, first, other, gains)


def per_device(tm, seq_size, *args):
    (
        large_view,
        small_view,
        clip_ids,
        first_gain,
        query_weight,
        key_weight,
        value_weight,
        output_weight,
        second_gain,
        up_weight,
        down_weight,
        query_gain,
        context_gain,
        cross_query,
        cross_key,
        cross_value,
        cross_output,
        cotangent,
    ) = args
    seqs, count, width = large_view.shape
    side = tm // 4
    gains = jnp.concatenate((first_gain, second_gain, query_gain, context_gain))
    gains = gains.astype(f32).reshape(4, width)
    first_gain, second_gain, query_gain, context_gain = (gains[i : i + 1] for i in range(4))

    tm_at = lax.axis_index("tm")
    seq_at = lax.axis_index("seq")
    z, x = tm_at // side, tm_at % side
    y, core = seq_at // 2, seq_at % 2
    places = [
        (pz, px, py, pc)
        for pz in range(4)
        for px in range(side)
        for py in range(2)
        for pc in range(2)
    ]

    def number(place):
        return (place[0] * side + place[1]) * seq_size + place[2] * 2 + place[3]

    def permute(value, place):
        pairs = [(number(at), number(place(*at))) for at in places]
        return lax.ppermute(value, ("tm", "seq"), pairs)

    def inverse(place):
        table = {place(*at): at for at in places}
        return lambda *at: table[at]

    go = (
        lambda z, x, y, c: (2 * c + z % 2, x, y, z // 2),
        lambda z, x, y, c: (2 * c + 1 - z % 2, x, y, z // 2),
    )
    back_home = tuple(inverse(place) for place in go)
    other_core = lambda value: permute(value, lambda z, x, y, c: (z, x, y, 1 - c))
    other_y = lambda value: permute(value, lambda z, x, y, c: (z, x, 1 - y, c))
    by_x = lambda value, d: permute(value, lambda z, x, y, c: (z, (x + d) % side, y, c))
    odd = z % 2 == 1

    def relocate(value):
        near = jnp.where(odd, value[1], value[0])
        far = jnp.where(odd, value[0], value[1])
        return jnp.concatenate([permute(near, go[0]), permute(far, go[1])], axis=0)

    def restore(value):
        rows = value.shape[0] // 2
        near, far = permute(value[:rows], back_home[0]), permute(value[rows:], back_home[1])
        return jnp.where(odd, jnp.stack([far, near]), jnp.stack([near, far]))

    def join(parts, axis):
        return parts[0] if len(parts) == 1 else jnp.concatenate(parts, axis=axis)

    def gather(value, axis=1):
        across = join([by_x(value, d) for d in range(1, side)], axis)
        return (value, across, other_core(value), other_core(across))

    def add(a, b):
        return (a.astype(f32) + b.astype(f32)).astype(bf16)

    def scatter_core(keep, send):
        return add(keep, other_core(send))

    def scatter_x(sums):
        rows = sums.shape[1] // side
        total = sums[:, :rows].astype(f32)
        for d in range(1, side):
            total = total + by_x(sums[:, d * rows : (d + 1) * rows], -d).astype(f32)
        return total.astype(bf16)

    if side == 2:
        clip = jnp.broadcast_to(
            clip_ids[:, ::2].astype(bf16)[:, :, None], (seqs, count // 2, LANES)
        )
        (
            large, small, grad_out, large_kv, small_kv, cross_kv, large_normed, small_normed,
            large_q, small_q, large_mixed, large_logsum, small_mixed, small_logsum, small_merged,
            *small_saved, context, large_mask_q, large_mask_k, small_mask_q, small_mask_k,
            first_gain, second_gain, query_gain, context_gain, united_grad,
        ) = begin(
            large_view, small_view, cotangent, clip,
            (query_weight, key_weight, value_weight, output_weight, up_weight, down_weight,
             cross_key, cross_value, cross_output),
            gains,
        )
        large_merged, *large_saved, asked, cross_q = rest(
            large, [large_mixed], output_weight, second_gain, up_weight, down_weight,
            query_gain, (cross_query,),
        )
        united, cross_logsum = cross_attend(cross_q, cross_kv, large_mask_q, small_mask_k)
        return paired_end(
            (large, small),
            (large_normed, small_normed, asked, context),
            (large_q, large_mixed, large_logsum, large_mask_q, large_mask_k, large_kv),
            (small_q, small_mixed, small_logsum, small_mask_q, small_mask_k, small_kv),
            (cross_q, united, cross_logsum, cross_kv, united_grad, grad_out),
            (large_merged, large_saved, small_merged, small_saved),
            (query_weight, key_weight, value_weight, output_weight, up_weight, down_weight),
            (cross_query, cross_key, cross_value, cross_output),
            (first_gain, second_gain, query_gain, context_gain),
        )

    groups = 3
    part = width // groups
    short_clips = gather(relocate(clip_ids[:, ::2].astype(f32)), 0)
    small = relocate(small_view)
    large = relocate(large_view)
    grad_out = relocate(after(cotangent, large))
    spot = lax.broadcasted_iota(jnp.int32, (1, LANES), 1) % HALF

    def mask_of_keys(numbers):
        away = numbers.astype(jnp.int32)[:, None] != spot
        return jnp.where((spot < 4) & away, NEGATIVE, 0.0).astype(bf16)

    def mask_of_queries(numbers):
        same = numbers.astype(jnp.int32)[:, None] == spot
        return jnp.where((spot < 4) & same, 1.0, 0.0).astype(bf16)

    short = jnp.concatenate(short_clips)
    small_mask_k = mask_of_keys(short)
    large_mask_k = mask_of_keys(jnp.repeat(short, 2))
    small_mask_q = mask_of_queries(short_clips[0])
    large_mask_q = mask_of_queries(jnp.repeat(short_clips[0], 2))

    small_normed, small_q, small_kv = front(
        small, first_gain, query_weight, key_weight, value_weight, 1
    )
    small_kv = gather(small_kv[0])
    large_normed, large_q, large_kv = front(
        large, first_gain, query_weight, key_weight, value_weight, groups
    )
    large_kv = [gather(kv) for kv in large_kv]
    small_mixed, small_logsum = attend(small_q, small_kv, small_mask_q, small_mask_k, 0, width)
    small_merged, *small_saved, context, cross_kv = rest(
        small, [small_mixed], output_weight, second_gain, up_weight, down_weight,
        context_gain, (cross_key, cross_value),
    )
    cross_kv = gather(cross_kv)
    united_grad = dot(grad_out, cross_output, NT).astype(bf16)
    large_out = ()
    for group, kv in enumerate(large_kv):
        large_out = attend(large_q, kv, large_mask_q, large_mask_k, group * part, part, large_out)
    large_mixed, large_logsum = large_out
    large_merged, *large_saved, asked, cross_q = rest(
        large, [large_mixed], output_weight, second_gain, up_weight, down_weight,
        query_gain, (cross_query,),
    )
    united, cross_logsum = attend(cross_q, cross_kv, large_mask_q, small_mask_k, 0, width)
    united_view = restore((large_merged + dot(united, cross_output)).astype(bf16))

    bits = side.bit_length() - 1
    moves = {"zh": lambda z, x, y, c: (z ^ 2, x, y, c), "zl": lambda z, x, y, c: (z ^ 1, x, y, c)}
    mine = {"zh": z // 2, "zl": z % 2}
    axes = {"zh": 0, "zl": 1}
    for bit in range(bits):
        flip = 1 << (bits - 1 - bit)
        moves[f"x{bit}"] = lambda z, x, y, c, flip=flip: (z, x ^ flip, y, c)
        mine[f"x{bit}"] = (x // flip) % 2
        axes[f"x{bit}"] = 2 + bit
    moves["core"] = lambda z, x, y, c: (z, x, y, 1 - c)
    moves["y"] = lambda z, x, y, c: (z, x, 1 - y, c)
    mine["core"], mine["y"] = core, y
    axes["core"], axes["y"] = 2 + bits, 3 + bits
    by_y = ["core", "y", "zl"] + [f"x{bit}" for bit in range(bits)] + ["zh"]
    by_zl = ["core", "zl", "y"] + [f"x{bit}" for bit in range(bits)] + ["zh"]
    by_yx = ["core", "y"] + [f"x{bit}" for bit in range(bits)] + ["zl", "zh"]

    class Sum:
        def __init__(self, local, order):
            rows, wide = local.shape
            self.value = local.reshape((2,) * (2 + bits) + (rows // tm, wide))
            self.todo = list(order)
            self.rows, self.wide = rows // tm, wide

        def step(self, *needed):
            name = self.todo.pop(0)
            axis = axes[name]
            size = self.value.shape[axis] // 2
            at = mine[name]
            keep = lax.dynamic_slice_in_dim(self.value, at * size, size, axis)
            send = lax.dynamic_slice_in_dim(self.value, (1 - at) * size, size, axis)
            self.value = add(keep, permute(send, moves[name]))
            return self.value

        def finish(self):
            while self.todo:
                self.step()
            value = self.value.reshape(self.rows // 2, self.wide // 2)
            other = other_y(value)
            value = jnp.where(
                y == 0,
                jnp.concatenate([value, other], axis=1),
                jnp.concatenate([other, value], axis=1),
            )
            other = other_core(value)
            return jnp.where(
                core == 0,
                jnp.concatenate([value, other], axis=0),
                jnp.concatenate([other, value], axis=0),
            ).astype(f32)

    cross_groups = 2
    cross_part = width // cross_groups
    dcq, dckv = [], []
    for group in range(cross_groups):
        query = after(cross_q, *dcq[-1:])
        at = group * cross_part
        dq, keep, send = attend_back(
            query, cross_kv, united_grad, united, cross_logsum,
            large_mask_q, small_mask_k, at, at, at, cross_part,
        )
        dcq.append(dq)
        dckv.append(scatter_x(scatter_core(keep, send)))
    dcq = jnp.concatenate(dcq, axis=1)
    dck = jnp.concatenate([kv[0] for kv in dckv], axis=1)
    dcv = jnp.concatenate([kv[1] for kv in dckv], axis=1)
    extra, query_gain_grad = norm_back(dot(dcq, cross_query, NT), large_merged, query_gain)
    large_merged_grad = grad_out.astype(f32) + extra
    small_merged_grad, context_gain_grad = norm_back(
        dot(dck, cross_key, NT) + dot(dcv, cross_value, NT), small_merged, context_gain
    )
    cross_parts = [
        dot(united, grad_out, TN).astype(bf16),
        dot(asked, dcq, TN).astype(bf16),
        dot(context, dck, TN).astype(bf16),
        dot(context, dcv, TN).astype(bf16),
    ]
    (
        large_hidden_grad,
        small_hidden_grad,
        large_mixed_grad,
        small_mixed_grad,
        up_grad,
        down_grad,
        output_grad,
        second_gain_grad,
    ) = back(
        large_merged_grad, small_merged_grad, large_saved, small_saved, [large_mixed], small_mixed,
        output_weight, second_gain, up_weight, down_weight, False,
    )
    cross_sum = Sum(jnp.concatenate(cross_parts, axis=1), by_y)
    up_sum = Sum(up_grad, by_y)
    down_sum = Sum(down_grad, by_zl)
    cross_sum.step()
    small_dq, keep, send = attend_back(
        after(small_q, cross_sum.value), small_kv, small_mixed_grad, small_mixed, small_logsum,
        small_mask_q, small_mask_k, 0, 0, 0, width,
    )
    small_sums = scatter_core(keep, send)
    up_sum.step()
    down_sum.step()
    cross_sum.step()
    needed = [small_dq, up_sum.value, down_sum.value]
    normed = jnp.concatenate([large_normed, small_normed], axis=0)
    last_sums, dqs, dkvs = [], [], []
    pending = None
    for group in range(groups):
        at = group * part
        dq, keep, send = attend_back(
            after(large_q, *needed), large_kv[group], large_mixed_grad, large_mixed, large_logsum,
            large_mask_q, large_mask_k, at, at, 0, part,
        )
        sums = scatter_core(keep, send)
        dqs.append(dq)
        needed = [dq]
        if group == 0:
            small_dkv = scatter_x(small_sums)
            needed += [cross_sum.value, small_sums]
        if group == 1:
            needed += [small_dkv, up_sum.step(), down_sum.step(), cross_sum.step()]
        if pending is not None:
            needed.append(pending.step())
        dkv = scatter_x(sums)
        dkvs.append(dkv)
        local = jnp.concatenate(
            [
                jnp.concatenate([dq, dkv[0], dkv[1]], axis=1),
                jnp.concatenate(
                    [
                        small_dq[:, at : at + part],
                        small_dkv[0, :, at : at + part],
                        small_dkv[1, :, at : at + part],
                    ],
                    axis=1,
                ),
            ],
            axis=0,
        )
        local = dot(normed, local, TN).astype(bf16)
        pending = Sum(local, by_yx)
        last_sums.append(pending)

    def front_back(view, hidden_grad, dq, dk, dv):
        grad = (
            dot(dq, query_weight, NT) + dot(dk, key_weight, NT) + dot(dv, value_weight, NT)
        )
        extra, gain_part = norm_back(grad, view.astype(f32), first_gain)
        return (hidden_grad + extra).astype(bf16), gain_part

    small_grad, small_gain = front_back(
        small, small_hidden_grad, small_dq, small_dkv[0], small_dkv[1]
    )
    large_grad, large_gain = front_back(
        large,
        large_hidden_grad,
        jnp.concatenate(dqs, axis=1),
        jnp.concatenate([kv[0] for kv in dkvs], axis=1),
        jnp.concatenate([kv[1] for kv in dkvs], axis=1),
    )
    small_grad = restore(small_grad).astype(f32)
    large_grad = restore(large_grad).astype(f32)
    output_sum = Sum(output_grad, by_yx)
    gain_rows = jnp.concatenate(
        [large_gain + small_gain, second_gain_grad, query_gain_grad, context_gain_grad], axis=0
    )
    wide = width // tm
    gain_rows = jnp.transpose(gain_rows.reshape(4, tm, wide), (1, 0, 2)).astype(bf16)
    gain_rows = jnp.pad(gain_rows, ((0, 0), (0, 28), (0, 2 * LANES - wide)))
    gain_sum = Sum(gain_rows.reshape(tm * 32, 2 * LANES), by_yx)

    cross_total = cross_sum.finish()
    up_total = up_sum.finish()
    down_total = down_sum.finish()
    output_total = output_sum.finish()
    last_totals = [total.finish() for total in last_sums]
    gain_total = gain_sum.finish()
    cross_grads = [cross_total[:, i * width : (i + 1) * width] for i in range(4)]
    last_grads = [
        jnp.concatenate([total[:, i * part : (i + 1) * part] for total in last_totals], axis=1)
        for i in range(3)
    ]
    gain_grads = [gain_total[i, :wide] for i in range(4)]
    return (
        united_view,
        large_grad,
        small_grad,
        gain_grads[0],
        last_grads[0],
        last_grads[1],
        last_grads[2],
        output_total,
        gain_grads[1],
        up_total,
        down_total,
        gain_grads[2],
        gain_grads[3],
        cross_grads[1],
        cross_grads[2],
        cross_grads[3],
        cross_grads[0],
    )


def solution(mesh):
    token = P("seq", "tm", None)
    in_specs = (token, token, P("seq", "tm")) + (P(),) * 14 + (token,)
    vector, matrix = P("tm"), P("tm", None)
    out_specs = (
        (token, token, token, vector)
        + (matrix,) * 4
        + (vector, matrix, matrix, vector, vector)
        + (matrix,) * 4
    )
    return jax.shard_map(
        functools.partial(per_device, mesh.shape["tm"], mesh.shape["seq"]),
        mesh=mesh,
        in_specs=in_specs,
        out_specs=out_specs,
        check_vma=False,
    )
```

```python
import functools

import jax
import jax.numpy as jnp
from jax import lax
from jax.experimental import pallas as pl
from jax.experimental.pallas import tpu as pltpu
from jax.sharding import PartitionSpec as P

HEADS = 12
EPS = 1e-05
NEGATIVE = -1e30
LOG2E = 1.4426950408889634
LN2 = 0.6931471805599453
LANES = 128
HALF = 64

bf16 = jnp.bfloat16
f32 = jnp.float32
NT = (((1,), (1,)), ((), ()))
NN = (((1,), (0,)), ((), ()))
TN = (((0,), (0,)), ((), ()))


def dot(a, b, dims=NN):
    return lax.dot_general(a, b, dims, preferred_element_type=f32)


def largest_block(rows, most):
    block = min(rows, most)
    while rows % block or block % 16:
        block -= 1
    return block


def columns(rows, at):
    return pl.BlockSpec((rows, LANES), lambda i: (0, i + at))


def pair_columns(rows, at):
    return pl.BlockSpec((2, rows, LANES), lambda i: (0, 0, i + at))


def whole(shape):
    return pl.BlockSpec(shape, lambda i: (0,) * len(shape))


def attend_kernel(parts, block, *refs):
    q_ref, mq_ref, mk_ref = refs[:3]
    kv_refs = refs[3 : 3 + parts]
    o_ref, l_ref, ka0, ka1, va0, va1 = refs[-6:]
    count = q_ref.shape[0]
    first = 0
    for kv_ref in kv_refs:
        rows = kv_ref.shape[1]
        low = lax.broadcasted_iota(jnp.int32, (rows, LANES), 1) < HALF
        here = pl.ds(first, rows)
        keys, values, mask = kv_ref[0], kv_ref[1], mk_ref[here, :]
        one = jnp.ones_like(values)
        ka0[here, :] = jnp.where(low, keys, mask)
        ka1[here, :] = jnp.where(low, mask, keys)
        va0[here, :] = jnp.where(low, values, one)
        va1[here, :] = jnp.where(low, one, values)
        first += rows
    low = lax.broadcasted_iota(jnp.int32, (block, LANES), 1) < HALF
    for number in range(count // block):
        here = pl.ds(number * block, block)
        query, mask = q_ref[here, :], mq_ref[here, :]
        tops, sums = [], []
        for head, keys, values in ((0, ka0, va0), (1, ka1, va1)):
            mine = jnp.where(low, query, mask) if head == 0 else jnp.where(low, mask, query)
            score = dot(mine, keys[...], NT)
            top = jnp.max(score, axis=1, keepdims=True)
            weight = jnp.exp2(score - top).astype(bf16)
            sums.append(dot(weight, values[...]))
            tops.append(jnp.broadcast_to(top, (block, LANES)))
        total = jnp.where(low, sums[1], sums[0])
        top = jnp.where(low, tops[1], tops[0])
        out = jnp.where(low, sums[0], sums[1])
        o_ref[here, :] = (out / pltpu.roll(total, HALF, 1)).astype(bf16)
        l_ref[here, :] = top + jnp.log2(total)


def attend(query, kv, mask_q, mask_k, at, width, earlier=()):
    count = query.shape[0]
    total = sum(part.shape[1] for part in kv)
    out = lambda kind: jax.ShapeDtypeStruct((count, query.shape[1]), kind)
    given = 3 + len(kv)
    return pl.pallas_call(
        functools.partial(attend_kernel, len(kv), largest_block(count, 256)),
        grid=(width // LANES,),
        in_specs=[columns(count, at // LANES), whole((count, LANES)), whole((total, LANES))]
        + [pair_columns(part.shape[1], 0) for part in kv]
        + [pl.BlockSpec(memory_space=pl.ANY)] * len(earlier),
        out_specs=[columns(count, at // LANES)] * 2,
        out_shape=[out(bf16), out(f32)],
        scratch_shapes=[pltpu.VMEM((total, LANES), bf16)] * 4,
        input_output_aliases={given + i: i for i in range(len(earlier))},
        compiler_params=pltpu.CompilerParams(vmem_limit_bytes=40 << 20),
        cost_estimate=pl.CostEstimate(
            flops=16 * count * total * width,
            bytes_accessed=width * (count * 8 + total * 4),
            transcendentals=count * total * width // HALF,
        ),
        name="attend",
    )(query, mask_q, mask_k, *kv, *earlier)


def three(value):
    first = value.astype(bf16)
    rest = value - first.astype(f32)
    second = rest.astype(bf16)
    return first, second, (rest - second.astype(f32)).astype(bf16)


def attend_back_kernel(parts, block, *refs):
    q_ref, do_ref, o_ref, l_ref, mq_ref, mk_ref = refs[:6]
    kv_refs = refs[6 : 6 + parts]
    dq_ref, keep_ref, send_ref, keys_at, values_at = refs[6 + parts :]
    count = q_ref.shape[0]
    first = 0
    for kv_ref in kv_refs:
        here = pl.ds(first, kv_ref.shape[1])
        keys_at[here, :] = kv_ref[0]
        values_at[here, :] = kv_ref[1]
        first += kv_ref.shape[1]
    lane = lax.broadcasted_iota(jnp.int32, (count, LANES), 1)
    low = lane < HALF
    spot = lane % HALF
    query, grad, mask = q_ref[...], do_ref[...], mq_ref[...]
    zero = jnp.zeros_like(query)
    product = grad.astype(f32) * o_ref[...].astype(f32)
    delta0 = jnp.sum(jnp.where(low, product, 0.0), axis=1, keepdims=True)
    delta1 = jnp.sum(jnp.where(low, 0.0, product), axis=1, keepdims=True)
    delta = jnp.where(low, delta1, delta0)

    def beside(base, value):
        a, b, c = three(-value)
        return jnp.where(spot == 4, a, jnp.where(spot == 5, b, jnp.where(spot == 6, c, base)))

    query_side = beside(mask, l_ref[...])
    grad_side = beside(zero, delta)
    query_a = (jnp.where(low, query, query_side), jnp.where(low, query_side, query))
    grad_a = (jnp.where(low, grad, grad_side), jnp.where(low, grad_side, grad))
    query_m = (jnp.where(low, query, zero), jnp.where(low, zero, query))
    grad_m = (jnp.where(low, grad, zero), jnp.where(low, zero, grad))
    lane_k = lax.broadcasted_iota(jnp.int32, (block, LANES), 1)
    low_k = lane_k < HALF
    spot_k = lane_k % HALF
    one = jnp.where((spot_k >= 4) & (spot_k < 7), 1.0, 0.0).astype(bf16)
    dq = jnp.zeros((count, LANES), f32)
    for number in range(first // block):
        here = pl.ds(number * block, block)
        keys, values = keys_at[here, :], values_at[here, :]
        side = mk_ref[here, :] + one
        nought = jnp.zeros_like(keys)
        dk = jnp.zeros((block, LANES), f32)
        dv = jnp.zeros((block, LANES), f32)
        for head in (0, 1):
            pick = lambda a, b: jnp.where(low_k, a, b) if head == 0 else jnp.where(low_k, b, a)
            prob = jnp.exp2(dot(query_a[head], pick(keys, side), NT))
            change = dot(grad_a[head], pick(values, one), NT)
            score_grad = (prob * change).astype(bf16)
            dv += dot(prob.astype(bf16), grad_m[head], TN)
            dk += dot(score_grad, query_m[head], TN)
            dq += dot(score_grad, pick(keys, nought))
        out_ref = keep_ref if number * block < first // 2 else send_ref
        there = pl.ds(number * block % (first // 2), block)
        out_ref[0, there, :] = (dk * LN2).astype(bf16)
        out_ref[1, there, :] = dv.astype(bf16)
    dq_ref[...] = (dq * HALF**-0.5).astype(bf16)


def attend_back(query, kv, grad, out, logsum, mask_q, mask_k, at, at_out, at_kv, width):
    count = query.shape[0]
    total = sum(part.shape[1] for part in kv)
    return pl.pallas_call(
        functools.partial(attend_back_kernel, len(kv), largest_block(total // 2, 512)),
        grid=(width // LANES,),
        in_specs=[columns(count, at // LANES)] * 2
        + [columns(count, at_out // LANES)] * 2
        + [whole((count, LANES)), whole((total, LANES))]
        + [pair_columns(part.shape[1], at_kv // LANES) for part in kv],
        out_specs=[columns(count, 0)] + [pair_columns(total // 2, 0)] * 2,
        out_shape=[jax.ShapeDtypeStruct((count, width), bf16)]
        + [jax.ShapeDtypeStruct((2, total // 2, width), bf16)] * 2,
        scratch_shapes=[pltpu.VMEM((total, LANES), bf16)] * 2,
        compiler_params=pltpu.CompilerParams(vmem_limit_bytes=40 << 20),
        cost_estimate=pl.CostEstimate(
            flops=20 * count * total * width,
            bytes_accessed=width * (count * 12 + total * 8),
            transcendentals=count * total * width // HALF,
        ),
        name="attend_back",
    )(query, grad, out, logsum, mask_q, mask_k, *kv)


def norm_stats(value):
    mean = jnp.mean(value, axis=-1, keepdims=True)
    centred = value - mean
    spread = jnp.mean(centred * centred, axis=-1, keepdims=True)
    return centred, lax.rsqrt(spread + EPS)


def norm(value, gain):
    centred, scale = norm_stats(value)
    return (centred * scale * gain).astype(bf16)


def norm_back(grad, value, gain):
    centred, scale = norm_stats(value)
    unit = centred * scale
    gain_grad = jnp.sum(grad * unit, axis=0, keepdims=True)
    grad = grad * gain
    extra = scale * (
        grad
        - jnp.mean(grad, axis=-1, keepdims=True)
        - unit * jnp.mean(grad * unit, axis=-1, keepdims=True)
    )
    return extra, gain_grad


Q_SCALE = LOG2E * HALF**-0.5


def front_kernel(x_ref, gain_ref, wq_ref, wk_ref, wv_ref, n_ref, q_ref, *kv_refs):
    normed = norm(x_ref[...].astype(f32), gain_ref[...])
    n_ref[...] = normed
    width = kv_refs[0].shape[2]
    keys = dot(normed, wk_ref[...]).astype(bf16)
    values = dot(normed, wv_ref[...]).astype(bf16)
    for group, kv_ref in enumerate(kv_refs):
        kv_ref[0] = keys[:, group * width : (group + 1) * width]
        kv_ref[1] = values[:, group * width : (group + 1) * width]
    q_ref[...] = (dot(normed, wq_ref[...]) * Q_SCALE).astype(bf16)


def front(view, gain, wq, wk, wv, groups):
    rows, width = view.shape
    part = width // groups
    result = pl.pallas_call(
        front_kernel,
        out_shape=[jax.ShapeDtypeStruct((rows, width), bf16)] * 2
        + [jax.ShapeDtypeStruct((2, rows, part), bf16)] * groups,
        compiler_params=pltpu.CompilerParams(vmem_limit_bytes=40 << 20),
        cost_estimate=pl.CostEstimate(
            flops=6 * rows * width * width,
            bytes_accessed=6 * width * width + 10 * rows * width,
            transcendentals=0,
        ),
        name="front",
    )(view, gain, wq, wk, wv)
    return result[0], result[1], result[2:]


GELU_A = 0.7978845608028654
GELU_B = 0.044715


def gelu_both(value):
    square = value * value
    bent = jnp.tanh(GELU_A * value * (1.0 + GELU_B * square))
    half = 0.5 * (1.0 + bent)
    slope = half + 0.5 * value * (1.0 - bent * bent) * (
        GELU_A * (1.0 + 3.0 * GELU_B * square)
    )
    return value * half, slope


def fill_wide(wide, refs, rows, first):
    at, there = 0, pl.ds(first, rows)
    for ref in refs:
        if len(ref.shape) == 3:
            for pair in range(ref.shape[0]):
                wide[there, at : at + LANES] = ref[pair]
                at += LANES
        else:
            wide[there, at : at + ref.shape[1]] = ref[...]
            at += ref.shape[1]


def rest_kernel(steps, mixes, is_query, *refs):
    x_ref = refs[0]
    mixed_refs = refs[1 : 1 + mixes]
    wo_ref, gain_ref, up_ref, down_ref, next_gain_ref = refs[1 + mixes : 6 + mixes]
    next_refs = refs[6 + mixes : -9]
    merged_ref, hidden_ref, second_ref, active_ref, slope_ref = refs[-9:-4]
    asked_ref, out_ref, total, scratch = refs[-4:]
    step = pl.program_id(0)

    @pl.when(step == 0)
    def _():
        hidden = x_ref[...].astype(f32)
        fill_wide(scratch, mixed_refs, scratch.shape[0], 0)
        hidden = hidden + dot(scratch[...], wo_ref[...])
        hidden_ref[...] = hidden
        second_ref[...] = norm(hidden, gain_ref[...])
        total[...] = hidden

    rows = total.shape[0] // 2
    halves = [pl.ds(at * rows, rows) for at in (0, 1)]
    inners = [dot(second_ref[half, :], up_ref[...]) for half in halves]
    for half, inner in zip(halves, inners):
        active, slope = gelu_both(inner)
        active = active.astype(bf16)
        active_ref[half, :] = active
        slope_ref[half, :] = slope.astype(bf16)
        total[half, :] += dot(active, down_ref[...])

    @pl.when(step == steps - 1)
    def _():
        merged = total[...]
        merged_ref[...] = merged
        asked = norm(merged, next_gain_ref[...])
        asked_ref[...] = asked
        if is_query:
            query = (dot(asked, next_refs[0][...]) * Q_SCALE).astype(bf16)
            if len(out_ref.shape) == 3:
                for pair in range(out_ref.shape[0]):
                    out_ref[pair] = query[:, pair * LANES : (pair + 1) * LANES]
            else:
                out_ref[...] = query
        else:
            out_ref[0] = dot(asked, next_refs[0][...]).astype(bf16)
            out_ref[1] = dot(asked, next_refs[1][...]).astype(bf16)


def rest(view, mixed, wo, gain, up, down, next_gain, next_weights):
    rows, width = view.shape
    steps = up.shape[1] // width
    is_query = len(next_weights) == 1
    flat = whole((rows, width))
    slab = pl.BlockSpec((rows, width), lambda i: (0, i))
    square = whole((width, width))
    shape = lambda kind: jax.ShapeDtypeStruct((rows, width), kind)
    wide = jax.ShapeDtypeStruct((rows, up.shape[1]), bf16)
    last = (rows, width) if is_query else (2, rows, width)
    if len(mixed[0].shape) == 3:
        last = (width // LANES, rows, LANES)
    return pl.pallas_call(
        functools.partial(rest_kernel, steps, len(mixed), is_query),
        grid=(steps,),
        in_specs=[flat]
        + [whole(m.shape) for m in mixed]
        + [square, whole((1, width))]
        + [slab_of(width, width), pl.BlockSpec((width, width), lambda i: (i, 0))]
        + [whole((1, width))]
        + [square] * len(next_weights),
        out_specs=[flat, flat, flat, slab, slab, flat, whole(last)],
        out_shape=[shape(f32), shape(f32), shape(bf16), wide, wide, shape(bf16)]
        + [jax.ShapeDtypeStruct(last, bf16)],
        scratch_shapes=[pltpu.VMEM((rows, width), f32), pltpu.VMEM((rows, width), bf16)],
        compiler_params=pltpu.CompilerParams(vmem_limit_bytes=62 << 20),
        cost_estimate=pl.CostEstimate(
            flops=2 * rows * width * (4 * up.shape[1] // 2 + 2 * width),
            bytes_accessed=width * width * 22 + rows * width * 32,
            transcendentals=rows * up.shape[1],
        ),
        name="rest",
    )(view, *mixed, wo, gain, up, down, next_gain, *next_weights)


def slab_of(rows, width):
    return pl.BlockSpec((rows, width), lambda i: (0, i))


def back_kernel(steps, mixes, sizes, laid, orders, *refs):
    gl_ref, gs_ref, al_ref, as_ref, sl_ref, ss_ref = refs[:6]
    cl_ref, cs_ref, hl_ref, hs_ref = refs[6:10]
    mixed_refs = refs[10 : 10 + mixes]
    mixed_s_ref, wo_ref, gain_ref, up_ref, down_ref = refs[10 + mixes : 15 + mixes]
    flows = len(orders)
    locals_, outs = refs[15 + mixes : 15 + mixes + flows], refs[15 + mixes + flows :]
    (hgl_ref, hgs_ref, ml_ref, ms_ref, dup_ref, ddown_ref, dwo_ref, dgain_ref) = outs[:8]
    sums, outs = outs[8 : 8 + flows], outs[8 + flows :]
    branch, second, total, active, inner_grad, mixed = outs[:6]
    large, small = sizes
    top, bottom = pl.ds(0, large), pl.ds(large, small)
    step = pl.program_id(0)
    if flows:
        here = Here()
        rest_refs = list(outs[6:])
        running = [
            Flow(here, order, local, rest_refs, True, False)
            for order, local in zip(orders, locals_)
        ]

        @pl.when(step == 0)
        def _():
            here.hail(*ALL_PARTNERS)
            here.heard(len(ALL_PARTNERS))
            for flow in running:
                flow.act(0)

    @pl.when(step == 0)
    def _():
        branch[top, :] = gl_ref[...].astype(bf16)
        branch[bottom, :] = gs_ref[...].astype(bf16)
        second[top, :] = cl_ref[...]
        second[bottom, :] = cs_ref[...]
        total[...] = jnp.zeros_like(total)

    grad = dot(branch[...], down_ref[...], NT)
    inner_grad[top, :] = (grad[:large] * sl_ref[...].astype(f32)).astype(bf16)
    inner_grad[bottom, :] = (grad[large:] * ss_ref[...].astype(f32)).astype(bf16)
    active[top, :] = al_ref[...]
    active[bottom, :] = as_ref[...]
    down = dot(active[...], branch[...], TN).astype(bf16)
    upper = dot(second[...], inner_grad[...], TN).astype(bf16)
    if laid:
        rows = dup_ref.shape[1]
        for at in range(8):
            zl, x, zh = at // 4, at // 2 % 2, at % 2
            first = ((zh * 2 + zl) * 2 + x) * rows
            dup_ref[at] = upper[first : first + rows]
        for x, core, y in ((a, b, c) for a in (0, 1) for b in (0, 1) for c in (0, 1)):
            first = (x * 4 + core * 2 + y) * rows
            there = core * 16 + (step % 2) * 8 + y * 4 + x * 2 + step // 2
            ddown_ref[there] = down[first : first + rows]
    else:
        dup_ref[...] = upper
        ddown_ref[...] = down
    total[...] += dot(inner_grad[...], up_ref[...], NT)

    @pl.when(step == steps - 1)
    def _():
        extra, gain_l = norm_back(total[top, :], hl_ref[...], gain_ref[...])
        hidden_grad = gl_ref[...] + extra
        hgl_ref[...] = hidden_grad
        branch[top, :] = hidden_grad.astype(bf16)
        extra, gain_s = norm_back(total[bottom, :], hs_ref[...], gain_ref[...])
        hidden_grad = gs_ref[...] + extra
        hgs_ref[...] = hidden_grad
        branch[bottom, :] = hidden_grad.astype(bf16)
        dgain_ref[...] = gain_l + gain_s
        mixed_grad = dot(branch[...], wo_ref[...], NT).astype(bf16)
        ml_ref[...] = mixed_grad[:large]
        ms_ref[...] = mixed_grad[large:]
        fill_wide(mixed, mixed_refs, large, 0)
        fill_wide(mixed, [mixed_s_ref], small, large)
        value = dot(mixed[...], branch[...], TN).astype(bf16)
        if laid:
            rows, wide = dwo_ref.shape[1:]
            for at, (core, y, tm) in enumerate(spots(BY_Y)):
                first = (tm * 2 + core) * rows
                dwo_ref[at] = value[first : first + rows, y * wide : (y + 1) * wide]
        else:
            dwo_ref[...] = value

    for flow in range(flows):
        for stage, when in enumerate((0, steps - 1)):

            @pl.when(step == when)
            def _(flow=flow, stage=stage):
                running[flow].act(stage + 1)
                if stage == 1:
                    sums[flow][...] = running[flow].result()


def back(
    grad_l, grad_s, saved_l, saved_s, mixed_l, mixed_s, wo, gain, up, down, laid, flows=(), orders=()
):
    (hidden_l, second_l, active_l, slope_l) = saved_l
    (hidden_s, second_s, active_s, slope_s) = saved_s
    large, width = grad_l.shape
    small = grad_s.shape[0]
    rows = large + small
    hidden = up.shape[1]
    part = width
    steps = hidden // part
    fl, fs = whole((large, width)), whole((small, width))
    square = whole((width, width))
    up_slab = slab_of(width, part)
    down_slab = pl.BlockSpec((part, width), lambda i: (i, 0))
    shape = jax.ShapeDtypeStruct
    results = [flow_result(o, f.shape[1:], False) for o, f in zip(orders, flows)]
    scratch = [s for o, f in zip(orders, flows) for s in flow_scratch(o, f.shape[1:], True, False)]
    out_up, out_down, out_square = up_slab, down_slab, square
    up_shape, down_shape, square_shape = up.shape, down.shape, (width, width)
    if laid:
        block = (width // 8, width)
        up_shape = down_shape = (32,) + block
        square_shape = (32, width // 16, width // 2)
        out_up = pl.BlockSpec((8,) + block, lambda i: (i, 0, 0))
        out_down, out_square = whole(down_shape), whole(square_shape)
    return pl.pallas_call(
        functools.partial(back_kernel, steps, len(mixed_l), (large, small), laid, orders),
        grid=(steps,),
        in_specs=[fl, fs]
        + [slab_of(large, part), slab_of(small, part)] * 2
        + [fl, fs, fl, fs]
        + [whole(m.shape) for m in mixed_l]
        + [whole(mixed_s.shape), square, whole((1, width)), up_slab, down_slab]
        + [pl.BlockSpec(memory_space=pl.ANY)] * len(flows),
        out_specs=[fl, fs, fl, fs, out_up, out_down, out_square, whole((1, width))]
        + [whole(result.shape) for result in results],
        out_shape=[
            shape((large, width), f32),
            shape((small, width), f32),
            shape((large, width), bf16),
            shape((small, width), bf16),
            shape(up_shape, bf16),
            shape(down_shape, bf16),
            shape(square_shape, bf16),
            shape((1, width), f32),
        ]
        + results,
        scratch_shapes=[
            pltpu.VMEM((rows, width), bf16),
            pltpu.VMEM((rows, width), bf16),
            pltpu.VMEM((rows, width), f32),
            pltpu.VMEM((rows, part), bf16),
            pltpu.VMEM((rows, part), bf16),
            pltpu.VMEM((rows, width), bf16),
        ]
        + scratch,
        compiler_params=pltpu.CompilerParams(
            vmem_limit_bytes=60 << 20,
            has_side_effects=bool(flows),
            collective_id=0 if flows else None,
        ),
        cost_estimate=pl.CostEstimate(
            flops=2 * rows * width * (4 * hidden + 2 * width),
            bytes_accessed=width * width * 36 + rows * width * 40,
            transcendentals=0,
        ),
        name="back",
    )(
        grad_l, grad_s, active_l, active_s, slope_l, slope_s, second_l, second_s, hidden_l, hidden_s,
        *mixed_l, mixed_s, wo, gain, up, down, *flows,
    )


MESH = pl.DeviceIdType.MESH
BY_Y = ("core", "y", "zl", "x", "zh")
BY_ZL = ("core", "zl", "y", "x", "zh")
BY_X = ("core", "x", "zl", "y", "zh")
BY_YX = ("core", "y", "x", "zl", "zh")


def spots(order):
    out = []
    for at in range(32):
        bit = {name: (at >> (4 - i)) & 1 for i, name in enumerate(order)}
        out.append((bit["core"], bit["y"], (bit["zh"] * 2 + bit["zl"]) * 2 + bit["x"]))
    return out


class Here:
    def __init__(self):
        tm, seq = lax.axis_index("tm"), lax.axis_index("seq")
        self.tm, self.seq = tm, seq
        self.bit = {
            "zh": tm // 4,
            "zl": (tm // 2) % 2,
            "x": tm % 2,
            "y": seq // 2,
            "core": seq % 2,
        }

    def partner(self, *names):
        tm, seq = self.tm, self.seq
        for name in names:
            one = 1 - 2 * self.bit[name]
            if name in ("y", "core"):
                seq = seq + one * (2 if name == "y" else 1)
            else:
                tm = tm + one * {"zh": 4, "zl": 2, "x": 1}[name]
        return (tm, seq)

    def hail(self, *partners):
        self.hail_all([self.partner(*names) for names in partners])

    def hail_line(self, *more):
        z, core = self.tm // 2, self.bit["core"]
        self.hail_all(
            [
                (
                    lax.rem(z + dz, 4) * 2 + self.bit["x"],
                    self.bit["y"] * 2 + lax.rem(core + dc, 2),
                )
                for dz in range(4)
                for dc in range(2)
                if dz or dc
            ]
            + [self.partner(name) for name in more]
        )

    def hail_all(self, places):
        barrier = pltpu.get_barrier_semaphore()
        for place in places:
            pl.semaphore_signal(barrier, inc=1, device_id=place, device_id_type=MESH)

    def heard(self, count):
        pl.semaphore_wait(pltpu.get_barrier_semaphore(), count)


ALL_PARTNERS = (("core",), ("y",), ("zl",), ("x",), ("zh",))


class Restore:
    def __init__(self, here, held, got, sems):
        self.held, self.got, self.sems = held, got, sems
        self.rows = got.shape[1]
        z, core = here.tm // 2, here.bit["core"]
        self.odd = lax.rem(z, 2)
        self.stay = core == z // 2
        turns = (self.odd, 1 - self.odd)
        self.places = [
            ((2 * core + turn) * 2 + here.bit["x"], here.bit["y"] * 2 + z // 2) for turn in turns
        ]

    def far(self, turn, arriving=False):
        at = 1 - self.odd if arriving and turn else self.odd
        return pltpu.make_async_remote_copy(
            src_ref=self.held.at[pl.ds(turn * self.rows, self.rows)],
            dst_ref=self.got.at[at],
            send_sem=self.sems.at[0, turn],
            recv_sem=self.sems.at[1, turn],
            device_id=self.places[turn],
            device_id_type=MESH,
        )

    def near(self):
        return pltpu.make_async_copy(
            self.held.at[pl.ds(0, self.rows)], self.got.at[self.odd], self.sems.at[1, 0]
        )

    def start(self):
        self.far(1).start()

        @pl.when(self.stay)
        def _():
            self.near().start()

        @pl.when(jnp.logical_not(self.stay))
        def _():
            self.far(0).start()

    def finish(self):
        self.far(1).wait_send()
        self.far(1, True).wait_recv()

        @pl.when(self.stay)
        def _():
            self.near().wait()

        @pl.when(jnp.logical_not(self.stay))
        def _():
            self.far(0).wait_send()
            self.far(0).wait_recv()


def restore_scratch(rows, width):
    return [
        pltpu.VMEM((2 * rows, width), bf16),
        pltpu.VMEM((2, rows, width), bf16),
        pltpu.SemaphoreType.DMA((2, 2)),
    ]


class Flow:
    def __init__(self, here, order, local, refs, keep, ends):
        self.here, self.order, self.local = here, order, local
        self.keep = refs.pop(0) if keep else None
        self.got = [refs.pop(0) for _ in order]
        self.out = refs.pop(0) if ends else None
        self.sem = refs.pop(0)
        self.last = len(order)
        self.ends = ends

    def copy(self, step):
        name = self.order[step]
        half = 1 << (self.last - 1 - step)
        source = self.local if step == 0 else self.got[step - 1]
        at = (1 - self.here.bit[name]) * half
        return pltpu.make_async_remote_copy(
            src_ref=source.at[pl.ds(at, half)],
            dst_ref=self.got[step],
            send_sem=self.sem.at[0, step],
            recv_sem=self.sem.at[1, step],
            device_id=self.here.partner(name),
            device_id_type=MESH,
        )

    def keep_copy(self):
        half = 1 << (self.last - 1)
        at = self.here.bit[self.order[0]] * half
        return pltpu.make_async_copy(
            self.local.at[pl.ds(at, half)], self.keep, self.sem.at[0, self.last + 2]
        )

    def start(self, step):
        self.copy(step).start()
        if step == 0 and self.keep is not None:
            self.keep_copy().start()

    def finish(self, step):
        half = 1 << (self.last - 1 - step)
        self.copy(step).wait()
        got = self.got[step]
        at = self.here.bit[self.order[step]] * half
        if step == 0 and self.keep is not None:
            self.keep_copy().wait()
            source, at = self.keep, 0
        else:
            source = self.local if step == 0 else self.got[step - 1]

        def body(i, carry):
            got[i] = got[i] + source[at + i]
            return carry

        if half == 1:
            got[0] = got[0] + source[at]
        else:
            lax.fori_loop(0, half, body, 0)

    def spread_copy(self, which):
        here = self.here
        own = here.bit["core"] * 2
        if which == 0:
            source, there = self.got[-1].at[0], self.out.at[own + here.bit["y"]]
        else:
            source = there = self.out.at[pl.ds(own, 2)]
        return pltpu.make_async_remote_copy(
            src_ref=source,
            dst_ref=there,
            send_sem=self.sem.at[0, self.last + which],
            recv_sem=self.sem.at[1, self.last + which],
            device_id=here.partner(("y", "core")[which]),
            device_id_type=MESH,
        )

    def act(self, stage):
        if stage == 0:
            self.start(0)
        elif stage < self.last:
            self.finish(stage - 1)
            self.start(stage)
        elif stage == self.last:
            self.finish(stage - 1)
            if self.ends:
                self.spread_copy(0).start()
                self.out[self.here.bit["core"] * 2 + self.here.bit["y"]] = self.got[-1][0]
        elif stage == self.last + 1 and self.ends:
            self.spread_copy(0).wait()
            self.spread_copy(1).start()
        elif stage == self.last + 2 and self.ends:
            self.spread_copy(1).wait()

    def result(self):
        return self.out[...] if self.ends else self.got[-1][...]


def flow_scratch(order, block, keep, ends):
    steps = len(order)
    blocks = [pltpu.VMEM((1 << (steps - 1),) + block, bf16)] if keep else []
    for step in range(steps):
        blocks.append(pltpu.VMEM((1 << (steps - 1 - step),) + block, bf16))
    if ends:
        blocks.append(pltpu.VMEM((4,) + block, bf16))
    return blocks + [pltpu.SemaphoreType.DMA((2, steps + 3))]


def flow_result(order, block, ends):
    left = 4 if ends else 1
    return jax.ShapeDtypeStruct((left,) + block, bf16)


def pair_back(query, grad, out, logsum, mask, keys_at, values_at, mk_ref, block, exchange, pair):
    count = query.shape[0]
    total = keys_at.shape[0]
    lane = lax.broadcasted_iota(jnp.int32, (count, LANES), 1)
    low = lane < HALF
    spot = lane % HALF
    zero = jnp.zeros_like(query)
    product = grad.astype(f32) * out.astype(f32)
    delta0 = jnp.sum(jnp.where(low, product, 0.0), axis=1, keepdims=True)
    delta1 = jnp.sum(jnp.where(low, 0.0, product), axis=1, keepdims=True)
    delta = jnp.where(low, delta1, delta0)

    def beside(base, value):
        a, b, c = three(-value)
        return jnp.where(spot == 4, a, jnp.where(spot == 5, b, jnp.where(spot == 6, c, base)))

    query_side = beside(mask, logsum)
    grad_side = beside(zero, delta)
    query_a = (jnp.where(low, query, query_side), jnp.where(low, query_side, query))
    grad_a = (jnp.where(low, grad, grad_side), jnp.where(low, grad_side, grad))
    query_m = (jnp.where(low, query, zero), jnp.where(low, zero, query))
    grad_m = (jnp.where(low, grad, zero), jnp.where(low, zero, grad))
    lane_k = lax.broadcasted_iota(jnp.int32, (block, LANES), 1)
    low_k = lane_k < HALF
    spot_k = lane_k % HALF
    one = jnp.where((spot_k >= 4) & (spot_k < 7), 1.0, 0.0).astype(bf16)
    dq = jnp.zeros((count, LANES), f32)
    for number in exchange.turns(total // block):
        here = pl.ds(number * block, block)
        keys, values = keys_at[here, :], values_at[here, :]
        side = mk_ref[here, :] + one
        nought = jnp.zeros_like(keys)
        dk = jnp.zeros((block, LANES), f32)
        dv = jnp.zeros((block, LANES), f32)
        for head in (0, 1):
            pick = lambda a, b: jnp.where(low_k, a, b) if head == 0 else jnp.where(low_k, b, a)
            prob = jnp.exp2(dot(query_a[head], pick(keys, side), NT))
            change = dot(grad_a[head], pick(values, one), NT)
            score_grad = (prob * change).astype(bf16)
            dv += dot(prob.astype(bf16), grad_m[head], TN)
            dk += dot(score_grad, query_m[head], TN)
            dq += dot(score_grad, pick(keys, nought))
        exchange.put(pair, number, block, (dk * LN2).astype(bf16), dv.astype(bf16))
    return (dq * HALF**-0.5).astype(bf16)


class Exchange:
    def __init__(self, here, rows, refs):
        self.here, self.rows = here, rows
        self.sums, self.send, self.got_core, self.across, self.got_x = refs[:5]
        self.sems = refs[5]
        self.before = None

    def turns(self, blocks):
        return (3, 1, 0, 2) if blocks == 4 else tuple(reversed(range(blocks)))

    def copy_core(self, pair, far):
        rows = pl.ds(far * self.rows, self.rows)
        return pltpu.make_async_remote_copy(
            src_ref=self.send.at[pair % 2, :, rows, :],
            dst_ref=self.got_core.at[pair, :, rows, :],
            send_sem=self.sems.at[2 * far, pair],
            recv_sem=self.sems.at[2 * far + 1, pair],
            device_id=self.here.partner("core"),
            device_id_type=MESH,
        )

    def copy_x(self, pair):
        return pltpu.make_async_remote_copy(
            src_ref=self.across.at[pair],
            dst_ref=self.got_x.at[pair],
            send_sem=self.sems.at[4, pair],
            recv_sem=self.sems.at[5, pair],
            device_id=self.here.partner("x"),
            device_id_type=MESH,
        )

    def end(self):
        pairs = self.got_x.shape[0]
        for pair in range(pairs):
            if pair >= pairs - 2:
                self.free(pair)
            self.copy_x(pair).wait_send()

    def free(self, pair):
        for far in (0, 1):
            self.copy_core(pair, far).wait_send()

    def put(self, pair, number, block, dk, dv):
        half = 2 * self.rows
        there = pl.ds(number * block % half, block)
        ref, slot = (self.sums, pair) if number * block < half else (self.send, pair % 2)
        ref[slot, 0, there, :] = dk
        ref[slot, 1, there, :] = dv
        if 2 * half == 4 * block:
            if number == 3:
                if self.before is not None:
                    self.before()
                self.copy_core(pair, 1).start()
            elif number == 2:
                self.copy_core(pair, 0).start()
            elif number == 0:
                self.pass_on(pair)
        elif number == 1:
            if self.before is not None:
                self.before()
            for far in (1, 0):
                self.copy_core(pair, far).start()
        else:
            self.pass_on(pair)

    def pass_on(self, pair):
        rows = self.rows
        self.copy_core(pair, 1).wait_recv()
        far = pl.ds(rows, rows)
        for i in (0, 1):
            self.across[pair, i] = self.sums[pair, i, far, :] + self.got_core[pair, i, far, :]
        self.copy_x(pair).start()

    def take(self, pair, out_ref):
        near = pl.ds(0, self.rows)
        self.copy_core(pair, 0).wait_recv()
        self.copy_x(pair).wait_recv()
        for i in (0, 1):
            out_ref[pair, i] = (
                self.sums[pair, i, near, :].astype(f32)
                + self.got_core[pair, i, near, :].astype(f32)
                + self.got_x[pair, i].astype(f32)
            ).astype(bf16)


def exchange_scratch(pairs, rows):
    return [
        pltpu.VMEM((pairs, 2, 2 * rows, LANES), bf16),
        pltpu.VMEM((2, 2, 2 * rows, LANES), bf16),
        pltpu.VMEM((pairs, 2, 2 * rows, LANES), bf16),
        pltpu.VMEM((pairs, 2, rows, LANES), bf16),
        pltpu.VMEM((pairs, 2, rows, LANES), bf16),
        pltpu.SemaphoreType.DMA((6, pairs)),
    ]


def fill_keys(keys_at, values_at, kv_ref):
    rows = kv_ref.shape[3]
    for part in range(kv_ref.shape[0]):
        there = pl.ds(part * rows, rows)
        keys_at[there, :] = kv_ref[part, 0, 0]
        values_at[there, :] = kv_ref[part, 0, 1]


def selves_kernel(pairs, plan, blocks, *refs):
    orders, ends, stages = plan
    large_refs, kv_large, refs = refs[:6], refs[6], refs[7:]
    small_refs, kv_small, refs = refs[:6], refs[6], refs[7:]
    flows = len(orders)
    locals_, refs = refs[:flows], refs[flows:]
    given, gain, refs = refs[:5], refs[5], refs[6:]
    dq_l, dkv_l, dq_s, dkv_s, view_ref, gain_ref = refs[:6]
    sums, refs = refs[6 : 6 + flows], refs[6 + flows :]
    held, load_sems, dq_all, grads, home_refs, refs = refs[:5], refs[5], refs[6], refs[7], refs[8:11], refs[11:]
    keys_l, values_l, keys_s, values_s = refs[:4]
    ex_l, ex_s, refs = refs[4:10], refs[10:16], refs[16:]
    here = Here()
    rows_l, rows_s = keys_l.shape[0] // 4, keys_s.shape[0] // 4
    large, small = Exchange(here, rows_l, ex_l), Exchange(here, rows_s, ex_s)
    refs = list(refs)
    running = [
        Flow(here, orders[flow], locals_[flow], refs, True, ends[flow]) for flow in range(flows)
    ]
    step = pl.program_id(0)
    home = Restore(here, *home_refs)
    loads = [
        pltpu.make_async_copy(source, there, load_sems.at[i])
        for i, (source, there) in enumerate(zip(given, held))
    ]

    @pl.when(step == 0)
    def _():
        here.hail_line("x", "y")
        for load in loads:
            load.start()

    def before():
        @pl.when(step == 0)
        def _():
            here.heard(9)
            for flow in running:
                flow.act(0)

    large.before = before

    def attention(exchange, pair, refs, kv_ref, keys_at, values_at, block, dq_ref):
        q_ref, do_ref, o_ref, l_ref, mq_ref, mk_ref = refs
        fill_keys(keys_at, values_at, kv_ref)

        @pl.when(pair >= 2)
        def _():
            exchange.free(pair - 2)

        dq_ref[...] = pair_back(
            q_ref[0], do_ref[...], o_ref[0], l_ref[0], mq_ref[...], keys_at, values_at, mk_ref,
            block, exchange, pair,
        )

    @pl.when(step < pairs)
    def _():
        attention(large, step, large_refs, kv_large, keys_l, values_l, blocks[0], dq_l)
        dq_all[step] = dq_l[...]

    @pl.when(step >= pairs)
    def _():
        attention(small, step - pairs, small_refs, kv_small, keys_s, values_s, blocks[1], dq_s)

    for pair in range(pairs):

        @pl.when(step == pair + 2 + pair // (pairs - 1))
        def _(pair=pair):
            large.take(pair, dkv_l)

    @pl.when(step == pairs + 2)
    def _():
        *weights, hidden_grad, view = held
        for load in loads:
            load.wait()
        total = None
        for which, weight in enumerate(weights):
            for pair in range(pairs):
                lanes = slice(pair * LANES, (pair + 1) * LANES)
                grads[:, lanes] = dkv_l[pair, which - 1] if which else dq_all[pair]
            product = dot(grads[...], weight[...], NT)
            total = product if total is None else total + product
        extra, gain_ref[...] = norm_back(total, view[...].astype(f32), gain[...])
        home_refs[0][...] = (hidden_grad[...] + extra).astype(bf16)
        home.start()

    for at in range(2 * pairs):
        todo = []
        for flow in range(flows):
            for stage, when in enumerate(stages[flow]):
                if when == at:
                    todo.append((running[flow], stage + 1))
        if todo:

            @pl.when(step == at)
            def _(todo=todo):
                for flow, stage in todo:
                    flow.act(stage)

    @pl.when(step == 2 * pairs - 1)
    def _():
        for pair in range(pairs):
            small.take(pair, dkv_s)
        small.end()
        large.end()
        for flow, sum_ref in zip(running, sums):
            sum_ref[...] = flow.result()
        home.finish()
        view_ref[...] = home_refs[1][...]


def selves_back(large, large_kv, small, small_kv, flows, view, gain, orders, ends, stages):
    count, width = large[1].shape
    few = small[1].shape[0]
    pairs = width // LANES
    total, less = large[5].shape[0], small[5].shape[0]
    shapes = [flow.shape[1:] for flow in flows]
    results = [flow_result(*flow) for flow in zip(orders, shapes, ends)]
    blocks = (largest_block(total // 2, 512), largest_block(less // 2, 512))
    first = lambda i: jnp.minimum(i, pairs - 1)
    last = lambda i: jnp.maximum(i - pairs, 0)
    in_specs = []
    for rows, keys, at in ((count, total, first), (few, less, last)):
        major = pl.BlockSpec((1, rows, LANES), lambda i, at=at: (at(i), 0, 0))
        minor = pl.BlockSpec((rows, LANES), lambda i, at=at: (0, at(i)))
        in_specs += [major, minor, major, major, whole((rows, LANES)), whole((keys, LANES))]
        in_specs.append(
            pl.BlockSpec((4, 1, 2, rows, LANES), lambda i, at=at: (0, at(i), 0, 0, 0))
        )
    in_specs += [pl.BlockSpec(memory_space=pl.ANY)] * (len(flows) + len(view))
    in_specs.append(whole((1, width)))
    shape = jax.ShapeDtypeStruct
    out_shape = [
        shape((count, width), bf16),
        shape((pairs, 2, count, LANES), bf16),
        shape((few, width), bf16),
        shape((pairs, 2, few, LANES), bf16),
        shape((2, count // 2, width), bf16),
        shape((1, width), f32),
    ] + results
    out_specs = [
        pl.BlockSpec((count, LANES), lambda i: (0, first(i))),
        whole((pairs, 2, count, LANES)),
        pl.BlockSpec((few, LANES), lambda i: (0, last(i))),
        whole((pairs, 2, few, LANES)),
        whole((2, count // 2, width)),
        whole((1, width)),
    ] + [whole(result.shape) for result in results]
    scratch = [pltpu.VMEM(value.shape, value.dtype) for value in view]
    scratch += [pltpu.SemaphoreType.DMA((len(view),)), pltpu.VMEM((pairs, count, LANES), bf16)]
    scratch += [pltpu.VMEM((count, width), bf16)] + restore_scratch(count // 2, width)
    scratch += [pltpu.VMEM((total, LANES), bf16)] * 2 + [pltpu.VMEM((less, LANES), bf16)] * 2
    scratch += exchange_scratch(pairs, count) + exchange_scratch(pairs, few)
    for flow in range(len(flows)):
        scratch += flow_scratch(orders[flow], shapes[flow], True, ends[flow])
    result = pl.pallas_call(
        functools.partial(selves_kernel, pairs, (orders, ends, stages), blocks),
        grid=(2 * pairs,),
        in_specs=in_specs,
        out_specs=out_specs,
        out_shape=out_shape,
        scratch_shapes=scratch,
        compiler_params=pltpu.CompilerParams(
            vmem_limit_bytes=60 << 20, collective_id=1, has_side_effects=True
        ),
        cost_estimate=pl.CostEstimate(
            flops=20 * width * (count * total + few * less),
            bytes_accessed=64 * count * width,
            transcendentals=count * total * width // HALF,
        ),
        name="selves_back",
    )(*large, large_kv, *small, small_kv, *flows, *view, gain)
    return result[:4], result[4:6], result[6:]


LAST_ORDERS = (BY_YX, BY_X, BY_YX)
GAIN_ORDER = ("core", "y", "x", "zl", "zh")
LATE_ORDER = ("x", "zh")
LATE_ORDERS = (LATE_ORDER,) * 3
LATE_STAGES = {3: 2, 5: 3, 6: 4}


def last_kernel(pairs, sizes, late, *refs):
    refs = list(refs)
    take = lambda count: [refs.pop(0) for _ in range(count)]
    given, late_refs = take(11), take(late)
    gain, gain_l, second_gain, query_gain, context_gain = take(5)
    (gs_ref,) = take(1)
    sum_refs = take(3 + late)
    (gain_ref,) = take(1)
    held = take(11)
    dql, dkvl, dqs, dkvs, nl, ns, wq, wk, wv, xs, hs = held
    load_sems, normed, *grads = take(5)
    small_back = take(3)
    here = Here()
    flows = []
    for order in LAST_ORDERS:
        flows.append(Flow(here, order, refs.pop(0), refs, False, True))
    late_flows = [
        Flow(here, order, ref, refs, True, True) for order, ref in zip(LATE_ORDERS, late_refs)
    ]
    state, got, gain_sems = refs
    large, small = sizes
    top, bottom = pl.ds(0, large), pl.ds(large, small)
    loads = [
        pltpu.make_async_copy(source, there, load_sems.at[i])
        for i, (source, there) in enumerate(zip(given, held))
    ]
    here.hail_line("x", "y")
    for load in loads:
        load.start()
    home = Restore(here, *small_back)

    def gain_copy(step):
        return pltpu.make_async_remote_copy(
            src_ref=state.at[step],
            dst_ref=got.at[step],
            send_sem=gain_sems.at[0, step],
            recv_sem=gain_sems.at[1, step],
            device_id=here.partner(GAIN_ORDER[step]),
            device_id_type=MESH,
        )

    for load in loads[:6]:
        load.wait()
    normed[top, :] = nl[...]
    normed[bottom, :] = ns[...]
    for which, flow in enumerate(flows):
        if which == 0:
            grads[0][top, :] = dql[...]
            grads[0][bottom, :] = dqs[...]
        else:
            for pair in range(pairs):
                lanes = pl.ds(pair * LANES, LANES)
                grads[which][top, lanes] = dkvl[pair, which - 1]
                grads[which][bottom, lanes] = dkvs[pair, which - 1]
        value = dot(normed[...], grads[which][...], TN).astype(bf16)
        if which == 0:
            here.heard(9)
            for late_flow in late_flows:
                late_flow.act(0)
        rows, wide = flow.local.shape[1:]
        for at, (core, y, tm) in enumerate(spots(flow.order)):
            first = tm * 2 * rows + core * rows
            flow.local[at] = value[first : first + rows, y * wide : (y + 1) * wide]
        flow.act(0)
    total = None
    for which, weight in enumerate((wq, wk, wv)):
        loads[6 + which].wait()
        part = dot(grads[which][bottom, :], weight[...], NT)
        total = part if total is None else total + part
    for load in loads[9:]:
        load.wait()
    for flow in flows:
        flow.act(1)
    for flow in late_flows:
        flow.act(1)
    extra, gain_s = norm_back(total, xs[...].astype(f32), gain[...])
    small_back[0][...] = (hs[...] + extra).astype(bf16)
    home.start()
    state[0] = jnp.zeros(state.shape[1:], f32)
    for row, value in enumerate(
        (gain_l[...] + gain_s, second_gain[...], query_gain[...], context_gain[...])
    ):
        state[0, row : row + 1, :] = value
    gain_copy(0).start()
    for stage in range(1, 8):
        if stage > 1:
            for flow in flows:
                flow.act(stage)
        if stage in LATE_STAGES:
            for flow in late_flows:
                flow.act(LATE_STAGES[stage])
        if stage <= 5:
            gain_copy(stage - 1).wait()
            total = state[stage - 1] + got[stage - 1]
            if stage < 5:
                state[stage] = total
                gain_copy(stage).start()
            else:
                wide = total.shape[1]
                turned = pltpu.roll(total, lax.rem(wide - here.tm * (wide // 8), wide), 1)
                gain_ref[...] = turned[:, : gain_ref.shape[1]]
    for flow, sum_ref in zip(flows + late_flows, sum_refs):
        sum_ref[...] = flow.result()
    home.finish()
    gs_ref[...] = small_back[1][...]


def last_sums(given, late, gains):
    count, width = given[0].shape
    few = given[2].shape[0]
    block = (width // 16, width // 2)
    shape = jax.ShapeDtypeStruct
    tokens = count + few
    scratch = [pltpu.VMEM(value.shape, value.dtype) for value in given]
    scratch += [pltpu.SemaphoreType.DMA((len(given),))]
    scratch += [pltpu.VMEM((tokens, width), bf16)] * 4
    scratch += restore_scratch(few // 2, width)
    for order in LAST_ORDERS:
        scratch.append(pltpu.VMEM((32,) + block, bf16))
        scratch += flow_scratch(order, block, False, True)
    for order, local in zip(LATE_ORDERS, late):
        scratch += flow_scratch(order, local.shape[1:], True, True)
    scratch += [
        pltpu.VMEM((5, 8, width), f32),
        pltpu.VMEM((5, 8, width), f32),
        pltpu.SemaphoreType.DMA((2, 5)),
    ]
    anywhere = pl.BlockSpec(memory_space=pl.ANY)
    vmem = pl.BlockSpec(memory_space=pltpu.VMEM)
    result = pl.pallas_call(
        functools.partial(last_kernel, width // LANES, (count, few), len(late)),
        in_specs=[anywhere] * (len(given) + len(late)) + [vmem] * 5,
        out_shape=[
            shape((2, few // 2, width), bf16),
        ]
        + [shape((4,) + block, bf16)] * 3
        + [shape((4,) + local.shape[1:], bf16) for local in late]
        + [shape((8, LANES), f32)],
        scratch_shapes=scratch,
        compiler_params=pltpu.CompilerParams(
            vmem_limit_bytes=60 << 20, collective_id=2, has_side_effects=True
        ),
        cost_estimate=pl.CostEstimate(
            flops=40 * tokens * width * width,
            bytes_accessed=40 * tokens * width,
            transcendentals=0,
        ),
        name="last_sums",
    )(*given, *late, *gains)
    return result[0], result[1:4], result[4:-1], result[-1]


def results_kernel(*refs):
    outs, given, sems = refs[12:29], refs[29:41], refs[41]
    loads = [
        pltpu.make_async_copy(source, there, sems.at[i])
        for i, (source, there) in enumerate(zip(refs, given))
    ]
    for load in loads:
        load.start()
    for load in loads:
        load.wait()
    united, large, small, q, k, v, up, down, output, first, other, gains = given
    for source, there in zip((united, large, small), outs[:3]):
        there[...] = source[...].astype(there.dtype)
    for source, there in zip((q, k, v, output), (outs[4], outs[5], outs[6], outs[7])):
        rows, wide = source.shape[1:]
        for at in range(4):
            core, y = at // 2, at % 2
            there[core * rows : (core + 1) * rows, y * wide : (y + 1) * wide] = source[at].astype(f32)
    rows, wide = up.shape[1:]
    for at in range(4):
        outs[9][:, at * wide : (at + 1) * wide] = up[at].astype(f32)
        outs[10][at * rows : (at + 1) * rows, :] = down[at].astype(f32)
        half = rows // 2
        there = slice(at % 2 * half, (at % 2 + 1) * half)
        (outs[16] if at < 2 else outs[13])[there, :] = first[at].astype(f32)
        (outs[14] if at < 2 else outs[15])[there, :] = other[at].astype(f32)
    for row, at in enumerate((3, 8, 11, 12)):
        outs[at][...] = gains[row : row + 1, : outs[at].shape[1]]


def results(united, large, small, last, late, first, other, gains):
    shape = jax.ShapeDtypeStruct
    rows, width = late[0].shape[1:]
    square, vector = shape((rows, width), f32), shape((1, rows), f32)
    given = (united, large, small, *last, *late, first, other, gains)
    out = pl.pallas_call(
        results_kernel,
        in_specs=[pl.BlockSpec(memory_space=pl.ANY)] * len(given),
        scratch_shapes=[pltpu.VMEM(value.shape, value.dtype) for value in given]
        + [pltpu.SemaphoreType.DMA((len(given),))],
        out_shape=[
            shape(united.shape, bf16), shape(large.shape, f32), shape(small.shape, f32), vector,
            square, square, square, square, vector,
            shape((rows, 4 * width), f32), shape((4 * rows, width), f32), vector, vector,
            square, square, square, square,
        ],
        compiler_params=pltpu.CompilerParams(vmem_limit_bytes=60 << 20),
        cost_estimate=pl.CostEstimate(flops=0, bytes_accessed=14 << 20, transcendentals=0),
        name="results",
    )(*given)
    return tuple(value.reshape(rows) if value.shape == (1, rows) else value for value in out)


def cross_kernel(pairs, block, *refs):
    (q_ref, do_ref, o_ref, l_ref, mq_ref, mk_ref), refs = refs[:6], refs[6:]
    kv_ref, given, gains, refs = refs[0], refs[1:11], refs[11:13], refs[13:]
    view_ref, gl_ref, gs_ref, a_ref, b_ref, gain_l_ref, gain_s_ref = refs[:7]
    keys_at, values_at, exchange_refs, refs = refs[7], refs[8], refs[9:15], refs[15:]
    dkv, dq, dk, dv = refs[:4]
    held, sems, home_refs = refs[4:14], refs[14], refs[15:18]
    united, wo, merged_l, asked, context, grad_out, merged_s, wq, wk, wv = held
    here = Here()
    exchange = Exchange(here, keys_at.shape[0] // 4, exchange_refs)
    step = pl.program_id(0)
    loads = [
        pltpu.make_async_copy(source, there, sems.at[i])
        for i, (source, there) in enumerate(zip(given, held))
    ]

    @pl.when(step == 0)
    def _():
        here.hail_line("x")
        for load in loads:
            load.start()

    def before():
        @pl.when(step == 0)
        def _():
            here.heard(8)

    exchange.before = before
    home = Restore(here, *home_refs)

    fill_keys(keys_at, values_at, kv_ref)

    @pl.when(step >= 2)
    def _():
        exchange.free(step - 2)

    dq[step] = pair_back(
        q_ref[0], do_ref[...], o_ref[0], l_ref[0], mq_ref[...], keys_at, values_at, mk_ref,
        block, exchange, step,
    )

    @pl.when(step == 1)
    def _():
        for load in loads[:3]:
            load.wait()
        wide = jnp.concatenate([united[i] for i in range(pairs)], axis=1)
        home_refs[0][...] = (merged_l[...] + dot(wide, wo[...])).astype(bf16)
        home.start()

    @pl.when(step >= 3)
    def _():
        exchange.take(step - 3, dkv)

    def lay(out_ref, which, value, order):
        left = 32 // out_ref.shape[0]
        rows = out_ref.shape[1] // left
        for at, (core, y, tm) in enumerate(spots(order)):
            if core == which:
                first, there = (tm * 2 + y) * rows, at % left * rows
                out_ref[at // left, there : there + rows, :] = value[first : first + rows]

    @pl.when(step == pairs - 1)
    def _():
        for load in loads[3:]:
            load.wait()
        grads = jnp.concatenate([united[i] for i in range(pairs)], axis=1)
        lay(a_ref, 0, dot(grads, grad_out[...], TN).astype(bf16), BY_Y)
        grads = jnp.concatenate([dq[i] for i in range(pairs)], axis=1)
        lay(a_ref, 1, dot(asked[...], grads, TN).astype(bf16), BY_Y)
        extra, gain_l_ref[...] = norm_back(dot(grads, wq[...], NT), merged_l[...], gains[0][...])
        gl_ref[...] = grad_out[...].astype(f32) + extra
        for pair in range(pairs - 3, pairs):
            exchange.take(pair, dkv)
        for pair in range(pairs):
            lanes = pl.ds(pair * LANES, LANES)
            dk[:, lanes] = dkv[pair, 0]
            dv[:, lanes] = dkv[pair, 1]
        lay(b_ref, 0, dot(context[...], dk[...], TN).astype(bf16), BY_ZL)
        lay(b_ref, 1, dot(context[...], dv[...], TN).astype(bf16), BY_ZL)
        grad = dot(dk[...], wk[...], NT) + dot(dv[...], wv[...], NT)
        gs_ref[...], gain_s_ref[...] = norm_back(grad, merged_s[...], gains[1][...])
        exchange.end()
        home.finish()
        view_ref[...] = home_refs[1][...]


def cross_back(attention, kv, given, gains):
    count, width = attention[1].shape
    few = kv.shape[3]
    major = pl.BlockSpec((1, count, LANES), lambda i: (i, 0, 0))
    pairs = width // LANES
    total = attention[5].shape[0]
    block = largest_block(total // 2, 512)
    shape = jax.ShapeDtypeStruct
    laid = (4, 8 * width // 16, width)
    return pl.pallas_call(
        functools.partial(cross_kernel, pairs, block),
        grid=(pairs,),
        in_specs=[major, columns(count, 0), major, major]
        + [whole((count, LANES)), whole((total, LANES))]
        + [pl.BlockSpec((4, 1, 2, few, LANES), lambda i: (0, i, 0, 0, 0))]
        + [pl.BlockSpec(memory_space=pl.ANY)] * len(given)
        + [whole((1, width))] * 2,
        out_specs=[
            whole((2, count // 2, width)), whole((count, width)), whole((few, width)), whole(laid), whole(laid),
            whole((1, width)), whole((1, width)),
        ],
        out_shape=[
            shape((2, count // 2, width), bf16),
            shape((count, width), f32), shape((few, width), f32), shape(laid, bf16), shape(laid, bf16),
            shape((1, width), f32), shape((1, width), f32),
        ],
        scratch_shapes=[pltpu.VMEM((total, LANES), bf16)] * 2
        + exchange_scratch(pairs, few)
        + [pltpu.VMEM((pairs, 2, few, LANES), bf16), pltpu.VMEM((pairs, count, LANES), bf16)]
        + [pltpu.VMEM((few, width), bf16)] * 2
        + [pltpu.VMEM(value.shape, value.dtype) for value in given]
        + [pltpu.SemaphoreType.DMA((len(given),))]
        + restore_scratch(count // 2, width),
        compiler_params=pltpu.CompilerParams(
            vmem_limit_bytes=60 << 20, collective_id=3, has_side_effects=True
        ),
        cost_estimate=pl.CostEstimate(
            flops=20 * width * count * total,
            bytes_accessed=64 * count * width,
            transcendentals=count * total * width // HALF,
        ),
        name="cross_back",
    )(*attention, kv, *given, *gains)


def attend_pair(pair, q_ref, kv, mq_ref, mk_ref, spaces, o_ref, l_ref):
    parts, rows = kv.shape[0], kv.shape[3]
    total = parts * rows
    ka0, ka1, va0, va1 = (space.at[pl.ds(0, total), :] for space in spaces)
    low = lax.broadcasted_iota(jnp.int32, (rows, LANES), 1) < HALF
    for part in range(parts):
        here = pl.ds(part * rows, rows)
        keys, values, mask = kv[part, pair, 0], kv[part, pair, 1], mk_ref[here, :]
        one = jnp.ones_like(values)
        ka0[here, :] = jnp.where(low, keys, mask)
        ka1[here, :] = jnp.where(low, mask, keys)
        va0[here, :] = jnp.where(low, values, one)
        va1[here, :] = jnp.where(low, one, values)
    count = q_ref.shape[1]
    block = largest_block(count, 256)
    low = lax.broadcasted_iota(jnp.int32, (block, LANES), 1) < HALF
    for number in range(count // block):
        here = pl.ds(number * block, block)
        query, mask = q_ref[pair, here, :], mq_ref[here, :]
        tops, sums = [], []
        for head, keys, values in ((0, ka0, va0), (1, ka1, va1)):
            mine = jnp.where(low, query, mask) if head == 0 else jnp.where(low, mask, query)
            score = dot(mine, keys[...], NT)
            top = jnp.max(score, axis=1, keepdims=True)
            weight = jnp.exp2(score - top).astype(bf16)
            sums.append(dot(weight, values[...]))
            tops.append(jnp.broadcast_to(top, (block, LANES)))
        total = jnp.where(low, sums[1], sums[0])
        top = jnp.where(low, tops[1], tops[0])
        out = jnp.where(low, sums[0], sums[1])
        o_ref[pair, here, :] = (out / pltpu.roll(total, HALF, 1)).astype(bf16)
        l_ref[pair, here, :] = top + jnp.log2(total)


class Gather:
    def __init__(self, here, kv, sems):
        self.here, self.kv, self.sems = here, kv, sems

    def copy(self, kind, at, size, sem):
        source, there = ((0, 1), (0, 2), (1, 3))[kind]
        pairs = pl.ds(at, size)
        return pltpu.make_async_remote_copy(
            src_ref=self.kv.at[source, pairs],
            dst_ref=self.kv.at[there, pairs],
            send_sem=self.sems.at[0, 3 * sem + kind],
            recv_sem=self.sems.at[1, 3 * sem + kind],
            device_id=self.here.partner(("x", "core", "core")[kind]),
            device_id_type=MESH,
        )


def begin_kernel(pairs, *refs):
    refs = list(refs)
    take = lambda count: [refs.pop(0) for _ in range(count)]
    large_ref, small_ref, cot_ref, clip_ref = take(4)
    weight_refs = take(9)
    (gains,) = take(1)
    first_gain, second_gain, query_gain, context_gain = (
        gains.at[i : i + 1, :] for i in range(4)
    )
    xl_out, xs_out, cot_out, kvl_out, kvs_out, ckv_out = take(6)
    nl_ref, ns_ref, ql_ref, qs_ref, ol_ref, ll_ref, os_ref, ls_ref = take(8)
    merged_ref, hidden_ref, second_ref, active_ref, slope_ref, context_ref = take(6)
    mql_ref, mkl_ref, mqs_ref, mks_ref = take(4)
    for gain, gain_out in zip((first_gain, second_gain, query_gain, context_gain), take(4)):
        gain_out[...] = gain[...]
    (grad_ref,) = take(1)
    xl, xs, cot, clip, kvl, kvs, ckv = take(7)
    wq, wk, wv, wo, up, down, wck, wcv, wco = weights = take(9)
    spaces = take(4)
    wide, total = take(2)
    move_sems, gather_l, gather_s, gather_c, gather_clip, load_sems, out_sems = take(7)
    near_l, near_s, near_c, x_sems = take(4)
    here = Here()
    z, core = here.tm // 2, here.bit["core"]
    stay = core == z // 2

    here.hail_line("x")

    odd = lax.rem(z, 2)
    from_seq = (odd, 1 - odd)

    def far(which, turn, source, there):
        rows = source.shape[1]
        place = (
            (2 * core + from_seq[turn]) * 2 + here.bit["x"],
            here.bit["y"] * 2 + z // 2,
        )
        return pltpu.make_async_remote_copy(
            src_ref=source.at[from_seq[turn]],
            dst_ref=there.at[pl.ds(turn * rows, rows)],
            send_sem=move_sems.at[0, 2 * which + turn],
            recv_sem=move_sems.at[1, 2 * which + turn],
            device_id=place,
            device_id_type=MESH,
        )

    def near(which, source, there):
        return pltpu.make_async_copy(
            source.at[from_seq[0]],
            there.at[pl.ds(0, source.shape[1])],
            move_sems.at[1, 2 * which],
        )

    def move(which, source, there):
        far(which, 1, source, there).start()

        @pl.when(stay)
        def _():
            near(which, source, there).start()

        @pl.when(jnp.logical_not(stay))
        def _():
            far(which, 0, source, there).start()

    def moved_out(which, source, there):
        far(which, 1, source, there).wait_send()

        @pl.when(jnp.logical_not(stay))
        def _():
            far(which, 0, source, there).wait_send()

    def moved_in(which, source, there):
        far(which, 1, source, there).wait_recv()

        @pl.when(stay)
        def _():
            near(which, source, there).wait()

        @pl.when(jnp.logical_not(stay))
        def _():
            far(which, 0, source, there).wait_recv()

    moves = ((0, clip_ref, clip.at[0, 0]), (1, small_ref, xs), (2, large_ref, xl), (3, cot_ref, cot))
    here.heard(8)
    move(*moves[0])
    move(*moves[1])
    loads = [
        pltpu.make_async_copy(source, there, load_sems.at[i])
        for i, (source, there) in enumerate(zip(weight_refs, weights))
    ]
    for load in loads:
        load.start()
    moved_out(*moves[0])
    moved_out(*moves[1])
    move(*moves[2])
    outs = []

    def keep(source, there):
        copy = pltpu.make_async_copy(source, there, out_sems.at[len(outs)])
        copy.start()
        outs.append(copy)

    def split(kv, part, value, key_weight, value_weight):
        keys = dot(value, key_weight[...]).astype(bf16)
        values = dot(value, value_weight[...]).astype(bf16)
        for pair in range(pairs):
            lanes = slice(pair * LANES, (pair + 1) * LANES)
            kv[part, pair, 0] = keys[:, lanes]
            kv[part, pair, 1] = values[:, lanes]

    def to_x(which, source, there):
        return pltpu.make_async_remote_copy(
            src_ref=source,
            dst_ref=there,
            send_sem=x_sems.at[0, which],
            recv_sem=x_sems.at[1, which],
            device_id=here.partner("x"),
            device_id_type=MESH,
        )

    x_small, x_large, x_cross = (
        to_x(0, ns_ref, near_s), to_x(1, nl_ref, near_l), to_x(2, context_ref, near_c)
    )

    def query_into(n_ref, q_ref):
        query = (dot(n_ref[...], wq[...]) * Q_SCALE).astype(bf16)
        for pair in range(pairs):
            q_ref[pair] = query[:, pair * LANES : (pair + 1) * LANES]

    large, small = Gather(here, kvl, gather_l), Gather(here, kvs, gather_s)
    cross, clips = Gather(here, ckv, gather_c), Gather(here, clip, gather_clip)

    moved_in(*moves[0])
    for kind in (0, 1):
        clips.copy(kind, 0, 1, 0).start()
    moved_in(*moves[1])
    keep(xs, xs_out)
    ns_ref[...] = norm(xs[...].astype(f32), first_gain[...])
    x_small.start()
    for i in (0, 1, 2):
        loads[i].wait()
    split(kvs, 0, ns_ref[...], wk, wv)
    small.copy(1, 0, pairs, 0).start()
    query_into(ns_ref, qs_ref)
    clips.copy(0, 0, 1, 0).wait_recv()
    clips.copy(2, 0, 1, 0).start()
    for kind in (1, 2):
        clips.copy(kind, 0, 1, 0).wait_recv()

    few = clip.shape[2]
    spot = lax.broadcasted_iota(jnp.int32, (1, LANES), 1) % HALF
    number = spot.astype(f32)
    some = spot < 4
    row = lax.broadcasted_iota(jnp.int32, (2 * few, few), 0) // 2
    twice = jnp.where(row == lax.broadcasted_iota(jnp.int32, (2 * few, few), 1), 1.0, 0.0)
    twice = twice.astype(bf16)
    for part in range(4):
        mine = clip[part, 0]
        for value, mk_ref, mq_ref in (
            (mine.astype(f32), mks_ref, mqs_ref),
            (dot(twice, mine), mkl_ref, mql_ref),
        ):
            rows = value.shape[0]
            mk_ref[pl.ds(part * rows, rows), :] = jnp.where(
                some & (value != number), NEGATIVE, 0.0
            ).astype(bf16)
            if part == 0:
                mq_ref[...] = jnp.where(some & (value == number), 1.0, 0.0).astype(bf16)

    x_small.wait_recv()
    split(kvs, 1, near_s[...], wk, wv)
    small.copy(2, 0, pairs, 0).start()
    moved_in(*moves[2])
    moved_out(*moves[2])
    move(*moves[3])
    keep(xl, xl_out)
    nl_ref[...] = norm(xl[...].astype(f32), first_gain[...])
    x_large.start()
    split(kvl, 0, nl_ref[...], wk, wv)
    large.copy(1, 0, pairs, 0).start()
    query_into(nl_ref, ql_ref)

    small.copy(1, 0, pairs, 0).wait_recv()
    small.copy(2, 0, pairs, 0).wait_recv()
    keep(kvs, kvs_out)

    def small_pair(pair, carry):
        attend_pair(pair, qs_ref, kvs, mqs_ref, mks_ref, spaces, os_ref, ls_ref)
        return carry

    lax.fori_loop(0, pairs, small_pair, 0)
    loads[3].wait()
    for pair in range(pairs):
        wide[:, pair * LANES : (pair + 1) * LANES] = os_ref[pair]
    hidden = xs[...].astype(f32) + dot(wide[...], wo[...])
    hidden_ref[...] = hidden
    second_ref[...] = norm(hidden, second_gain[...])
    total[...] = hidden
    loads[4].wait()
    loads[5].wait()
    width = wide.shape[1]
    steps = up.shape[1] // width
    for step in range(steps):
        lanes = slice(step * width, (step + 1) * width)
        active, slope = gelu_both(dot(second_ref[...], up[:, lanes]))
        active = active.astype(bf16)
        active_ref[:, lanes] = active
        slope_ref[:, lanes] = slope.astype(bf16)
        total[...] += dot(active, down[lanes, :])
    merged = total[...]
    merged_ref[...] = merged
    context = norm(merged, context_gain[...])
    context_ref[...] = context
    x_cross.start()
    x_large.wait_recv()
    split(kvl, 1, near_l[...], wk, wv)
    large.copy(2, 0, pairs, 0).start()
    loads[6].wait()
    loads[7].wait()
    split(ckv, 0, context, wck, wcv)
    cross.copy(1, 0, pairs, 0).start()

    def large_pair(pair, carry):
        attend_pair(pair, ql_ref, kvl, mql_ref, mkl_ref, spaces, ol_ref, ll_ref)
        return carry

    large.copy(1, 0, pairs, 0).wait_recv()
    large.copy(2, 0, pairs, 0).wait_recv()
    keep(kvl, kvl_out)
    lax.fori_loop(0, pairs // 2, large_pair, 0)
    x_cross.wait_recv()
    split(ckv, 1, near_c[...], wck, wcv)
    cross.copy(2, 0, pairs, 0).start()
    moved_in(*moves[3])
    moved_out(*moves[3])
    keep(cot, cot_out)
    loads[8].wait()
    grad_ref[...] = dot(cot[...], wco[...], NT).astype(bf16)
    lax.fori_loop(pairs // 2, pairs, large_pair, 0)
    cross.copy(1, 0, pairs, 0).wait_recv()
    cross.copy(2, 0, pairs, 0).wait_recv()
    keep(ckv, ckv_out)
    for kind in (0, 1, 2):
        clips.copy(kind, 0, 1, 0).wait_send()
        if kind:
            for gathered in (small, large, cross):
                gathered.copy(kind, 0, pairs, 0).wait_send()
    for copy in (x_small, x_large, x_cross):
        copy.wait_send()
    for copy in outs:
        copy.wait()


def begin(large, small, cotangent, clip, weights, gains):
    seqs, count, width = large.shape
    few = small.shape[1]
    count, few = 2 * count, 2 * few
    pairs = width // LANES
    hidden = weights[4].shape[1]
    shape = jax.ShapeDtypeStruct
    kv_l, kv_s = (4, pairs, 2, count, LANES), (4, pairs, 2, few, LANES)
    anywhere = pl.BlockSpec(memory_space=pl.ANY)
    vmem = pl.BlockSpec(memory_space=pltpu.VMEM)
    out_shape = [
        shape((count, width), bf16),
        shape((few, width), bf16),
        shape((count, width), bf16),
        shape(kv_l, bf16),
        shape(kv_s, bf16),
        shape(kv_s, bf16),
        shape((count, width), bf16),
        shape((few, width), bf16),
        shape((pairs, count, LANES), bf16),
        shape((pairs, few, LANES), bf16),
        shape((pairs, count, LANES), bf16),
        shape((pairs, count, LANES), f32),
        shape((pairs, few, LANES), bf16),
        shape((pairs, few, LANES), f32),
        shape((few, width), f32),
        shape((few, width), f32),
        shape((few, width), bf16),
        shape((few, hidden), bf16),
        shape((few, hidden), bf16),
        shape((few, width), bf16),
        shape((count, LANES), bf16),
        shape((4 * count, LANES), bf16),
        shape((few, LANES), bf16),
        shape((4 * few, LANES), bf16),
        *[shape((1, width), f32)] * 4,
        shape((count, width), bf16),
    ]
    dma = pltpu.SemaphoreType.DMA
    scratch = [
        pltpu.VMEM((count, width), bf16),
        pltpu.VMEM((few, width), bf16),
        pltpu.VMEM((count, width), bf16),
        pltpu.VMEM((4, 1, few, LANES), bf16),
        pltpu.VMEM(kv_l, bf16),
        pltpu.VMEM(kv_s, bf16),
        pltpu.VMEM(kv_s, bf16),
    ]
    scratch += [pltpu.VMEM(weight.shape, bf16) for weight in weights]
    scratch += [pltpu.VMEM((4 * count, LANES), bf16)] * 4
    scratch += [pltpu.VMEM((few, width), bf16), pltpu.VMEM((few, width), f32)]
    scratch += [dma((2, 8))] + [dma((2, 3))] * 4 + [dma((9,)), dma((6,))]
    scratch += [
        pltpu.VMEM((count, width), bf16),
        pltpu.VMEM((few, width), bf16),
        pltpu.VMEM((few, width), bf16),
        dma((2, 3)),
    ]
    return pl.pallas_call(
        functools.partial(begin_kernel, pairs),
        in_specs=[anywhere] * 13 + [vmem],
        out_specs=[anywhere] * 6 + [vmem] * 23,
        out_shape=out_shape,
        scratch_shapes=scratch,
        compiler_params=pltpu.CompilerParams(
            vmem_limit_bytes=62 << 20, collective_id=4, has_side_effects=True
        ),
        cost_estimate=pl.CostEstimate(
            flops=16 * count * 4 * count * width + 18 * few * width * hidden,
            bytes_accessed=40 << 20,
            transcendentals=count * count * 4 * width // HALF,
        ),
        name="begin",
    )(large, small, cotangent, clip, *weights, gains)


def cross_attend_kernel(q_ref, kv_ref, mq_ref, mk_ref, o_ref, l_ref, *spaces):
    attend_pair(0, q_ref, kv_ref, mq_ref, mk_ref, spaces, o_ref, l_ref)


def cross_attend(query, kv, mask_q, mask_k):
    pairs, count = query.shape[:2]
    rows = kv.shape[3]
    one = pl.BlockSpec((1, count, LANES), lambda i: (i, 0, 0))
    return pl.pallas_call(
        cross_attend_kernel,
        grid=(pairs,),
        in_specs=[
            one,
            pl.BlockSpec((4, 1, 2, rows, LANES), lambda i: (0, i, 0, 0, 0)),
            whole((count, LANES)),
            whole((4 * rows, LANES)),
        ],
        out_specs=[one, one],
        out_shape=[
            jax.ShapeDtypeStruct(query.shape, bf16),
            jax.ShapeDtypeStruct(query.shape, f32),
        ],
        scratch_shapes=[pltpu.VMEM((4 * rows, LANES), bf16)] * 4,
        compiler_params=pltpu.CompilerParams(vmem_limit_bytes=62 << 20),
        cost_estimate=pl.CostEstimate(
            flops=64 * count * rows * pairs * LANES,
            bytes_accessed=32 * count * pairs * LANES,
            transcendentals=8 * count * rows * pairs,
        ),
        name="cross_attend",
    )(query, kv, mask_q, mask_k)


def after(value, *needed):
    return lax.optimization_barrier((value, needed))[0]


CROSS_ORDERS = (BY_Y[:2], BY_ZL[:2])
SELVES_ORDERS = (BY_Y[:3], BY_ZL[:3], BY_Y[:3], BY_Y[2:], BY_ZL[2:])
SELVES_ENDS = (False, False, False, True, True)
SELVES_STAGES = (
    (0, 4, 11),
    (0, 4, 11),
    (0, 6, 11),
    (1, 3, 6, 8, 10),
    (1, 3, 6, 8, 10),
)


def paired_end(views, normed, large, small, cross, merged, weights, crosses, gains):
    large_view, small_view = views
    large_normed, small_normed, asked, context = normed
    large_q, large_mixed, large_logsum, large_mask_q, large_mask_k, large_kv = large
    small_q, small_mixed, small_logsum, small_mask_q, small_mask_k, small_kv = small
    cross_q, united, cross_logsum, cross_kv, united_grad, grad_out = cross
    large_merged, large_saved, small_merged, small_saved = merged
    query_weight, key_weight, value_weight, output_weight, up_weight, down_weight = weights
    first_gain, second_gain, query_gain, context_gain = gains
    width = large_view.shape[1]
    rows = width // 8
    (
        united_view, large_grad, small_grad, first, other, query_gain_grad, context_gain_grad,
    ) = cross_back(
        (cross_q, united_grad, united, cross_logsum, large_mask_q, small_mask_k),
        cross_kv,
        (united, crosses[3], large_merged, asked, context, grad_out, small_merged) + crosses[:3],
        (query_gain, context_gain),
    )
    (
        large_hidden, small_hidden, large_mixed_grad, small_mixed_grad, up_grad, down_grad,
        output_grad, second_gain_grad, first, other,
    ) = back(
        large_grad, small_grad, large_saved, small_saved, [large_mixed], small_mixed, output_weight,
        second_gain, up_weight, down_weight, True, (first, other), CROSS_ORDERS,
    )
    still = (8, rows // 2, width)
    selves, (large_grad, large_gain), sums = selves_back(
        (large_q, large_mixed_grad, large_mixed, large_logsum, large_mask_q, large_mask_k),
        large_kv,
        (small_q, small_mixed_grad, small_mixed, small_logsum, small_mask_q, small_mask_k),
        small_kv,
        (
            up_grad.reshape(8, 4 * rows, width), down_grad.reshape(8, 4 * rows, width),
            output_grad.reshape(8, 2 * rows, width // 2),
            first.reshape(still), other.reshape(still),
        ),
        (query_weight, key_weight, value_weight, large_hidden, large_view), first_gain,
        SELVES_ORDERS, SELVES_ENDS, SELVES_STAGES,
    )
    up, down, output, first, other = sums
    small_grad, last, late, gains = last_sums(
        tuple(selves) + (large_normed, small_normed, query_weight, key_weight, value_weight)
        + (small_view, small_hidden),
        (
            up.reshape(4, rows, width), down.reshape(4, rows, width),
            output.reshape(4, rows // 2, width // 2),
        ),
        (first_gain, large_gain, second_gain_grad, query_gain_grad, context_gain_grad),
    )
    return results(united_view, large_grad, small_grad, last, late, first, other, gains)


def per_device(tm, seq_size, *args):
    (
        large_view,
        small_view,
        clip_ids,
        first_gain,
        query_weight,
        key_weight,
        value_weight,
        output_weight,
        second_gain,
        up_weight,
        down_weight,
        query_gain,
        context_gain,
        cross_query,
        cross_key,
        cross_value,
        cross_output,
        cotangent,
    ) = args
    seqs, count, width = large_view.shape
    side = tm // 4
    gains = jnp.concatenate((first_gain, second_gain, query_gain, context_gain))
    gains = gains.astype(f32).reshape(4, width)
    first_gain, second_gain, query_gain, context_gain = (gains[i : i + 1] for i in range(4))

    tm_at = lax.axis_index("tm")
    seq_at = lax.axis_index("seq")
    z, x = tm_at // side, tm_at % side
    y, core = seq_at // 2, seq_at % 2
    places = [
        (pz, px, py, pc)
        for pz in range(4)
        for px in range(side)
        for py in range(2)
        for pc in range(2)
    ]

    def number(place):
        return (place[0] * side + place[1]) * seq_size + place[2] * 2 + place[3]

    def permute(value, place):
        pairs = [(number(at), number(place(*at))) for at in places]
        return lax.ppermute(value, ("tm", "seq"), pairs)

    def inverse(place):
        table = {place(*at): at for at in places}
        return lambda *at: table[at]

    go = (
        lambda z, x, y, c: (2 * c + z % 2, x, y, z // 2),
        lambda z, x, y, c: (2 * c + 1 - z % 2, x, y, z // 2),
    )
    back_home = tuple(inverse(place) for place in go)
    other_core = lambda value: permute(value, lambda z, x, y, c: (z, x, y, 1 - c))
    other_y = lambda value: permute(value, lambda z, x, y, c: (z, x, 1 - y, c))
    by_x = lambda value, d: permute(value, lambda z, x, y, c: (z, (x + d) % side, y, c))
    odd = z % 2 == 1

    def relocate(value):
        near = jnp.where(odd, value[1], value[0])
        far = jnp.where(odd, value[0], value[1])
        return jnp.concatenate([permute(near, go[0]), permute(far, go[1])], axis=0)

    def restore(value):
        rows = value.shape[0] // 2
        near, far = permute(value[:rows], back_home[0]), permute(value[rows:], back_home[1])
        return jnp.where(odd, jnp.stack([far, near]), jnp.stack([near, far]))

    def join(parts, axis):
        return parts[0] if len(parts) == 1 else jnp.concatenate(parts, axis=axis)

    def gather(value, axis=1):
        across = join([by_x(value, d) for d in range(1, side)], axis)
        return (value, across, other_core(value), other_core(across))

    def add(a, b):
        return (a.astype(f32) + b.astype(f32)).astype(bf16)

    def scatter_core(keep, send):
        return add(keep, other_core(send))

    def scatter_x(sums):
        rows = sums.shape[1] // side
        total = sums[:, :rows].astype(f32)
        for d in range(1, side):
            total = total + by_x(sums[:, d * rows : (d + 1) * rows], -d).astype(f32)
        return total.astype(bf16)

    if side == 2:
        clip = jnp.broadcast_to(
            clip_ids[:, ::2].astype(bf16)[:, :, None], (seqs, count // 2, LANES)
        )
        (
            large, small, grad_out, large_kv, small_kv, cross_kv, large_normed, small_normed,
            large_q, small_q, large_mixed, large_logsum, small_mixed, small_logsum, small_merged,
            *small_saved, context, large_mask_q, large_mask_k, small_mask_q, small_mask_k,
            first_gain, second_gain, query_gain, context_gain, united_grad,
        ) = begin(
            large_view, small_view, cotangent, clip,
            (query_weight, key_weight, value_weight, output_weight, up_weight, down_weight,
             cross_key, cross_value, cross_output),
            gains,
        )
        large_merged, *large_saved, asked, cross_q = rest(
            large, [large_mixed], output_weight, second_gain, up_weight, down_weight,
            query_gain, (cross_query,),
        )
        united, cross_logsum = cross_attend(cross_q, cross_kv, large_mask_q, small_mask_k)
        return paired_end(
            (large, small),
            (large_normed, small_normed, asked, context),
            (large_q, large_mixed, large_logsum, large_mask_q, large_mask_k, large_kv),
            (small_q, small_mixed, small_logsum, small_mask_q, small_mask_k, small_kv),
            (cross_q, united, cross_logsum, cross_kv, united_grad, grad_out),
            (large_merged, large_saved, small_merged, small_saved),
            (query_weight, key_weight, value_weight, output_weight, up_weight, down_weight),
            (cross_query, cross_key, cross_value, cross_output),
            (first_gain, second_gain, query_gain, context_gain),
        )

    groups = 3
    part = width // groups
    short_clips = gather(relocate(clip_ids[:, ::2].astype(f32)), 0)
    small = relocate(small_view)
    large = relocate(large_view)
    grad_out = relocate(after(cotangent, large))
    spot = lax.broadcasted_iota(jnp.int32, (1, LANES), 1) % HALF

    def mask_of_keys(numbers):
        away = numbers.astype(jnp.int32)[:, None] != spot
        return jnp.where((spot < 4) & away, NEGATIVE, 0.0).astype(bf16)

    def mask_of_queries(numbers):
        same = numbers.astype(jnp.int32)[:, None] == spot
        return jnp.where((spot < 4) & same, 1.0, 0.0).astype(bf16)

    short = jnp.concatenate(short_clips)
    small_mask_k = mask_of_keys(short)
    large_mask_k = mask_of_keys(jnp.repeat(short, 2))
    small_mask_q = mask_of_queries(short_clips[0])
    large_mask_q = mask_of_queries(jnp.repeat(short_clips[0], 2))

    small_normed, small_q, small_kv = front(
        small, first_gain, query_weight, key_weight, value_weight, 1
    )
    small_kv = gather(small_kv[0])
    large_normed, large_q, large_kv = front(
        large, first_gain, query_weight, key_weight, value_weight, groups
    )
    large_kv = [gather(kv) for kv in large_kv]
    small_mixed, small_logsum = attend(small_q, small_kv, small_mask_q, small_mask_k, 0, width)
    small_merged, *small_saved, context, cross_kv = rest(
        small, [small_mixed], output_weight, second_gain, up_weight, down_weight,
        context_gain, (cross_key, cross_value),
    )
    cross_kv = gather(cross_kv)
    united_grad = dot(grad_out, cross_output, NT).astype(bf16)
    large_out = ()
    for group, kv in enumerate(large_kv):
        large_out = attend(large_q, kv, large_mask_q, large_mask_k, group * part, part, large_out)
    large_mixed, large_logsum = large_out
    large_merged, *large_saved, asked, cross_q = rest(
        large, [large_mixed], output_weight, second_gain, up_weight, down_weight,
        query_gain, (cross_query,),
    )
    united, cross_logsum = attend(cross_q, cross_kv, large_mask_q, small_mask_k, 0, width)
    united_view = restore((large_merged + dot(united, cross_output)).astype(bf16))

    bits = side.bit_length() - 1
    moves = {"zh": lambda z, x, y, c: (z ^ 2, x, y, c), "zl": lambda z, x, y, c: (z ^ 1, x, y, c)}
    mine = {"zh": z // 2, "zl": z % 2}
    axes = {"zh": 0, "zl": 1}
    for bit in range(bits):
        flip = 1 << (bits - 1 - bit)
        moves[f"x{bit}"] = lambda z, x, y, c, flip=flip: (z, x ^ flip, y, c)
        mine[f"x{bit}"] = (x // flip) % 2
        axes[f"x{bit}"] = 2 + bit
    moves["core"] = lambda z, x, y, c: (z, x, y, 1 - c)
    moves["y"] = lambda z, x, y, c: (z, x, 1 - y, c)
    mine["core"], mine["y"] = core, y
    axes["core"], axes["y"] = 2 + bits, 3 + bits
    by_y = ["core", "y", "zl"] + [f"x{bit}" for bit in range(bits)] + ["zh"]
    by_zl = ["core", "zl", "y"] + [f"x{bit}" for bit in range(bits)] + ["zh"]
    by_yx = ["core", "y"] + [f"x{bit}" for bit in range(bits)] + ["zl", "zh"]

    class Sum:
        def __init__(self, local, order):
            rows, wide = local.shape
            self.value = local.reshape((2,) * (2 + bits) + (rows // tm, wide))
            self.todo = list(order)
            self.rows, self.wide = rows // tm, wide

        def step(self, *needed):
            name = self.todo.pop(0)
            axis = axes[name]
            size = self.value.shape[axis] // 2
            at = mine[name]
            keep = lax.dynamic_slice_in_dim(self.value, at * size, size, axis)
            send = lax.dynamic_slice_in_dim(self.value, (1 - at) * size, size, axis)
            self.value = add(keep, permute(send, moves[name]))
            return self.value

        def finish(self):
            while self.todo:
                self.step()
            value = self.value.reshape(self.rows // 2, self.wide // 2)
            other = other_y(value)
            value = jnp.where(
                y == 0,
                jnp.concatenate([value, other], axis=1),
                jnp.concatenate([other, value], axis=1),
            )
            other = other_core(value)
            return jnp.where(
                core == 0,
                jnp.concatenate([value, other], axis=0),
                jnp.concatenate([other, value], axis=0),
            ).astype(f32)

    cross_groups = 2
    cross_part = width // cross_groups
    dcq, dckv = [], []
    for group in range(cross_groups):
        query = after(cross_q, *dcq[-1:])
        at = group * cross_part
        dq, keep, send = attend_back(
            query, cross_kv, united_grad, united, cross_logsum,
            large_mask_q, small_mask_k, at, at, at, cross_part,
        )
        dcq.append(dq)
        dckv.append(scatter_x(scatter_core(keep, send)))
    dcq = jnp.concatenate(dcq, axis=1)
    dck = jnp.concatenate([kv[0] for kv in dckv], axis=1)
    dcv = jnp.concatenate([kv[1] for kv in dckv], axis=1)
    extra, query_gain_grad = norm_back(dot(dcq, cross_query, NT), large_merged, query_gain)
    large_merged_grad = grad_out.astype(f32) + extra
    small_merged_grad, context_gain_grad = norm_back(
        dot(dck, cross_key, NT) + dot(dcv, cross_value, NT), small_merged, context_gain
    )
    cross_parts = [
        dot(united, grad_out, TN).astype(bf16),
        dot(asked, dcq, TN).astype(bf16),
        dot(context, dck, TN).astype(bf16),
        dot(context, dcv, TN).astype(bf16),
    ]
    (
        large_hidden_grad,
        small_hidden_grad,
        large_mixed_grad,
        small_mixed_grad,
        up_grad,
        down_grad,
        output_grad,
        second_gain_grad,
    ) = back(
        large_merged_grad, small_merged_grad, large_saved, small_saved, [large_mixed], small_mixed,
        output_weight, second_gain, up_weight, down_weight, False,
    )
    cross_sum = Sum(jnp.concatenate(cross_parts, axis=1), by_y)
    up_sum = Sum(up_grad, by_y)
    down_sum = Sum(down_grad, by_zl)
    cross_sum.step()
    small_dq, keep, send = attend_back(
        after(small_q, cross_sum.value), small_kv, small_mixed_grad, small_mixed, small_logsum,
        small_mask_q, small_mask_k, 0, 0, 0, width,
    )
    small_sums = scatter_core(keep, send)
    up_sum.step()
    down_sum.step()
    cross_sum.step()
    needed = [small_dq, up_sum.value, down_sum.value]
    normed = jnp.concatenate([large_normed, small_normed], axis=0)
    last_sums, dqs, dkvs = [], [], []
    pending = None
    for group in range(groups):
        at = group * part
        dq, keep, send = attend_back(
            after(large_q, *needed), large_kv[group], large_mixed_grad, large_mixed, large_logsum,
            large_mask_q, large_mask_k, at, at, 0, part,
        )
        sums = scatter_core(keep, send)
        dqs.append(dq)
        needed = [dq]
        if group == 0:
            small_dkv = scatter_x(small_sums)
            needed += [cross_sum.value, small_sums]
        if group == 1:
            needed += [small_dkv, up_sum.step(), down_sum.step(), cross_sum.step()]
        if pending is not None:
            needed.append(pending.step())
        dkv = scatter_x(sums)
        dkvs.append(dkv)
        local = jnp.concatenate(
            [
                jnp.concatenate([dq, dkv[0], dkv[1]], axis=1),
                jnp.concatenate(
                    [
                        small_dq[:, at : at + part],
                        small_dkv[0, :, at : at + part],
                        small_dkv[1, :, at : at + part],
                    ],
                    axis=1,
                ),
            ],
            axis=0,
        )
        local = dot(normed, local, TN).astype(bf16)
        pending = Sum(local, by_yx)
        last_sums.append(pending)

    def front_back(view, hidden_grad, dq, dk, dv):
        grad = (
            dot(dq, query_weight, NT) + dot(dk, key_weight, NT) + dot(dv, value_weight, NT)
        )
        extra, gain_part = norm_back(grad, view.astype(f32), first_gain)
        return (hidden_grad + extra).astype(bf16), gain_part

    small_grad, small_gain = front_back(
        small, small_hidden_grad, small_dq, small_dkv[0], small_dkv[1]
    )
    large_grad, large_gain = front_back(
        large,
        large_hidden_grad,
        jnp.concatenate(dqs, axis=1),
        jnp.concatenate([kv[0] for kv in dkvs], axis=1),
        jnp.concatenate([kv[1] for kv in dkvs], axis=1),
    )
    small_grad = restore(small_grad).astype(f32)
    large_grad = restore(large_grad).astype(f32)
    output_sum = Sum(output_grad, by_yx)
    gain_rows = jnp.concatenate(
        [large_gain + small_gain, second_gain_grad, query_gain_grad, context_gain_grad], axis=0
    )
    wide = width // tm
    gain_rows = jnp.transpose(gain_rows.reshape(4, tm, wide), (1, 0, 2)).astype(bf16)
    gain_rows = jnp.pad(gain_rows, ((0, 0), (0, 28), (0, 2 * LANES - wide)))
    gain_sum = Sum(gain_rows.reshape(tm * 32, 2 * LANES), by_yx)

    cross_total = cross_sum.finish()
    up_total = up_sum.finish()
    down_total = down_sum.finish()
    output_total = output_sum.finish()
    last_totals = [total.finish() for total in last_sums]
    gain_total = gain_sum.finish()
    cross_grads = [cross_total[:, i * width : (i + 1) * width] for i in range(4)]
    last_grads = [
        jnp.concatenate([total[:, i * part : (i + 1) * part] for total in last_totals], axis=1)
        for i in range(3)
    ]
    gain_grads = [gain_total[i, :wide] for i in range(4)]
    return (
        united_view,
        large_grad,
        small_grad,
        gain_grads[0],
        last_grads[0],
        last_grads[1],
        last_grads[2],
        output_total,
        gain_grads[1],
        up_total,
        down_total,
        gain_grads[2],
        gain_grads[3],
        cross_grads[1],
        cross_grads[2],
        cross_grads[3],
        cross_grads[0],
    )


def solution(mesh):
    token = P("seq", "tm", None)
    in_specs = (token, token, P("seq", "tm")) + (P(),) * 14 + (token,)
    vector, matrix = P("tm"), P("tm", None)
    out_specs = (
        (token, token, token, vector)
        + (matrix,) * 4
        + (vector, matrix, matrix, vector, vector)
        + (matrix,) * 4
    )
    return jax.shard_map(
        functools.partial(per_device, mesh.shape["tm"], mesh.shape["seq"]),
        mesh=mesh,
        in_specs=in_specs,
        out_specs=out_specs,
        check_vma=False,
    )
```

```python
import functools

import jax
import jax.numpy as jnp
from jax import lax
from jax.experimental import pallas as pl
from jax.experimental.pallas import tpu as pltpu
from jax.sharding import PartitionSpec as P

HEADS = 12
EPS = 1e-05
NEGATIVE = -1e30
LOG2E = 1.4426950408889634
LN2 = 0.6931471805599453
LANES = 128
HALF = 64

bf16 = jnp.bfloat16
f32 = jnp.float32
NT = (((1,), (1,)), ((), ()))
NN = (((1,), (0,)), ((), ()))
TN = (((0,), (0,)), ((), ()))


def dot(a, b, dims=NN):
    return lax.dot_general(a, b, dims, preferred_element_type=f32)


def largest_block(rows, most):
    block = min(rows, most)
    while rows % block or block % 16:
        block -= 1
    return block


def columns(rows, at):
    return pl.BlockSpec((rows, LANES), lambda i: (0, i + at))


def pair_columns(rows, at):
    return pl.BlockSpec((2, rows, LANES), lambda i: (0, 0, i + at))


def whole(shape):
    return pl.BlockSpec(shape, lambda i: (0,) * len(shape))


def attend_kernel(parts, block, *refs):
    q_ref, mq_ref, mk_ref = refs[:3]
    kv_refs = refs[3 : 3 + parts]
    o_ref, l_ref, ka0, ka1, va0, va1 = refs[-6:]
    count = q_ref.shape[0]
    first = 0
    for kv_ref in kv_refs:
        rows = kv_ref.shape[1]
        low = lax.broadcasted_iota(jnp.int32, (rows, LANES), 1) < HALF
        here = pl.ds(first, rows)
        keys, values, mask = kv_ref[0], kv_ref[1], mk_ref[here, :]
        one = jnp.ones_like(values)
        ka0[here, :] = jnp.where(low, keys, mask)
        ka1[here, :] = jnp.where(low, mask, keys)
        va0[here, :] = jnp.where(low, values, one)
        va1[here, :] = jnp.where(low, one, values)
        first += rows
    low = lax.broadcasted_iota(jnp.int32, (block, LANES), 1) < HALF
    for number in range(count // block):
        here = pl.ds(number * block, block)
        query, mask = q_ref[here, :], mq_ref[here, :]
        tops, sums = [], []
        for head, keys, values in ((0, ka0, va0), (1, ka1, va1)):
            mine = jnp.where(low, query, mask) if head == 0 else jnp.where(low, mask, query)
            score = dot(mine, keys[...], NT)
            top = jnp.max(score, axis=1, keepdims=True)
            weight = jnp.exp2(score - top).astype(bf16)
            sums.append(dot(weight, values[...]))
            tops.append(jnp.broadcast_to(top, (block, LANES)))
        total = jnp.where(low, sums[1], sums[0])
        top = jnp.where(low, tops[1], tops[0])
        out = jnp.where(low, sums[0], sums[1])
        o_ref[here, :] = (out / pltpu.roll(total, HALF, 1)).astype(bf16)
        l_ref[here, :] = top + jnp.log2(total)


def attend(query, kv, mask_q, mask_k, at, width, earlier=()):
    count = query.shape[0]
    total = sum(part.shape[1] for part in kv)
    out = lambda kind: jax.ShapeDtypeStruct((count, query.shape[1]), kind)
    given = 3 + len(kv)
    return pl.pallas_call(
        functools.partial(attend_kernel, len(kv), largest_block(count, 256)),
        grid=(width // LANES,),
        in_specs=[columns(count, at // LANES), whole((count, LANES)), whole((total, LANES))]
        + [pair_columns(part.shape[1], 0) for part in kv]
        + [pl.BlockSpec(memory_space=pl.ANY)] * len(earlier),
        out_specs=[columns(count, at // LANES)] * 2,
        out_shape=[out(bf16), out(f32)],
        scratch_shapes=[pltpu.VMEM((total, LANES), bf16)] * 4,
        input_output_aliases={given + i: i for i in range(len(earlier))},
        compiler_params=pltpu.CompilerParams(vmem_limit_bytes=40 << 20),
        cost_estimate=pl.CostEstimate(
            flops=16 * count * total * width,
            bytes_accessed=width * (count * 8 + total * 4),
            transcendentals=count * total * width // HALF,
        ),
        name="attend",
    )(query, mask_q, mask_k, *kv, *earlier)


def three(value):
    first = value.astype(bf16)
    rest = value - first.astype(f32)
    second = rest.astype(bf16)
    return first, second, (rest - second.astype(f32)).astype(bf16)


def attend_back_kernel(parts, block, *refs):
    q_ref, do_ref, o_ref, l_ref, mq_ref, mk_ref = refs[:6]
    kv_refs = refs[6 : 6 + parts]
    dq_ref, keep_ref, send_ref, keys_at, values_at = refs[6 + parts :]
    count = q_ref.shape[0]
    first = 0
    for kv_ref in kv_refs:
        here = pl.ds(first, kv_ref.shape[1])
        keys_at[here, :] = kv_ref[0]
        values_at[here, :] = kv_ref[1]
        first += kv_ref.shape[1]
    lane = lax.broadcasted_iota(jnp.int32, (count, LANES), 1)
    low = lane < HALF
    spot = lane % HALF
    query, grad, mask = q_ref[...], do_ref[...], mq_ref[...]
    zero = jnp.zeros_like(query)
    product = grad.astype(f32) * o_ref[...].astype(f32)
    delta0 = jnp.sum(jnp.where(low, product, 0.0), axis=1, keepdims=True)
    delta1 = jnp.sum(jnp.where(low, 0.0, product), axis=1, keepdims=True)
    delta = jnp.where(low, delta1, delta0)

    def beside(base, value):
        a, b, c = three(-value)
        return jnp.where(spot == 4, a, jnp.where(spot == 5, b, jnp.where(spot == 6, c, base)))

    query_side = beside(mask, l_ref[...])
    grad_side = beside(zero, delta)
    query_a = (jnp.where(low, query, query_side), jnp.where(low, query_side, query))
    grad_a = (jnp.where(low, grad, grad_side), jnp.where(low, grad_side, grad))
    query_m = (jnp.where(low, query, zero), jnp.where(low, zero, query))
    grad_m = (jnp.where(low, grad, zero), jnp.where(low, zero, grad))
    lane_k = lax.broadcasted_iota(jnp.int32, (block, LANES), 1)
    low_k = lane_k < HALF
    spot_k = lane_k % HALF
    one = jnp.where((spot_k >= 4) & (spot_k < 7), 1.0, 0.0).astype(bf16)
    dq = jnp.zeros((count, LANES), f32)
    for number in range(first // block):
        here = pl.ds(number * block, block)
        keys, values = keys_at[here, :], values_at[here, :]
        side = mk_ref[here, :] + one
        nought = jnp.zeros_like(keys)
        dk = jnp.zeros((block, LANES), f32)
        dv = jnp.zeros((block, LANES), f32)
        for head in (0, 1):
            pick = lambda a, b: jnp.where(low_k, a, b) if head == 0 else jnp.where(low_k, b, a)
            prob = jnp.exp2(dot(query_a[head], pick(keys, side), NT))
            change = dot(grad_a[head], pick(values, one), NT)
            score_grad = (prob * change).astype(bf16)
            dv += dot(prob.astype(bf16), grad_m[head], TN)
            dk += dot(score_grad, query_m[head], TN)
            dq += dot(score_grad, pick(keys, nought))
        out_ref = keep_ref if number * block < first // 2 else send_ref
        there = pl.ds(number * block % (first // 2), block)
        out_ref[0, there, :] = (dk * LN2).astype(bf16)
        out_ref[1, there, :] = dv.astype(bf16)
    dq_ref[...] = (dq * HALF**-0.5).astype(bf16)


def attend_back(query, kv, grad, out, logsum, mask_q, mask_k, at, at_out, at_kv, width):
    count = query.shape[0]
    total = sum(part.shape[1] for part in kv)
    return pl.pallas_call(
        functools.partial(attend_back_kernel, len(kv), largest_block(total // 2, 512)),
        grid=(width // LANES,),
        in_specs=[columns(count, at // LANES)] * 2
        + [columns(count, at_out // LANES)] * 2
        + [whole((count, LANES)), whole((total, LANES))]
        + [pair_columns(part.shape[1], at_kv // LANES) for part in kv],
        out_specs=[columns(count, 0)] + [pair_columns(total // 2, 0)] * 2,
        out_shape=[jax.ShapeDtypeStruct((count, width), bf16)]
        + [jax.ShapeDtypeStruct((2, total // 2, width), bf16)] * 2,
        scratch_shapes=[pltpu.VMEM((total, LANES), bf16)] * 2,
        compiler_params=pltpu.CompilerParams(vmem_limit_bytes=40 << 20),
        cost_estimate=pl.CostEstimate(
            flops=20 * count * total * width,
            bytes_accessed=width * (count * 12 + total * 8),
            transcendentals=count * total * width // HALF,
        ),
        name="attend_back",
    )(query, grad, out, logsum, mask_q, mask_k, *kv)


def norm_stats(value):
    mean = jnp.mean(value, axis=-1, keepdims=True)
    centred = value - mean
    spread = jnp.mean(centred * centred, axis=-1, keepdims=True)
    return centred, lax.rsqrt(spread + EPS)


def norm(value, gain):
    centred, scale = norm_stats(value)
    return (centred * scale * gain).astype(bf16)


def norm_back(grad, value, gain):
    centred, scale = norm_stats(value)
    unit = centred * scale
    gain_grad = jnp.sum(grad * unit, axis=0, keepdims=True)
    grad = grad * gain
    extra = scale * (
        grad
        - jnp.mean(grad, axis=-1, keepdims=True)
        - unit * jnp.mean(grad * unit, axis=-1, keepdims=True)
    )
    return extra, gain_grad


Q_SCALE = LOG2E * HALF**-0.5


def front_kernel(x_ref, gain_ref, wq_ref, wk_ref, wv_ref, n_ref, q_ref, *kv_refs):
    normed = norm(x_ref[...].astype(f32), gain_ref[...])
    n_ref[...] = normed
    width = kv_refs[0].shape[2]
    keys = dot(normed, wk_ref[...]).astype(bf16)
    values = dot(normed, wv_ref[...]).astype(bf16)
    for group, kv_ref in enumerate(kv_refs):
        kv_ref[0] = keys[:, group * width : (group + 1) * width]
        kv_ref[1] = values[:, group * width : (group + 1) * width]
    q_ref[...] = (dot(normed, wq_ref[...]) * Q_SCALE).astype(bf16)


def front(view, gain, wq, wk, wv, groups):
    rows, width = view.shape
    part = width // groups
    result = pl.pallas_call(
        front_kernel,
        out_shape=[jax.ShapeDtypeStruct((rows, width), bf16)] * 2
        + [jax.ShapeDtypeStruct((2, rows, part), bf16)] * groups,
        compiler_params=pltpu.CompilerParams(vmem_limit_bytes=40 << 20),
        cost_estimate=pl.CostEstimate(
            flops=6 * rows * width * width,
            bytes_accessed=6 * width * width + 10 * rows * width,
            transcendentals=0,
        ),
        name="front",
    )(view, gain, wq, wk, wv)
    return result[0], result[1], result[2:]


GELU_A = 0.7978845608028654
GELU_B = 0.044715


def gelu_both(value):
    square = value * value
    bent = jnp.tanh(GELU_A * value * (1.0 + GELU_B * square))
    half = 0.5 * (1.0 + bent)
    slope = half + 0.5 * value * (1.0 - bent * bent) * (
        GELU_A * (1.0 + 3.0 * GELU_B * square)
    )
    return value * half, slope


def fill_wide(wide, refs, rows, first):
    at, there = 0, pl.ds(first, rows)
    for ref in refs:
        if len(ref.shape) == 3:
            for pair in range(ref.shape[0]):
                wide[there, at : at + LANES] = ref[pair]
                at += LANES
        else:
            wide[there, at : at + ref.shape[1]] = ref[...]
            at += ref.shape[1]


def rest_kernel(steps, mixes, is_query, *refs):
    x_ref = refs[0]
    mixed_refs = refs[1 : 1 + mixes]
    wo_ref, gain_ref, up_ref, down_ref, next_gain_ref = refs[1 + mixes : 6 + mixes]
    next_refs = refs[6 + mixes : -9]
    merged_ref, hidden_ref, second_ref, active_ref, slope_ref = refs[-9:-4]
    asked_ref, out_ref, total, scratch = refs[-4:]
    step = pl.program_id(0)

    @pl.when(step == 0)
    def _():
        hidden = x_ref[...].astype(f32)
        fill_wide(scratch, mixed_refs, scratch.shape[0], 0)
        hidden = hidden + dot(scratch[...], wo_ref[...])
        hidden_ref[...] = hidden
        second_ref[...] = norm(hidden, gain_ref[...])
        total[...] = hidden

    rows = total.shape[0] // 2
    halves = [pl.ds(at * rows, rows) for at in (0, 1)]
    inners = [dot(second_ref[half, :], up_ref[...]) for half in halves]
    for half, inner in zip(halves, inners):
        active, slope = gelu_both(inner)
        active = active.astype(bf16)
        active_ref[half, :] = active
        slope_ref[half, :] = slope.astype(bf16)
        total[half, :] += dot(active, down_ref[...])

    @pl.when(step == steps - 1)
    def _():
        merged = total[...]
        merged_ref[...] = merged
        asked = norm(merged, next_gain_ref[...])
        asked_ref[...] = asked
        if is_query:
            query = (dot(asked, next_refs[0][...]) * Q_SCALE).astype(bf16)
            if len(out_ref.shape) == 3:
                for pair in range(out_ref.shape[0]):
                    out_ref[pair] = query[:, pair * LANES : (pair + 1) * LANES]
            else:
                out_ref[...] = query
        else:
            out_ref[0] = dot(asked, next_refs[0][...]).astype(bf16)
            out_ref[1] = dot(asked, next_refs[1][...]).astype(bf16)


def rest(view, mixed, wo, gain, up, down, next_gain, next_weights):
    rows, width = view.shape
    steps = up.shape[1] // width
    is_query = len(next_weights) == 1
    flat = whole((rows, width))
    slab = pl.BlockSpec((rows, width), lambda i: (0, i))
    square = whole((width, width))
    shape = lambda kind: jax.ShapeDtypeStruct((rows, width), kind)
    wide = jax.ShapeDtypeStruct((rows, up.shape[1]), bf16)
    last = (rows, width) if is_query else (2, rows, width)
    if len(mixed[0].shape) == 3:
        last = (width // LANES, rows, LANES)
    return pl.pallas_call(
        functools.partial(rest_kernel, steps, len(mixed), is_query),
        grid=(steps,),
        in_specs=[flat]
        + [whole(m.shape) for m in mixed]
        + [square, whole((1, width))]
        + [slab_of(width, width), pl.BlockSpec((width, width), lambda i: (i, 0))]
        + [whole((1, width))]
        + [square] * len(next_weights),
        out_specs=[flat, flat, flat, slab, slab, flat, whole(last)],
        out_shape=[shape(f32), shape(f32), shape(bf16), wide, wide, shape(bf16)]
        + [jax.ShapeDtypeStruct(last, bf16)],
        scratch_shapes=[pltpu.VMEM((rows, width), f32), pltpu.VMEM((rows, width), bf16)],
        compiler_params=pltpu.CompilerParams(vmem_limit_bytes=62 << 20),
        cost_estimate=pl.CostEstimate(
            flops=2 * rows * width * (4 * up.shape[1] // 2 + 2 * width),
            bytes_accessed=width * width * 22 + rows * width * 32,
            transcendentals=rows * up.shape[1],
        ),
        name="rest",
    )(view, *mixed, wo, gain, up, down, next_gain, *next_weights)


def slab_of(rows, width):
    return pl.BlockSpec((rows, width), lambda i: (0, i))


def back_kernel(steps, mixes, sizes, laid, orders, *refs):
    gl_ref, gs_ref, al_ref, as_ref, sl_ref, ss_ref = refs[:6]
    cl_ref, cs_ref, hl_ref, hs_ref = refs[6:10]
    mixed_refs = refs[10 : 10 + mixes]
    mixed_s_ref, wo_ref, gain_ref, up_ref, down_ref = refs[10 + mixes : 15 + mixes]
    flows = len(orders)
    locals_, outs = refs[15 + mixes : 15 + mixes + flows], refs[15 + mixes + flows :]
    (hgl_ref, hgs_ref, ml_ref, ms_ref, dup_ref, ddown_ref, dwo_ref, dgain_ref) = outs[:8]
    sums, outs = outs[8 : 8 + flows], outs[8 + flows :]
    branch, second, total, active, inner_grad, mixed = outs[:6]
    large, small = sizes
    top, bottom = pl.ds(0, large), pl.ds(large, small)
    step = pl.program_id(0)
    if flows:
        here = Here()
        rest_refs = list(outs[6:])
        running = [
            Flow(here, order, local, rest_refs, True, False)
            for order, local in zip(orders, locals_)
        ]

        @pl.when(step == 0)
        def _():
            here.hail(*ALL_PARTNERS)
            here.heard(len(ALL_PARTNERS))
            for flow in running:
                flow.act(0)

    @pl.when(step == 0)
    def _():
        branch[top, :] = gl_ref[...].astype(bf16)
        branch[bottom, :] = gs_ref[...].astype(bf16)
        second[top, :] = cl_ref[...]
        second[bottom, :] = cs_ref[...]
        total[...] = jnp.zeros_like(total)

    grad = dot(branch[...], down_ref[...], NT)
    inner_grad[top, :] = (grad[:large] * sl_ref[...].astype(f32)).astype(bf16)
    inner_grad[bottom, :] = (grad[large:] * ss_ref[...].astype(f32)).astype(bf16)
    active[top, :] = al_ref[...]
    active[bottom, :] = as_ref[...]
    down = dot(active[...], branch[...], TN).astype(bf16)
    upper = dot(second[...], inner_grad[...], TN).astype(bf16)
    if laid:
        rows = dup_ref.shape[1]
        for at in range(8):
            zl, x, zh = at // 4, at // 2 % 2, at % 2
            first = ((zh * 2 + zl) * 2 + x) * rows
            dup_ref[at] = upper[first : first + rows]
        for x, core, y in ((a, b, c) for a in (0, 1) for b in (0, 1) for c in (0, 1)):
            first = (x * 4 + core * 2 + y) * rows
            there = core * 16 + (step % 2) * 8 + y * 4 + x * 2 + step // 2
            ddown_ref[there] = down[first : first + rows]
    else:
        dup_ref[...] = upper
        ddown_ref[...] = down
    total[...] += dot(inner_grad[...], up_ref[...], NT)

    @pl.when(step == steps - 1)
    def _():
        extra, gain_l = norm_back(total[top, :], hl_ref[...], gain_ref[...])
        hidden_grad = gl_ref[...] + extra
        hgl_ref[...] = hidden_grad
        branch[top, :] = hidden_grad.astype(bf16)
        extra, gain_s = norm_back(total[bottom, :], hs_ref[...], gain_ref[...])
        hidden_grad = gs_ref[...] + extra
        hgs_ref[...] = hidden_grad
        branch[bottom, :] = hidden_grad.astype(bf16)
        dgain_ref[...] = gain_l + gain_s
        mixed_grad = dot(branch[...], wo_ref[...], NT).astype(bf16)
        ml_ref[...] = mixed_grad[:large]
        ms_ref[...] = mixed_grad[large:]
        fill_wide(mixed, mixed_refs, large, 0)
        fill_wide(mixed, [mixed_s_ref], small, large)
        value = dot(mixed[...], branch[...], TN).astype(bf16)
        if laid:
            rows, wide = dwo_ref.shape[1:]
            for at, (core, y, tm) in enumerate(spots(BY_Y)):
                first = (tm * 2 + core) * rows
                dwo_ref[at] = value[first : first + rows, y * wide : (y + 1) * wide]
        else:
            dwo_ref[...] = value

    for flow in range(flows):
        for stage, when in enumerate((0, steps - 1)):

            @pl.when(step == when)
            def _(flow=flow, stage=stage):
                running[flow].act(stage + 1)
                if stage == 1:
                    sums[flow][...] = running[flow].result()


def back(
    grad_l, grad_s, saved_l, saved_s, mixed_l, mixed_s, wo, gain, up, down, laid, flows=(), orders=()
):
    (hidden_l, second_l, active_l, slope_l) = saved_l
    (hidden_s, second_s, active_s, slope_s) = saved_s
    large, width = grad_l.shape
    small = grad_s.shape[0]
    rows = large + small
    hidden = up.shape[1]
    part = width
    steps = hidden // part
    fl, fs = whole((large, width)), whole((small, width))
    square = whole((width, width))
    up_slab = slab_of(width, part)
    down_slab = pl.BlockSpec((part, width), lambda i: (i, 0))
    shape = jax.ShapeDtypeStruct
    results = [flow_result(o, f.shape[1:], False) for o, f in zip(orders, flows)]
    scratch = [s for o, f in zip(orders, flows) for s in flow_scratch(o, f.shape[1:], True, False)]
    out_up, out_down, out_square = up_slab, down_slab, square
    up_shape, down_shape, square_shape = up.shape, down.shape, (width, width)
    if laid:
        block = (width // 8, width)
        up_shape = down_shape = (32,) + block
        square_shape = (32, width // 16, width // 2)
        out_up = pl.BlockSpec((8,) + block, lambda i: (i, 0, 0))
        out_down, out_square = whole(down_shape), whole(square_shape)
    return pl.pallas_call(
        functools.partial(back_kernel, steps, len(mixed_l), (large, small), laid, orders),
        grid=(steps,),
        in_specs=[fl, fs]
        + [slab_of(large, part), slab_of(small, part)] * 2
        + [fl, fs, fl, fs]
        + [whole(m.shape) for m in mixed_l]
        + [whole(mixed_s.shape), square, whole((1, width)), up_slab, down_slab]
        + [pl.BlockSpec(memory_space=pl.ANY)] * len(flows),
        out_specs=[fl, fs, fl, fs, out_up, out_down, out_square, whole((1, width))]
        + [whole(result.shape) for result in results],
        out_shape=[
            shape((large, width), f32),
            shape((small, width), f32),
            shape((large, width), bf16),
            shape((small, width), bf16),
            shape(up_shape, bf16),
            shape(down_shape, bf16),
            shape(square_shape, bf16),
            shape((1, width), f32),
        ]
        + results,
        scratch_shapes=[
            pltpu.VMEM((rows, width), bf16),
            pltpu.VMEM((rows, width), bf16),
            pltpu.VMEM((rows, width), f32),
            pltpu.VMEM((rows, part), bf16),
            pltpu.VMEM((rows, part), bf16),
            pltpu.VMEM((rows, width), bf16),
        ]
        + scratch,
        compiler_params=pltpu.CompilerParams(
            vmem_limit_bytes=60 << 20,
            has_side_effects=bool(flows),
            collective_id=0 if flows else None,
        ),
        cost_estimate=pl.CostEstimate(
            flops=2 * rows * width * (4 * hidden + 2 * width),
            bytes_accessed=width * width * 36 + rows * width * 40,
            transcendentals=0,
        ),
        name="back",
    )(
        grad_l, grad_s, active_l, active_s, slope_l, slope_s, second_l, second_s, hidden_l, hidden_s,
        *mixed_l, mixed_s, wo, gain, up, down, *flows,
    )


MESH = pl.DeviceIdType.MESH
BY_Y = ("core", "y", "zl", "x", "zh")
BY_ZL = ("core", "zl", "y", "x", "zh")
BY_X = ("core", "x", "zl", "y", "zh")
BY_YX = ("core", "y", "x", "zl", "zh")


def spots(order):
    out = []
    for at in range(32):
        bit = {name: (at >> (4 - i)) & 1 for i, name in enumerate(order)}
        out.append((bit["core"], bit["y"], (bit["zh"] * 2 + bit["zl"]) * 2 + bit["x"]))
    return out


class Here:
    def __init__(self):
        tm, seq = lax.axis_index("tm"), lax.axis_index("seq")
        self.tm, self.seq = tm, seq
        self.bit = {
            "zh": tm // 4,
            "zl": (tm // 2) % 2,
            "x": tm % 2,
            "y": seq // 2,
            "core": seq % 2,
        }

    def partner(self, *names):
        tm, seq = self.tm, self.seq
        for name in names:
            one = 1 - 2 * self.bit[name]
            if name in ("y", "core"):
                seq = seq + one * (2 if name == "y" else 1)
            else:
                tm = tm + one * {"zh": 4, "zl": 2, "x": 1}[name]
        return (tm, seq)

    def hail(self, *partners):
        self.hail_all([self.partner(*names) for names in partners])

    def hail_line(self, *more):
        z, core = self.tm // 2, self.bit["core"]
        self.hail_all(
            [
                (
                    lax.rem(z + dz, 4) * 2 + self.bit["x"],
                    self.bit["y"] * 2 + lax.rem(core + dc, 2),
                )
                for dz in range(4)
                for dc in range(2)
                if dz or dc
            ]
            + [self.partner(name) for name in more]
        )

    def hail_all(self, places):
        barrier = pltpu.get_barrier_semaphore()
        for place in places:
            pl.semaphore_signal(barrier, inc=1, device_id=place, device_id_type=MESH)

    def heard(self, count):
        pl.semaphore_wait(pltpu.get_barrier_semaphore(), count)


ALL_PARTNERS = (("core",), ("y",), ("zl",), ("x",), ("zh",))


class Restore:
    def __init__(self, here, held, got, sems):
        self.held, self.got, self.sems = held, got, sems
        self.rows = got.shape[1]
        z, core = here.tm // 2, here.bit["core"]
        self.odd = lax.rem(z, 2)
        self.stay = core == z // 2
        turns = (self.odd, 1 - self.odd)
        self.places = [
            ((2 * core + turn) * 2 + here.bit["x"], here.bit["y"] * 2 + z // 2) for turn in turns
        ]

    def far(self, turn, arriving=False):
        at = 1 - self.odd if arriving and turn else self.odd
        return pltpu.make_async_remote_copy(
            src_ref=self.held.at[pl.ds(turn * self.rows, self.rows)],
            dst_ref=self.got.at[at],
            send_sem=self.sems.at[0, turn],
            recv_sem=self.sems.at[1, turn],
            device_id=self.places[turn],
            device_id_type=MESH,
        )

    def near(self):
        return pltpu.make_async_copy(
            self.held.at[pl.ds(0, self.rows)], self.got.at[self.odd], self.sems.at[1, 0]
        )

    def start(self):
        self.far(1).start()

        @pl.when(self.stay)
        def _():
            self.near().start()

        @pl.when(jnp.logical_not(self.stay))
        def _():
            self.far(0).start()

    def finish(self):
        self.far(1).wait_send()
        self.far(1, True).wait_recv()

        @pl.when(self.stay)
        def _():
            self.near().wait()

        @pl.when(jnp.logical_not(self.stay))
        def _():
            self.far(0).wait_send()
            self.far(0).wait_recv()


def restore_scratch(rows, width):
    return [
        pltpu.VMEM((2 * rows, width), bf16),
        pltpu.VMEM((2, rows, width), bf16),
        pltpu.SemaphoreType.DMA((2, 2)),
    ]


class Flow:
    def __init__(self, here, order, local, refs, keep, ends):
        self.here, self.order, self.local = here, order, local
        self.keep = refs.pop(0) if keep else None
        self.got = [refs.pop(0) for _ in order]
        self.out = refs.pop(0) if ends else None
        self.sem = refs.pop(0)
        self.last = len(order)
        self.ends = ends

    def copy(self, step):
        name = self.order[step]
        half = 1 << (self.last - 1 - step)
        source = self.local if step == 0 else self.got[step - 1]
        at = (1 - self.here.bit[name]) * half
        return pltpu.make_async_remote_copy(
            src_ref=source.at[pl.ds(at, half)],
            dst_ref=self.got[step],
            send_sem=self.sem.at[0, step],
            recv_sem=self.sem.at[1, step],
            device_id=self.here.partner(name),
            device_id_type=MESH,
        )

    def keep_copy(self):
        half = 1 << (self.last - 1)
        at = self.here.bit[self.order[0]] * half
        return pltpu.make_async_copy(
            self.local.at[pl.ds(at, half)], self.keep, self.sem.at[0, self.last + 2]
        )

    def start(self, step):
        self.copy(step).start()
        if step == 0 and self.keep is not None:
            self.keep_copy().start()

    def finish(self, step):
        half = 1 << (self.last - 1 - step)
        self.copy(step).wait()
        got = self.got[step]
        at = self.here.bit[self.order[step]] * half
        if step == 0 and self.keep is not None:
            self.keep_copy().wait()
            source, at = self.keep, 0
        else:
            source = self.local if step == 0 else self.got[step - 1]

        def body(i, carry):
            got[i] = got[i] + source[at + i]
            return carry

        if half == 1:
            got[0] = got[0] + source[at]
        else:
            lax.fori_loop(0, half, body, 0)

    def spread_copy(self, which):
        here = self.here
        own = here.bit["core"] * 2
        if which == 0:
            source, there = self.got[-1].at[0], self.out.at[own + here.bit["y"]]
        else:
            source = there = self.out.at[pl.ds(own, 2)]
        return pltpu.make_async_remote_copy(
            src_ref=source,
            dst_ref=there,
            send_sem=self.sem.at[0, self.last + which],
            recv_sem=self.sem.at[1, self.last + which],
            device_id=here.partner(("y", "core")[which]),
            device_id_type=MESH,
        )

    def act(self, stage):
        if stage == 0:
            self.start(0)
        elif stage < self.last:
            self.finish(stage - 1)
            self.start(stage)
        elif stage == self.last:
            self.finish(stage - 1)
            if self.ends:
                self.spread_copy(0).start()
                self.out[self.here.bit["core"] * 2 + self.here.bit["y"]] = self.got[-1][0]
        elif stage == self.last + 1 and self.ends:
            self.spread_copy(0).wait()
            self.spread_copy(1).start()
        elif stage == self.last + 2 and self.ends:
            self.spread_copy(1).wait()

    def result(self):
        return self.out[...] if self.ends else self.got[-1][...]


def flow_scratch(order, block, keep, ends):
    steps = len(order)
    blocks = [pltpu.VMEM((1 << (steps - 1),) + block, bf16)] if keep else []
    for step in range(steps):
        blocks.append(pltpu.VMEM((1 << (steps - 1 - step),) + block, bf16))
    if ends:
        blocks.append(pltpu.VMEM((4,) + block, bf16))
    return blocks + [pltpu.SemaphoreType.DMA((2, steps + 3))]


def flow_result(order, block, ends):
    left = 4 if ends else 1
    return jax.ShapeDtypeStruct((left,) + block, bf16)


def pair_back(query, grad, out, logsum, mask, keys_at, values_at, mk_ref, block, exchange, pair):
    count = query.shape[0]
    total = keys_at.shape[0]
    lane = lax.broadcasted_iota(jnp.int32, (count, LANES), 1)
    low = lane < HALF
    spot = lane % HALF
    zero = jnp.zeros_like(query)
    product = grad.astype(f32) * out.astype(f32)
    delta0 = jnp.sum(jnp.where(low, product, 0.0), axis=1, keepdims=True)
    delta1 = jnp.sum(jnp.where(low, 0.0, product), axis=1, keepdims=True)
    delta = jnp.where(low, delta1, delta0)

    def beside(base, value):
        a, b, c = three(-value)
        return jnp.where(spot == 4, a, jnp.where(spot == 5, b, jnp.where(spot == 6, c, base)))

    query_side = beside(mask, logsum)
    grad_side = beside(zero, delta)
    query_a = (jnp.where(low, query, query_side), jnp.where(low, query_side, query))
    grad_a = (jnp.where(low, grad, grad_side), jnp.where(low, grad_side, grad))
    query_m = (jnp.where(low, query, zero), jnp.where(low, zero, query))
    grad_m = (jnp.where(low, grad, zero), jnp.where(low, zero, grad))
    lane_k = lax.broadcasted_iota(jnp.int32, (block, LANES), 1)
    low_k = lane_k < HALF
    spot_k = lane_k % HALF
    one = jnp.where((spot_k >= 4) & (spot_k < 7), 1.0, 0.0).astype(bf16)
    dq = jnp.zeros((count, LANES), f32)
    for number in exchange.turns(total // block):
        here = pl.ds(number * block, block)
        keys, values = keys_at[here, :], values_at[here, :]
        side = mk_ref[here, :] + one
        nought = jnp.zeros_like(keys)
        dk = jnp.zeros((block, LANES), f32)
        dv = jnp.zeros((block, LANES), f32)
        for head in (0, 1):
            pick = lambda a, b: jnp.where(low_k, a, b) if head == 0 else jnp.where(low_k, b, a)
            prob = jnp.exp2(dot(query_a[head], pick(keys, side), NT))
            change = dot(grad_a[head], pick(values, one), NT)
            score_grad = (prob * change).astype(bf16)
            dv += dot(prob.astype(bf16), grad_m[head], TN)
            dk += dot(score_grad, query_m[head], TN)
            dq += dot(score_grad, pick(keys, nought))
        exchange.put(pair, number, block, (dk * LN2).astype(bf16), dv.astype(bf16))
    return (dq * HALF**-0.5).astype(bf16)


class Exchange:
    def __init__(self, here, rows, refs):
        self.here, self.rows = here, rows
        self.sums, self.send, self.got_core, self.across, self.got_x = refs[:5]
        self.sems = refs[5]
        self.before = None

    def turns(self, blocks):
        return (3, 1, 0, 2) if blocks == 4 else tuple(reversed(range(blocks)))

    def copy_core(self, pair, far):
        rows = pl.ds(far * self.rows, self.rows)
        return pltpu.make_async_remote_copy(
            src_ref=self.send.at[pair % 2, :, rows, :],
            dst_ref=self.got_core.at[pair, :, rows, :],
            send_sem=self.sems.at[2 * far, pair],
            recv_sem=self.sems.at[2 * far + 1, pair],
            device_id=self.here.partner("core"),
            device_id_type=MESH,
        )

    def copy_x(self, pair):
        return pltpu.make_async_remote_copy(
            src_ref=self.across.at[pair],
            dst_ref=self.got_x.at[pair],
            send_sem=self.sems.at[4, pair],
            recv_sem=self.sems.at[5, pair],
            device_id=self.here.partner("x"),
            device_id_type=MESH,
        )

    def end(self):
        pairs = self.got_x.shape[0]
        for pair in range(pairs):
            if pair >= pairs - 2:
                self.free(pair)
            self.copy_x(pair).wait_send()

    def free(self, pair):
        for far in (0, 1):
            self.copy_core(pair, far).wait_send()

    def put(self, pair, number, block, dk, dv):
        half = 2 * self.rows
        there = pl.ds(number * block % half, block)
        ref, slot = (self.sums, pair) if number * block < half else (self.send, pair % 2)
        ref[slot, 0, there, :] = dk
        ref[slot, 1, there, :] = dv
        if 2 * half == 4 * block:
            if number == 3:
                if self.before is not None:
                    self.before()
                self.copy_core(pair, 1).start()
            elif number == 2:
                self.copy_core(pair, 0).start()
            elif number == 0:
                self.pass_on(pair)
        elif number == 1:
            if self.before is not None:
                self.before()
            for far in (1, 0):
                self.copy_core(pair, far).start()
        else:
            self.pass_on(pair)

    def pass_on(self, pair):
        rows = self.rows
        self.copy_core(pair, 1).wait_recv()
        far = pl.ds(rows, rows)
        for i in (0, 1):
            self.across[pair, i] = self.sums[pair, i, far, :] + self.got_core[pair, i, far, :]
        self.copy_x(pair).start()

    def take(self, pair, out_ref):
        near = pl.ds(0, self.rows)
        self.copy_core(pair, 0).wait_recv()
        self.copy_x(pair).wait_recv()
        for i in (0, 1):
            out_ref[pair, i] = (
                self.sums[pair, i, near, :].astype(f32)
                + self.got_core[pair, i, near, :].astype(f32)
                + self.got_x[pair, i].astype(f32)
            ).astype(bf16)


def exchange_scratch(pairs, rows):
    return [
        pltpu.VMEM((pairs, 2, 2 * rows, LANES), bf16),
        pltpu.VMEM((2, 2, 2 * rows, LANES), bf16),
        pltpu.VMEM((pairs, 2, 2 * rows, LANES), bf16),
        pltpu.VMEM((pairs, 2, rows, LANES), bf16),
        pltpu.VMEM((pairs, 2, rows, LANES), bf16),
        pltpu.SemaphoreType.DMA((6, pairs)),
    ]


def fill_keys(keys_at, values_at, kv_ref):
    rows = kv_ref.shape[3]
    for part in range(kv_ref.shape[0]):
        there = pl.ds(part * rows, rows)
        keys_at[there, :] = kv_ref[part, 0, 0]
        values_at[there, :] = kv_ref[part, 0, 1]


def selves_kernel(pairs, plan, blocks, *refs):
    orders, ends, stages = plan
    large_refs, kv_large, refs = refs[:6], refs[6], refs[7:]
    small_refs, kv_small, refs = refs[:6], refs[6], refs[7:]
    flows = len(orders)
    locals_, refs = refs[:flows], refs[flows:]
    given, gain, refs = refs[:5], refs[5], refs[6:]
    dq_l, dkv_l, dq_s, dkv_s, view_ref, gain_ref = refs[:6]
    sums, refs = refs[6 : 6 + flows], refs[6 + flows :]
    held, load_sems, dq_all, grads, home_refs, refs = refs[:5], refs[5], refs[6], refs[7], refs[8:11], refs[11:]
    keys_l, values_l, keys_s, values_s = refs[:4]
    ex_l, ex_s, refs = refs[4:10], refs[10:16], refs[16:]
    here = Here()
    rows_l, rows_s = keys_l.shape[0] // 4, keys_s.shape[0] // 4
    large, small = Exchange(here, rows_l, ex_l), Exchange(here, rows_s, ex_s)
    refs = list(refs)
    running = [
        Flow(here, orders[flow], locals_[flow], refs, True, ends[flow]) for flow in range(flows)
    ]
    step = pl.program_id(0)
    home = Restore(here, *home_refs)
    loads = [
        pltpu.make_async_copy(source, there, load_sems.at[i])
        for i, (source, there) in enumerate(zip(given, held))
    ]

    @pl.when(step == 0)
    def _():
        here.hail_line("x", "y")
        for load in loads:
            load.start()

    def before():
        @pl.when(step == 0)
        def _():
            here.heard(9)
            for flow in running:
                flow.act(0)

    large.before = before

    def attention(exchange, pair, refs, kv_ref, keys_at, values_at, block, dq_ref):
        q_ref, do_ref, o_ref, l_ref, mq_ref, mk_ref = refs
        fill_keys(keys_at, values_at, kv_ref)

        @pl.when(pair >= 2)
        def _():
            exchange.free(pair - 2)

        dq_ref[...] = pair_back(
            q_ref[0], do_ref[...], o_ref[0], l_ref[0], mq_ref[...], keys_at, values_at, mk_ref,
            block, exchange, pair,
        )

    @pl.when(step < pairs)
    def _():
        attention(large, step, large_refs, kv_large, keys_l, values_l, blocks[0], dq_l)
        dq_all[step] = dq_l[...]

    @pl.when(step >= pairs)
    def _():
        attention(small, step - pairs, small_refs, kv_small, keys_s, values_s, blocks[1], dq_s)

    for pair in range(pairs):

        @pl.when(step == pair + 2 + pair // (pairs - 1))
        def _(pair=pair):
            large.take(pair, dkv_l)

    @pl.when(step == pairs + 2)
    def _():
        *weights, hidden_grad, view = held
        for load in loads:
            load.wait()
        total = None
        for which, weight in enumerate(weights):
            for pair in range(pairs):
                lanes = slice(pair * LANES, (pair + 1) * LANES)
                grads[:, lanes] = dkv_l[pair, which - 1] if which else dq_all[pair]
            product = dot(grads[...], weight[...], NT)
            total = product if total is None else total + product
        extra, gain_ref[...] = norm_back(total, view[...].astype(f32), gain[...])
        home_refs[0][...] = (hidden_grad[...] + extra).astype(bf16)
        home.start()

    for at in range(2 * pairs):
        todo = []
        for flow in range(flows):
            for stage, when in enumerate(stages[flow]):
                if when == at:
                    todo.append((running[flow], stage + 1))
        if todo:

            @pl.when(step == at)
            def _(todo=todo):
                for flow, stage in todo:
                    flow.act(stage)

    @pl.when(step == 2 * pairs - 1)
    def _():
        for pair in range(pairs):
            small.take(pair, dkv_s)
        small.end()
        large.end()
        for flow, sum_ref in zip(running, sums):
            sum_ref[...] = flow.result()
        home.finish()
        view_ref[...] = home_refs[1][...]


def selves_back(large, large_kv, small, small_kv, flows, view, gain, orders, ends, stages):
    count, width = large[1].shape
    few = small[1].shape[0]
    pairs = width // LANES
    total, less = large[5].shape[0], small[5].shape[0]
    shapes = [flow.shape[1:] for flow in flows]
    results = [flow_result(*flow) for flow in zip(orders, shapes, ends)]
    blocks = (largest_block(total // 2, 512), largest_block(less // 2, 512))
    first = lambda i: jnp.minimum(i, pairs - 1)
    last = lambda i: jnp.maximum(i - pairs, 0)
    in_specs = []
    for rows, keys, at in ((count, total, first), (few, less, last)):
        major = pl.BlockSpec((1, rows, LANES), lambda i, at=at: (at(i), 0, 0))
        minor = pl.BlockSpec((rows, LANES), lambda i, at=at: (0, at(i)))
        in_specs += [major, minor, major, major, whole((rows, LANES)), whole((keys, LANES))]
        in_specs.append(
            pl.BlockSpec((4, 1, 2, rows, LANES), lambda i, at=at: (0, at(i), 0, 0, 0))
        )
    in_specs += [pl.BlockSpec(memory_space=pl.ANY)] * (len(flows) + len(view))
    in_specs.append(whole((1, width)))
    shape = jax.ShapeDtypeStruct
    out_shape = [
        shape((count, width), bf16),
        shape((pairs, 2, count, LANES), bf16),
        shape((few, width), bf16),
        shape((pairs, 2, few, LANES), bf16),
        shape((2, count // 2, width), bf16),
        shape((1, width), f32),
    ] + results
    out_specs = [
        pl.BlockSpec((count, LANES), lambda i: (0, first(i))),
        whole((pairs, 2, count, LANES)),
        pl.BlockSpec((few, LANES), lambda i: (0, last(i))),
        whole((pairs, 2, few, LANES)),
        whole((2, count // 2, width)),
        whole((1, width)),
    ] + [whole(result.shape) for result in results]
    scratch = [pltpu.VMEM(value.shape, value.dtype) for value in view]
    scratch += [pltpu.SemaphoreType.DMA((len(view),)), pltpu.VMEM((pairs, count, LANES), bf16)]
    scratch += [pltpu.VMEM((count, width), bf16)] + restore_scratch(count // 2, width)
    scratch += [pltpu.VMEM((total, LANES), bf16)] * 2 + [pltpu.VMEM((less, LANES), bf16)] * 2
    scratch += exchange_scratch(pairs, count) + exchange_scratch(pairs, few)
    for flow in range(len(flows)):
        scratch += flow_scratch(orders[flow], shapes[flow], True, ends[flow])
    result = pl.pallas_call(
        functools.partial(selves_kernel, pairs, (orders, ends, stages), blocks),
        grid=(2 * pairs,),
        in_specs=in_specs,
        out_specs=out_specs,
        out_shape=out_shape,
        scratch_shapes=scratch,
        compiler_params=pltpu.CompilerParams(
            vmem_limit_bytes=60 << 20, collective_id=1, has_side_effects=True
        ),
        cost_estimate=pl.CostEstimate(
            flops=20 * width * (count * total + few * less),
            bytes_accessed=64 * count * width,
            transcendentals=count * total * width // HALF,
        ),
        name="selves_back",
    )(*large, large_kv, *small, small_kv, *flows, *view, gain)
    return result[:4], result[4:6], result[6:]


LAST_ORDERS = (BY_YX, BY_X, BY_YX)
GAIN_ORDER = ("core", "y", "x", "zl", "zh")
LATE_ORDER = ("x", "zh")
LATE_ORDERS = (LATE_ORDER,) * 3
LATE_STAGES = {3: 2, 5: 3, 6: 4}


def last_kernel(pairs, sizes, late, *refs):
    refs = list(refs)
    take = lambda count: [refs.pop(0) for _ in range(count)]
    given, late_refs = take(11), take(late)
    gain, gain_l, second_gain, query_gain, context_gain = take(5)
    (gs_ref,) = take(1)
    sum_refs = take(3 + late)
    (gain_ref,) = take(1)
    held = take(11)
    dql, dkvl, dqs, dkvs, nl, ns, wq, wk, wv, xs, hs = held
    load_sems, normed, *grads = take(5)
    small_back = take(3)
    here = Here()
    flows = []
    for order in LAST_ORDERS:
        flows.append(Flow(here, order, refs.pop(0), refs, False, True))
    late_flows = [
        Flow(here, order, ref, refs, True, True) for order, ref in zip(LATE_ORDERS, late_refs)
    ]
    state, got, gain_sems = refs
    large, small = sizes
    top, bottom = pl.ds(0, large), pl.ds(large, small)
    loads = [
        pltpu.make_async_copy(source, there, load_sems.at[i])
        for i, (source, there) in enumerate(zip(given, held))
    ]
    here.hail_line("x", "y")
    for load in loads:
        load.start()
    home = Restore(here, *small_back)

    def gain_copy(step):
        return pltpu.make_async_remote_copy(
            src_ref=state.at[step],
            dst_ref=got.at[step],
            send_sem=gain_sems.at[0, step],
            recv_sem=gain_sems.at[1, step],
            device_id=here.partner(GAIN_ORDER[step]),
            device_id_type=MESH,
        )

    for load in loads[:6]:
        load.wait()
    normed[top, :] = nl[...]
    normed[bottom, :] = ns[...]
    for which, flow in enumerate(flows):
        if which == 0:
            grads[0][top, :] = dql[...]
            grads[0][bottom, :] = dqs[...]
        else:
            for pair in range(pairs):
                lanes = pl.ds(pair * LANES, LANES)
                grads[which][top, lanes] = dkvl[pair, which - 1]
                grads[which][bottom, lanes] = dkvs[pair, which - 1]
        value = dot(normed[...], grads[which][...], TN).astype(bf16)
        if which == 0:
            here.heard(9)
            for late_flow in late_flows:
                late_flow.act(0)
        rows, wide = flow.local.shape[1:]
        for at, (core, y, tm) in enumerate(spots(flow.order)):
            first = tm * 2 * rows + core * rows
            flow.local[at] = value[first : first + rows, y * wide : (y + 1) * wide]
        flow.act(0)
    total = None
    for which, weight in enumerate((wq, wk, wv)):
        loads[6 + which].wait()
        part = dot(grads[which][bottom, :], weight[...], NT)
        total = part if total is None else total + part
    for load in loads[9:]:
        load.wait()
    for flow in flows:
        flow.act(1)
    for flow in late_flows:
        flow.act(1)
    extra, gain_s = norm_back(total, xs[...].astype(f32), gain[...])
    small_back[0][...] = (hs[...] + extra).astype(bf16)
    home.start()
    state[0] = jnp.zeros(state.shape[1:], f32)
    for row, value in enumerate(
        (gain_l[...] + gain_s, second_gain[...], query_gain[...], context_gain[...])
    ):
        state[0, row : row + 1, :] = value
    gain_copy(0).start()
    for stage in range(1, 8):
        if stage > 1:
            for flow in flows:
                flow.act(stage)
        if stage in LATE_STAGES:
            for flow in late_flows:
                flow.act(LATE_STAGES[stage])
        if stage <= 5:
            gain_copy(stage - 1).wait()
            total = state[stage - 1] + got[stage - 1]
            if stage < 5:
                state[stage] = total
                gain_copy(stage).start()
            else:
                wide = total.shape[1]
                turned = pltpu.roll(total, lax.rem(wide - here.tm * (wide // 8), wide), 1)
                gain_ref[...] = turned[:, : gain_ref.shape[1]]
    for flow, sum_ref in zip(flows + late_flows, sum_refs):
        sum_ref[...] = flow.result()
    home.finish()
    gs_ref[...] = small_back[1][...]


def last_sums(given, late, gains):
    count, width = given[0].shape
    few = given[2].shape[0]
    block = (width // 16, width // 2)
    shape = jax.ShapeDtypeStruct
    tokens = count + few
    scratch = [pltpu.VMEM(value.shape, value.dtype) for value in given]
    scratch += [pltpu.SemaphoreType.DMA((len(given),))]
    scratch += [pltpu.VMEM((tokens, width), bf16)] * 4
    scratch += restore_scratch(few // 2, width)
    for order in LAST_ORDERS:
        scratch.append(pltpu.VMEM((32,) + block, bf16))
        scratch += flow_scratch(order, block, False, True)
    for order, local in zip(LATE_ORDERS, late):
        scratch += flow_scratch(order, local.shape[1:], True, True)
    scratch += [
        pltpu.VMEM((5, 8, width), f32),
        pltpu.VMEM((5, 8, width), f32),
        pltpu.SemaphoreType.DMA((2, 5)),
    ]
    anywhere = pl.BlockSpec(memory_space=pl.ANY)
    vmem = pl.BlockSpec(memory_space=pltpu.VMEM)
    result = pl.pallas_call(
        functools.partial(last_kernel, width // LANES, (count, few), len(late)),
        in_specs=[anywhere] * (len(given) + len(late)) + [vmem] * 5,
        out_shape=[
            shape((2, few // 2, width), bf16),
        ]
        + [shape((4,) + block, bf16)] * 3
        + [shape((4,) + local.shape[1:], bf16) for local in late]
        + [shape((8, LANES), f32)],
        scratch_shapes=scratch,
        compiler_params=pltpu.CompilerParams(
            vmem_limit_bytes=60 << 20, collective_id=2, has_side_effects=True
        ),
        cost_estimate=pl.CostEstimate(
            flops=40 * tokens * width * width,
            bytes_accessed=40 * tokens * width,
            transcendentals=0,
        ),
        name="last_sums",
    )(*given, *late, *gains)
    return result[0], result[1:4], result[4:-1], result[-1]


def results_kernel(*refs):
    outs, given, sems = refs[12:29], refs[29:41], refs[41]
    loads = [
        pltpu.make_async_copy(source, there, sems.at[i])
        for i, (source, there) in enumerate(zip(refs, given))
    ]
    for load in loads:
        load.start()
    for load in loads:
        load.wait()
    united, large, small, q, k, v, up, down, output, first, other, gains = given
    for source, there in zip((united, large, small), outs[:3]):
        there[...] = source[...].astype(there.dtype)
    for source, there in zip((q, k, v, output), (outs[4], outs[5], outs[6], outs[7])):
        rows, wide = source.shape[1:]
        for at in range(4):
            core, y = at // 2, at % 2
            there[core * rows : (core + 1) * rows, y * wide : (y + 1) * wide] = source[at].astype(f32)
    rows, wide = up.shape[1:]
    for at in range(4):
        outs[9][:, at * wide : (at + 1) * wide] = up[at].astype(f32)
        outs[10][at * rows : (at + 1) * rows, :] = down[at].astype(f32)
        half = rows // 2
        there = slice(at % 2 * half, (at % 2 + 1) * half)
        (outs[16] if at < 2 else outs[13])[there, :] = first[at].astype(f32)
        (outs[14] if at < 2 else outs[15])[there, :] = other[at].astype(f32)
    for row, at in enumerate((3, 8, 11, 12)):
        outs[at][...] = gains[row : row + 1, : outs[at].shape[1]]


def results(united, large, small, last, late, first, other, gains):
    shape = jax.ShapeDtypeStruct
    rows, width = late[0].shape[1:]
    square, vector = shape((rows, width), f32), shape((1, rows), f32)
    given = (united, large, small, *last, *late, first, other, gains)
    out = pl.pallas_call(
        results_kernel,
        in_specs=[pl.BlockSpec(memory_space=pl.ANY)] * len(given),
        scratch_shapes=[pltpu.VMEM(value.shape, value.dtype) for value in given]
        + [pltpu.SemaphoreType.DMA((len(given),))],
        out_shape=[
            shape(united.shape, bf16), shape(large.shape, f32), shape(small.shape, f32), vector,
            square, square, square, square, vector,
            shape((rows, 4 * width), f32), shape((4 * rows, width), f32), vector, vector,
            square, square, square, square,
        ],
        compiler_params=pltpu.CompilerParams(vmem_limit_bytes=60 << 20),
        cost_estimate=pl.CostEstimate(flops=0, bytes_accessed=14 << 20, transcendentals=0),
        name="results",
    )(*given)
    return tuple(value.reshape(rows) if value.shape == (1, rows) else value for value in out)


def cross_kernel(pairs, block, *refs):
    (q_ref, do_ref, o_ref, l_ref, mq_ref, mk_ref), refs = refs[:6], refs[6:]
    kv_ref, given, gains, refs = refs[0], refs[1:11], refs[11:13], refs[13:]
    view_ref, gl_ref, gs_ref, a_ref, b_ref, gain_l_ref, gain_s_ref = refs[:7]
    keys_at, values_at, exchange_refs, refs = refs[7], refs[8], refs[9:15], refs[15:]
    dkv, dq, dk, dv = refs[:4]
    held, sems, home_refs = refs[4:14], refs[14], refs[15:18]
    united, wo, merged_l, asked, context, grad_out, merged_s, wq, wk, wv = held
    here = Here()
    exchange = Exchange(here, keys_at.shape[0] // 4, exchange_refs)
    step = pl.program_id(0)
    loads = [
        pltpu.make_async_copy(source, there, sems.at[i])
        for i, (source, there) in enumerate(zip(given, held))
    ]

    @pl.when(step == 0)
    def _():
        here.hail_line("x")
        for load in loads:
            load.start()

    def before():
        @pl.when(step == 0)
        def _():
            here.heard(8)

    exchange.before = before
    home = Restore(here, *home_refs)

    fill_keys(keys_at, values_at, kv_ref)

    @pl.when(step >= 2)
    def _():
        exchange.free(step - 2)

    dq[step] = pair_back(
        q_ref[0], do_ref[...], o_ref[0], l_ref[0], mq_ref[...], keys_at, values_at, mk_ref,
        block, exchange, step,
    )

    @pl.when(step == 1)
    def _():
        for load in loads[:3]:
            load.wait()
        wide = jnp.concatenate([united[i] for i in range(pairs)], axis=1)
        home_refs[0][...] = (merged_l[...] + dot(wide, wo[...])).astype(bf16)
        home.start()

    @pl.when(step >= 3)
    def _():
        exchange.take(step - 3, dkv)

    def lay(out_ref, which, value, order):
        left = 32 // out_ref.shape[0]
        rows = out_ref.shape[1] // left
        for at, (core, y, tm) in enumerate(spots(order)):
            if core == which:
                first, there = (tm * 2 + y) * rows, at % left * rows
                out_ref[at // left, there : there + rows, :] = value[first : first + rows]

    @pl.when(step == pairs - 1)
    def _():
        for load in loads[3:]:
            load.wait()
        grads = jnp.concatenate([united[i] for i in range(pairs)], axis=1)
        lay(a_ref, 0, dot(grads, grad_out[...], TN).astype(bf16), BY_Y)
        grads = jnp.concatenate([dq[i] for i in range(pairs)], axis=1)
        lay(a_ref, 1, dot(asked[...], grads, TN).astype(bf16), BY_Y)
        extra, gain_l_ref[...] = norm_back(dot(grads, wq[...], NT), merged_l[...], gains[0][...])
        gl_ref[...] = grad_out[...].astype(f32) + extra
        for pair in range(pairs - 3, pairs):
            exchange.take(pair, dkv)
        for pair in range(pairs):
            lanes = pl.ds(pair * LANES, LANES)
            dk[:, lanes] = dkv[pair, 0]
            dv[:, lanes] = dkv[pair, 1]
        lay(b_ref, 0, dot(context[...], dk[...], TN).astype(bf16), BY_ZL)
        lay(b_ref, 1, dot(context[...], dv[...], TN).astype(bf16), BY_ZL)
        grad = dot(dk[...], wk[...], NT) + dot(dv[...], wv[...], NT)
        gs_ref[...], gain_s_ref[...] = norm_back(grad, merged_s[...], gains[1][...])
        exchange.end()
        home.finish()
        view_ref[...] = home_refs[1][...]


def cross_back(attention, kv, given, gains):
    count, width = attention[1].shape
    few = kv.shape[3]
    major = pl.BlockSpec((1, count, LANES), lambda i: (i, 0, 0))
    pairs = width // LANES
    total = attention[5].shape[0]
    block = largest_block(total // 2, 512)
    shape = jax.ShapeDtypeStruct
    laid = (4, 8 * width // 16, width)
    return pl.pallas_call(
        functools.partial(cross_kernel, pairs, block),
        grid=(pairs,),
        in_specs=[major, columns(count, 0), major, major]
        + [whole((count, LANES)), whole((total, LANES))]
        + [pl.BlockSpec((4, 1, 2, few, LANES), lambda i: (0, i, 0, 0, 0))]
        + [pl.BlockSpec(memory_space=pl.ANY)] * len(given)
        + [whole((1, width))] * 2,
        out_specs=[
            whole((2, count // 2, width)), whole((count, width)), whole((few, width)), whole(laid), whole(laid),
            whole((1, width)), whole((1, width)),
        ],
        out_shape=[
            shape((2, count // 2, width), bf16),
            shape((count, width), f32), shape((few, width), f32), shape(laid, bf16), shape(laid, bf16),
            shape((1, width), f32), shape((1, width), f32),
        ],
        scratch_shapes=[pltpu.VMEM((total, LANES), bf16)] * 2
        + exchange_scratch(pairs, few)
        + [pltpu.VMEM((pairs, 2, few, LANES), bf16), pltpu.VMEM((pairs, count, LANES), bf16)]
        + [pltpu.VMEM((few, width), bf16)] * 2
        + [pltpu.VMEM(value.shape, value.dtype) for value in given]
        + [pltpu.SemaphoreType.DMA((len(given),))]
        + restore_scratch(count // 2, width),
        compiler_params=pltpu.CompilerParams(
            vmem_limit_bytes=60 << 20, collective_id=3, has_side_effects=True
        ),
        cost_estimate=pl.CostEstimate(
            flops=20 * width * count * total,
            bytes_accessed=64 * count * width,
            transcendentals=count * total * width // HALF,
        ),
        name="cross_back",
    )(*attention, kv, *given, *gains)


def attend_pair(pair, q_ref, kv, mq_ref, mk_ref, spaces, o_ref, l_ref):
    parts, rows = kv.shape[0], kv.shape[3]
    total = parts * rows
    ka0, ka1, va0, va1 = (space.at[pl.ds(0, total), :] for space in spaces)
    low = lax.broadcasted_iota(jnp.int32, (rows, LANES), 1) < HALF
    for part in range(parts):
        here = pl.ds(part * rows, rows)
        keys, values, mask = kv[part, pair, 0], kv[part, pair, 1], mk_ref[here, :]
        one = jnp.ones_like(values)
        ka0[here, :] = jnp.where(low, keys, mask)
        ka1[here, :] = jnp.where(low, mask, keys)
        va0[here, :] = jnp.where(low, values, one)
        va1[here, :] = jnp.where(low, one, values)
    count = q_ref.shape[1]
    block = largest_block(count, 256 if total > 1024 else 512)
    low = lax.broadcasted_iota(jnp.int32, (block, LANES), 1) < HALF
    for number in range(count // block):
        here = pl.ds(number * block, block)
        query, mask = q_ref[pair, here, :], mq_ref[here, :]
        tops, sums = [], []
        for head, keys, values in ((0, ka0, va0), (1, ka1, va1)):
            mine = jnp.where(low, query, mask) if head == 0 else jnp.where(low, mask, query)
            score = dot(mine, keys[...], NT)
            top = jnp.max(score, axis=1, keepdims=True)
            weight = jnp.exp2(score - top).astype(bf16)
            sums.append(dot(weight, values[...]))
            tops.append(jnp.broadcast_to(top, (block, LANES)))
        total = jnp.where(low, sums[1], sums[0])
        top = jnp.where(low, tops[1], tops[0])
        out = jnp.where(low, sums[0], sums[1])
        o_ref[pair, here, :] = (out / pltpu.roll(total, HALF, 1)).astype(bf16)
        l_ref[pair, here, :] = top + jnp.log2(total)


class Gather:
    def __init__(self, here, kv, sems):
        self.here, self.kv, self.sems = here, kv, sems

    def copy(self, kind, at, size, sem):
        source, there = ((0, 1), (0, 2), (1, 3))[kind]
        pairs = pl.ds(at, size)
        return pltpu.make_async_remote_copy(
            src_ref=self.kv.at[source, pairs],
            dst_ref=self.kv.at[there, pairs],
            send_sem=self.sems.at[0, 3 * sem + kind],
            recv_sem=self.sems.at[1, 3 * sem + kind],
            device_id=self.here.partner(("x", "core", "core")[kind]),
            device_id_type=MESH,
        )


def begin_kernel(pairs, *refs):
    refs = list(refs)
    take = lambda count: [refs.pop(0) for _ in range(count)]
    large_ref, small_ref, cot_ref, clip_ref = take(4)
    weight_refs = take(9)
    (gains,) = take(1)
    first_gain, second_gain, query_gain, context_gain = (
        gains.at[i : i + 1, :] for i in range(4)
    )
    xl_out, xs_out, cot_out, kvl_out, kvs_out, ckv_out = take(6)
    nl_ref, ns_ref, ql_ref, qs_ref, ol_ref, ll_ref, os_ref, ls_ref = take(8)
    merged_ref, hidden_ref, second_ref, active_ref, slope_ref, context_ref = take(6)
    mql_ref, mkl_ref, mqs_ref, mks_ref = take(4)
    for gain, gain_out in zip((first_gain, second_gain, query_gain, context_gain), take(4)):
        gain_out[...] = gain[...]
    (grad_ref,) = take(1)
    xl, xs, cot, clip, kvl, kvs, ckv = take(7)
    wq, wk, wv, wo, up, down, wck, wcv, wco = weights = take(9)
    spaces = take(4)
    wide, total = take(2)
    move_sems, gather_l, gather_s, gather_c, gather_clip, load_sems, out_sems = take(7)
    near_l, near_s, near_c, x_sems = take(4)
    here = Here()
    z, core = here.tm // 2, here.bit["core"]
    stay = core == z // 2

    here.hail_line("x")

    odd = lax.rem(z, 2)
    from_seq = (odd, 1 - odd)

    def far(which, turn, source, there):
        rows = source.shape[1]
        place = (
            (2 * core + from_seq[turn]) * 2 + here.bit["x"],
            here.bit["y"] * 2 + z // 2,
        )
        return pltpu.make_async_remote_copy(
            src_ref=source.at[from_seq[turn]],
            dst_ref=there.at[pl.ds(turn * rows, rows)],
            send_sem=move_sems.at[0, 2 * which + turn],
            recv_sem=move_sems.at[1, 2 * which + turn],
            device_id=place,
            device_id_type=MESH,
        )

    def near(which, source, there):
        return pltpu.make_async_copy(
            source.at[from_seq[0]],
            there.at[pl.ds(0, source.shape[1])],
            move_sems.at[1, 2 * which],
        )

    def move(which, source, there):
        far(which, 1, source, there).start()

        @pl.when(stay)
        def _():
            near(which, source, there).start()

        @pl.when(jnp.logical_not(stay))
        def _():
            far(which, 0, source, there).start()

    def moved_out(which, source, there):
        far(which, 1, source, there).wait_send()

        @pl.when(jnp.logical_not(stay))
        def _():
            far(which, 0, source, there).wait_send()

    def moved_in(which, source, there):
        far(which, 1, source, there).wait_recv()

        @pl.when(stay)
        def _():
            near(which, source, there).wait()

        @pl.when(jnp.logical_not(stay))
        def _():
            far(which, 0, source, there).wait_recv()

    moves = ((0, clip_ref, clip.at[0, 0]), (1, small_ref, xs), (2, large_ref, xl), (3, cot_ref, cot))
    here.heard(8)
    move(*moves[0])
    move(*moves[1])
    loads = [
        pltpu.make_async_copy(source, there, load_sems.at[i])
        for i, (source, there) in enumerate(zip(weight_refs, weights))
    ]
    for load in loads:
        load.start()
    moved_out(*moves[0])
    moved_out(*moves[1])
    move(*moves[2])
    outs = []

    def keep(source, there):
        copy = pltpu.make_async_copy(source, there, out_sems.at[len(outs)])
        copy.start()
        outs.append(copy)

    def split(kv, part, value, key_weight, value_weight):
        keys = dot(value, key_weight[...]).astype(bf16)
        values = dot(value, value_weight[...]).astype(bf16)
        for pair in range(pairs):
            lanes = slice(pair * LANES, (pair + 1) * LANES)
            kv[part, pair, 0] = keys[:, lanes]
            kv[part, pair, 1] = values[:, lanes]

    def to_x(which, source, there):
        return pltpu.make_async_remote_copy(
            src_ref=source,
            dst_ref=there,
            send_sem=x_sems.at[0, which],
            recv_sem=x_sems.at[1, which],
            device_id=here.partner("x"),
            device_id_type=MESH,
        )

    x_small, x_large, x_cross = (
        to_x(0, ns_ref, near_s), to_x(1, nl_ref, near_l), to_x(2, context_ref, near_c)
    )

    def query_into(n_ref, q_ref):
        query = (dot(n_ref[...], wq[...]) * Q_SCALE).astype(bf16)
        for pair in range(pairs):
            q_ref[pair] = query[:, pair * LANES : (pair + 1) * LANES]

    large, small = Gather(here, kvl, gather_l), Gather(here, kvs, gather_s)
    cross, clips = Gather(here, ckv, gather_c), Gather(here, clip, gather_clip)

    moved_in(*moves[0])
    for kind in (0, 1):
        clips.copy(kind, 0, 1, 0).start()
    moved_in(*moves[1])
    keep(xs, xs_out)
    ns_ref[...] = norm(xs[...].astype(f32), first_gain[...])
    x_small.start()
    for i in (0, 1, 2):
        loads[i].wait()
    split(kvs, 0, ns_ref[...], wk, wv)
    small.copy(1, 0, pairs, 0).start()
    query_into(ns_ref, qs_ref)
    clips.copy(0, 0, 1, 0).wait_recv()
    clips.copy(2, 0, 1, 0).start()
    for kind in (1, 2):
        clips.copy(kind, 0, 1, 0).wait_recv()

    few = clip.shape[2]
    spot = lax.broadcasted_iota(jnp.int32, (1, LANES), 1) % HALF
    number = spot.astype(f32)
    some = spot < 4
    row = lax.broadcasted_iota(jnp.int32, (2 * few, few), 0) // 2
    twice = jnp.where(row == lax.broadcasted_iota(jnp.int32, (2 * few, few), 1), 1.0, 0.0)
    twice = twice.astype(bf16)
    for part in range(4):
        mine = clip[part, 0]
        for value, mk_ref, mq_ref in (
            (mine.astype(f32), mks_ref, mqs_ref),
            (dot(twice, mine), mkl_ref, mql_ref),
        ):
            rows = value.shape[0]
            mk_ref[pl.ds(part * rows, rows), :] = jnp.where(
                some & (value != number), NEGATIVE, 0.0
            ).astype(bf16)
            if part == 0:
                mq_ref[...] = jnp.where(some & (value == number), 1.0, 0.0).astype(bf16)

    x_small.wait_recv()
    split(kvs, 1, near_s[...], wk, wv)
    small.copy(2, 0, pairs, 0).start()
    moved_in(*moves[2])
    moved_out(*moves[2])
    move(*moves[3])
    keep(xl, xl_out)
    nl_ref[...] = norm(xl[...].astype(f32), first_gain[...])
    x_large.start()
    split(kvl, 0, nl_ref[...], wk, wv)
    large.copy(1, 0, pairs, 0).start()
    query_into(nl_ref, ql_ref)

    small.copy(1, 0, pairs, 0).wait_recv()
    small.copy(2, 0, pairs, 0).wait_recv()
    keep(kvs, kvs_out)

    def small_pair(pair, carry):
        attend_pair(pair, qs_ref, kvs, mqs_ref, mks_ref, spaces, os_ref, ls_ref)
        return carry

    lax.fori_loop(0, pairs, small_pair, 0)
    loads[3].wait()
    for pair in range(pairs):
        wide[:, pair * LANES : (pair + 1) * LANES] = os_ref[pair]
    hidden = xs[...].astype(f32) + dot(wide[...], wo[...])
    hidden_ref[...] = hidden
    second_ref[...] = norm(hidden, second_gain[...])
    total[...] = hidden
    loads[4].wait()
    loads[5].wait()
    width = wide.shape[1]
    steps = up.shape[1] // width
    for step in range(steps):
        lanes = slice(step * width, (step + 1) * width)
        active, slope = gelu_both(dot(second_ref[...], up[:, lanes]))
        active = active.astype(bf16)
        active_ref[:, lanes] = active
        slope_ref[:, lanes] = slope.astype(bf16)
        total[...] += dot(active, down[lanes, :])
    merged = total[...]
    merged_ref[...] = merged
    context = norm(merged, context_gain[...])
    context_ref[...] = context
    x_cross.start()
    x_large.wait_recv()
    split(kvl, 1, near_l[...], wk, wv)
    large.copy(2, 0, pairs, 0).start()
    loads[6].wait()
    loads[7].wait()
    split(ckv, 0, context, wck, wcv)
    cross.copy(1, 0, pairs, 0).start()

    def large_pair(pair, carry):
        attend_pair(pair, ql_ref, kvl, mql_ref, mkl_ref, spaces, ol_ref, ll_ref)
        return carry

    large.copy(1, 0, pairs, 0).wait_recv()
    large.copy(2, 0, pairs, 0).wait_recv()
    keep(kvl, kvl_out)
    lax.fori_loop(0, pairs // 2, large_pair, 0)
    x_cross.wait_recv()
    split(ckv, 1, near_c[...], wck, wcv)
    cross.copy(2, 0, pairs, 0).start()
    moved_in(*moves[3])
    moved_out(*moves[3])
    keep(cot, cot_out)
    loads[8].wait()
    grad_ref[...] = dot(cot[...], wco[...], NT).astype(bf16)
    lax.fori_loop(pairs // 2, pairs, large_pair, 0)
    cross.copy(1, 0, pairs, 0).wait_recv()
    cross.copy(2, 0, pairs, 0).wait_recv()
    keep(ckv, ckv_out)
    for kind in (0, 1, 2):
        clips.copy(kind, 0, 1, 0).wait_send()
        if kind:
            for gathered in (small, large, cross):
                gathered.copy(kind, 0, pairs, 0).wait_send()
    for copy in (x_small, x_large, x_cross):
        copy.wait_send()
    for copy in outs:
        copy.wait()


def begin(large, small, cotangent, clip, weights, gains):
    seqs, count, width = large.shape
    few = small.shape[1]
    count, few = 2 * count, 2 * few
    pairs = width // LANES
    hidden = weights[4].shape[1]
    shape = jax.ShapeDtypeStruct
    kv_l, kv_s = (4, pairs, 2, count, LANES), (4, pairs, 2, few, LANES)
    anywhere = pl.BlockSpec(memory_space=pl.ANY)
    vmem = pl.BlockSpec(memory_space=pltpu.VMEM)
    out_shape = [
        shape((count, width), bf16),
        shape((few, width), bf16),
        shape((count, width), bf16),
        shape(kv_l, bf16),
        shape(kv_s, bf16),
        shape(kv_s, bf16),
        shape((count, width), bf16),
        shape((few, width), bf16),
        shape((pairs, count, LANES), bf16),
        shape((pairs, few, LANES), bf16),
        shape((pairs, count, LANES), bf16),
        shape((pairs, count, LANES), f32),
        shape((pairs, few, LANES), bf16),
        shape((pairs, few, LANES), f32),
        shape((few, width), f32),
        shape((few, width), f32),
        shape((few, width), bf16),
        shape((few, hidden), bf16),
        shape((few, hidden), bf16),
        shape((few, width), bf16),
        shape((count, LANES), bf16),
        shape((4 * count, LANES), bf16),
        shape((few, LANES), bf16),
        shape((4 * few, LANES), bf16),
        *[shape((1, width), f32)] * 4,
        shape((count, width), bf16),
    ]
    dma = pltpu.SemaphoreType.DMA
    scratch = [
        pltpu.VMEM((count, width), bf16),
        pltpu.VMEM((few, width), bf16),
        pltpu.VMEM((count, width), bf16),
        pltpu.VMEM((4, 1, few, LANES), bf16),
        pltpu.VMEM(kv_l, bf16),
        pltpu.VMEM(kv_s, bf16),
        pltpu.VMEM(kv_s, bf16),
    ]
    scratch += [pltpu.VMEM(weight.shape, bf16) for weight in weights]
    scratch += [pltpu.VMEM((4 * count, LANES), bf16)] * 4
    scratch += [pltpu.VMEM((few, width), bf16), pltpu.VMEM((few, width), f32)]
    scratch += [dma((2, 8))] + [dma((2, 3))] * 4 + [dma((9,)), dma((6,))]
    scratch += [
        pltpu.VMEM((count, width), bf16),
        pltpu.VMEM((few, width), bf16),
        pltpu.VMEM((few, width), bf16),
        dma((2, 3)),
    ]
    return pl.pallas_call(
        functools.partial(begin_kernel, pairs),
        in_specs=[anywhere] * 13 + [vmem],
        out_specs=[anywhere] * 6 + [vmem] * 23,
        out_shape=out_shape,
        scratch_shapes=scratch,
        compiler_params=pltpu.CompilerParams(
            vmem_limit_bytes=62 << 20, collective_id=4, has_side_effects=True
        ),
        cost_estimate=pl.CostEstimate(
            flops=16 * count * 4 * count * width + 18 * few * width * hidden,
            bytes_accessed=40 << 20,
            transcendentals=count * count * 4 * width // HALF,
        ),
        name="begin",
    )(large, small, cotangent, clip, *weights, gains)


def cross_attend_kernel(q_ref, kv_ref, mq_ref, mk_ref, o_ref, l_ref, *spaces):
    attend_pair(0, q_ref, kv_ref, mq_ref, mk_ref, spaces, o_ref, l_ref)


def cross_attend(query, kv, mask_q, mask_k):
    pairs, count = query.shape[:2]
    rows = kv.shape[3]
    one = pl.BlockSpec((1, count, LANES), lambda i: (i, 0, 0))
    return pl.pallas_call(
        cross_attend_kernel,
        grid=(pairs,),
        in_specs=[
            one,
            pl.BlockSpec((4, 1, 2, rows, LANES), lambda i: (0, i, 0, 0, 0)),
            whole((count, LANES)),
            whole((4 * rows, LANES)),
        ],
        out_specs=[one, one],
        out_shape=[
            jax.ShapeDtypeStruct(query.shape, bf16),
            jax.ShapeDtypeStruct(query.shape, f32),
        ],
        scratch_shapes=[pltpu.VMEM((4 * rows, LANES), bf16)] * 4,
        compiler_params=pltpu.CompilerParams(vmem_limit_bytes=62 << 20),
        cost_estimate=pl.CostEstimate(
            flops=64 * count * rows * pairs * LANES,
            bytes_accessed=32 * count * pairs * LANES,
            transcendentals=8 * count * rows * pairs,
        ),
        name="cross_attend",
    )(query, kv, mask_q, mask_k)


def after(value, *needed):
    return lax.optimization_barrier((value, needed))[0]


CROSS_ORDERS = (BY_Y[:2], BY_ZL[:2])
SELVES_ORDERS = (BY_Y[:3], BY_ZL[:3], BY_Y[:3], BY_Y[2:], BY_ZL[2:])
SELVES_ENDS = (False, False, False, True, True)
SELVES_STAGES = (
    (0, 4, 11),
    (0, 4, 11),
    (0, 6, 11),
    (1, 3, 6, 8, 10),
    (1, 3, 6, 8, 10),
)


def paired_end(views, normed, large, small, cross, merged, weights, crosses, gains):
    large_view, small_view = views
    large_normed, small_normed, asked, context = normed
    large_q, large_mixed, large_logsum, large_mask_q, large_mask_k, large_kv = large
    small_q, small_mixed, small_logsum, small_mask_q, small_mask_k, small_kv = small
    cross_q, united, cross_logsum, cross_kv, united_grad, grad_out = cross
    large_merged, large_saved, small_merged, small_saved = merged
    query_weight, key_weight, value_weight, output_weight, up_weight, down_weight = weights
    first_gain, second_gain, query_gain, context_gain = gains
    width = large_view.shape[1]
    rows = width // 8
    (
        united_view, large_grad, small_grad, first, other, query_gain_grad, context_gain_grad,
    ) = cross_back(
        (cross_q, united_grad, united, cross_logsum, large_mask_q, small_mask_k),
        cross_kv,
        (united, crosses[3], large_merged, asked, context, grad_out, small_merged) + crosses[:3],
        (query_gain, context_gain),
    )
    (
        large_hidden, small_hidden, large_mixed_grad, small_mixed_grad, up_grad, down_grad,
        output_grad, second_gain_grad, first, other,
    ) = back(
        large_grad, small_grad, large_saved, small_saved, [large_mixed], small_mixed, output_weight,
        second_gain, up_weight, down_weight, True, (first, other), CROSS_ORDERS,
    )
    still = (8, rows // 2, width)
    selves, (large_grad, large_gain), sums = selves_back(
        (large_q, large_mixed_grad, large_mixed, large_logsum, large_mask_q, large_mask_k),
        large_kv,
        (small_q, small_mixed_grad, small_mixed, small_logsum, small_mask_q, small_mask_k),
        small_kv,
        (
            up_grad.reshape(8, 4 * rows, width), down_grad.reshape(8, 4 * rows, width),
            output_grad.reshape(8, 2 * rows, width // 2),
            first.reshape(still), other.reshape(still),
        ),
        (query_weight, key_weight, value_weight, large_hidden, large_view), first_gain,
        SELVES_ORDERS, SELVES_ENDS, SELVES_STAGES,
    )
    up, down, output, first, other = sums
    small_grad, last, late, gains = last_sums(
        tuple(selves) + (large_normed, small_normed, query_weight, key_weight, value_weight)
        + (small_view, small_hidden),
        (
            up.reshape(4, rows, width), down.reshape(4, rows, width),
            output.reshape(4, rows // 2, width // 2),
        ),
        (first_gain, large_gain, second_gain_grad, query_gain_grad, context_gain_grad),
    )
    return results(united_view, large_grad, small_grad, last, late, first, other, gains)


def per_device(tm, seq_size, *args):
    (
        large_view,
        small_view,
        clip_ids,
        first_gain,
        query_weight,
        key_weight,
        value_weight,
        output_weight,
        second_gain,
        up_weight,
        down_weight,
        query_gain,
        context_gain,
        cross_query,
        cross_key,
        cross_value,
        cross_output,
        cotangent,
    ) = args
    seqs, count, width = large_view.shape
    side = tm // 4
    gains = jnp.concatenate((first_gain, second_gain, query_gain, context_gain))
    gains = gains.astype(f32).reshape(4, width)
    first_gain, second_gain, query_gain, context_gain = (gains[i : i + 1] for i in range(4))

    tm_at = lax.axis_index("tm")
    seq_at = lax.axis_index("seq")
    z, x = tm_at // side, tm_at % side
    y, core = seq_at // 2, seq_at % 2
    places = [
        (pz, px, py, pc)
        for pz in range(4)
        for px in range(side)
        for py in range(2)
        for pc in range(2)
    ]

    def number(place):
        return (place[0] * side + place[1]) * seq_size + place[2] * 2 + place[3]

    def permute(value, place):
        pairs = [(number(at), number(place(*at))) for at in places]
        return lax.ppermute(value, ("tm", "seq"), pairs)

    def inverse(place):
        table = {place(*at): at for at in places}
        return lambda *at: table[at]

    go = (
        lambda z, x, y, c: (2 * c + z % 2, x, y, z // 2),
        lambda z, x, y, c: (2 * c + 1 - z % 2, x, y, z // 2),
    )
    back_home = tuple(inverse(place) for place in go)
    other_core = lambda value: permute(value, lambda z, x, y, c: (z, x, y, 1 - c))
    other_y = lambda value: permute(value, lambda z, x, y, c: (z, x, 1 - y, c))
    by_x = lambda value, d: permute(value, lambda z, x, y, c: (z, (x + d) % side, y, c))
    odd = z % 2 == 1

    def relocate(value):
        near = jnp.where(odd, value[1], value[0])
        far = jnp.where(odd, value[0], value[1])
        return jnp.concatenate([permute(near, go[0]), permute(far, go[1])], axis=0)

    def restore(value):
        rows = value.shape[0] // 2
        near, far = permute(value[:rows], back_home[0]), permute(value[rows:], back_home[1])
        return jnp.where(odd, jnp.stack([far, near]), jnp.stack([near, far]))

    def join(parts, axis):
        return parts[0] if len(parts) == 1 else jnp.concatenate(parts, axis=axis)

    def gather(value, axis=1):
        across = join([by_x(value, d) for d in range(1, side)], axis)
        return (value, across, other_core(value), other_core(across))

    def add(a, b):
        return (a.astype(f32) + b.astype(f32)).astype(bf16)

    def scatter_core(keep, send):
        return add(keep, other_core(send))

    def scatter_x(sums):
        rows = sums.shape[1] // side
        total = sums[:, :rows].astype(f32)
        for d in range(1, side):
            total = total + by_x(sums[:, d * rows : (d + 1) * rows], -d).astype(f32)
        return total.astype(bf16)

    if side == 2:
        clip = jnp.broadcast_to(
            clip_ids[:, ::2].astype(bf16)[:, :, None], (seqs, count // 2, LANES)
        )
        (
            large, small, grad_out, large_kv, small_kv, cross_kv, large_normed, small_normed,
            large_q, small_q, large_mixed, large_logsum, small_mixed, small_logsum, small_merged,
            *small_saved, context, large_mask_q, large_mask_k, small_mask_q, small_mask_k,
            first_gain, second_gain, query_gain, context_gain, united_grad,
        ) = begin(
            large_view, small_view, cotangent, clip,
            (query_weight, key_weight, value_weight, output_weight, up_weight, down_weight,
             cross_key, cross_value, cross_output),
            gains,
        )
        large_merged, *large_saved, asked, cross_q = rest(
            large, [large_mixed], output_weight, second_gain, up_weight, down_weight,
            query_gain, (cross_query,),
        )
        united, cross_logsum = cross_attend(cross_q, cross_kv, large_mask_q, small_mask_k)
        return paired_end(
            (large, small),
            (large_normed, small_normed, asked, context),
            (large_q, large_mixed, large_logsum, large_mask_q, large_mask_k, large_kv),
            (small_q, small_mixed, small_logsum, small_mask_q, small_mask_k, small_kv),
            (cross_q, united, cross_logsum, cross_kv, united_grad, grad_out),
            (large_merged, large_saved, small_merged, small_saved),
            (query_weight, key_weight, value_weight, output_weight, up_weight, down_weight),
            (cross_query, cross_key, cross_value, cross_output),
            (first_gain, second_gain, query_gain, context_gain),
        )

    groups = 3
    part = width // groups
    short_clips = gather(relocate(clip_ids[:, ::2].astype(f32)), 0)
    small = relocate(small_view)
    large = relocate(large_view)
    grad_out = relocate(after(cotangent, large))
    spot = lax.broadcasted_iota(jnp.int32, (1, LANES), 1) % HALF

    def mask_of_keys(numbers):
        away = numbers.astype(jnp.int32)[:, None] != spot
        return jnp.where((spot < 4) & away, NEGATIVE, 0.0).astype(bf16)

    def mask_of_queries(numbers):
        same = numbers.astype(jnp.int32)[:, None] == spot
        return jnp.where((spot < 4) & same, 1.0, 0.0).astype(bf16)

    short = jnp.concatenate(short_clips)
    small_mask_k = mask_of_keys(short)
    large_mask_k = mask_of_keys(jnp.repeat(short, 2))
    small_mask_q = mask_of_queries(short_clips[0])
    large_mask_q = mask_of_queries(jnp.repeat(short_clips[0], 2))

    small_normed, small_q, small_kv = front(
        small, first_gain, query_weight, key_weight, value_weight, 1
    )
    small_kv = gather(small_kv[0])
    large_normed, large_q, large_kv = front(
        large, first_gain, query_weight, key_weight, value_weight, groups
    )
    large_kv = [gather(kv) for kv in large_kv]
    small_mixed, small_logsum = attend(small_q, small_kv, small_mask_q, small_mask_k, 0, width)
    small_merged, *small_saved, context, cross_kv = rest(
        small, [small_mixed], output_weight, second_gain, up_weight, down_weight,
        context_gain, (cross_key, cross_value),
    )
    cross_kv = gather(cross_kv)
    united_grad = dot(grad_out, cross_output, NT).astype(bf16)
    large_out = ()
    for group, kv in enumerate(large_kv):
        large_out = attend(large_q, kv, large_mask_q, large_mask_k, group * part, part, large_out)
    large_mixed, large_logsum = large_out
    large_merged, *large_saved, asked, cross_q = rest(
        large, [large_mixed], output_weight, second_gain, up_weight, down_weight,
        query_gain, (cross_query,),
    )
    united, cross_logsum = attend(cross_q, cross_kv, large_mask_q, small_mask_k, 0, width)
    united_view = restore((large_merged + dot(united, cross_output)).astype(bf16))

    bits = side.bit_length() - 1
    moves = {"zh": lambda z, x, y, c: (z ^ 2, x, y, c), "zl": lambda z, x, y, c: (z ^ 1, x, y, c)}
    mine = {"zh": z // 2, "zl": z % 2}
    axes = {"zh": 0, "zl": 1}
    for bit in range(bits):
        flip = 1 << (bits - 1 - bit)
        moves[f"x{bit}"] = lambda z, x, y, c, flip=flip: (z, x ^ flip, y, c)
        mine[f"x{bit}"] = (x // flip) % 2
        axes[f"x{bit}"] = 2 + bit
    moves["core"] = lambda z, x, y, c: (z, x, y, 1 - c)
    moves["y"] = lambda z, x, y, c: (z, x, 1 - y, c)
    mine["core"], mine["y"] = core, y
    axes["core"], axes["y"] = 2 + bits, 3 + bits
    by_y = ["core", "y", "zl"] + [f"x{bit}" for bit in range(bits)] + ["zh"]
    by_zl = ["core", "zl", "y"] + [f"x{bit}" for bit in range(bits)] + ["zh"]
    by_yx = ["core", "y"] + [f"x{bit}" for bit in range(bits)] + ["zl", "zh"]

    class Sum:
        def __init__(self, local, order):
            rows, wide = local.shape
            self.value = local.reshape((2,) * (2 + bits) + (rows // tm, wide))
            self.todo = list(order)
            self.rows, self.wide = rows // tm, wide

        def step(self, *needed):
            name = self.todo.pop(0)
            axis = axes[name]
            size = self.value.shape[axis] // 2
            at = mine[name]
            keep = lax.dynamic_slice_in_dim(self.value, at * size, size, axis)
            send = lax.dynamic_slice_in_dim(self.value, (1 - at) * size, size, axis)
            self.value = add(keep, permute(send, moves[name]))
            return self.value

        def finish(self):
            while self.todo:
                self.step()
            value = self.value.reshape(self.rows // 2, self.wide // 2)
            other = other_y(value)
            value = jnp.where(
                y == 0,
                jnp.concatenate([value, other], axis=1),
                jnp.concatenate([other, value], axis=1),
            )
            other = other_core(value)
            return jnp.where(
                core == 0,
                jnp.concatenate([value, other], axis=0),
                jnp.concatenate([other, value], axis=0),
            ).astype(f32)

    cross_groups = 2
    cross_part = width // cross_groups
    dcq, dckv = [], []
    for group in range(cross_groups):
        query = after(cross_q, *dcq[-1:])
        at = group * cross_part
        dq, keep, send = attend_back(
            query, cross_kv, united_grad, united, cross_logsum,
            large_mask_q, small_mask_k, at, at, at, cross_part,
        )
        dcq.append(dq)
        dckv.append(scatter_x(scatter_core(keep, send)))
    dcq = jnp.concatenate(dcq, axis=1)
    dck = jnp.concatenate([kv[0] for kv in dckv], axis=1)
    dcv = jnp.concatenate([kv[1] for kv in dckv], axis=1)
    extra, query_gain_grad = norm_back(dot(dcq, cross_query, NT), large_merged, query_gain)
    large_merged_grad = grad_out.astype(f32) + extra
    small_merged_grad, context_gain_grad = norm_back(
        dot(dck, cross_key, NT) + dot(dcv, cross_value, NT), small_merged, context_gain
    )
    cross_parts = [
        dot(united, grad_out, TN).astype(bf16),
        dot(asked, dcq, TN).astype(bf16),
        dot(context, dck, TN).astype(bf16),
        dot(context, dcv, TN).astype(bf16),
    ]
    (
        large_hidden_grad,
        small_hidden_grad,
        large_mixed_grad,
        small_mixed_grad,
        up_grad,
        down_grad,
        output_grad,
        second_gain_grad,
    ) = back(
        large_merged_grad, small_merged_grad, large_saved, small_saved, [large_mixed], small_mixed,
        output_weight, second_gain, up_weight, down_weight, False,
    )
    cross_sum = Sum(jnp.concatenate(cross_parts, axis=1), by_y)
    up_sum = Sum(up_grad, by_y)
    down_sum = Sum(down_grad, by_zl)
    cross_sum.step()
    small_dq, keep, send = attend_back(
        after(small_q, cross_sum.value), small_kv, small_mixed_grad, small_mixed, small_logsum,
        small_mask_q, small_mask_k, 0, 0, 0, width,
    )
    small_sums = scatter_core(keep, send)
    up_sum.step()
    down_sum.step()
    cross_sum.step()
    needed = [small_dq, up_sum.value, down_sum.value]
    normed = jnp.concatenate([large_normed, small_normed], axis=0)
    last_sums, dqs, dkvs = [], [], []
    pending = None
    for group in range(groups):
        at = group * part
        dq, keep, send = attend_back(
            after(large_q, *needed), large_kv[group], large_mixed_grad, large_mixed, large_logsum,
            large_mask_q, large_mask_k, at, at, 0, part,
        )
        sums = scatter_core(keep, send)
        dqs.append(dq)
        needed = [dq]
        if group == 0:
            small_dkv = scatter_x(small_sums)
            needed += [cross_sum.value, small_sums]
        if group == 1:
            needed += [small_dkv, up_sum.step(), down_sum.step(), cross_sum.step()]
        if pending is not None:
            needed.append(pending.step())
        dkv = scatter_x(sums)
        dkvs.append(dkv)
        local = jnp.concatenate(
            [
                jnp.concatenate([dq, dkv[0], dkv[1]], axis=1),
                jnp.concatenate(
                    [
                        small_dq[:, at : at + part],
                        small_dkv[0, :, at : at + part],
                        small_dkv[1, :, at : at + part],
                    ],
                    axis=1,
                ),
            ],
            axis=0,
        )
        local = dot(normed, local, TN).astype(bf16)
        pending = Sum(local, by_yx)
        last_sums.append(pending)

    def front_back(view, hidden_grad, dq, dk, dv):
        grad = (
            dot(dq, query_weight, NT) + dot(dk, key_weight, NT) + dot(dv, value_weight, NT)
        )
        extra, gain_part = norm_back(grad, view.astype(f32), first_gain)
        return (hidden_grad + extra).astype(bf16), gain_part

    small_grad, small_gain = front_back(
        small, small_hidden_grad, small_dq, small_dkv[0], small_dkv[1]
    )
    large_grad, large_gain = front_back(
        large,
        large_hidden_grad,
        jnp.concatenate(dqs, axis=1),
        jnp.concatenate([kv[0] for kv in dkvs], axis=1),
        jnp.concatenate([kv[1] for kv in dkvs], axis=1),
    )
    small_grad = restore(small_grad).astype(f32)
    large_grad = restore(large_grad).astype(f32)
    output_sum = Sum(output_grad, by_yx)
    gain_rows = jnp.concatenate(
        [large_gain + small_gain, second_gain_grad, query_gain_grad, context_gain_grad], axis=0
    )
    wide = width // tm
    gain_rows = jnp.transpose(gain_rows.reshape(4, tm, wide), (1, 0, 2)).astype(bf16)
    gain_rows = jnp.pad(gain_rows, ((0, 0), (0, 28), (0, 2 * LANES - wide)))
    gain_sum = Sum(gain_rows.reshape(tm * 32, 2 * LANES), by_yx)

    cross_total = cross_sum.finish()
    up_total = up_sum.finish()
    down_total = down_sum.finish()
    output_total = output_sum.finish()
    last_totals = [total.finish() for total in last_sums]
    gain_total = gain_sum.finish()
    cross_grads = [cross_total[:, i * width : (i + 1) * width] for i in range(4)]
    last_grads = [
        jnp.concatenate([total[:, i * part : (i + 1) * part] for total in last_totals], axis=1)
        for i in range(3)
    ]
    gain_grads = [gain_total[i, :wide] for i in range(4)]
    return (
        united_view,
        large_grad,
        small_grad,
        gain_grads[0],
        last_grads[0],
        last_grads[1],
        last_grads[2],
        output_total,
        gain_grads[1],
        up_total,
        down_total,
        gain_grads[2],
        gain_grads[3],
        cross_grads[1],
        cross_grads[2],
        cross_grads[3],
        cross_grads[0],
    )


def solution(mesh):
    token = P("seq", "tm", None)
    in_specs = (token, token, P("seq", "tm")) + (P(),) * 14 + (token,)
    vector, matrix = P("tm"), P("tm", None)
    out_specs = (
        (token, token, token, vector)
        + (matrix,) * 4
        + (vector, matrix, matrix, vector, vector)
        + (matrix,) * 4
    )
    return jax.shard_map(
        functools.partial(per_device, mesh.shape["tm"], mesh.shape["seq"]),
        mesh=mesh,
        in_specs=in_specs,
        out_specs=out_specs,
        check_vma=False,
    )
```
